32 devices in a mesh: groups: 2 (over y), blk: 8 (over z, x), tensor: 2 (over core).
Axes of the slice: x: 2, y: 2, z: 4, core: 2. Of those that a mesh axis runs over, the one named last changes fastest.
Arguments:
- hidden: bfloat16 [128, 64, 4096], P(('groups', 'blk'), None, 'tensor'), parts along dimension 0
- cotangent: bfloat16 [128, 64, 4096], P(('groups', 'blk'), None, 'tensor'), parts along dimension 0
- token_loss_mask: int32 [128, 64], P(('groups', 'blk')), parts along dimension 0, may hold values 0 or 1
- adapter_down_factor: bfloat16 [16, 4096], P(None, 'tensor'), may hold values from -0.09375 to 0.09375
- adapter_up_factor: bfloat16 [4096, 16], P('tensor'), may hold values from -0.09375 to 0.09375
- sign_table_salts: int32 [4], replicated, may hold values from 0 to 1048575
Outputs:
- kernel: float32 [128, 64], P(('groups', 'blk', 'tensor')), parts along dimension 0
The draws below stay inside these ranges and needn't reach their ends.
There are 2 independent parts, one for each index of `groups`. The reference program is written for one: setup_inputs(seed, part) draws one part's arguments, and reference() takes and returns one part's arrays. A program takes and returns all parts, laid end to end along the dimension named above; an argument that names none is the same for every part. Nothing has to cross between parts.
All inputs are finite; a program needn't handle non-finite values. No bound on the sum of `token_loss_mask` on one device may be relied on, other than what follows from the above.
Results may differ from the reference program's by a relative error of at most 0.00035.
Values may be sent and summed in bfloat16 or wider, within the bound.
No kernel may reach another device: no remote copies, remote signals or barrier semaphores. Data moves between devices by JAX's collectives and lax.ppermute only.
A program may use at most 64 MiB of HBM per device.

```python
import math
import jax
import jax.numpy as jnp
from jax import lax

MODEL_WIDTH = 4096
ADAPTER_RANK = 16
PROJ_ROWS = 256
SEQ = 64
EX_DEV = 8
PROJ = 8192
EXAMPLES = 64


def mixed_field(key, shared_weight, own_weight):
    shared_key, own_key = jax.random.split(key, 2)
    shared = jax.random.normal(shared_key, (SEQ, MODEL_WIDTH), jnp.float32)
    owned = jax.random.normal(own_key, (EXAMPLES, SEQ, MODEL_WIDTH), jnp.float32)
    value = shared_weight * shared[None] + own_weight * owned
    return value.astype(jnp.bfloat16)


def draw_hidden(key, part):
    key = jax.random.fold_in(key, 11)
    return mixed_field(key, 0.8, 0.6)


def draw_cotangent(key, part):
    key = jax.random.fold_in(key, 23)
    return mixed_field(key, 0.8, 0.6)


def touch_ends(array, key, smallest, high):
    index_at = [jax.random.randint(jax.random.fold_in(key, axis), (), 0, length) for axis, length in enumerate(array.shape)]
    longest = array.shape.index(max(array.shape))
    neighbour = index_at[:longest] + [(index_at[longest] + 1) % array.shape[longest]] + index_at[longest + 1:]
    return array.at[tuple(index_at)].set(smallest).at[tuple(neighbour)].set(high)


def shard_levels(rng, dims, shards, least, high):
    level = 1.0
    for dim, shards_of in shards:
        steps = jax.random.uniform(jax.random.fold_in(jax.random.fold_in(rng, 6), dim), (shards_of,), jnp.float32, least / len(shards), high / len(shards))
        level = level * jnp.repeat(jnp.exp(steps), dims[dim] // shards_of).reshape((-1,) + (1,) * (len(dims) - 1 - dim))
    return level


def bell_draw(rng, dims, spread, limit, pieces=(), held_as=jnp.bfloat16):
    gain = shard_levels(rng, dims, pieces, -0.22, 0.18) if pieces else 1.0
    drawn = jax.random.normal(rng, dims, jnp.float32) * spread * gain
    return jnp.minimum(jnp.maximum(drawn, -limit), limit).astype(held_as)


def setup_inputs(seed: int = 0, part: int = 0) -> dict:
    arg_keys = jax.random.split(jax.random.key(seed), 7)
    part_keys = jax.random.split(jax.random.fold_in(arg_keys[6], part), 7)
    return {
        "hidden": draw_hidden(jax.random.fold_in(jax.random.fold_in(arg_keys[6], part), 71), part),
        "cotangent": draw_cotangent(jax.random.fold_in(jax.random.fold_in(arg_keys[6], part), 71), part),
        "token_loss_mask": touch_ends((jax.random.randint(part_keys[2], (EXAMPLES, SEQ), 0, 4) < 3).astype(jnp.int32), jax.random.fold_in(part_keys[2], 1), 0, 1),
        "adapter_down_factor": bell_draw(arg_keys[3], (ADAPTER_RANK, MODEL_WIDTH), MODEL_WIDTH ** -0.5, 0.09375, ((1, 2),)),
        "adapter_up_factor": bell_draw(arg_keys[4], (MODEL_WIDTH, ADAPTER_RANK), MODEL_WIDTH ** -0.5, 0.09375, ((0, 2),)),
        "sign_table_salts": touch_ends(jax.random.randint(arg_keys[5], (4,), 0, 1048576), jax.random.fold_in(arg_keys[5], 1), 0, 1048575).astype(jnp.int32),
    }


def shifted(value, amount):
    return jnp.right_shift(value, amount) & (1 << 32 - amount) - 1

def rademacher(rows, cols, row_start, salt_value):
    row_ids = jnp.arange(rows, dtype=jnp.int32)[:, None] + row_start
    col_ids = jnp.arange(cols, dtype=jnp.int32)[None, :]
    hashed = (row_ids * cols + col_ids) * -1640531535 + salt_value * 668265263
    hashed = hashed ^ shifted(hashed, 15)
    hashed = hashed * -2048144789
    hashed = hashed ^ shifted(hashed, 13)
    hashed = hashed * -1028477387
    hashed = hashed ^ shifted(hashed, 16)
    lowbit = shifted(hashed, 9) & 1
    return (2 * lowbit - 1).astype(jnp.float32)

def reference(hidden, cotangent, token_loss_mask, adapter_down_factor, adapter_up_factor, sign_table_salts):
    zero_start = jnp.int32(0)
    highest = lax.Precision.HIGHEST
    sketch_up = rademacher(MODEL_WIDTH, PROJ_ROWS, zero_start, sign_table_salts[0])
    mixer_up = rademacher(ADAPTER_RANK, ADAPTER_RANK, zero_start, sign_table_salts[1])
    sketch_down = rademacher(MODEL_WIDTH, PROJ_ROWS, zero_start, sign_table_salts[2])
    mixer_down = rademacher(ADAPTER_RANK, ADAPTER_RANK, zero_start, sign_table_salts[3])
    feature_scale = 1.0 / math.sqrt(PROJ_ROWS * ADAPTER_RANK * ADAPTER_RANK * SEQ * MODEL_WIDTH)
    complete_down_factor = adapter_down_factor.astype(jnp.float32)
    complete_up_factor = adapter_up_factor.astype(jnp.float32)

    def featurize(block):
        acts, grads, weights = block
        masked_values = grads * weights[:, :, None].astype(jnp.bfloat16)
        acts_full = acts.astype(jnp.float32)
        masked_full = masked_values.astype(jnp.float32)
        adapter_in = jnp.einsum('gkv,xv->gkx', acts_full, complete_down_factor, precision=highest)
        adapter_back = jnp.einsum('gab,bz->gaz', masked_full, complete_up_factor, precision=highest)
        up_coeffs = jnp.dot(adapter_in, mixer_up, precision=highest).astype(jnp.bfloat16)
        down_coeffs = jnp.dot(adapter_back, mixer_down, precision=highest).astype(jnp.bfloat16)
        grad_up = jnp.einsum('esd,esr->edr', masked_full, up_coeffs.astype(jnp.float32), precision=highest).astype(jnp.bfloat16)
        grad_down = jnp.einsum('esd,esr->edr', acts_full, down_coeffs.astype(jnp.float32), precision=highest).astype(jnp.bfloat16)
        proj_up = jnp.einsum('edr,dj->ejr', grad_up.astype(jnp.float32), sketch_up, precision=highest)
        proj_down = jnp.einsum('edr,dj->ejr', grad_down.astype(jnp.float32), sketch_down, precision=highest)
        count = acts.shape[0]
        joined = jnp.concatenate([proj_up.reshape(count, PROJ_ROWS * ADAPTER_RANK), proj_down.reshape(count, PROJ_ROWS * ADAPTER_RANK)], axis=1)
        return (joined * feature_scale).astype(jnp.bfloat16)
    blocks = EXAMPLES // EX_DEV
    features = lax.map(featurize, (hidden.reshape(blocks, EX_DEV, SEQ, MODEL_WIDTH), cotangent.reshape(blocks, EX_DEV, SEQ, MODEL_WIDTH), token_loss_mask.reshape(blocks, EX_DEV, SEQ)))
    features = features.reshape(EXAMPLES, PROJ)
    return jnp.dot(features, features.T, preferred_element_type=jnp.float32)
```

```python
import math

import jax
import jax.numpy as jnp
from jax import lax
from jax.sharding import PartitionSpec as P

MODEL_WIDTH = 4096
ADAPTER_RANK = 16
PROJ_ROWS = 256
SEQ = 64


def shifted(value, amount):
    return jnp.right_shift(value, amount) & (1 << 32 - amount) - 1


def rademacher(rows, cols, row_start, salt_value):
    row_ids = jnp.arange(rows, dtype=jnp.int32)[:, None] + row_start
    col_ids = jnp.arange(cols, dtype=jnp.int32)[None, :]
    hashed = (row_ids * cols + col_ids) * -1640531535 + salt_value * 668265263
    hashed = hashed ^ shifted(hashed, 15)
    hashed = hashed * -2048144789
    hashed = hashed ^ shifted(hashed, 13)
    hashed = hashed * -1028477387
    hashed = hashed ^ shifted(hashed, 16)
    lowbit = shifted(hashed, 9) & 1
    return (2 * lowbit - 1).astype(jnp.float32)


def body(
    hidden, cotangent, token_loss_mask, adapter_down_factor, adapter_up_factor, sign_table_salts
):
    highest = lax.Precision.HIGHEST
    f32 = jnp.float32
    bf16 = jnp.bfloat16
    width_half = hidden.shape[2]
    ex_rows = hidden.shape[0]
    blk_count = lax.axis_size("blk")
    peers = blk_count * 2
    row_start = lax.axis_index("tensor") * width_half
    zero_start = jnp.int32(0)
    feature_scale = 1.0 / math.sqrt(PROJ_ROWS * ADAPTER_RANK * ADAPTER_RANK * SEQ * MODEL_WIDTH)
    mask = token_loss_mask.astype(f32)
    adapter_in = jnp.einsum("esd,rd->res", hidden, adapter_down_factor, preferred_element_type=f32)
    adapter_back = jnp.einsum(
        "esd,dr->res", cotangent, adapter_up_factor, preferred_element_type=f32
    ) * mask
    own = jnp.stack([adapter_in, adapter_back])
    other = lax.ppermute(own, "tensor", [(0, 1), (1, 0)])
    sketch_up = rademacher(width_half, PROJ_ROWS, row_start, sign_table_salts[0]).astype(bf16)
    sketch_down = rademacher(width_half, PROJ_ROWS, row_start, sign_table_salts[2]).astype(bf16)
    mixer_up = rademacher(ADAPTER_RANK, ADAPTER_RANK, zero_start, sign_table_salts[1])
    mixer_down = rademacher(ADAPTER_RANK, ADAPTER_RANK, zero_start, sign_table_salts[3])
    rows_up = jnp.einsum("esd,dj->esj", cotangent, sketch_up, preferred_element_type=f32)
    rows_up = (rows_up * mask[:, :, None]).astype(bf16)
    rows_down = jnp.einsum("esd,dj->esj", hidden, sketch_down, preferred_element_type=f32)
    rows_down = rows_down.astype(bf16)
    whole = own + other
    up_coeffs = jnp.einsum("xes,xr->res", whole[0], mixer_up, precision=highest).astype(bf16)
    down_coeffs = jnp.einsum("xes,xr->res", whole[1], mixer_down, precision=highest).astype(bf16)
    proj_up = jnp.einsum("res,esj->erj", up_coeffs, rows_up, preferred_element_type=f32)
    proj_down = jnp.einsum("res,esj->erj", down_coeffs, rows_down, preferred_element_type=f32)
    partial = jnp.concatenate([proj_up, proj_down], axis=1) * feature_scale
    rank_share = 2 * ADAPTER_RANK * PROJ_ROWS // peers
    parts = partial.astype(bf16).reshape(ex_rows, peers, rank_share).swapaxes(0, 1)
    got = lax.all_to_all(parts, ("blk", "tensor"), 0, 0, tiled=True)
    got = got.reshape(blk_count, 2, ex_rows, rank_share).astype(f32)
    features = (got[:, 0] + got[:, 1]).astype(bf16).reshape(blk_count * ex_rows, rank_share)
    pairs = jnp.einsum("ep,fp->ef", features, features, preferred_element_type=f32)
    rows_own = ex_rows // 2
    pairs = pairs.reshape(peers, rows_own, blk_count * ex_rows)
    terms = lax.all_to_all(pairs, ("blk", "tensor"), 0, 0, tiled=True)
    return jnp.sum(terms, axis=0)


def solution(mesh):
    placed = (
        P(("groups", "blk"), None, "tensor"),
        P(("groups", "blk"), None, "tensor"),
        P(("groups", "blk"), None),
        P(None, "tensor"),
        P("tensor", None),
        P(),
    )
    return jax.shard_map(
        body,
        mesh=mesh,
        in_specs=placed,
        out_specs=P(("groups", "blk", "tensor"), None),
        check_vma=False,
    )
```

```python
import functools
import math

import jax
import jax.numpy as jnp
from jax import lax
from jax.experimental import pallas as pl
from jax.experimental.pallas import tpu as pltpu
from jax.sharding import PartitionSpec as P

MODEL_WIDTH = 4096
ADAPTER_RANK = 16
PROJ_ROWS = 256
SEQ = 64
SCALE = 1.0 / math.sqrt(PROJ_ROWS * ADAPTER_RANK * ADAPTER_RANK * SEQ * MODEL_WIDTH)

F32 = jnp.float32
BF16 = jnp.bfloat16
I32 = jnp.int32
NT = (((1,), (1,)), ((), ()))
TN = (((0,), (0,)), ((), ()))
VMEM = pl.BlockSpec(memory_space=pltpu.VMEM)
SMEM = pl.BlockSpec(memory_space=pltpu.SMEM)
ANY = pl.BlockSpec(memory_space=pl.ANY)
PARAMS = pltpu.CompilerParams(vmem_limit_bytes=32 * 1024 * 1024)

INDEX_MUL = -1640531535
SALT_MUL = 668265263


def int32_wrap(value):
    return (value + 2**31) % 2**32 - 2**31


def hash_sign(hashed):
    hashed = hashed ^ lax.shift_right_logical(hashed, 15)
    hashed = hashed * -2048144789
    hashed = hashed ^ lax.shift_right_logical(hashed, 13)
    hashed = hashed * -1028477387
    hashed = hashed ^ lax.shift_right_logical(hashed, 16)
    return jnp.where((hashed & 512) != 0, 1.0, -1.0).astype(F32)


def iota(shape, dim):
    return lax.broadcasted_iota(I32, shape, dim)


def token_owner(ex_rows, tokens):
    return iota((ex_rows, tokens), 1) // SEQ == iota((ex_rows, tokens), 0)


def spread_mask(mask_ref):
    ex_rows, seq = mask_ref.shape
    tiled = jnp.concatenate([mask_ref[...].astype(F32)] * ex_rows, axis=1)
    return jnp.where(token_owner(ex_rows, ex_rows * seq), tiled, 0.0)


def rank_kernel(chunk, mask_ref, down_ref, up_ref, hid_hbm, cot_hbm, out_ref, hid, cot, sems):
    tokens = hid.shape[0]
    copies = []
    for kind, (src, dst) in enumerate(((hid_hbm, hid), (cot_hbm, cot))):
        for step in range(tokens // chunk):
            rows = pl.ds(step * chunk, chunk)
            copy = pltpu.make_async_copy(
                src.at[rows], dst.at[rows], sems.at[kind * (tokens // chunk) + step]
            )
            copy.start()
            copies.append((kind, step, copy))
    token_mask = jnp.sum(spread_mask(mask_ref), axis=0, keepdims=True)
    for kind, step, copy in copies:
        copy.wait()
        rows = slice(step * chunk, (step + 1) * chunk)
        held, factor = ((hid, down_ref), (cot, up_ref))[kind]
        got = lax.dot_general(held[rows, :], factor[...], NT, preferred_element_type=F32).T
        if kind == 1:
            got = jnp.where(token_mask[:, rows] != 0, got, 0.0)
        out_ref[kind * ADAPTER_RANK : (kind + 1) * ADAPTER_RANK, rows] = got


def rank_partials(hidden, cotangent, mask, down, up):
    tokens, width = hidden.shape
    chunk = tokens // 4
    return pl.pallas_call(
        functools.partial(rank_kernel, chunk),
        out_shape=jax.ShapeDtypeStruct((2 * ADAPTER_RANK, tokens), F32),
        in_specs=[VMEM, VMEM, VMEM, ANY, ANY],
        out_specs=VMEM,
        scratch_shapes=[
            pltpu.VMEM((tokens, width), BF16),
            pltpu.VMEM((tokens, width), BF16),
            pltpu.SemaphoreType.DMA((8,)),
        ],
        compiler_params=PARAMS,
        cost_estimate=pl.CostEstimate(
            flops=4 * tokens * width * 128, bytes_accessed=4 * tokens * width, transcendentals=0
        ),
    )(mask, down, up, hidden, cotangent)


def sketch_kernel(
    salts_ref, mask_ref, cot_hbm, hid_hbm, up_ref, down_ref, cot, hid, table_up, table_down, sems
):
    copy_cot = pltpu.make_async_copy(cot_hbm, cot, sems.at[0])
    copy_hid = pltpu.make_async_copy(hid_hbm, hid, sems.at[1])
    copy_cot.start()
    copy_hid.start()
    width = cot.shape[1]
    first = lax.axis_index("tensor") * int32_wrap(width * PROJ_ROWS * INDEX_MUL)
    group = 16
    index = iota((group, PROJ_ROWS), 0) * PROJ_ROWS + iota((group, PROJ_ROWS), 1)
    start = index * INDEX_MUL

    def fill(table, salt):
        offset = first + salt * SALT_MUL
        for step in range(width // group):
            shift = offset + int32_wrap(step * group * PROJ_ROWS * INDEX_MUL)
            table[step * group : (step + 1) * group, :] = hash_sign(start + shift).astype(BF16)

    fill(table_up, salts_ref[0])
    copy_cot.wait()
    rows = jnp.dot(cot[...], table_up[...], preferred_element_type=F32)
    spread = spread_mask(mask_ref)
    keep = lax.dot_general(
        spread.astype(BF16),
        jnp.ones((spread.shape[0], PROJ_ROWS), BF16),
        TN,
        preferred_element_type=F32,
    )
    up_ref[...] = jnp.where(keep != 0, rows, 0.0).astype(BF16)
    fill(table_down, salts_ref[2])
    copy_hid.wait()
    rows = jnp.dot(hid[...], table_down[...], preferred_element_type=F32)
    down_ref[...] = rows.astype(BF16)


def sketch_rows(salts, mask, cotangent, hidden):
    tokens, width = hidden.shape
    return pl.pallas_call(
        sketch_kernel,
        out_shape=[jax.ShapeDtypeStruct((tokens, PROJ_ROWS), BF16)] * 2,
        in_specs=[SMEM, VMEM, ANY, ANY],
        out_specs=[VMEM, VMEM],
        scratch_shapes=[
            pltpu.VMEM((tokens, width), BF16),
            pltpu.VMEM((tokens, width), BF16),
            pltpu.VMEM((width, PROJ_ROWS), BF16),
            pltpu.VMEM((width, PROJ_ROWS), BF16),
            pltpu.SemaphoreType.DMA((2,)),
        ],
        compiler_params=PARAMS,
        cost_estimate=pl.CostEstimate(
            flops=4 * tokens * width * PROJ_ROWS,
            bytes_accessed=4 * tokens * width,
            transcendentals=0,
        ),
    )(salts, mask, cotangent, hidden)


def feature_kernel(ex_rows, salts_ref, own_ref, other_ref, up_ref, down_ref, *rest):
    *out_refs, held = rest
    tokens = own_ref.shape[1]
    rows = ADAPTER_RANK * ex_rows
    row = iota((rows, ADAPTER_RANK), 0)
    mix_index = (iota((rows, ADAPTER_RANK), 1) * ADAPTER_RANK + row // ex_rows) * INDEX_MUL
    owned = iota((rows, tokens), 1) // SEQ == iota((rows, tokens), 0) % ex_rows
    for kind, rows_ref in enumerate((up_ref, down_ref)):
        ranks = slice(kind * ADAPTER_RANK, (kind + 1) * ADAPTER_RANK)
        rest_of = own_ref[ranks, :] + other_ref[ranks, :]
        salt = salts_ref[1 + 2 * kind]
        mixer = hash_sign(mix_index + salt * SALT_MUL).astype(BF16)
        coeffs = jnp.zeros((rows, tokens), F32)
        for _ in range(3):
            term = rest_of.astype(BF16)
            rest_of = rest_of - term.astype(F32)
            coeffs = coeffs + jnp.dot(mixer, term, preferred_element_type=F32)
        coeffs = jnp.where(owned, coeffs, 0.0).astype(BF16)
        projected = jnp.dot(coeffs, rows_ref[...], preferred_element_type=F32)
        held[kind * rows : (kind + 1) * rows, :] = (projected * SCALE).astype(BF16)
    if len(out_refs) == 1:
        out_refs[0][...] = held[...]
        return
    share = held.shape[0] // len(out_refs)
    me = lax.axis_index("blk") * 2 + lax.axis_index("tensor")
    for step, out_ref in enumerate(out_refs):
        first = pl.multiple_of((me ^ step) * share, share)
        out_ref[...] = held[pl.ds(first, share), :]


def feature_parts(salts, own, other, up_rows, down_rows, ex_rows, parts):
    rows = 2 * ADAPTER_RANK * ex_rows
    return pl.pallas_call(
        functools.partial(feature_kernel, ex_rows),
        out_shape=[jax.ShapeDtypeStruct((rows // parts, PROJ_ROWS), BF16)] * parts,
        in_specs=[SMEM, VMEM, VMEM, VMEM, VMEM],
        out_specs=[VMEM] * parts,
        scratch_shapes=[pltpu.VMEM((rows, PROJ_ROWS), BF16)],
        compiler_params=PARAMS,
    )(salts, own, other, up_rows, down_rows)


def pair_kernel(ex_rows, *refs):
    peers = (len(refs) - 2) // 2
    got_refs, out_refs = refs[:peers], refs[peers : 2 * peers]
    features, pairs = refs[2 * peers :]
    ranks = features.shape[0]
    blk = lax.axis_index("blk")
    core = lax.axis_index("tensor")
    for step in range(peers // 2):
        whole = got_refs[2 * step][...].astype(F32) + got_refs[2 * step + 1][...].astype(F32)
        first = pl.multiple_of((blk ^ step) * ex_rows, ex_rows)
        for rank in range(ranks):
            features[rank, pl.ds(first, ex_rows), :] = whole[
                rank * ex_rows : (rank + 1) * ex_rows, :
            ]
    total = None
    for rank in range(ranks):
        rounded = features[rank].astype(BF16)
        term = lax.dot_general(rounded, rounded, NT, preferred_element_type=F32)
        total = term if total is None else total + term
    pairs[...] = total
    half = ex_rows // 2
    for step, out_ref in enumerate(out_refs):
        first = pl.multiple_of((blk ^ (step // 2)) * ex_rows, ex_rows)
        rows = pairs[pl.ds(first, ex_rows), :]
        out_ref[...] = jnp.where((core ^ (step % 2)) == 0, rows[:half], rows[half:])


def pair_parts(got, ex_rows):
    peers = len(got)
    examples = ex_rows * peers // 2
    ranks = got[0].shape[0] // ex_rows
    return pl.pallas_call(
        functools.partial(pair_kernel, ex_rows),
        out_shape=[jax.ShapeDtypeStruct((ex_rows // 2, examples), F32)] * peers,
        in_specs=[VMEM] * peers,
        out_specs=[VMEM] * peers,
        scratch_shapes=[
            pltpu.VMEM((ranks, examples, PROJ_ROWS), F32),
            pltpu.VMEM((examples, examples), F32),
        ],
        compiler_params=PARAMS,
    )(*got)


def swap_parts(parts):
    peers = len(parts)
    return [parts[0]] + [
        lax.ppermute(parts[step], ("blk", "tensor"), [(i, i ^ step) for i in range(peers)])
        for step in range(1, peers)
    ]


def body(
    hidden, cotangent, token_loss_mask, adapter_down_factor, adapter_up_factor, sign_table_salts
):
    ex_rows, seq, width_half = hidden.shape
    blk_count = lax.axis_size("blk")
    peers = blk_count * 2
    hidden = hidden.reshape(ex_rows * seq, width_half)
    cotangent = cotangent.reshape(ex_rows * seq, width_half)
    own = rank_partials(
        hidden, cotangent, token_loss_mask, adapter_down_factor, adapter_up_factor.T
    )
    other = lax.ppermute(own, "tensor", [(0, 1), (1, 0)])
    up_rows, down_rows = sketch_rows(sign_table_salts, token_loss_mask, cotangent, hidden)
    if 2 * ADAPTER_RANK % peers == 0:
        parts = feature_parts(
            sign_table_salts, own, other, up_rows, down_rows, ex_rows, peers
        )
        terms = swap_parts(pair_parts(swap_parts(parts), ex_rows))
        return functools.reduce(lambda a, b: a + b, terms)
    (whole,) = feature_parts(sign_table_salts, own, other, up_rows, down_rows, ex_rows, 1)
    share = 2 * ADAPTER_RANK * PROJ_ROWS // peers
    parts = whole.reshape(2 * ADAPTER_RANK, ex_rows, PROJ_ROWS // share, share)
    parts = parts.swapaxes(1, 2).reshape(peers, ex_rows, share)
    got = lax.all_to_all(parts, ("blk", "tensor"), 0, 0, tiled=True)
    got = got.reshape(blk_count, 2, ex_rows, share).astype(F32)
    features = (got[:, 0] + got[:, 1]).astype(BF16).reshape(blk_count * ex_rows, share)
    pairs = jnp.einsum("ep,fp->ef", features, features, preferred_element_type=F32)
    pairs = pairs.reshape(peers, ex_rows // 2, blk_count * ex_rows)
    return jnp.sum(lax.all_to_all(pairs, ("blk", "tensor"), 0, 0, tiled=True), axis=0)


def solution(mesh):
    placed = (
        P(("groups", "blk"), None, "tensor"),
        P(("groups", "blk"), None, "tensor"),
        P(("groups", "blk"), None),
        P(None, "tensor"),
        P("tensor", None),
        P(),
    )
    return jax.shard_map(
        body,
        mesh=mesh,
        in_specs=placed,
        out_specs=P(("groups", "blk", "tensor"), None),
        check_vma=False,
    )
```

```python
import functools
import math

import jax
import jax.numpy as jnp
from jax import lax
from jax.experimental import pallas as pl
from jax.experimental.pallas import tpu as pltpu
from jax.sharding import PartitionSpec as P

MODEL_WIDTH = 4096
ADAPTER_RANK = 16
PROJ_ROWS = 256
SEQ = 64
SCALE = 1.0 / math.sqrt(PROJ_ROWS * ADAPTER_RANK * ADAPTER_RANK * SEQ * MODEL_WIDTH)

F32 = jnp.float32
BF16 = jnp.bfloat16
I32 = jnp.int32
NT = (((1,), (1,)), ((), ()))
TN = (((0,), (0,)), ((), ()))
VMEM = pl.BlockSpec(memory_space=pltpu.VMEM)
SMEM = pl.BlockSpec(memory_space=pltpu.SMEM)
ANY = pl.BlockSpec(memory_space=pl.ANY)
PARAMS = pltpu.CompilerParams(vmem_limit_bytes=60 * 1024 * 1024)

INDEX_MUL = -1640531535
SALT_MUL = 668265263


def int32_wrap(value):
    return (value + 2**31) % 2**32 - 2**31


def hash_sign(hashed):
    hashed = hashed ^ lax.shift_right_logical(hashed, 15)
    hashed = hashed * -2048144789
    hashed = hashed ^ lax.shift_right_logical(hashed, 13)
    hashed = hashed * -1028477387
    hashed = hashed ^ lax.shift_right_logical(hashed, 16)
    return jnp.where((hashed & 512) != 0, 1.0, -1.0).astype(F32)


def iota(shape, dim):
    return lax.broadcasted_iota(I32, shape, dim)


def token_owner(ex_rows, tokens):
    return iota((ex_rows, tokens), 1) // SEQ == iota((ex_rows, tokens), 0)


def spread_mask(mask_ref):
    ex_rows, seq = mask_ref.shape
    tiled = jnp.concatenate([mask_ref[...].astype(F32)] * ex_rows, axis=1)
    return jnp.where(token_owner(ex_rows, ex_rows * seq), tiled, 0.0)


def rank_kernel(steps, mask_hbm, down_hbm, up_hbm, hid_hbm, cot_hbm, out_ref, mask, down, up, hid, cot, sems):
    width = hid.shape[1]
    share = width // steps
    slots = iter(range(2 * steps + 3))

    def begin(src, dst):
        copy = pltpu.make_async_copy(src, dst, sems.at[next(slots)])
        copy.start()
        return copy

    small = [begin(down_hbm, down), begin(up_hbm, up), begin(mask_hbm, mask)]
    streams = []
    for src, dst in ((hid_hbm, hid), (cot_hbm, cot)):
        parts = [pl.ds(step * share, share) for step in range(steps)]
        streams.append([begin(src.at[:, part], dst.at[:, part]) for part in parts])
    for copy in small:
        copy.wait()
    token_mask = jnp.sum(spread_mask(mask), axis=0, keepdims=True)
    for kind, (held, factor) in enumerate(((hid, down), (cot, up))):
        total = None
        for step, copy in enumerate(streams[kind]):
            copy.wait()
            part = slice(step * share, (step + 1) * share)
            term = lax.dot_general(held[:, part], factor[:, part], NT, preferred_element_type=F32)
            total = term if total is None else total + term
        total = total.T
        if kind == 1:
            total = jnp.where(token_mask != 0, total, 0.0)
        out_ref[kind * ADAPTER_RANK : (kind + 1) * ADAPTER_RANK, :] = total


def rank_partials(hidden, cotangent, mask, down, up):
    tokens, width = hidden.shape
    steps = 4
    return pl.pallas_call(
        functools.partial(rank_kernel, steps),
        out_shape=jax.ShapeDtypeStruct((2 * ADAPTER_RANK, tokens), F32),
        in_specs=[ANY] * 5,
        out_specs=VMEM,
        scratch_shapes=[
            pltpu.VMEM(mask.shape, I32),
            pltpu.VMEM((ADAPTER_RANK, width), BF16),
            pltpu.VMEM((ADAPTER_RANK, width), BF16),
            pltpu.VMEM((tokens, width), BF16),
            pltpu.VMEM((tokens, width), BF16),
            pltpu.SemaphoreType.DMA((2 * steps + 3,)),
        ],
        compiler_params=PARAMS,
        cost_estimate=pl.CostEstimate(
            flops=4 * tokens * width * 128, bytes_accessed=4 * tokens * width, transcendentals=0
        ),
    )(mask, down, up, hidden, cotangent)


def sketch_kernel(
    salts_ref, mask_ref, cot_hbm, hid_hbm, up_ref, down_ref, cot, hid, table_up, table_down, sems
):
    copy_cot = pltpu.make_async_copy(cot_hbm, cot, sems.at[0])
    copy_hid = pltpu.make_async_copy(hid_hbm, hid, sems.at[1])
    copy_cot.start()
    copy_hid.start()
    width = cot.shape[1]
    first = lax.axis_index("tensor") * int32_wrap(width * PROJ_ROWS * INDEX_MUL)
    group = 16
    index = iota((group, PROJ_ROWS), 0) * PROJ_ROWS + iota((group, PROJ_ROWS), 1)
    start = index * INDEX_MUL

    def fill(table, salt):
        offset = first + salt * SALT_MUL
        for step in range(width // group):
            shift = offset + int32_wrap(step * group * PROJ_ROWS * INDEX_MUL)
            table[step * group : (step + 1) * group, :] = hash_sign(start + shift).astype(BF16)

    fill(table_up, salts_ref[0])
    copy_cot.wait()
    rows = jnp.dot(cot[...], table_up[...], preferred_element_type=F32)
    spread = spread_mask(mask_ref)
    keep = lax.dot_general(
        spread.astype(BF16),
        jnp.ones((spread.shape[0], PROJ_ROWS), BF16),
        TN,
        preferred_element_type=F32,
    )
    up_ref[...] = jnp.where(keep != 0, rows, 0.0).astype(BF16)
    fill(table_down, salts_ref[2])
    copy_hid.wait()
    rows = jnp.dot(hid[...], table_down[...], preferred_element_type=F32)
    down_ref[...] = rows.astype(BF16)


def sketch_rows(salts, mask, cotangent, hidden):
    tokens, width = hidden.shape
    return pl.pallas_call(
        sketch_kernel,
        out_shape=[jax.ShapeDtypeStruct((tokens, PROJ_ROWS), BF16)] * 2,
        in_specs=[SMEM, VMEM, ANY, ANY],
        out_specs=[VMEM, VMEM],
        scratch_shapes=[
            pltpu.VMEM((tokens, width), BF16),
            pltpu.VMEM((tokens, width), BF16),
            pltpu.VMEM((width, PROJ_ROWS), BF16),
            pltpu.VMEM((width, PROJ_ROWS), BF16),
            pltpu.SemaphoreType.DMA((2,)),
        ],
        compiler_params=PARAMS,
        cost_estimate=pl.CostEstimate(
            flops=4 * tokens * width * PROJ_ROWS,
            bytes_accessed=4 * tokens * width,
            transcendentals=0,
        ),
    )(salts, mask, cotangent, hidden)


def feature_kernel(ex_rows, salts_ref, own_ref, other_ref, up_ref, down_ref, out_ref):
    tokens = own_ref.shape[1]
    rows = ADAPTER_RANK * ex_rows
    row = iota((rows, ADAPTER_RANK), 0)
    mix_index = (iota((rows, ADAPTER_RANK), 1) * ADAPTER_RANK + row // ex_rows) * INDEX_MUL
    owned = iota((rows, tokens), 1) // SEQ == iota((rows, tokens), 0) % ex_rows
    for kind, rows_ref in enumerate((up_ref, down_ref)):
        ranks = slice(kind * ADAPTER_RANK, (kind + 1) * ADAPTER_RANK)
        rest_of = own_ref[ranks, :] + other_ref[ranks, :]
        salt = salts_ref[1 + 2 * kind]
        mixer = hash_sign(mix_index + salt * SALT_MUL).astype(BF16)
        coeffs = jnp.zeros((rows, tokens), F32)
        for _ in range(3):
            term = rest_of.astype(BF16)
            rest_of = rest_of - term.astype(F32)
            coeffs = coeffs + jnp.dot(mixer, term, preferred_element_type=F32)
        coeffs = jnp.where(owned, coeffs, 0.0).astype(BF16)
        projected = jnp.dot(coeffs, rows_ref[...], preferred_element_type=F32)
        out_ref[kind * rows : (kind + 1) * rows, :] = (projected * SCALE).astype(BF16)


def feature_terms(salts, own, other, up_rows, down_rows, ex_rows):
    return pl.pallas_call(
        functools.partial(feature_kernel, ex_rows),
        out_shape=jax.ShapeDtypeStruct((2 * ADAPTER_RANK * ex_rows, PROJ_ROWS), BF16),
        in_specs=[SMEM, VMEM, VMEM, VMEM, VMEM],
        out_specs=VMEM,
    )(salts, own, other, up_rows, down_rows)


def pair_kernel(ex_rows, got_ref, peer_ref, out_ref):
    blocks, rows, _ = got_ref.shape
    whole = got_ref[...].astype(F32) + peer_ref[...].astype(F32)
    total = None
    for first in range(0, rows, ex_rows):
        rank = jnp.concatenate([whole[b, first : first + ex_rows] for b in range(blocks)], axis=0)
        rank = rank.astype(BF16)
        term = lax.dot_general(rank, rank, NT, preferred_element_type=F32)
        total = term if total is None else total + term
    half = ex_rows // 2
    core = lax.axis_index("tensor")
    out_ref[...] = jnp.zeros_like(out_ref)
    for b in range(blocks):
        block = total[b * ex_rows : (b + 1) * ex_rows]
        out_ref[b, :half, : total.shape[1]] = jnp.where(core == 0, block[:half], block[half:])


def pair_terms(got, peer, ex_rows):
    blocks = got.shape[0]
    return pl.pallas_call(
        functools.partial(pair_kernel, ex_rows),
        out_shape=jax.ShapeDtypeStruct((blocks, 8, 128), F32),
        in_specs=[VMEM, VMEM],
        out_specs=VMEM,
    )(got, peer)


def swap_cores(value):
    return lax.ppermute(value, "tensor", [(0, 1), (1, 0)])


def body(
    hidden, cotangent, token_loss_mask, adapter_down_factor, adapter_up_factor, sign_table_salts
):
    ex_rows, seq, width_half = hidden.shape
    blocks = lax.axis_size("blk")
    hidden = hidden.reshape(ex_rows * seq, width_half)
    cotangent = cotangent.reshape(ex_rows * seq, width_half)
    own = rank_partials(
        hidden, cotangent, token_loss_mask, adapter_down_factor, adapter_up_factor.T
    )
    other = swap_cores(own)
    up_rows, down_rows = sketch_rows(sign_table_salts, token_loss_mask, cotangent, hidden)
    parts = feature_terms(sign_table_salts, own, other, up_rows, down_rows, ex_rows)
    if 2 * ADAPTER_RANK % blocks == 0 and blocks * ex_rows <= 128:
        parts = parts.reshape(blocks, -1, PROJ_ROWS)
        got = lax.all_to_all(parts, "blk", 0, 0, tiled=True)
        pairs = pair_terms(got, swap_cores(got), ex_rows)
        whole = jnp.sum(lax.all_to_all(pairs, "blk", 0, 0, tiled=True), axis=0)
        return whole[: ex_rows // 2, : blocks * ex_rows]
    else:
        share = 2 * ADAPTER_RANK * PROJ_ROWS // blocks
        parts = parts.reshape(2 * ADAPTER_RANK, ex_rows, PROJ_ROWS // share, share)
        parts = parts.swapaxes(1, 2).reshape(blocks, ex_rows, share)
        got = lax.all_to_all(parts, "blk", 0, 0, tiled=True)
        features = (got.astype(F32) + swap_cores(got).astype(F32)).astype(BF16)
        rows = features.reshape(blocks, 2, ex_rows // 2, share)
        rows = lax.dynamic_index_in_dim(rows, lax.axis_index("tensor"), 1, keepdims=False)
        pairs = jnp.einsum(
            "bep,fp->bef",
            rows,
            features.reshape(blocks * ex_rows, share),
            preferred_element_type=F32,
        )
    return jnp.sum(lax.all_to_all(pairs, "blk", 0, 0, tiled=True), axis=0)


def solution(mesh):
    placed = (
        P(("groups", "blk"), None, "tensor"),
        P(("groups", "blk"), None, "tensor"),
        P(("groups", "blk"), None),
        P(None, "tensor"),
        P("tensor", None),
        P(),
    )
    return jax.shard_map(
        body,
        mesh=mesh,
        in_specs=placed,
        out_specs=P(("groups", "blk", "tensor"), None),
        check_vma=False,
    )
```

```python
import functools
import math

import jax
import jax.numpy as jnp
from jax import lax
from jax.experimental import pallas as pl
from jax.experimental.pallas import tpu as pltpu
from jax.sharding import PartitionSpec as P

MODEL_WIDTH = 4096
ADAPTER_RANK = 16
PROJ_ROWS = 256
SEQ = 64
SCALE = 1.0 / math.sqrt(PROJ_ROWS * ADAPTER_RANK * ADAPTER_RANK * SEQ * MODEL_WIDTH)
PIECES = 3

F32 = jnp.float32
BF16 = jnp.bfloat16
I32 = jnp.int32
NT = (((1,), (1,)), ((), ()))
VMEM = pl.BlockSpec(memory_space=pltpu.VMEM)
SMEM = pl.BlockSpec(memory_space=pltpu.SMEM)
HBM = pl.BlockSpec(memory_space=pltpu.HBM)

INDEX_MUL = -1640531535
SALT_MUL = 668265263


def int32_wrap(value):
    return (value + 2**31) % 2**32 - 2**31


def hash_sign(hashed):
    hashed = hashed ^ lax.shift_right_logical(hashed, 15)
    hashed = hashed * -2048144789
    hashed = hashed ^ lax.shift_right_logical(hashed, 13)
    hashed = hashed * -1028477387
    hashed = hashed ^ lax.shift_right_logical(hashed, 16)
    return jnp.where((hashed & 512) != 0, 1.0, -1.0).astype(F32)


def iota(shape, dim):
    return lax.broadcasted_iota(I32, shape, dim)


def token_row(mask):
    ex_rows, seq = mask.shape
    tokens = ex_rows * seq
    tiled = jnp.concatenate([mask.astype(F32)] * ex_rows, axis=1)
    owner = iota((ex_rows, tokens), 1) // seq == iota((ex_rows, tokens), 0)
    return jnp.sum(jnp.where(owner, tiled, 0.0), axis=0, keepdims=True)


def split_pieces(value):
    pieces = []
    for _ in range(PIECES):
        pieces.append(value.astype(BF16))
        value = value - pieces[-1].astype(F32)
    return jnp.concatenate(pieces, axis=0)


def rows_kernel(
    salts_hbm, mask_hbm, down_hbm, up_hbm, hid_hbm, cot_hbm,
    keep_ref, send_ref,
    salts, mask, far_left, near_left, far, near, sems,
):
    tokens, width = near.shape
    core = lax.axis_index("tensor")
    parts = 4
    share = tokens // parts

    def copies(inputs, factor, left, held, first):
        out = [
            pltpu.make_async_copy(
                inputs.at[pl.ds(i * share, share)],
                held.at[pl.ds(i * share, share)],
                sems.at[first + i],
            )
            for i in range(parts)
        ]
        rows = left.at[pl.ds(PROJ_ROWS, ADAPTER_RANK)]
        return out + [pltpu.make_async_copy(factor, rows, sems.at[first + parts])]

    def wait_for(left, held, first):
        for copy in copies(hid_hbm, down_hbm, left, held, first):
            copy.wait()

    salts_copy = pltpu.make_async_copy(salts_hbm, salts, sems.at[2 * parts + 3])
    salts_copy.start()
    mask_copy = pltpu.make_async_copy(mask_hbm, mask, sems.at[2 * parts + 2])
    mask_copy.start()

    @pl.when(core == 0)
    def _():
        for copy in copies(hid_hbm, down_hbm, far_left, far, 0):
            copy.start()
        for copy in copies(cot_hbm, up_hbm, near_left, near, parts + 1):
            copy.start()

    @pl.when(core == 1)
    def _():
        for copy in copies(cot_hbm, up_hbm, far_left, far, 0):
            copy.start()
        for copy in copies(hid_hbm, down_hbm, near_left, near, parts + 1):
            copy.start()

    high, wide = 16, 256
    index = iota((high, wide), 1) * PROJ_ROWS + iota((high, wide), 0)
    start = index * INDEX_MUL
    first = core * int32_wrap(width * PROJ_ROWS * INDEX_MUL)

    def fill(left, salt):
        offset = first + salt * SALT_MUL
        for col in range(0, width, wide):
            for row in range(0, PROJ_ROWS, high):
                shift = offset + int32_wrap((col * PROJ_ROWS + row) * INDEX_MUL)
                signs = hash_sign(start + shift).astype(BF16)
                left[row : row + high, col : col + wide] = signs

    salts_copy.wait()
    fill(far_left, salts[2 - 2 * core])
    mask_copy.wait()
    counted = token_row(mask[...]) != 0
    wait_for(far_left, far, 0)
    got = lax.dot_general(far_left[...], far[...], NT, preferred_element_type=F32)
    got = jnp.where(counted | (core == 0), got, 0.0)
    send_ref[:PROJ_ROWS] = got[:PROJ_ROWS].astype(BF16)
    keep_ref[PROJ_ROWS:] = split_pieces(got[PROJ_ROWS:])
    fill(near_left, salts[2 * core])
    wait_for(near_left, near, parts + 1)
    got = lax.dot_general(near_left[...], near[...], NT, preferred_element_type=F32)
    got = jnp.where(counted | (core == 1), got, 0.0)
    keep_ref[:PROJ_ROWS] = got[:PROJ_ROWS].astype(BF16)
    send_ref[PROJ_ROWS:] = split_pieces(got[PROJ_ROWS:])


def sketch_rows(salts, mask, down, up, hidden, cotangent):
    tokens, width = hidden.shape
    rows = PROJ_ROWS + PIECES * ADAPTER_RANK
    arrays = (salts, mask, down, up, hidden, cotangent)
    return pl.pallas_call(
        rows_kernel,
        out_shape=[jax.ShapeDtypeStruct((rows, tokens), BF16)] * 2,
        in_specs=[HBM] * 6,
        out_specs=[VMEM, VMEM],
        scratch_shapes=[
            pltpu.SMEM(salts.shape, I32),
            pltpu.VMEM(mask.shape, I32),
            pltpu.VMEM((PROJ_ROWS + ADAPTER_RANK, width), BF16),
            pltpu.VMEM((PROJ_ROWS + ADAPTER_RANK, width), BF16),
            pltpu.VMEM((tokens, width), BF16),
            pltpu.VMEM((tokens, width), BF16),
            pltpu.SemaphoreType.DMA((12,)),
        ],
        compiler_params=pltpu.CompilerParams(vmem_limit_bytes=32 * 1024 * 1024),
    )(*[pltpu.with_memory_space_constraint(x, pltpu.HBM) for x in arrays])


def feature_kernel(ex_rows, salts_ref, own_ref, other_ref, *rest):
    *out_refs, held = rest
    tokens = own_ref.shape[1]
    rows = ADAPTER_RANK * ex_rows
    salt = salts_ref[1 + 2 * lax.axis_index("tensor")]
    shape = (rows, 2 * PIECES * ADAPTER_RANK)
    mixed, rank = iota(shape, 0) // ex_rows, iota(shape, 1) % ADAPTER_RANK
    mixer = hash_sign((rank * ADAPTER_RANK + mixed) * INDEX_MUL + salt * SALT_MUL).astype(BF16)
    pieces = jnp.concatenate([own_ref[PROJ_ROWS:], other_ref[PROJ_ROWS:]], axis=0)
    coeffs = jnp.dot(mixer, pieces, preferred_element_type=F32)
    owned = iota((rows, tokens), 1) // SEQ == iota((rows, tokens), 0) % ex_rows
    coeffs = jnp.where(owned, coeffs, 0.0).astype(BF16)
    projected = lax.dot_general(coeffs, own_ref[:PROJ_ROWS], NT, preferred_element_type=F32)
    projected += lax.dot_general(coeffs, other_ref[:PROJ_ROWS], NT, preferred_element_type=F32)
    held[...] = (projected * SCALE).astype(BF16)
    if len(out_refs) == 1:
        out_refs[0][...] = held[...]
        return
    share = rows // len(out_refs)
    high = lax.axis_index("blk") // 2
    for step, out_ref in enumerate(out_refs):
        out_ref[...] = held[pl.ds(pl.multiple_of((high ^ step) * share, share), share), :]


def feature_parts(salts, own, other, ex_rows, parts):
    rows = ADAPTER_RANK * ex_rows
    return pl.pallas_call(
        functools.partial(feature_kernel, ex_rows),
        out_shape=[jax.ShapeDtypeStruct((rows // parts, PROJ_ROWS), BF16)] * parts,
        in_specs=[SMEM, VMEM, VMEM],
        out_specs=[VMEM] * parts,
        scratch_shapes=[pltpu.VMEM((rows, PROJ_ROWS), BF16)],
    )(salts, own, other)


def pair_kernel(ex_rows, own_ref, other_ref, *rest):
    *out_refs, features = rest
    parts, rows, _ = own_ref.shape
    blk = lax.axis_index("blk")
    own = own_ref[...].astype(F32)
    other = other_ref[...].astype(F32)
    for step in range(parts):
        for held, block in ((own[step], blk ^ (2 * step)), (other[step], blk ^ (2 * step + 1))):
            first = pl.multiple_of(block * ex_rows, ex_rows)
            for rank in range(rows // ex_rows):
                features[rank, pl.ds(first, ex_rows), :] = held[
                    rank * ex_rows : (rank + 1) * ex_rows
                ]
    total = None
    for rank in range(rows // ex_rows):
        part = slice(rank * ex_rows, (rank + 1) * ex_rows)
        left = jnp.concatenate([own[step, part] for step in range(parts)], axis=0).astype(BF16)
        term = lax.dot_general(
            left, features[rank].astype(BF16), NT, preferred_element_type=F32
        )
        total = term if total is None else total + term
    for step, out_ref in enumerate(out_refs):
        out_ref[...] = total[step * ex_rows : (step + 1) * ex_rows]


def pair_parts(own, other, ex_rows):
    parts, rows, wide = own.shape
    examples = 2 * parts * ex_rows
    return pl.pallas_call(
        functools.partial(pair_kernel, ex_rows),
        out_shape=[jax.ShapeDtypeStruct((ex_rows, examples), F32)] * parts,
        in_specs=[VMEM, VMEM],
        out_specs=[VMEM] * parts,
        scratch_shapes=[pltpu.VMEM((rows // ex_rows, examples, wide), F32)],
    )(own, other)


def halves_kernel(*refs):
    *term_refs, keep_ref, send_ref = refs
    total = functools.reduce(lambda a, b: a + b, [ref[...] for ref in term_refs])
    half = keep_ref.shape[0]
    low = lax.axis_index("tensor") == 0
    keep_ref[...] = jnp.where(low, total[:half], total[half:])
    send_ref[...] = jnp.where(low, total[half:], total[:half])


def sum_halves(*terms):
    rows, examples = terms[0].shape
    return pl.pallas_call(
        halves_kernel,
        out_shape=[jax.ShapeDtypeStruct((rows // 2, examples), F32)] * 2,
        in_specs=[VMEM] * len(terms),
        out_specs=[VMEM, VMEM],
    )(*terms)


def swap_cores(value):
    return lax.ppermute(value, "tensor", [(0, 1), (1, 0)])


def swap_blocks(value, step):
    blocks = lax.axis_size("blk")
    return lax.ppermute(value, "blk", [(i, i ^ step) for i in range(blocks)])


def body(
    hidden, cotangent, token_loss_mask, adapter_down_factor, adapter_up_factor, sign_table_salts
):
    ex_rows, seq, width_half = hidden.shape
    blocks = lax.axis_size("blk")
    keep, send = sketch_rows(
        sign_table_salts,
        token_loss_mask,
        adapter_down_factor,
        adapter_up_factor.T,
        hidden.reshape(ex_rows * seq, width_half),
        cotangent.reshape(ex_rows * seq, width_half),
    )
    other = swap_cores(send)
    if blocks == 8 and ex_rows == 8:
        parts = feature_parts(sign_table_salts, keep, other, ex_rows, 4)
        own = jnp.stack([parts[0]] + [swap_blocks(parts[k], 2 * k) for k in (1, 2, 3)])
        rows = pair_parts(own, swap_blocks(own, 1), ex_rows)
        terms = [rows[0]] + [swap_blocks(rows[k], 2 * k) for k in (1, 2, 3)]
        keep, send = sum_halves(*terms)
        return keep + swap_cores(send)
    (whole,) = feature_parts(sign_table_salts, keep, other, ex_rows, 1)
    share = ADAPTER_RANK * PROJ_ROWS // blocks
    parts = whole.reshape(ADAPTER_RANK, ex_rows, PROJ_ROWS // share, share)
    parts = parts.swapaxes(1, 2).reshape(blocks, ex_rows, share)
    features = lax.all_to_all(parts, "blk", 0, 0, tiled=True).reshape(blocks * ex_rows, share)
    pairs = jnp.einsum("ep,fp->ef", features, features, preferred_element_type=F32)
    pairs = pairs.reshape(blocks, ex_rows, blocks * ex_rows)
    total = jnp.sum(lax.all_to_all(pairs, "blk", 0, 0, tiled=True), axis=0)
    halves = total.reshape(2, ex_rows // 2, blocks * ex_rows)
    core = lax.axis_index("tensor")
    send = lax.dynamic_index_in_dim(halves, 1 - core, 0, keepdims=False)
    return lax.dynamic_index_in_dim(halves, core, 0, keepdims=False) + swap_cores(send)


def solution(mesh):
    placed = (
        P(("groups", "blk"), None, "tensor"),
        P(("groups", "blk"), None, "tensor"),
        P(("groups", "blk"), None),
        P(None, "tensor"),
        P("tensor", None),
        P(),
    )
    return jax.shard_map(
        body,
        mesh=mesh,
        in_specs=placed,
        out_specs=P(("groups", "blk", "tensor"), None),
        check_vma=False,
    )
```

```python
import functools
import math

import jax
import jax.numpy as jnp
from jax import lax
from jax.experimental import pallas as pl
from jax.experimental.pallas import tpu as pltpu
from jax.sharding import PartitionSpec as P

MODEL_WIDTH = 4096
ADAPTER_RANK = 16
PROJ_ROWS = 256
SEQ = 64
SCALE = 1.0 / math.sqrt(PROJ_ROWS * ADAPTER_RANK * ADAPTER_RANK * SEQ * MODEL_WIDTH)
PIECES = 3
LANES = 128

F32 = jnp.float32
BF16 = jnp.bfloat16
I32 = jnp.int32
NT = (((1,), (1,)), ((), ()))
VMEM = pl.BlockSpec(memory_space=pltpu.VMEM)
SMEM = pl.BlockSpec(memory_space=pltpu.SMEM)
HBM = pl.BlockSpec(memory_space=pltpu.HBM)
SMALL = pltpu.CompilerParams(vmem_limit_bytes=16 * 1024 * 1024)

INDEX_MUL = -1640531535
SALT_MUL = 668265263


def int32_wrap(value):
    return (value + 2**31) % 2**32 - 2**31


def hash_sign(hashed):
    hashed = hashed ^ lax.shift_right_logical(hashed, 15)
    hashed = hashed * -2048144789
    hashed = hashed ^ lax.shift_right_logical(hashed, 13)
    hashed = hashed * -1028477387
    hashed = hashed ^ lax.shift_right_logical(hashed, 16)
    return jnp.where((hashed & 512) != 0, 1.0, -1.0).astype(F32)


def iota(shape, dim):
    return lax.broadcasted_iota(I32, shape, dim)


def token_row(mask):
    ex_rows, seq = mask.shape
    tokens = ex_rows * seq
    tiled = jnp.concatenate([mask.astype(F32)] * ex_rows, axis=1)
    owner = iota((ex_rows, tokens), 1) // seq == iota((ex_rows, tokens), 0)
    return jnp.sum(jnp.where(owner, tiled, 0.0), axis=0, keepdims=True)


def split_pieces(value):
    pieces = []
    for _ in range(PIECES):
        pieces.append(value.astype(BF16))
        value = value - pieces[-1].astype(F32)
    return jnp.concatenate(pieces, axis=0)


def rows_kernel(
    salts_hbm, mask_hbm, down_hbm, up_hbm, hid_hbm, cot_hbm,
    keep_ref, send_ref,
    salts, mask, far_left, near_left, far, near, sems,
):
    tokens, width = near.shape
    core = lax.axis_index("tensor")
    parts = 4
    share = tokens // parts

    def copies(inputs, factor, left, held, first):
        out = [
            pltpu.make_async_copy(
                inputs.at[pl.ds(i * share, share)],
                held.at[pl.ds(i * share, share)],
                sems.at[first + i],
            )
            for i in range(parts)
        ]
        rows = left.at[pl.ds(PROJ_ROWS, ADAPTER_RANK)]
        return out + [pltpu.make_async_copy(factor, rows, sems.at[first + parts])]

    def wait_for(left, held, first):
        for copy in copies(hid_hbm, down_hbm, left, held, first):
            copy.wait()

    salts_copy = pltpu.make_async_copy(salts_hbm, salts, sems.at[2 * parts + 3])
    salts_copy.start()
    mask_copy = pltpu.make_async_copy(mask_hbm, mask, sems.at[2 * parts + 2])
    mask_copy.start()

    @pl.when(core == 0)
    def _():
        for copy in copies(hid_hbm, down_hbm, far_left, far, 0):
            copy.start()
        for copy in copies(cot_hbm, up_hbm, near_left, near, parts + 1):
            copy.start()

    @pl.when(core == 1)
    def _():
        for copy in copies(cot_hbm, up_hbm, far_left, far, 0):
            copy.start()
        for copy in copies(hid_hbm, down_hbm, near_left, near, parts + 1):
            copy.start()

    high, wide = 16, 256
    index = iota((high, wide), 1) * PROJ_ROWS + iota((high, wide), 0)
    start = index * INDEX_MUL
    first = core * int32_wrap(width * PROJ_ROWS * INDEX_MUL)

    def fill(left, salt):
        offset = first + salt * SALT_MUL
        for col in range(0, width, wide):
            for row in range(0, PROJ_ROWS, high):
                shift = offset + int32_wrap((col * PROJ_ROWS + row) * INDEX_MUL)
                signs = hash_sign(start + shift).astype(BF16)
                left[row : row + high, col : col + wide] = signs

    salts_copy.wait()
    fill(far_left, salts[2 - 2 * core])
    mask_copy.wait()
    counted = token_row(mask[...]) != 0
    wait_for(far_left, far, 0)
    got = lax.dot_general(far_left[...], far[...], NT, preferred_element_type=F32)
    got = jnp.where(counted | (core == 0), got, 0.0)
    send_ref[:PROJ_ROWS] = got[:PROJ_ROWS].astype(BF16)
    keep_ref[PROJ_ROWS:] = split_pieces(got[PROJ_ROWS:])
    fill(near_left, salts[2 * core])
    wait_for(near_left, near, parts + 1)
    got = lax.dot_general(near_left[...], near[...], NT, preferred_element_type=F32)
    got = jnp.where(counted | (core == 1), got, 0.0)
    keep_ref[:PROJ_ROWS] = got[:PROJ_ROWS].astype(BF16)
    send_ref[PROJ_ROWS:] = split_pieces(got[PROJ_ROWS:])


def sketch_rows(salts, mask, down, up, hidden, cotangent):
    tokens, width = hidden.shape
    rows = PROJ_ROWS + PIECES * ADAPTER_RANK
    arrays = (salts, mask, down, up, hidden, cotangent)
    return pl.pallas_call(
        rows_kernel,
        out_shape=[jax.ShapeDtypeStruct((rows, tokens), BF16)] * 2,
        in_specs=[HBM] * 6,
        out_specs=[VMEM, VMEM],
        scratch_shapes=[
            pltpu.SMEM(salts.shape, I32),
            pltpu.VMEM(mask.shape, I32),
            pltpu.VMEM((PROJ_ROWS + ADAPTER_RANK, width), BF16),
            pltpu.VMEM((PROJ_ROWS + ADAPTER_RANK, width), BF16),
            pltpu.VMEM((tokens, width), BF16),
            pltpu.VMEM((tokens, width), BF16),
            pltpu.SemaphoreType.DMA((12,)),
        ],
        compiler_params=pltpu.CompilerParams(vmem_limit_bytes=32 * 1024 * 1024),
    )(*[pltpu.with_memory_space_constraint(x, pltpu.HBM) for x in arrays])


def feature_kernel(ex_rows, salts_ref, own_ref, other_ref, out_ref):
    tokens = own_ref.shape[1]
    rows = ADAPTER_RANK * ex_rows
    salt = salts_ref[1 + 2 * lax.axis_index("tensor")]
    shape = (rows, 2 * PIECES * ADAPTER_RANK)
    mixed, rank = iota(shape, 0) // ex_rows, iota(shape, 1) % ADAPTER_RANK
    mixer = hash_sign((rank * ADAPTER_RANK + mixed) * INDEX_MUL + salt * SALT_MUL).astype(BF16)
    pieces = jnp.concatenate([own_ref[PROJ_ROWS:], other_ref[PROJ_ROWS:]], axis=0)
    coeffs = jnp.dot(mixer, pieces, preferred_element_type=F32)
    owned = iota((rows, tokens), 1) // SEQ == iota((rows, tokens), 0) % ex_rows
    coeffs = jnp.where(owned, coeffs, 0.0).astype(BF16)
    projected = lax.dot_general(coeffs, own_ref[:PROJ_ROWS], NT, preferred_element_type=F32)
    projected += lax.dot_general(coeffs, other_ref[:PROJ_ROWS], NT, preferred_element_type=F32)
    features = (projected * SCALE).astype(BF16)
    for copy in range(out_ref.shape[0]):
        out_ref[copy] = features


def feature_rows(salts, own, other, ex_rows, copies):
    rows = ADAPTER_RANK * ex_rows
    return pl.pallas_call(
        functools.partial(feature_kernel, ex_rows),
        out_shape=jax.ShapeDtypeStruct((copies, rows, PROJ_ROWS), BF16),
        in_specs=[SMEM, VMEM, VMEM],
        out_specs=VMEM,
        compiler_params=SMALL,
    )(salts, own, other)


def fold_ranks(terms):
    half = terms.shape[0] // 2
    return terms[:half] + pltpu.roll(terms[half:], LANES - half, 1)


def pack_lanes(rows, ex_rows):
    parts = [rows[:, i : i + ex_rows] for i in range(0, LANES, 2 * ex_rows)]
    return jnp.concatenate(parts, axis=1)


def pair_kernel(ex_rows, got_ref, keep_ref, send_ref):
    blocks, rows, _ = got_ref.shape
    blk = lax.axis_index("blk")
    total = None
    for first in range(0, rows, 2 * ex_rows):
        part = pl.ds(first, 2 * ex_rows)
        right = jnp.concatenate([got_ref[b, part, :] for b in range(blocks)], axis=0)
        term = lax.dot_general(got_ref[blk, part, :], right, NT, preferred_element_type=F32)
        total = term if total is None else total + term
    total = fold_ranks(total)
    half = ex_rows // 2
    low = lax.axis_index("tensor") == 0
    keep_ref[...] = jnp.where(low, total[:half], total[half:])
    send_ref[...] = jnp.where(low, total[half:], total[:half])


def pair_halves(got, ex_rows):
    return pl.pallas_call(
        functools.partial(pair_kernel, ex_rows),
        out_shape=[jax.ShapeDtypeStruct((ex_rows // 2, LANES), F32)] * 2,
        in_specs=[VMEM],
        out_specs=[VMEM, VMEM],
        compiler_params=SMALL,
    )(got)


def sum_kernel(ex_rows, keep_ref, got_ref, out_ref):
    out_ref[...] = pack_lanes(keep_ref[...] + got_ref[...], ex_rows)


def sum_rows(keep, got, ex_rows):
    return pl.pallas_call(
        functools.partial(sum_kernel, ex_rows),
        out_shape=jax.ShapeDtypeStruct((keep.shape[0], LANES // 2), F32),
        in_specs=[VMEM, VMEM],
        out_specs=VMEM,
        compiler_params=SMALL,
    )(keep, got)


def swap_cores(value):
    return lax.ppermute(value, "tensor", [(0, 1), (1, 0)])


def body(
    hidden, cotangent, token_loss_mask, adapter_down_factor, adapter_up_factor, sign_table_salts
):
    ex_rows, seq, width_half = hidden.shape
    blocks = lax.axis_size("blk")
    keep, send = sketch_rows(
        sign_table_salts,
        token_loss_mask,
        adapter_down_factor,
        adapter_up_factor.T,
        hidden.reshape(ex_rows * seq, width_half),
        cotangent.reshape(ex_rows * seq, width_half),
    )
    other = swap_cores(send)
    if 2 * blocks * ex_rows == LANES and ex_rows == 8:
        copies = feature_rows(sign_table_salts, keep, other, ex_rows, blocks)
        got = lax.all_to_all(copies, "blk", 0, 0, tiled=True)
        keep, send = pair_halves(got, ex_rows)
        return sum_rows(keep, swap_cores(send), ex_rows)
    whole = feature_rows(sign_table_salts, keep, other, ex_rows, 1)
    share = ADAPTER_RANK * PROJ_ROWS // blocks
    parts = whole.reshape(ADAPTER_RANK, ex_rows, PROJ_ROWS // share, share)
    parts = parts.swapaxes(1, 2).reshape(blocks, ex_rows, share)
    features = lax.all_to_all(parts, "blk", 0, 0, tiled=True).reshape(blocks * ex_rows, share)
    pairs = jnp.einsum("ep,fp->ef", features, features, preferred_element_type=F32)
    pairs = pairs.reshape(blocks, ex_rows, blocks * ex_rows)
    total = jnp.sum(lax.all_to_all(pairs, "blk", 0, 0, tiled=True), axis=0)
    halves = total.reshape(2, ex_rows // 2, blocks * ex_rows)
    core = lax.axis_index("tensor")
    send = lax.dynamic_index_in_dim(halves, 1 - core, 0, keepdims=False)
    return lax.dynamic_index_in_dim(halves, core, 0, keepdims=False) + swap_cores(send)


def solution(mesh):
    placed = (
        P(("groups", "blk"), None, "tensor"),
        P(("groups", "blk"), None, "tensor"),
        P(("groups", "blk"), None),
        P(None, "tensor"),
        P("tensor", None),
        P(),
    )
    return jax.shard_map(
        body,
        mesh=mesh,
        in_specs=placed,
        out_specs=P(("groups", "blk", "tensor"), None),
        check_vma=False,
    )
```

```python
import functools
import math

import jax
import jax.numpy as jnp
from jax import lax
from jax.experimental import pallas as pl
from jax.experimental.pallas import tpu as pltpu
from jax.sharding import PartitionSpec as P

MODEL_WIDTH = 4096
ADAPTER_RANK = 16
PROJ_ROWS = 256
SEQ = 64
SCALE = 1.0 / math.sqrt(PROJ_ROWS * ADAPTER_RANK * ADAPTER_RANK * SEQ * MODEL_WIDTH)
PIECES = 3
LANES = 128

F32 = jnp.float32
BF16 = jnp.bfloat16
I32 = jnp.int32
NT = (((1,), (1,)), ((), ()))
VMEM = pl.BlockSpec(memory_space=pltpu.VMEM)
SMEM = pl.BlockSpec(memory_space=pltpu.SMEM)
HBM = pl.BlockSpec(memory_space=pltpu.HBM)
SMALL = pltpu.CompilerParams(vmem_limit_bytes=16 * 1024 * 1024)

INDEX_MUL = -1640531535
SALT_MUL = 668265263


def int32_wrap(value):
    return (value + 2**31) % 2**32 - 2**31


def hash_sign(hashed):
    hashed = hashed ^ lax.shift_right_logical(hashed, 15)
    hashed = hashed * -2048144789
    hashed = hashed ^ lax.shift_right_logical(hashed, 13)
    hashed = hashed * -1028477387
    hashed = hashed ^ lax.shift_right_logical(hashed, 16)
    return jnp.where((hashed & 512) != 0, 1.0, -1.0).astype(F32)


def iota(shape, dim):
    return lax.broadcasted_iota(I32, shape, dim)


def token_row(mask):
    ex_rows, seq = mask.shape
    tokens = ex_rows * seq
    tiled = jnp.concatenate([mask.astype(F32)] * ex_rows, axis=1)
    owner = iota((ex_rows, tokens), 1) // seq == iota((ex_rows, tokens), 0)
    return jnp.sum(jnp.where(owner, tiled, 0.0), axis=0, keepdims=True)


def split_pieces(value):
    pieces = []
    for _ in range(PIECES):
        pieces.append(value.astype(BF16))
        value = value - pieces[-1].astype(F32)
    return jnp.concatenate(pieces, axis=0)


def rows_kernel(
    salts_hbm, mask_hbm, down_hbm, up_hbm, hid_hbm, cot_hbm,
    keep_ref, send_ref,
    salts, mask, far_left, near_left, far, near, sems,
):
    tokens, width = near.shape
    core = lax.axis_index("tensor")
    parts = 4
    share = tokens // parts

    def copies(inputs, factor, left, held, first):
        out = [
            pltpu.make_async_copy(
                inputs.at[pl.ds(i * share, share)],
                held.at[pl.ds(i * share, share)],
                sems.at[first + i],
            )
            for i in range(parts)
        ]
        rows = left.at[pl.ds(PROJ_ROWS, ADAPTER_RANK)]
        return out + [pltpu.make_async_copy(factor, rows, sems.at[first + parts])]

    def wait_for(left, held, first):
        for copy in copies(hid_hbm, down_hbm, left, held, first):
            copy.wait()

    salts_copy = pltpu.make_async_copy(salts_hbm, salts, sems.at[2 * parts + 3])
    salts_copy.start()
    mask_copy = pltpu.make_async_copy(mask_hbm, mask, sems.at[2 * parts + 2])
    mask_copy.start()

    @pl.when(core == 0)
    def _():
        for copy in copies(hid_hbm, down_hbm, far_left, far, 0):
            copy.start()
        for copy in copies(cot_hbm, up_hbm, near_left, near, parts + 1):
            copy.start()

    @pl.when(core == 1)
    def _():
        for copy in copies(cot_hbm, up_hbm, far_left, far, 0):
            copy.start()
        for copy in copies(hid_hbm, down_hbm, near_left, near, parts + 1):
            copy.start()

    high, wide = 16, 256
    index = iota((high, wide), 1) * PROJ_ROWS + iota((high, wide), 0)
    start = index * INDEX_MUL
    first = core * int32_wrap(width * PROJ_ROWS * INDEX_MUL)

    def fill(left, salt):
        offset = first + salt * SALT_MUL
        for col in range(0, width, wide):
            for row in range(0, PROJ_ROWS, high):
                shift = offset + int32_wrap((col * PROJ_ROWS + row) * INDEX_MUL)
                signs = hash_sign(start + shift).astype(BF16)
                left[row : row + high, col : col + wide] = signs

    salts_copy.wait()
    fill(far_left, salts[2 - 2 * core])
    mask_copy.wait()
    counted = token_row(mask[...]) != 0
    wait_for(far_left, far, 0)
    got = lax.dot_general(far_left[...], far[...], NT, preferred_element_type=F32)
    got = jnp.where(counted | (core == 0), got, 0.0)
    send_ref[:PROJ_ROWS] = got[:PROJ_ROWS].astype(BF16)
    keep_ref[PROJ_ROWS:] = split_pieces(got[PROJ_ROWS:])
    fill(near_left, salts[2 * core])
    wait_for(near_left, near, parts + 1)
    got = lax.dot_general(near_left[...], near[...], NT, preferred_element_type=F32)
    got = jnp.where(counted | (core == 1), got, 0.0)
    keep_ref[:PROJ_ROWS] = got[:PROJ_ROWS].astype(BF16)
    send_ref[PROJ_ROWS:] = split_pieces(got[PROJ_ROWS:])


def sketch_rows(salts, mask, down, up, hidden, cotangent):
    tokens, width = hidden.shape
    rows = PROJ_ROWS + PIECES * ADAPTER_RANK
    arrays = (salts, mask, down, up, hidden, cotangent)
    return pl.pallas_call(
        rows_kernel,
        out_shape=[jax.ShapeDtypeStruct((rows, tokens), BF16)] * 2,
        in_specs=[HBM] * 6,
        out_specs=[VMEM, VMEM],
        scratch_shapes=[
            pltpu.SMEM(salts.shape, I32),
            pltpu.VMEM(mask.shape, I32),
            pltpu.VMEM((PROJ_ROWS + ADAPTER_RANK, width), BF16),
            pltpu.VMEM((PROJ_ROWS + ADAPTER_RANK, width), BF16),
            pltpu.VMEM((tokens, width), BF16),
            pltpu.VMEM((tokens, width), BF16),
            pltpu.SemaphoreType.DMA((12,)),
        ],
        compiler_params=pltpu.CompilerParams(vmem_limit_bytes=32 * 1024 * 1024),
    )(*[pltpu.with_memory_space_constraint(x, pltpu.HBM) for x in arrays])


def feature_kernel(ex_rows, salts_ref, own_ref, other_ref, out_ref):
    tokens = own_ref.shape[1]
    rows = ADAPTER_RANK * ex_rows
    salt = salts_ref[1 + 2 * lax.axis_index("tensor")]
    shape = (rows, 2 * PIECES * ADAPTER_RANK)
    mixed, rank = iota(shape, 0) // ex_rows, iota(shape, 1) % ADAPTER_RANK
    mixer = hash_sign((rank * ADAPTER_RANK + mixed) * INDEX_MUL + salt * SALT_MUL).astype(BF16)
    pieces = jnp.concatenate([own_ref[PROJ_ROWS:], other_ref[PROJ_ROWS:]], axis=0)
    coeffs = jnp.dot(mixer, pieces, preferred_element_type=F32)
    owned = iota((rows, tokens), 1) // SEQ == iota((rows, tokens), 0) % ex_rows
    coeffs = jnp.where(owned, coeffs, 0.0).astype(BF16)
    projected = lax.dot_general(coeffs, own_ref[:PROJ_ROWS], NT, preferred_element_type=F32)
    projected += lax.dot_general(coeffs, other_ref[:PROJ_ROWS], NT, preferred_element_type=F32)
    features = (projected * SCALE).astype(BF16)
    for copy in range(out_ref.shape[0]):
        out_ref[copy] = features


def feature_rows(salts, own, other, ex_rows, copies):
    rows = ADAPTER_RANK * ex_rows
    return pl.pallas_call(
        functools.partial(feature_kernel, ex_rows),
        out_shape=jax.ShapeDtypeStruct((copies, rows, PROJ_ROWS), BF16),
        in_specs=[SMEM, VMEM, VMEM],
        out_specs=VMEM,
        compiler_params=SMALL,
    )(salts, own, other)


def fold_ranks(terms):
    half = terms.shape[0] // 2
    return terms[:half] + pltpu.roll(terms[half:], LANES - half, 1)


def pack_lanes(rows, ex_rows):
    parts = [rows[:, i : i + ex_rows] for i in range(0, LANES, 2 * ex_rows)]
    return jnp.concatenate(parts, axis=1)


def pair_kernel(ex_rows, got_ref, out_ref):
    blocks, rows, _ = got_ref.shape
    held = jnp.concatenate([got_ref[b] for b in range(blocks)], axis=0)
    total = lax.dot_general(held, held, NT, preferred_element_type=F32)
    out_ref[...] = jnp.zeros_like(out_ref)
    half = ex_rows // 2
    for b in range(blocks):
        block = fold_ranks(total[b * rows : (b + 1) * rows])
        out_ref[2 * b, :half, :] = block[:half]
        out_ref[2 * b + 1, :half, :] = block[half:]


def pair_parts(got, ex_rows):
    blocks = got.shape[0]
    return pl.pallas_call(
        functools.partial(pair_kernel, ex_rows),
        out_shape=jax.ShapeDtypeStruct((2 * blocks, 8, LANES), F32),
        in_specs=[VMEM],
        out_specs=VMEM,
        compiler_params=SMALL,
    )(got)


def sum_kernel(ex_rows, terms_ref, out_ref):
    total = jnp.sum(terms_ref[...], axis=0)[: out_ref.shape[0]]
    out_ref[...] = pack_lanes(total, ex_rows)


def sum_rows(terms, ex_rows):
    return pl.pallas_call(
        functools.partial(sum_kernel, ex_rows),
        out_shape=jax.ShapeDtypeStruct((ex_rows // 2, LANES // 2), F32),
        in_specs=[VMEM],
        out_specs=VMEM,
        compiler_params=SMALL,
    )(terms)


def swap_cores(value):
    return lax.ppermute(value, "tensor", [(0, 1), (1, 0)])


def body(
    hidden, cotangent, token_loss_mask, adapter_down_factor, adapter_up_factor, sign_table_salts
):
    ex_rows, seq, width_half = hidden.shape
    blocks = lax.axis_size("blk")
    keep, send = sketch_rows(
        sign_table_salts,
        token_loss_mask,
        adapter_down_factor,
        adapter_up_factor.T,
        hidden.reshape(ex_rows * seq, width_half),
        cotangent.reshape(ex_rows * seq, width_half),
    )
    other = swap_cores(send)
    if 2 * blocks * ex_rows == LANES and ex_rows == 8:
        parts = feature_rows(sign_table_salts, keep, other, ex_rows, 1)
        parts = parts.reshape(blocks, 2 * ex_rows, PROJ_ROWS)
        got = lax.all_to_all(parts, "blk", 0, 0, tiled=True)
        terms = lax.all_to_all(pair_parts(got, ex_rows), ("blk", "tensor"), 0, 0, tiled=True)
        return sum_rows(terms, ex_rows)
    whole = feature_rows(sign_table_salts, keep, other, ex_rows, 1)
    share = ADAPTER_RANK * PROJ_ROWS // blocks
    parts = whole.reshape(ADAPTER_RANK, ex_rows, PROJ_ROWS // share, share)
    parts = parts.swapaxes(1, 2).reshape(blocks, ex_rows, share)
    features = lax.all_to_all(parts, "blk", 0, 0, tiled=True).reshape(blocks * ex_rows, share)
    pairs = jnp.einsum("ep,fp->ef", features, features, preferred_element_type=F32)
    pairs = pairs.reshape(blocks, ex_rows, blocks * ex_rows)
    total = jnp.sum(lax.all_to_all(pairs, "blk", 0, 0, tiled=True), axis=0)
    halves = total.reshape(2, ex_rows // 2, blocks * ex_rows)
    core = lax.axis_index("tensor")
    send = lax.dynamic_index_in_dim(halves, 1 - core, 0, keepdims=False)
    return lax.dynamic_index_in_dim(halves, core, 0, keepdims=False) + swap_cores(send)


def solution(mesh):
    placed = (
        P(("groups", "blk"), None, "tensor"),
        P(("groups", "blk"), None, "tensor"),
        P(("groups", "blk"), None),
        P(None, "tensor"),
        P("tensor", None),
        P(),
    )
    return jax.shard_map(
        body,
        mesh=mesh,
        in_specs=placed,
        out_specs=P(("groups", "blk", "tensor"), None),
        check_vma=False,
    )
```

```python
import functools
import math

import jax
import jax.numpy as jnp
from jax import lax
from jax.experimental import pallas as pl
from jax.experimental.pallas import tpu as pltpu
from jax.sharding import Mesh, PartitionSpec as P

MODEL_WIDTH = 4096
ADAPTER_RANK = 16
PROJ_ROWS = 256
SEQ = 64
SCALE = 1.0 / math.sqrt(PROJ_ROWS * ADAPTER_RANK * ADAPTER_RANK * SEQ * MODEL_WIDTH)
PIECES = 3
LANES = 128
BLK = ("z", "x")

F32 = jnp.float32
BF16 = jnp.bfloat16
I32 = jnp.int32
NT = (((1,), (1,)), ((), ()))
VMEM = pl.BlockSpec(memory_space=pltpu.VMEM)
SMEM = pl.BlockSpec(memory_space=pltpu.SMEM)
HBM = pl.BlockSpec(memory_space=pltpu.HBM)
SMALL = pltpu.CompilerParams(vmem_limit_bytes=16 * 1024 * 1024)

INDEX_MUL = -1640531535
SALT_MUL = 668265263


def int32_wrap(value):
    return (value + 2**31) % 2**32 - 2**31


def hash_sign(hashed):
    hashed = hashed ^ lax.shift_right_logical(hashed, 15)
    hashed = hashed * -2048144789
    hashed = hashed ^ lax.shift_right_logical(hashed, 13)
    hashed = hashed * -1028477387
    hashed = hashed ^ lax.shift_right_logical(hashed, 16)
    return jnp.where((hashed & 512) != 0, 1.0, -1.0).astype(F32)


def iota(shape, dim):
    return lax.broadcasted_iota(I32, shape, dim)


def token_row(mask):
    ex_rows, seq = mask.shape
    tokens = ex_rows * seq
    tiled = jnp.concatenate([mask.astype(F32)] * ex_rows, axis=1)
    owner = iota((ex_rows, tokens), 1) // seq == iota((ex_rows, tokens), 0)
    return jnp.sum(jnp.where(owner, tiled, 0.0), axis=0, keepdims=True)


def split_pieces(value):
    pieces = []
    for _ in range(PIECES):
        pieces.append(value.astype(BF16))
        value = value - pieces[-1].astype(F32)
    return jnp.concatenate(pieces, axis=0)


def rows_kernel(
    salts_hbm, mask_hbm, down_hbm, up_hbm, hid_hbm, cot_hbm,
    keep_ref, send_ref,
    salts, mask, far_left, near_left, far, near, sems,
):
    tokens, width = near.shape
    core = lax.axis_index("tensor")
    parts = 4
    share = tokens // parts

    def copies(inputs, factor, left, held, first):
        out = [
            pltpu.make_async_copy(
                inputs.at[pl.ds(i * share, share)],
                held.at[pl.ds(i * share, share)],
                sems.at[first + i],
            )
            for i in range(parts)
        ]
        rows = left.at[pl.ds(PROJ_ROWS, ADAPTER_RANK)]
        return out + [pltpu.make_async_copy(factor, rows, sems.at[first + parts])]

    def wait_for(left, held, first):
        for copy in copies(hid_hbm, down_hbm, left, held, first):
            copy.wait()

    salts_copy = pltpu.make_async_copy(salts_hbm, salts, sems.at[2 * parts + 3])
    salts_copy.start()
    mask_copy = pltpu.make_async_copy(mask_hbm, mask, sems.at[2 * parts + 2])
    mask_copy.start()

    @pl.when(core == 0)
    def _():
        for copy in copies(hid_hbm, down_hbm, far_left, far, 0):
            copy.start()
        for copy in copies(cot_hbm, up_hbm, near_left, near, parts + 1):
            copy.start()

    @pl.when(core == 1)
    def _():
        for copy in copies(cot_hbm, up_hbm, far_left, far, 0):
            copy.start()
        for copy in copies(hid_hbm, down_hbm, near_left, near, parts + 1):
            copy.start()

    high, wide = 16, 256
    index = iota((high, wide), 1) * PROJ_ROWS + iota((high, wide), 0)
    start = index * INDEX_MUL
    first = core * int32_wrap(width * PROJ_ROWS * INDEX_MUL)

    def fill(left, salt):
        offset = first + salt * SALT_MUL
        for col in range(0, width, wide):
            for row in range(0, PROJ_ROWS, high):
                shift = offset + int32_wrap((col * PROJ_ROWS + row) * INDEX_MUL)
                signs = hash_sign(start + shift).astype(BF16)
                left[row : row + high, col : col + wide] = signs

    salts_copy.wait()
    fill(far_left, salts[2 - 2 * core])
    mask_copy.wait()
    counted = token_row(mask[...]) != 0
    wait_for(far_left, far, 0)
    got = lax.dot_general(far_left[...], far[...], NT, preferred_element_type=F32)
    got = jnp.where(counted | (core == 0), got, 0.0)
    send_ref[:PROJ_ROWS] = got[:PROJ_ROWS].astype(BF16)
    keep_ref[PROJ_ROWS:] = split_pieces(got[PROJ_ROWS:])
    fill(near_left, salts[2 * core])
    wait_for(near_left, near, parts + 1)
    got = lax.dot_general(near_left[...], near[...], NT, preferred_element_type=F32)
    got = jnp.where(counted | (core == 1), got, 0.0)
    keep_ref[:PROJ_ROWS] = got[:PROJ_ROWS].astype(BF16)
    send_ref[PROJ_ROWS:] = split_pieces(got[PROJ_ROWS:])


def sketch_rows(salts, mask, down, up, hidden, cotangent):
    tokens, width = hidden.shape
    rows = PROJ_ROWS + PIECES * ADAPTER_RANK
    arrays = (salts, mask, down, up, hidden, cotangent)
    return pl.pallas_call(
        rows_kernel,
        out_shape=[jax.ShapeDtypeStruct((rows, tokens), BF16)] * 2,
        in_specs=[HBM] * 6,
        out_specs=[VMEM, VMEM],
        scratch_shapes=[
            pltpu.SMEM(salts.shape, I32),
            pltpu.VMEM(mask.shape, I32),
            pltpu.VMEM((PROJ_ROWS + ADAPTER_RANK, width), BF16),
            pltpu.VMEM((PROJ_ROWS + ADAPTER_RANK, width), BF16),
            pltpu.VMEM((tokens, width), BF16),
            pltpu.VMEM((tokens, width), BF16),
            pltpu.SemaphoreType.DMA((12,)),
        ],
        compiler_params=pltpu.CompilerParams(vmem_limit_bytes=32 * 1024 * 1024),
    )(*[pltpu.with_memory_space_constraint(x, pltpu.HBM) for x in arrays])


def feature_kernel(ex_rows, salts_ref, own_ref, other_ref, out_ref):
    tokens = own_ref.shape[1]
    rows = ADAPTER_RANK * ex_rows
    salt = salts_ref[1 + 2 * lax.axis_index("tensor")]
    shape = (rows, 2 * PIECES * ADAPTER_RANK)
    mixed, rank = iota(shape, 0) // ex_rows, iota(shape, 1) % ADAPTER_RANK
    mixer = hash_sign((rank * ADAPTER_RANK + mixed) * INDEX_MUL + salt * SALT_MUL).astype(BF16)
    pieces = jnp.concatenate([own_ref[PROJ_ROWS:], other_ref[PROJ_ROWS:]], axis=0)
    coeffs = jnp.dot(mixer, pieces, preferred_element_type=F32)
    owned = iota((rows, tokens), 1) // SEQ == iota((rows, tokens), 0) % ex_rows
    coeffs = jnp.where(owned, coeffs, 0.0).astype(BF16)
    projected = lax.dot_general(coeffs, own_ref[:PROJ_ROWS], NT, preferred_element_type=F32)
    projected += lax.dot_general(coeffs, other_ref[:PROJ_ROWS], NT, preferred_element_type=F32)
    features = (projected * SCALE).astype(BF16)
    parts = rows // out_ref.shape[1]
    for copy in range(out_ref.shape[0]):
        first = copy % parts * out_ref.shape[1]
        out_ref[copy] = features[first : first + out_ref.shape[1]]


def feature_rows(salts, own, other, ex_rows, copies, parts):
    rows = ADAPTER_RANK * ex_rows
    return pl.pallas_call(
        functools.partial(feature_kernel, ex_rows),
        out_shape=jax.ShapeDtypeStruct((copies, rows // parts, PROJ_ROWS), BF16),
        in_specs=[SMEM, VMEM, VMEM],
        out_specs=VMEM,
        compiler_params=SMALL,
    )(salts, own, other)


def fold_ranks(terms):
    half = terms.shape[0] // 2
    return terms[:half] + pltpu.roll(terms[half:], LANES - half, 1)


def pack_lanes(rows, ex_rows):
    parts = [rows[:, i : i + ex_rows] for i in range(0, LANES, 2 * ex_rows)]
    return jnp.concatenate(parts, axis=1)


def pair_kernel(ex_rows, got_ref, out_ref):
    blocks, rows, _ = got_ref.shape
    first = 2 * lax.axis_index("z")
    total = None
    for row in range(0, rows, 2 * ex_rows):
        part = pl.ds(row, 2 * ex_rows)
        left = jnp.concatenate([got_ref[first + x, part, :] for x in range(2)], axis=0)
        right = jnp.concatenate([got_ref[b, part, :] for b in range(blocks)], axis=0)
        term = lax.dot_general(left, right, NT, preferred_element_type=F32)
        total = term if total is None else total + term
    out_ref[...] = jnp.zeros_like(out_ref)
    half = ex_rows // 2
    for x in range(2):
        block = fold_ranks(total[2 * x * ex_rows : 2 * (x + 1) * ex_rows])
        out_ref[2 * x, :half, :] = block[:half]
        out_ref[2 * x + 1, :half, :] = block[half:]


def pair_parts(got, ex_rows):
    return pl.pallas_call(
        functools.partial(pair_kernel, ex_rows),
        out_shape=jax.ShapeDtypeStruct((4, 8, LANES), F32),
        in_specs=[VMEM],
        out_specs=VMEM,
        compiler_params=SMALL,
    )(got)


def sum_kernel(ex_rows, terms_ref, out_ref):
    total = jnp.sum(terms_ref[...], axis=0)[: out_ref.shape[0]]
    out_ref[...] = pack_lanes(total, ex_rows)


def sum_rows(terms, ex_rows):
    return pl.pallas_call(
        functools.partial(sum_kernel, ex_rows),
        out_shape=jax.ShapeDtypeStruct((ex_rows // 2, LANES // 2), F32),
        in_specs=[VMEM],
        out_specs=VMEM,
        compiler_params=SMALL,
    )(terms)


def swap_cores(value):
    return lax.ppermute(value, "tensor", [(0, 1), (1, 0)])


def body(
    hidden, cotangent, token_loss_mask, adapter_down_factor, adapter_up_factor, sign_table_salts
):
    ex_rows, seq, width_half = hidden.shape
    blocks = lax.axis_size("z") * lax.axis_size("x")
    keep, send = sketch_rows(
        sign_table_salts,
        token_loss_mask,
        adapter_down_factor,
        adapter_up_factor.T,
        hidden.reshape(ex_rows * seq, width_half),
        cotangent.reshape(ex_rows * seq, width_half),
    )
    other = swap_cores(send)
    if 2 * blocks * ex_rows == LANES and ex_rows == 8:
        parts = feature_rows(sign_table_salts, keep, other, ex_rows, blocks, 2)
        got = lax.all_to_all(parts, BLK, 0, 0, tiled=True)
        terms = lax.all_to_all(pair_parts(got, ex_rows), ("x", "tensor"), 0, 0, tiled=True)
        return sum_rows(terms, ex_rows)
    whole = feature_rows(sign_table_salts, keep, other, ex_rows, 1, 1)
    share = ADAPTER_RANK * PROJ_ROWS // blocks
    parts = whole.reshape(ADAPTER_RANK, ex_rows, PROJ_ROWS // share, share)
    parts = parts.swapaxes(1, 2).reshape(blocks, ex_rows, share)
    features = lax.all_to_all(parts, BLK, 0, 0, tiled=True).reshape(blocks * ex_rows, share)
    pairs = jnp.einsum("ep,fp->ef", features, features, preferred_element_type=F32)
    pairs = pairs.reshape(blocks, ex_rows, blocks * ex_rows)
    total = jnp.sum(lax.all_to_all(pairs, BLK, 0, 0, tiled=True), axis=0)
    halves = total.reshape(2, ex_rows // 2, blocks * ex_rows)
    core = lax.axis_index("tensor")
    send = lax.dynamic_index_in_dim(halves, 1 - core, 0, keepdims=False)
    return lax.dynamic_index_in_dim(halves, core, 0, keepdims=False) + swap_cores(send)


def solution(mesh):
    groups, blocks, cores = (mesh.shape[name] for name in ("groups", "blk", "tensor"))
    devices = mesh.devices.reshape(groups, blocks // 2, 2, cores)
    placed = (
        P(("groups", "z", "x"), None, "tensor"),
        P(("groups", "z", "x"), None, "tensor"),
        P(("groups", "z", "x"), None),
        P(None, "tensor"),
        P("tensor", None),
        P(),
    )
    return jax.shard_map(
        body,
        mesh=Mesh(devices, ("groups", "z", "x", "tensor")),
        in_specs=placed,
        out_specs=P(("groups", "z", "x", "tensor"), None),
        check_vma=False,
    )
```

```python
import functools
import math

import jax
import jax.numpy as jnp
from jax import lax
from jax.experimental import pallas as pl
from jax.experimental.pallas import tpu as pltpu
from jax.sharding import Mesh, PartitionSpec as P

MODEL_WIDTH = 4096
ADAPTER_RANK = 16
PROJ_ROWS = 256
SEQ = 64
SCALE = 1.0 / math.sqrt(PROJ_ROWS * ADAPTER_RANK * ADAPTER_RANK * SEQ * MODEL_WIDTH)
PIECES = 3
LANES = 128
BLK = ("z", "x")

F32 = jnp.float32
BF16 = jnp.bfloat16
I32 = jnp.int32
NT = (((1,), (1,)), ((), ()))
VMEM = pl.BlockSpec(memory_space=pltpu.VMEM)
SMEM = pl.BlockSpec(memory_space=pltpu.SMEM)
HBM = pl.BlockSpec(memory_space=pltpu.HBM)
SMALL = pltpu.CompilerParams(vmem_limit_bytes=16 * 1024 * 1024)

INDEX_MUL = -1640531535
SALT_MUL = 668265263


def int32_wrap(value):
    return (value + 2**31) % 2**32 - 2**31


def hash_sign(hashed):
    hashed = hashed ^ lax.shift_right_logical(hashed, 15)
    hashed = hashed * -2048144789
    hashed = hashed ^ lax.shift_right_logical(hashed, 13)
    hashed = hashed * int32_wrap(-1028477387 << 6)
    hashed = hashed ^ lax.shift_left(hashed, 16)
    return jnp.where(hashed < 0, 1.0, -1.0).astype(F32)


def iota(shape, dim):
    return lax.broadcasted_iota(I32, shape, dim)


def token_row(mask):
    ex_rows, seq = mask.shape
    tokens = ex_rows * seq
    tiled = jnp.concatenate([mask.astype(F32)] * ex_rows, axis=1)
    owner = iota((ex_rows, tokens), 1) // seq == iota((ex_rows, tokens), 0)
    return jnp.sum(jnp.where(owner, tiled, 0.0), axis=0, keepdims=True)


def split_pieces(value):
    pieces = []
    for _ in range(PIECES):
        pieces.append(value.astype(BF16))
        value = value - pieces[-1].astype(F32)
    return jnp.concatenate(pieces, axis=0)


def rows_kernel(
    salts_hbm, mask_hbm, down_hbm, up_hbm, hid_hbm, cot_hbm,
    keep_ref, send_ref,
    salts, mask, far_left, near_left, far, near, sems,
):
    tokens, width = near.shape
    core = lax.axis_index("tensor")
    parts = 4
    share = tokens // parts

    def copies(inputs, factor, left, held, first):
        out = [
            pltpu.make_async_copy(
                inputs.at[pl.ds(i * share, share)],
                held.at[pl.ds(i * share, share)],
                sems.at[first + i],
            )
            for i in range(parts)
        ]
        rows = left.at[pl.ds(PROJ_ROWS, ADAPTER_RANK)]
        return out + [pltpu.make_async_copy(factor, rows, sems.at[first + parts])]

    def wait_for(left, held, first):
        for copy in copies(hid_hbm, down_hbm, left, held, first):
            copy.wait()

    salts_copy = pltpu.make_async_copy(salts_hbm, salts, sems.at[2 * parts + 3])
    salts_copy.start()
    mask_copy = pltpu.make_async_copy(mask_hbm, mask, sems.at[2 * parts + 2])
    mask_copy.start()

    @pl.when(core == 0)
    def _():
        for copy in copies(hid_hbm, down_hbm, far_left, far, 0):
            copy.start()
        for copy in copies(cot_hbm, up_hbm, near_left, near, parts + 1):
            copy.start()

    @pl.when(core == 1)
    def _():
        for copy in copies(cot_hbm, up_hbm, far_left, far, 0):
            copy.start()
        for copy in copies(hid_hbm, down_hbm, near_left, near, parts + 1):
            copy.start()

    high, wide = 16, 256
    index = iota((high, wide), 1) * PROJ_ROWS + iota((high, wide), 0)
    start = index * INDEX_MUL
    first = core * int32_wrap(width * PROJ_ROWS * INDEX_MUL)

    def fill(left, salt):
        offset = first + salt * SALT_MUL
        for col in range(0, width, wide):
            for row in range(0, PROJ_ROWS, high):
                shift = offset + int32_wrap((col * PROJ_ROWS + row) * INDEX_MUL)
                signs = hash_sign(start + shift).astype(BF16)
                left[row : row + high, col : col + wide] = signs

    salts_copy.wait()
    fill(far_left, salts[2 - 2 * core])
    fill(near_left, salts[2 * core])
    mask_copy.wait()
    counted = token_row(mask[...]) != 0
    wait_for(far_left, far, 0)
    got = lax.dot_general(far_left[...], far[...], NT, preferred_element_type=F32)
    got = jnp.where(counted | (core == 0), got, 0.0)
    send_ref[:PROJ_ROWS] = got[:PROJ_ROWS].astype(BF16)
    keep_ref[PROJ_ROWS:] = split_pieces(got[PROJ_ROWS:])
    wait_for(near_left, near, parts + 1)
    got = lax.dot_general(near_left[...], near[...], NT, preferred_element_type=F32)
    got = jnp.where(counted | (core == 1), got, 0.0)
    keep_ref[:PROJ_ROWS] = got[:PROJ_ROWS].astype(BF16)
    send_ref[PROJ_ROWS:] = split_pieces(got[PROJ_ROWS:])


def sketch_rows(salts, mask, down, up, hidden, cotangent):
    tokens, width = hidden.shape
    rows = PROJ_ROWS + PIECES * ADAPTER_RANK
    arrays = (salts, mask, down, up, hidden, cotangent)
    return pl.pallas_call(
        rows_kernel,
        out_shape=[jax.ShapeDtypeStruct((rows, tokens), BF16)] * 2,
        in_specs=[HBM] * 6,
        out_specs=[VMEM, VMEM],
        scratch_shapes=[
            pltpu.SMEM(salts.shape, I32),
            pltpu.VMEM(mask.shape, I32),
            pltpu.VMEM((PROJ_ROWS + ADAPTER_RANK, width), BF16),
            pltpu.VMEM((PROJ_ROWS + ADAPTER_RANK, width), BF16),
            pltpu.VMEM((tokens, width), BF16),
            pltpu.VMEM((tokens, width), BF16),
            pltpu.SemaphoreType.DMA((12,)),
        ],
        compiler_params=pltpu.CompilerParams(vmem_limit_bytes=32 * 1024 * 1024),
    )(*[pltpu.with_memory_space_constraint(x, pltpu.HBM) for x in arrays])


def feature_kernel(ex_rows, salts_ref, own_ref, other_ref, out_ref):
    tokens = own_ref.shape[1]
    rows = ADAPTER_RANK * ex_rows
    salt = salts_ref[1 + 2 * lax.axis_index("tensor")]
    shape = (rows, 2 * PIECES * ADAPTER_RANK)
    mixed, rank = iota(shape, 0) // ex_rows, iota(shape, 1) % ADAPTER_RANK
    mixer = hash_sign((rank * ADAPTER_RANK + mixed) * INDEX_MUL + salt * SALT_MUL).astype(BF16)
    pieces = jnp.concatenate([own_ref[PROJ_ROWS:], other_ref[PROJ_ROWS:]], axis=0)
    coeffs = jnp.dot(mixer, pieces, preferred_element_type=F32)
    owned = iota((rows, tokens), 1) // SEQ == iota((rows, tokens), 0) % ex_rows
    coeffs = jnp.where(owned, coeffs, 0.0).astype(BF16)
    projected = lax.dot_general(coeffs, own_ref[:PROJ_ROWS], NT, preferred_element_type=F32)
    projected += lax.dot_general(coeffs, other_ref[:PROJ_ROWS], NT, preferred_element_type=F32)
    features = (projected * SCALE).astype(BF16)
    parts = rows // out_ref.shape[1]
    for copy in range(out_ref.shape[0]):
        first = copy % parts * out_ref.shape[1]
        out_ref[copy] = features[first : first + out_ref.shape[1]]


def feature_rows(salts, own, other, ex_rows, copies, parts):
    rows = ADAPTER_RANK * ex_rows
    return pl.pallas_call(
        functools.partial(feature_kernel, ex_rows),
        out_shape=jax.ShapeDtypeStruct((copies, rows // parts, PROJ_ROWS), BF16),
        in_specs=[SMEM, VMEM, VMEM],
        out_specs=VMEM,
        compiler_params=SMALL,
    )(salts, own, other)


def fold_ranks(terms):
    half = terms.shape[0] // 2
    return terms[:half] + pltpu.roll(terms[half:], LANES - half, 1)


def pack_lanes(rows, ex_rows):
    parts = [rows[:, i : i + ex_rows] for i in range(0, LANES, 2 * ex_rows)]
    return jnp.concatenate(parts, axis=1)


def pair_kernel(ex_rows, got_ref, *out_refs):
    blocks, rows, _ = got_ref.shape
    first = 2 * lax.axis_index("z")
    total = None
    for row in range(0, rows, 2 * ex_rows):
        part = pl.ds(row, 2 * ex_rows)
        left = jnp.concatenate([got_ref[first + x, part, :] for x in range(2)], axis=0)
        right = jnp.concatenate([got_ref[b, part, :] for b in range(blocks)], axis=0)
        term = lax.dot_general(left, right, NT, preferred_element_type=F32)
        total = term if total is None else total + term
    folded = [fold_ranks(total[2 * x * ex_rows : 2 * (x + 1) * ex_rows]) for x in range(2)]
    half = ex_rows // 2
    low = lax.axis_index("tensor") == 0
    near = lax.axis_index("x") == 0
    for step, out_ref in enumerate(out_refs):
        first, second = (folded[0], folded[1]) if step < 2 else (folded[1], folded[0])
        block = jnp.where(near, first, second)
        first, second = (block[:half], block[half:])[:: 1 - 2 * (step % 2)]
        out_ref[...] = jnp.where(low, first, second)


def pair_parts(got, ex_rows):
    return pl.pallas_call(
        functools.partial(pair_kernel, ex_rows),
        out_shape=[jax.ShapeDtypeStruct((ex_rows // 2, LANES), F32)] * 4,
        in_specs=[VMEM],
        out_specs=[VMEM] * 4,
        compiler_params=SMALL,
    )(got)


def sum_kernel(ex_rows, *refs):
    *term_refs, out_ref = refs
    total = functools.reduce(lambda a, b: a + b, [ref[...] for ref in term_refs])
    out_ref[...] = pack_lanes(total, ex_rows)


def sum_rows(terms, ex_rows):
    return pl.pallas_call(
        functools.partial(sum_kernel, ex_rows),
        out_shape=jax.ShapeDtypeStruct((ex_rows // 2, LANES // 2), F32),
        in_specs=[VMEM] * len(terms),
        out_specs=VMEM,
        compiler_params=SMALL,
    )(*terms)


def swap_cores(value):
    return lax.ppermute(value, "tensor", [(0, 1), (1, 0)])


def swap_near(value, step):
    return lax.ppermute(value, ("x", "tensor"), [(i, i ^ step) for i in range(4)])


def body(
    hidden, cotangent, token_loss_mask, adapter_down_factor, adapter_up_factor, sign_table_salts
):
    ex_rows, seq, width_half = hidden.shape
    blocks = lax.axis_size("z") * lax.axis_size("x")
    keep, send = sketch_rows(
        sign_table_salts,
        token_loss_mask,
        adapter_down_factor,
        adapter_up_factor.T,
        hidden.reshape(ex_rows * seq, width_half),
        cotangent.reshape(ex_rows * seq, width_half),
    )
    other = swap_cores(send)
    if 2 * blocks * ex_rows == LANES and ex_rows == 8:
        parts = feature_rows(sign_table_salts, keep, other, ex_rows, blocks, 2)
        got = lax.all_to_all(parts, BLK, 0, 0, tiled=True)
        terms = list(pair_parts(got, ex_rows))
        return sum_rows(terms[:1] + [swap_near(terms[k], k) for k in (1, 2, 3)], ex_rows)
    whole = feature_rows(sign_table_salts, keep, other, ex_rows, 1, 1)
    share = ADAPTER_RANK * PROJ_ROWS // blocks
    parts = whole.reshape(ADAPTER_RANK, ex_rows, PROJ_ROWS // share, share)
    parts = parts.swapaxes(1, 2).reshape(blocks, ex_rows, share)
    features = lax.all_to_all(parts, BLK, 0, 0, tiled=True).reshape(blocks * ex_rows, share)
    pairs = jnp.einsum("ep,fp->ef", features, features, preferred_element_type=F32)
    pairs = pairs.reshape(blocks, ex_rows, blocks * ex_rows)
    total = jnp.sum(lax.all_to_all(pairs, BLK, 0, 0, tiled=True), axis=0)
    halves = total.reshape(2, ex_rows // 2, blocks * ex_rows)
    core = lax.axis_index("tensor")
    send = lax.dynamic_index_in_dim(halves, 1 - core, 0, keepdims=False)
    return lax.dynamic_index_in_dim(halves, core, 0, keepdims=False) + swap_cores(send)


def solution(mesh):
    groups, blocks, cores = (mesh.shape[name] for name in ("groups", "blk", "tensor"))
    devices = mesh.devices.reshape(groups, blocks // 2, 2, cores)
    placed = (
        P(("groups", "z", "x"), None, "tensor"),
        P(("groups", "z", "x"), None, "tensor"),
        P(("groups", "z", "x"), None),
        P(None, "tensor"),
        P("tensor", None),
        P(),
    )
    return jax.shard_map(
        body,
        mesh=Mesh(devices, ("groups", "z", "x", "tensor")),
        in_specs=placed,
        out_specs=P(("groups", "z", "x", "tensor"), None),
        check_vma=False,
    )
```

```python
import functools
import math

import jax
import jax.numpy as jnp
from jax import lax
from jax.experimental import pallas as pl
from jax.experimental.pallas import tpu as pltpu
from jax.sharding import Mesh, PartitionSpec as P

MODEL_WIDTH = 4096
ADAPTER_RANK = 16
PROJ_ROWS = 256
SEQ = 64
SCALE = 1.0 / math.sqrt(PROJ_ROWS * ADAPTER_RANK * ADAPTER_RANK * SEQ * MODEL_WIDTH)
PIECES = 3
LANES = 128
BLK = ("z", "x")

F32 = jnp.float32
BF16 = jnp.bfloat16
I32 = jnp.int32
NT = (((1,), (1,)), ((), ()))
VMEM = pl.BlockSpec(memory_space=pltpu.VMEM)
SMEM = pl.BlockSpec(memory_space=pltpu.SMEM)
HBM = pl.BlockSpec(memory_space=pltpu.HBM)
SMALL = pltpu.CompilerParams(vmem_limit_bytes=16 * 1024 * 1024)

INDEX_MUL = -1640531535
SALT_MUL = 668265263


def int32_wrap(value):
    return (value + 2**31) % 2**32 - 2**31


def hash_sign(hashed):
    hashed = hashed ^ lax.shift_right_logical(hashed, 15)
    hashed = hashed * -2048144789
    hashed = hashed ^ lax.shift_right_logical(hashed, 13)
    hashed = hashed * int32_wrap(-1028477387 << 6)
    hashed = hashed ^ lax.shift_left(hashed, 16)
    return jnp.where(hashed < 0, 1.0, -1.0).astype(F32)


def iota(shape, dim):
    return lax.broadcasted_iota(I32, shape, dim)


def token_row(mask):
    ex_rows, seq = mask.shape
    tokens = ex_rows * seq
    tiled = jnp.concatenate([mask.astype(F32)] * ex_rows, axis=1)
    owner = iota((ex_rows, tokens), 1) // seq == iota((ex_rows, tokens), 0)
    return jnp.sum(jnp.where(owner, tiled, 0.0), axis=0, keepdims=True)


def split_pieces(value):
    pieces = []
    for _ in range(PIECES):
        pieces.append(value.astype(BF16))
        value = value - pieces[-1].astype(F32)
    return jnp.concatenate(pieces, axis=0)


def kind_of(cross):
    core = lax.axis_index("tensor")
    return core ^ (lax.axis_index("z") // (lax.axis_size("z") // 2)) if cross else core


def rows_kernel(
    cross, ex_rows,
    salts_hbm, mask_hbm, down_hbm, up_hbm, hid_hbm, cot_hbm,
    keep_ref, send_ref, mixer_ref,
    salts, mask, far_left, near_left, far, near, sems,
):
    tokens, width = near.shape
    kind = kind_of(cross)
    parts = 4
    share = tokens // parts

    def copies(inputs, factor, left, held, first):
        out = [
            pltpu.make_async_copy(
                inputs.at[pl.ds(i * share, share)],
                held.at[pl.ds(i * share, share)],
                sems.at[first + i],
            )
            for i in range(parts)
        ]
        rows = left.at[pl.ds(PROJ_ROWS, ADAPTER_RANK)]
        return [pltpu.make_async_copy(factor, rows, sems.at[first + parts])] + out

    salts_copy = pltpu.make_async_copy(salts_hbm, salts, sems.at[2 * parts + 3])
    salts_copy.start()
    mask_copy = pltpu.make_async_copy(mask_hbm, mask, sems.at[2 * parts + 2])
    mask_copy.start()

    @pl.when(kind == 0)
    def _():
        for copy in copies(hid_hbm, down_hbm, far_left, far, 0):
            copy.start()
        for copy in copies(cot_hbm, up_hbm, near_left, near, parts + 1):
            copy.start()

    @pl.when(kind == 1)
    def _():
        for copy in copies(cot_hbm, up_hbm, far_left, far, 0):
            copy.start()
        for copy in copies(hid_hbm, down_hbm, near_left, near, parts + 1):
            copy.start()

    high, wide = 16, 256
    index = iota((high, wide), 1) * PROJ_ROWS + iota((high, wide), 0)
    start = index * INDEX_MUL
    first = lax.axis_index("tensor") * int32_wrap(width * PROJ_ROWS * INDEX_MUL)

    def fill(left, salt, cols):
        offset = first + salt * SALT_MUL
        for col in range(cols.start, cols.stop, wide):
            for row in range(0, PROJ_ROWS, high):
                shift = offset + int32_wrap((col * PROJ_ROWS + row) * INDEX_MUL)
                signs = hash_sign(start + shift).astype(BF16)
                left[row : row + high, col : col + wide] = signs

    def product(left, held, waits, step, masked):
        for copy in waits:
            copy.wait()
        lanes = slice(step * tokens // 2, (step + 1) * tokens // 2)
        got = lax.dot_general(left[...], held[lanes, :], NT, preferred_element_type=F32)
        got = jnp.where(counted[:, lanes] | jnp.logical_not(masked), got, 0.0)
        return lanes, got[:PROJ_ROWS].astype(BF16), split_pieces(got[PROJ_ROWS:])

    far_waits = copies(hid_hbm, down_hbm, far_left, far, 0)
    near_waits = copies(hid_hbm, down_hbm, near_left, near, parts + 1)
    salts_copy.wait()
    fill(far_left, salts[2 - 2 * kind], slice(0, width))
    mask_copy.wait()
    counted = token_row(mask[...]) != 0
    half = parts // 2 + 1
    for step in range(2):
        waits = far_waits[half:] if step else far_waits[:half]
        lanes, rows, ranks = product(far_left, far, waits, step, kind == 1)
        send_ref[:PROJ_ROWS, lanes] = rows
        keep_ref[PROJ_ROWS:, lanes] = ranks
        fill(near_left, salts[2 * kind], slice(step * width // 2, (step + 1) * width // 2))
    for step in range(2):
        waits = near_waits[half:] if step else near_waits[:half]
        lanes, rows, ranks = product(near_left, near, waits, step, kind == 0)
        keep_ref[:PROJ_ROWS, lanes] = rows
        send_ref[PROJ_ROWS:, lanes] = ranks
    shape = mixer_ref.shape
    mixed, rank = iota(shape, 0) // ex_rows, iota(shape, 1) % ADAPTER_RANK
    index = (rank * ADAPTER_RANK + mixed) * INDEX_MUL
    mixer_ref[...] = hash_sign(index + salts[1 + 2 * kind] * SALT_MUL).astype(BF16)


def sketch_rows(salts, mask, down, up, hidden, cotangent, cross):
    ex_rows = mask.shape[0]
    tokens, width = hidden.shape
    rows = PROJ_ROWS + PIECES * ADAPTER_RANK
    arrays = (salts, mask, down, up, hidden, cotangent)
    return pl.pallas_call(
        functools.partial(rows_kernel, cross, ex_rows),
        out_shape=[jax.ShapeDtypeStruct((rows, tokens), BF16)] * 2
        + [jax.ShapeDtypeStruct((ADAPTER_RANK * ex_rows, 2 * PIECES * ADAPTER_RANK), BF16)],
        in_specs=[HBM] * 6,
        out_specs=[VMEM] * 3,
        scratch_shapes=[
            pltpu.SMEM(salts.shape, I32),
            pltpu.VMEM(mask.shape, I32),
            pltpu.VMEM((PROJ_ROWS + ADAPTER_RANK, width), BF16),
            pltpu.VMEM((PROJ_ROWS + ADAPTER_RANK, width), BF16),
            pltpu.VMEM((tokens, width), BF16),
            pltpu.VMEM((tokens, width), BF16),
            pltpu.SemaphoreType.DMA((12,)),
        ],
        compiler_params=pltpu.CompilerParams(vmem_limit_bytes=32 * 1024 * 1024),
    )(*[pltpu.with_memory_space_constraint(x, pltpu.HBM) for x in arrays])


def feature_kernel(ex_rows, mixer_ref, own_ref, other_ref, out_ref):
    tokens = own_ref.shape[1]
    rows = ADAPTER_RANK * ex_rows
    pieces = jnp.concatenate([own_ref[PROJ_ROWS:], other_ref[PROJ_ROWS:]], axis=0)
    coeffs = jnp.dot(mixer_ref[...], pieces, preferred_element_type=F32)
    owned = iota((rows, tokens), 1) // SEQ == iota((rows, tokens), 0) % ex_rows
    coeffs = jnp.where(owned, coeffs, 0.0).astype(BF16)
    projected = lax.dot_general(coeffs, own_ref[:PROJ_ROWS], NT, preferred_element_type=F32)
    projected += lax.dot_general(coeffs, other_ref[:PROJ_ROWS], NT, preferred_element_type=F32)
    features = (projected * SCALE).astype(BF16)
    parts = rows // out_ref.shape[1]
    for copy in range(out_ref.shape[0]):
        first = copy % parts * out_ref.shape[1]
        out_ref[copy] = features[first : first + out_ref.shape[1]]


def feature_rows(mixer, own, other, ex_rows, copies, parts):
    rows = ADAPTER_RANK * ex_rows
    return pl.pallas_call(
        functools.partial(feature_kernel, ex_rows),
        out_shape=jax.ShapeDtypeStruct((copies, rows // parts, PROJ_ROWS), BF16),
        in_specs=[VMEM, VMEM, VMEM],
        out_specs=VMEM,
        compiler_params=SMALL,
    )(mixer, own, other)


def fold_ranks(terms):
    half = terms.shape[0] // 2
    return terms[:half] + pltpu.roll(terms[half:], LANES - half, 1)


def pack_lanes(rows, ex_rows):
    parts = [rows[:, i : i + ex_rows] for i in range(0, LANES, 2 * ex_rows)]
    return jnp.concatenate(parts, axis=1)


def pair_kernel(ex_rows, got_ref, keep_ref, send_ref):
    blocks, rows, _ = got_ref.shape
    x = lax.axis_index("x")
    first = 2 * lax.axis_index("z")
    total = None
    for row in range(0, rows, 2 * ex_rows):
        part = pl.ds(row, 2 * ex_rows)
        left = [got_ref[first + x, part, :], got_ref[first + 1 - x, part, :]]
        left = jnp.concatenate(left, axis=0)
        right = jnp.concatenate([got_ref[b, part, :] for b in range(blocks)], axis=0)
        term = lax.dot_general(left, right, NT, preferred_element_type=F32)
        total = term if total is None else total + term
    keep_ref[...] = fold_ranks(total[: 2 * ex_rows])
    send_ref[...] = fold_ranks(total[2 * ex_rows :])


def pair_rows(got, ex_rows):
    return pl.pallas_call(
        functools.partial(pair_kernel, ex_rows),
        out_shape=[jax.ShapeDtypeStruct((ex_rows, LANES), F32)] * 2,
        in_specs=[VMEM],
        out_specs=[VMEM] * 2,
        compiler_params=SMALL,
    )(got)


def halves_kernel(own_ref, got_ref, keep_ref, send_ref):
    total = own_ref[...] + got_ref[...]
    half = keep_ref.shape[0]
    low = lax.axis_index("tensor") == 0
    keep_ref[...] = jnp.where(low, total[:half], total[half:])
    send_ref[...] = jnp.where(low, total[half:], total[:half])


def sum_halves(own, got):
    rows, lanes = own.shape
    return pl.pallas_call(
        halves_kernel,
        out_shape=[jax.ShapeDtypeStruct((rows // 2, lanes), F32)] * 2,
        in_specs=[VMEM] * 2,
        out_specs=[VMEM] * 2,
        compiler_params=SMALL,
    )(own, got)


def sum_kernel(ex_rows, keep_ref, got_ref, out_ref):
    out_ref[...] = pack_lanes(keep_ref[...] + got_ref[...], ex_rows)


def sum_rows(keep, got, ex_rows):
    return pl.pallas_call(
        functools.partial(sum_kernel, ex_rows),
        out_shape=jax.ShapeDtypeStruct((keep.shape[0], LANES // 2), F32),
        in_specs=[VMEM] * 2,
        out_specs=VMEM,
        compiler_params=SMALL,
    )(keep, got)


def swap_cores(value):
    return lax.ppermute(value, "tensor", [(0, 1), (1, 0)])


def swap_across(value):
    return lax.ppermute(value, ("x", "tensor"), [(i, i ^ 3) for i in range(4)])


def trade_kinds(parts):
    blocks, half = parts.shape[0], lax.axis_size("z") // 2
    groups = [[2 * b + (kind ^ (b // 2 // half)) for b in range(blocks)] for kind in range(2)]
    return lax.all_to_all(parts, BLK + ("tensor",), 0, 0, axis_index_groups=groups, tiled=True)


def body(
    hidden, cotangent, token_loss_mask, adapter_down_factor, adapter_up_factor, sign_table_salts
):
    ex_rows, seq, width_half = hidden.shape
    blocks = lax.axis_size("z") * lax.axis_size("x")
    fast = 2 * blocks * ex_rows == LANES and ex_rows == 8
    keep, send, mixer = sketch_rows(
        sign_table_salts,
        token_loss_mask,
        adapter_down_factor,
        adapter_up_factor.T,
        hidden.reshape(ex_rows * seq, width_half),
        cotangent.reshape(ex_rows * seq, width_half),
        fast,
    )
    other = swap_cores(send)
    if fast:
        got = trade_kinds(feature_rows(mixer, keep, other, ex_rows, blocks, 2))
        keep, send = pair_rows(got, ex_rows)
        keep, send = sum_halves(keep, swap_across(send))
        return sum_rows(keep, swap_cores(send), ex_rows)
    whole = feature_rows(mixer, keep, other, ex_rows, 1, 1)
    share = ADAPTER_RANK * PROJ_ROWS // blocks
    parts = whole.reshape(ADAPTER_RANK, ex_rows, PROJ_ROWS // share, share)
    parts = parts.swapaxes(1, 2).reshape(blocks, ex_rows, share)
    features = lax.all_to_all(parts, BLK, 0, 0, tiled=True).reshape(blocks * ex_rows, share)
    pairs = jnp.einsum("ep,fp->ef", features, features, preferred_element_type=F32)
    pairs = pairs.reshape(blocks, ex_rows, blocks * ex_rows)
    total = jnp.sum(lax.all_to_all(pairs, BLK, 0, 0, tiled=True), axis=0)
    halves = total.reshape(2, ex_rows // 2, blocks * ex_rows)
    core = lax.axis_index("tensor")
    send = lax.dynamic_index_in_dim(halves, 1 - core, 0, keepdims=False)
    return lax.dynamic_index_in_dim(halves, core, 0, keepdims=False) + swap_cores(send)


def solution(mesh):
    groups, blocks, cores = (mesh.shape[name] for name in ("groups", "blk", "tensor"))
    devices = mesh.devices.reshape(groups, blocks // 2, 2, cores)
    placed = (
        P(("groups", "z", "x"), None, "tensor"),
        P(("groups", "z", "x"), None, "tensor"),
        P(("groups", "z", "x"), None),
        P(None, "tensor"),
        P("tensor", None),
        P(),
    )
    return jax.shard_map(
        body,
        mesh=Mesh(devices, ("groups", "z", "x", "tensor")),
        in_specs=placed,
        out_specs=P(("groups", "z", "x", "tensor"), None),
        check_vma=False,
    )
```

```python
import functools
import math

import jax
import jax.numpy as jnp
from jax import lax
from jax.experimental import pallas as pl
from jax.experimental.pallas import tpu as pltpu
from jax.sharding import Mesh, PartitionSpec as P

MODEL_WIDTH = 4096
ADAPTER_RANK = 16
PROJ_ROWS = 256
SEQ = 64
SCALE = 1.0 / math.sqrt(PROJ_ROWS * ADAPTER_RANK * ADAPTER_RANK * SEQ * MODEL_WIDTH)
PIECES = 3
LANES = 128
BLK = ("z", "x")

F32 = jnp.float32
BF16 = jnp.bfloat16
I32 = jnp.int32
NT = (((1,), (1,)), ((), ()))
VMEM = pl.BlockSpec(memory_space=pltpu.VMEM)
SMEM = pl.BlockSpec(memory_space=pltpu.SMEM)
HBM = pl.BlockSpec(memory_space=pltpu.HBM)
SMALL = pltpu.CompilerParams(vmem_limit_bytes=16 * 1024 * 1024)

INDEX_MUL = -1640531535
SALT_MUL = 668265263


def int32_wrap(value):
    return (value + 2**31) % 2**32 - 2**31


def hash_sign(hashed):
    hashed = hashed ^ lax.shift_right_logical(hashed, 15)
    hashed = hashed * -2048144789
    hashed = hashed ^ lax.shift_right_logical(hashed, 13)
    hashed = hashed * int32_wrap(-1028477387 << 6)
    hashed = hashed ^ lax.shift_left(hashed, 16)
    return jnp.where(hashed < 0, 1.0, -1.0).astype(F32)


def iota(shape, dim):
    return lax.broadcasted_iota(I32, shape, dim)


def token_row(mask):
    ex_rows, seq = mask.shape
    tokens = ex_rows * seq
    tiled = jnp.concatenate([mask.astype(F32)] * ex_rows, axis=1)
    owner = iota((ex_rows, tokens), 1) // seq == iota((ex_rows, tokens), 0)
    return jnp.sum(jnp.where(owner, tiled, 0.0), axis=0, keepdims=True)


def split_pieces(value):
    pieces = []
    for _ in range(PIECES):
        pieces.append(value.astype(BF16))
        value = value - pieces[-1].astype(F32)
    return jnp.concatenate(pieces, axis=0)


def kind_of(cross):
    core = lax.axis_index("tensor")
    return core ^ (lax.axis_index("z") // (lax.axis_size("z") // 2)) if cross else core


def rows_kernel(
    cross, ex_rows,
    salts_hbm, mask_hbm, down_hbm, up_hbm, hid_hbm, cot_hbm,
    keep_ref, send_ref, mixer_ref,
    salts, mask, far_factor, near_factor, far, near, sems,
):
    tokens, width = near.shape
    kind = kind_of(cross)
    parts = 4
    share = width // parts

    def copies(inputs, factor, factor_held, held, first):
        out = [
            pltpu.make_async_copy(
                inputs.at[:, pl.ds(i * share, share)],
                held.at[:, pl.ds(i * share, share)],
                sems.at[first + i],
            )
            for i in range(parts)
        ]
        return [pltpu.make_async_copy(factor, factor_held, sems.at[first + parts])] + out

    salts_copy = pltpu.make_async_copy(salts_hbm, salts, sems.at[2 * parts + 3])
    salts_copy.start()
    mask_copy = pltpu.make_async_copy(mask_hbm, mask, sems.at[2 * parts + 2])

    @pl.when(kind == 0)
    def _():
        for copy in copies(hid_hbm, down_hbm, far_factor, far, 0):
            copy.start()
        for copy in copies(cot_hbm, up_hbm, near_factor, near, parts + 1):
            copy.start()

    @pl.when(kind == 1)
    def _():
        for copy in copies(cot_hbm, up_hbm, far_factor, far, 0):
            copy.start()
        for copy in copies(hid_hbm, down_hbm, near_factor, near, parts + 1):
            copy.start()

    mask_copy.start()
    high, wide = 16, 256
    index = iota((high, wide), 1) * PROJ_ROWS + iota((high, wide), 0)
    start = index * INDEX_MUL
    first = lax.axis_index("tensor") * int32_wrap(width * PROJ_ROWS * INDEX_MUL)

    def signs(salt, col):
        offset = first + salt * SALT_MUL
        rows = [
            hash_sign(start + (offset + int32_wrap((col * PROJ_ROWS + row) * INDEX_MUL)))
            for row in range(0, PROJ_ROWS, high)
        ]
        return [row.astype(BF16) for row in rows]

    def products(salt, factor, held, waits):
        waits[0].wait()
        total = None
        for col in range(0, width, wide):
            part = slice(col, col + wide)
            left = jnp.concatenate(signs(salt, col) + [factor[:, part]], axis=0)
            if col % share == 0:
                waits[1 + col // share].wait()
            term = lax.dot_general(left, held[:, part], NT, preferred_element_type=F32)
            total = term if total is None else total + term
        return total

    salts_copy.wait()
    waits = copies(hid_hbm, down_hbm, far_factor, far, 0)
    got = products(salts[2 - 2 * kind], far_factor, far, waits)
    mask_copy.wait()
    counted = token_row(mask[...]) != 0
    got = jnp.where(counted | (kind == 0), got, 0.0)
    send_ref[:PROJ_ROWS] = got[:PROJ_ROWS].astype(BF16)
    keep_ref[PROJ_ROWS:] = split_pieces(got[PROJ_ROWS:])
    waits = copies(hid_hbm, down_hbm, near_factor, near, parts + 1)
    got = products(salts[2 * kind], near_factor, near, waits)
    got = jnp.where(counted | (kind == 1), got, 0.0)
    keep_ref[:PROJ_ROWS] = got[:PROJ_ROWS].astype(BF16)
    send_ref[PROJ_ROWS:] = split_pieces(got[PROJ_ROWS:])
    shape = mixer_ref.shape
    mixed, rank = iota(shape, 0) // ex_rows, iota(shape, 1) % ADAPTER_RANK
    index = (rank * ADAPTER_RANK + mixed) * INDEX_MUL
    mixer_ref[...] = hash_sign(index + salts[1 + 2 * kind] * SALT_MUL).astype(BF16)


def sketch_rows(salts, mask, down, up, hidden, cotangent, cross):
    ex_rows = mask.shape[0]
    tokens, width = hidden.shape
    rows = PROJ_ROWS + PIECES * ADAPTER_RANK
    arrays = (salts, mask, down, up, hidden, cotangent)
    return pl.pallas_call(
        functools.partial(rows_kernel, cross, ex_rows),
        out_shape=[jax.ShapeDtypeStruct((rows, tokens), BF16)] * 2
        + [jax.ShapeDtypeStruct((ADAPTER_RANK * ex_rows, 2 * PIECES * ADAPTER_RANK), BF16)],
        in_specs=[HBM] * 6,
        out_specs=[VMEM] * 3,
        scratch_shapes=[
            pltpu.SMEM(salts.shape, I32),
            pltpu.VMEM(mask.shape, I32),
            pltpu.VMEM((ADAPTER_RANK, width), BF16),
            pltpu.VMEM((ADAPTER_RANK, width), BF16),
            pltpu.VMEM((tokens, width), BF16),
            pltpu.VMEM((tokens, width), BF16),
            pltpu.SemaphoreType.DMA((12,)),
        ],
        compiler_params=pltpu.CompilerParams(vmem_limit_bytes=32 * 1024 * 1024),
    )(*[pltpu.with_memory_space_constraint(x, pltpu.HBM) for x in arrays])


def feature_kernel(ex_rows, mixer_ref, own_ref, other_ref, out_ref):
    tokens = own_ref.shape[1]
    rows = ADAPTER_RANK * ex_rows
    pieces = jnp.concatenate([own_ref[PROJ_ROWS:], other_ref[PROJ_ROWS:]], axis=0)
    coeffs = jnp.dot(mixer_ref[...], pieces, preferred_element_type=F32)
    owned = iota((rows, tokens), 1) // SEQ == iota((rows, tokens), 0) % ex_rows
    coeffs = jnp.where(owned, coeffs, 0.0).astype(BF16)
    projected = lax.dot_general(coeffs, own_ref[:PROJ_ROWS], NT, preferred_element_type=F32)
    projected += lax.dot_general(coeffs, other_ref[:PROJ_ROWS], NT, preferred_element_type=F32)
    features = (projected * SCALE).astype(BF16)
    parts = rows // out_ref.shape[1]
    for copy in range(out_ref.shape[0]):
        first = copy % parts * out_ref.shape[1]
        out_ref[copy] = features[first : first + out_ref.shape[1]]


def feature_rows(mixer, own, other, ex_rows, copies, parts):
    rows = ADAPTER_RANK * ex_rows
    return pl.pallas_call(
        functools.partial(feature_kernel, ex_rows),
        out_shape=jax.ShapeDtypeStruct((copies, rows // parts, PROJ_ROWS), BF16),
        in_specs=[VMEM, VMEM, VMEM],
        out_specs=VMEM,
        compiler_params=SMALL,
    )(mixer, own, other)


def fold_ranks(terms):
    half = terms.shape[0] // 2
    return terms[:half] + pltpu.roll(terms[half:], LANES - half, 1)


def pack_lanes(rows, ex_rows):
    parts = [rows[:, i : i + ex_rows] for i in range(0, LANES, 2 * ex_rows)]
    return jnp.concatenate(parts, axis=1)


def pair_kernel(ex_rows, got_ref, keep_ref, send_ref):
    blocks, rows, _ = got_ref.shape
    x = lax.axis_index("x")
    first = 2 * lax.axis_index("z")
    total = None
    for row in range(0, rows, 2 * ex_rows):
        part = pl.ds(row, 2 * ex_rows)
        left = [got_ref[first + x, part, :], got_ref[first + 1 - x, part, :]]
        left = jnp.concatenate(left, axis=0)
        right = jnp.concatenate([got_ref[b, part, :] for b in range(blocks)], axis=0)
        term = lax.dot_general(left, right, NT, preferred_element_type=F32)
        total = term if total is None else total + term
    keep_ref[...] = fold_ranks(total[: 2 * ex_rows])
    send_ref[...] = fold_ranks(total[2 * ex_rows :])


def pair_rows(got, ex_rows):
    return pl.pallas_call(
        functools.partial(pair_kernel, ex_rows),
        out_shape=[jax.ShapeDtypeStruct((ex_rows, LANES), F32)] * 2,
        in_specs=[VMEM],
        out_specs=[VMEM] * 2,
        compiler_params=SMALL,
    )(got)


def halves_kernel(own_ref, got_ref, keep_ref, send_ref):
    total = own_ref[...] + got_ref[...]
    half = keep_ref.shape[0]
    low = lax.axis_index("tensor") == 0
    keep_ref[...] = jnp.where(low, total[:half], total[half:])
    send_ref[...] = jnp.where(low, total[half:], total[:half])


def sum_halves(own, got):
    rows, lanes = own.shape
    return pl.pallas_call(
        halves_kernel,
        out_shape=[jax.ShapeDtypeStruct((rows // 2, lanes), F32)] * 2,
        in_specs=[VMEM] * 2,
        out_specs=[VMEM] * 2,
        compiler_params=SMALL,
    )(own, got)


def sum_kernel(ex_rows, keep_ref, got_ref, out_ref):
    out_ref[...] = pack_lanes(keep_ref[...] + got_ref[...], ex_rows)


def sum_rows(keep, got, ex_rows):
    return pl.pallas_call(
        functools.partial(sum_kernel, ex_rows),
        out_shape=jax.ShapeDtypeStruct((keep.shape[0], LANES // 2), F32),
        in_specs=[VMEM] * 2,
        out_specs=VMEM,
        compiler_params=SMALL,
    )(keep, got)


def swap_cores(value):
    return lax.ppermute(value, "tensor", [(0, 1), (1, 0)])


def swap_across(value):
    return lax.ppermute(value, ("x", "tensor"), [(i, i ^ 3) for i in range(4)])


def trade_kinds(parts):
    blocks, half = parts.shape[0], lax.axis_size("z") // 2
    groups = [[2 * b + (kind ^ (b // 2 // half)) for b in range(blocks)] for kind in range(2)]
    return lax.all_to_all(parts, BLK + ("tensor",), 0, 0, axis_index_groups=groups, tiled=True)


def body(
    hidden, cotangent, token_loss_mask, adapter_down_factor, adapter_up_factor, sign_table_salts
):
    ex_rows, seq, width_half = hidden.shape
    blocks = lax.axis_size("z") * lax.axis_size("x")
    fast = 2 * blocks * ex_rows == LANES and ex_rows == 8
    keep, send, mixer = sketch_rows(
        sign_table_salts,
        token_loss_mask,
        adapter_down_factor,
        adapter_up_factor.T,
        hidden.reshape(ex_rows * seq, width_half),
        cotangent.reshape(ex_rows * seq, width_half),
        fast,
    )
    other = swap_cores(send)
    if fast:
        got = trade_kinds(feature_rows(mixer, keep, other, ex_rows, blocks, 2))
        keep, send = pair_rows(got, ex_rows)
        keep, send = sum_halves(keep, swap_across(send))
        return sum_rows(keep, swap_cores(send), ex_rows)
    whole = feature_rows(mixer, keep, other, ex_rows, 1, 1)
    share = ADAPTER_RANK * PROJ_ROWS // blocks
    parts = whole.reshape(ADAPTER_RANK, ex_rows, PROJ_ROWS // share, share)
    parts = parts.swapaxes(1, 2).reshape(blocks, ex_rows, share)
    features = lax.all_to_all(parts, BLK, 0, 0, tiled=True).reshape(blocks * ex_rows, share)
    pairs = jnp.einsum("ep,fp->ef", features, features, preferred_element_type=F32)
    pairs = pairs.reshape(blocks, ex_rows, blocks * ex_rows)
    total = jnp.sum(lax.all_to_all(pairs, BLK, 0, 0, tiled=True), axis=0)
    halves = total.reshape(2, ex_rows // 2, blocks * ex_rows)
    core = lax.axis_index("tensor")
    send = lax.dynamic_index_in_dim(halves, 1 - core, 0, keepdims=False)
    return lax.dynamic_index_in_dim(halves, core, 0, keepdims=False) + swap_cores(send)


def solution(mesh):
    groups, blocks, cores = (mesh.shape[name] for name in ("groups", "blk", "tensor"))
    devices = mesh.devices.reshape(groups, blocks // 2, 2, cores)
    placed = (
        P(("groups", "z", "x"), None, "tensor"),
        P(("groups", "z", "x"), None, "tensor"),
        P(("groups", "z", "x"), None),
        P(None, "tensor"),
        P("tensor", None),
        P(),
    )
    return jax.shard_map(
        body,
        mesh=Mesh(devices, ("groups", "z", "x", "tensor")),
        in_specs=placed,
        out_specs=P(("groups", "z", "x", "tensor"), None),
        check_vma=False,
    )
```

```python
import functools
import math

import jax
import jax.numpy as jnp
from jax import lax
from jax.experimental import pallas as pl
from jax.experimental.pallas import tpu as pltpu
from jax.sharding import Mesh, PartitionSpec as P

MODEL_WIDTH = 4096
ADAPTER_RANK = 16
PROJ_ROWS = 256
SEQ = 64
SCALE = 1.0 / math.sqrt(PROJ_ROWS * ADAPTER_RANK * ADAPTER_RANK * SEQ * MODEL_WIDTH)
PIECES = 3
LANES = 128
TILE = 256
BLK = ("z", "x")

F32 = jnp.float32
BF16 = jnp.bfloat16
I32 = jnp.int32
NT = (((1,), (1,)), ((), ()))
VMEM = pl.BlockSpec(memory_space=pltpu.VMEM)
SMEM = pl.BlockSpec(memory_space=pltpu.SMEM)
HBM = pl.BlockSpec(memory_space=pltpu.HBM)
SMALL = pltpu.CompilerParams(vmem_limit_bytes=16 * 1024 * 1024)

INDEX_MUL = -1640531535
SALT_MUL = 668265263


def int32_wrap(value):
    return (value + 2**31) % 2**32 - 2**31


def hash_sign(hashed):
    hashed = hashed ^ lax.shift_right_logical(hashed, 15)
    hashed = hashed * -2048144789
    hashed = hashed ^ lax.shift_right_logical(hashed, 13)
    hashed = hashed * int32_wrap(-1028477387 << 6)
    hashed = hashed ^ lax.shift_left(hashed, 16)
    return jnp.where(hashed < 0, 1.0, -1.0).astype(F32)


def iota(shape, dim):
    return lax.broadcasted_iota(I32, shape, dim)


def token_row(mask):
    ex_rows, seq = mask.shape
    tokens = ex_rows * seq
    tiled = jnp.concatenate([mask.astype(F32)] * ex_rows, axis=1)
    owner = iota((ex_rows, tokens), 1) // seq == iota((ex_rows, tokens), 0)
    return jnp.sum(jnp.where(owner, tiled, 0.0), axis=0, keepdims=True)


def split_pieces(value):
    pieces = []
    for _ in range(PIECES):
        pieces.append(value.astype(BF16))
        value = value - pieces[-1].astype(F32)
    return jnp.concatenate(pieces, axis=0)


def kind_of(cross):
    core = lax.axis_index("tensor")
    return core ^ (lax.axis_index("z") // (lax.axis_size("z") // 2)) if cross else core


def rows_kernel(
    cross, ex_rows,
    salts_hbm, mask_hbm, down_hbm, up_hbm, hid_hbm, cot_hbm,
    keep_ref, send_ref, mixer_ref,
    salts, mask, factor, held, left, total, sems, copy_sems,
):
    _, tokens, width = held.shape
    kind = kind_of(cross)
    steps = width // TILE
    small = [
        pltpu.make_async_copy(salts_hbm, salts, sems.at[0]),
        pltpu.make_async_copy(mask_hbm, mask, sems.at[1]),
        pltpu.make_async_copy(down_hbm, factor.at[kind], sems.at[2]),
        pltpu.make_async_copy(up_hbm, factor.at[1 - kind], sems.at[3]),
    ]

    def chunk(inputs, which, step):
        cols = pl.ds(pl.multiple_of(step * TILE, TILE), TILE)
        return pltpu.make_async_copy(
            inputs.at[:, cols], held.at[which, :, cols], copy_sems.at[which, step]
        )

    for copy in small:
        copy.start()

    @pl.when(kind == 0)
    def _():
        for which, inputs in enumerate((hid_hbm, cot_hbm)):
            for step in range(steps):
                chunk(inputs, which, step).start()

    @pl.when(kind == 1)
    def _():
        for which, inputs in enumerate((cot_hbm, hid_hbm)):
            for step in range(steps):
                chunk(inputs, which, step).start()

    high = 16
    index = iota((high, TILE), 1) * PROJ_ROWS + iota((high, TILE), 0)
    start = index * INDEX_MUL
    first = lax.axis_index("tensor") * int32_wrap(width * PROJ_ROWS * INDEX_MUL)

    def fill(which, step, slot):
        salt = salts[jnp.where(which == 0, 2 - 2 * kind, 2 * kind)]
        offset = first + salt * SALT_MUL + step * int32_wrap(TILE * PROJ_ROWS * INDEX_MUL)
        for row in range(0, PROJ_ROWS, high):
            signs = hash_sign(start + (offset + int32_wrap(row * INDEX_MUL)))
            left[slot, row : row + high, :] = signs.astype(BF16)
        cols = pl.ds(pl.multiple_of(step * TILE, TILE), TILE)
        left[slot, PROJ_ROWS:, :] = factor[which, :, cols]

    def step_of(turn, carry):
        which, step = turn // steps, turn % steps
        chunk(hid_hbm, which, step).wait()
        after = jnp.minimum(turn + 1, 2 * steps - 1)
        fill(after // steps, after % steps, (turn + 1) % 2)
        cols = pl.ds(pl.multiple_of(step * TILE, TILE), TILE)
        term = lax.dot_general(
            left[turn % 2], held[which, :, cols], NT, preferred_element_type=F32
        )
        total[which] += term
        return carry

    total[...] = jnp.zeros_like(total)
    for copy in small:
        copy.wait()
    fill(0, 0, 0)
    lax.fori_loop(0, 2 * steps, step_of, 0)
    counted = token_row(mask[...]) != 0
    got = jnp.where(counted | (kind == 0), total[0], 0.0)
    send_ref[:PROJ_ROWS] = got[:PROJ_ROWS].astype(BF16)
    keep_ref[PROJ_ROWS:] = split_pieces(got[PROJ_ROWS:])
    got = jnp.where(counted | (kind == 1), total[1], 0.0)
    keep_ref[:PROJ_ROWS] = got[:PROJ_ROWS].astype(BF16)
    send_ref[PROJ_ROWS:] = split_pieces(got[PROJ_ROWS:])
    shape = mixer_ref.shape
    mixed, rank = iota(shape, 0) // ex_rows, iota(shape, 1) % ADAPTER_RANK
    index = (rank * ADAPTER_RANK + mixed) * INDEX_MUL
    mixer_ref[...] = hash_sign(index + salts[1 + 2 * kind] * SALT_MUL).astype(BF16)


def sketch_rows(salts, mask, down, up, hidden, cotangent, cross):
    ex_rows = mask.shape[0]
    tokens, width = hidden.shape
    rows = PROJ_ROWS + PIECES * ADAPTER_RANK
    arrays = (salts, mask, down, up, hidden, cotangent)
    return pl.pallas_call(
        functools.partial(rows_kernel, cross, ex_rows),
        out_shape=[jax.ShapeDtypeStruct((rows, tokens), BF16)] * 2
        + [jax.ShapeDtypeStruct((ADAPTER_RANK * ex_rows, 2 * PIECES * ADAPTER_RANK), BF16)],
        in_specs=[HBM] * 6,
        out_specs=[VMEM] * 3,
        scratch_shapes=[
            pltpu.SMEM(salts.shape, I32),
            pltpu.VMEM(mask.shape, I32),
            pltpu.VMEM((2, ADAPTER_RANK, width), BF16),
            pltpu.VMEM((2, tokens, width), BF16),
            pltpu.VMEM((2, PROJ_ROWS + ADAPTER_RANK, TILE), BF16),
            pltpu.VMEM((2, PROJ_ROWS + ADAPTER_RANK, tokens), F32),
            pltpu.SemaphoreType.DMA((4,)),
            pltpu.SemaphoreType.DMA((2, width // TILE)),
        ],
        compiler_params=pltpu.CompilerParams(vmem_limit_bytes=32 * 1024 * 1024),
    )(*[pltpu.with_memory_space_constraint(x, pltpu.HBM) for x in arrays])


def feature_kernel(ex_rows, mixer_ref, own_ref, other_ref, out_ref):
    tokens = own_ref.shape[1]
    rows = ADAPTER_RANK * ex_rows
    pieces = jnp.concatenate([own_ref[PROJ_ROWS:], other_ref[PROJ_ROWS:]], axis=0)
    coeffs = jnp.dot(mixer_ref[...], pieces, preferred_element_type=F32)
    owned = iota((rows, tokens), 1) // SEQ == iota((rows, tokens), 0) % ex_rows
    coeffs = jnp.where(owned, coeffs, 0.0).astype(BF16)
    projected = lax.dot_general(coeffs, own_ref[:PROJ_ROWS], NT, preferred_element_type=F32)
    projected += lax.dot_general(coeffs, other_ref[:PROJ_ROWS], NT, preferred_element_type=F32)
    features = (projected * SCALE).astype(BF16)
    parts = rows // out_ref.shape[1]
    for copy in range(out_ref.shape[0]):
        first = copy % parts * out_ref.shape[1]
        out_ref[copy] = features[first : first + out_ref.shape[1]]


def feature_rows(mixer, own, other, ex_rows, copies, parts):
    rows = ADAPTER_RANK * ex_rows
    return pl.pallas_call(
        functools.partial(feature_kernel, ex_rows),
        out_shape=jax.ShapeDtypeStruct((copies, rows // parts, PROJ_ROWS), BF16),
        in_specs=[VMEM, VMEM, VMEM],
        out_specs=VMEM,
        compiler_params=SMALL,
    )(mixer, own, other)


def fold_ranks(terms):
    half = terms.shape[0] // 2
    return terms[:half] + pltpu.roll(terms[half:], LANES - half, 1)


def pack_lanes(rows, ex_rows):
    parts = [rows[:, i : i + ex_rows] for i in range(0, LANES, 2 * ex_rows)]
    return jnp.concatenate(parts, axis=1)


def pair_kernel(ex_rows, got_ref, keep_ref, send_ref):
    blocks, rows, _ = got_ref.shape
    x = lax.axis_index("x")
    first = 2 * lax.axis_index("z")
    total = None
    for row in range(0, rows, 2 * ex_rows):
        part = pl.ds(row, 2 * ex_rows)
        left = [got_ref[first + x, part, :], got_ref[first + 1 - x, part, :]]
        left = jnp.concatenate(left, axis=0)
        right = jnp.concatenate([got_ref[b, part, :] for b in range(blocks)], axis=0)
        term = lax.dot_general(left, right, NT, preferred_element_type=F32)
        total = term if total is None else total + term
    keep_ref[...] = fold_ranks(total[: 2 * ex_rows])
    send_ref[...] = fold_ranks(total[2 * ex_rows :])


def pair_rows(got, ex_rows):
    return pl.pallas_call(
        functools.partial(pair_kernel, ex_rows),
        out_shape=[jax.ShapeDtypeStruct((ex_rows, LANES), F32)] * 2,
        in_specs=[VMEM],
        out_specs=[VMEM] * 2,
        compiler_params=SMALL,
    )(got)


def halves_kernel(own_ref, got_ref, keep_ref, send_ref):
    total = own_ref[...] + got_ref[...]
    half = keep_ref.shape[0]
    low = lax.axis_index("tensor") == 0
    keep_ref[...] = jnp.where(low, total[:half], total[half:])
    send_ref[...] = jnp.where(low, total[half:], total[:half])


def sum_halves(own, got):
    rows, lanes = own.shape
    return pl.pallas_call(
        halves_kernel,
        out_shape=[jax.ShapeDtypeStruct((rows // 2, lanes), F32)] * 2,
        in_specs=[VMEM] * 2,
        out_specs=[VMEM] * 2,
        compiler_params=SMALL,
    )(own, got)


def sum_kernel(ex_rows, keep_ref, got_ref, out_ref):
    out_ref[...] = pack_lanes(keep_ref[...] + got_ref[...], ex_rows)


def sum_rows(keep, got, ex_rows):
    return pl.pallas_call(
        functools.partial(sum_kernel, ex_rows),
        out_shape=jax.ShapeDtypeStruct((keep.shape[0], LANES // 2), F32),
        in_specs=[VMEM] * 2,
        out_specs=VMEM,
        compiler_params=SMALL,
    )(keep, got)


def swap_cores(value):
    return lax.ppermute(value, "tensor", [(0, 1), (1, 0)])


def swap_across(value):
    return lax.ppermute(value, ("x", "tensor"), [(i, i ^ 3) for i in range(4)])


def trade_kinds(parts):
    blocks, half = parts.shape[0], lax.axis_size("z") // 2
    groups = [[2 * b + (kind ^ (b // 2 // half)) for b in range(blocks)] for kind in range(2)]
    return lax.all_to_all(parts, BLK + ("tensor",), 0, 0, axis_index_groups=groups, tiled=True)


def body(
    hidden, cotangent, token_loss_mask, adapter_down_factor, adapter_up_factor, sign_table_salts
):
    ex_rows, seq, width_half = hidden.shape
    blocks = lax.axis_size("z") * lax.axis_size("x")
    fast = 2 * blocks * ex_rows == LANES and ex_rows == 8
    keep, send, mixer = sketch_rows(
        sign_table_salts,
        token_loss_mask,
        adapter_down_factor,
        adapter_up_factor.T,
        hidden.reshape(ex_rows * seq, width_half),
        cotangent.reshape(ex_rows * seq, width_half),
        fast,
    )
    other = swap_cores(send)
    if fast:
        got = trade_kinds(feature_rows(mixer, keep, other, ex_rows, blocks, 2))
        keep, send = pair_rows(got, ex_rows)
        keep, send = sum_halves(keep, swap_across(send))
        return sum_rows(keep, swap_cores(send), ex_rows)
    whole = feature_rows(mixer, keep, other, ex_rows, 1, 1)
    share = ADAPTER_RANK * PROJ_ROWS // blocks
    parts = whole.reshape(ADAPTER_RANK, ex_rows, PROJ_ROWS // share, share)
    parts = parts.swapaxes(1, 2).reshape(blocks, ex_rows, share)
    features = lax.all_to_all(parts, BLK, 0, 0, tiled=True).reshape(blocks * ex_rows, share)
    pairs = jnp.einsum("ep,fp->ef", features, features, preferred_element_type=F32)
    pairs = pairs.reshape(blocks, ex_rows, blocks * ex_rows)
    total = jnp.sum(lax.all_to_all(pairs, BLK, 0, 0, tiled=True), axis=0)
    halves = total.reshape(2, ex_rows // 2, blocks * ex_rows)
    core = lax.axis_index("tensor")
    send = lax.dynamic_index_in_dim(halves, 1 - core, 0, keepdims=False)
    return lax.dynamic_index_in_dim(halves, core, 0, keepdims=False) + swap_cores(send)


def solution(mesh):
    groups, blocks, cores = (mesh.shape[name] for name in ("groups", "blk", "tensor"))
    devices = mesh.devices.reshape(groups, blocks // 2, 2, cores)
    placed = (
        P(("groups", "z", "x"), None, "tensor"),
        P(("groups", "z", "x"), None, "tensor"),
        P(("groups", "z", "x"), None),
        P(None, "tensor"),
        P("tensor", None),
        P(),
    )
    return jax.shard_map(
        body,
        mesh=Mesh(devices, ("groups", "z", "x", "tensor")),
        in_specs=placed,
        out_specs=P(("groups", "z", "x", "tensor"), None),
        check_vma=False,
    )
```

```python
import functools
import math

import jax
import jax.numpy as jnp
from jax import lax
from jax.experimental import pallas as pl
from jax.experimental.pallas import tpu as pltpu
from jax.sharding import Mesh, PartitionSpec as P

MODEL_WIDTH = 4096
ADAPTER_RANK = 16
PROJ_ROWS = 256
SEQ = 64
SCALE = 1.0 / math.sqrt(PROJ_ROWS * ADAPTER_RANK * ADAPTER_RANK * SEQ * MODEL_WIDTH)
PIECES = 3
LANES = 128
TILE = 512
BLK = ("z", "x")

F32 = jnp.float32
BF16 = jnp.bfloat16
I32 = jnp.int32
NT = (((1,), (1,)), ((), ()))
VMEM = pl.BlockSpec(memory_space=pltpu.VMEM)
SMEM = pl.BlockSpec(memory_space=pltpu.SMEM)
HBM = pl.BlockSpec(memory_space=pltpu.HBM)
SMALL = pltpu.CompilerParams(vmem_limit_bytes=16 * 1024 * 1024)

INDEX_MUL = -1640531535
SALT_MUL = 668265263


def int32_wrap(value):
    return (value + 2**31) % 2**32 - 2**31


def hash_sign(hashed):
    hashed = hashed ^ lax.shift_right_logical(hashed, 15)
    hashed = hashed * -2048144789
    hashed = hashed ^ lax.shift_right_logical(hashed, 13)
    hashed = hashed * int32_wrap(-1028477387 << 6)
    hashed = hashed ^ lax.shift_left(hashed, 16)
    return jnp.where(hashed < 0, 1.0, -1.0).astype(F32)


def iota(shape, dim):
    return lax.broadcasted_iota(I32, shape, dim)


def token_row(mask):
    ex_rows, seq = mask.shape
    tokens = ex_rows * seq
    tiled = jnp.concatenate([mask.astype(F32)] * ex_rows, axis=1)
    owner = iota((ex_rows, tokens), 1) // seq == iota((ex_rows, tokens), 0)
    return jnp.sum(jnp.where(owner, tiled, 0.0), axis=0, keepdims=True)


def split_pieces(value):
    pieces = []
    for _ in range(PIECES):
        pieces.append(value.astype(BF16))
        value = value - pieces[-1].astype(F32)
    return jnp.concatenate(pieces, axis=0)


def kind_of(cross):
    core = lax.axis_index("tensor")
    return core ^ (lax.axis_index("z") // (lax.axis_size("z") // 2)) if cross else core


def rows_kernel(
    cross, ex_rows,
    salts_hbm, mask_hbm, down_hbm, up_hbm, hid_hbm, cot_hbm,
    keep_ref, send_ref, mixer_ref,
    salts, mask, far_left, near_left, far, near, sems, far_sems, near_sems,
):
    tokens, width = near.shape
    kind = kind_of(cross)
    steps = width // TILE
    salts_copy = pltpu.make_async_copy(salts_hbm, salts, sems.at[0])
    mask_copy = pltpu.make_async_copy(mask_hbm, mask, sems.at[1])

    def copies(inputs, factor, left, held, held_sems):
        rows = left.at[pl.ds(PROJ_ROWS, ADAPTER_RANK)]
        out = [pltpu.make_async_copy(factor, rows, held_sems.at[steps])]
        for step in range(steps):
            cols = pl.ds(step * TILE, TILE)
            out.append(
                pltpu.make_async_copy(inputs.at[:, cols], held.at[:, cols], held_sems.at[step])
            )
        return out

    def start_copies(far_inputs, far_factor, near_inputs, near_factor):
        for copy in copies(far_inputs, far_factor, far_left, far, far_sems):
            copy.start()
        for copy in copies(near_inputs, near_factor, near_left, near, near_sems):
            copy.start()

    salts_copy.start()

    @pl.when(kind == 0)
    def _():
        start_copies(hid_hbm, down_hbm, cot_hbm, up_hbm)

    @pl.when(kind == 1)
    def _():
        start_copies(cot_hbm, up_hbm, hid_hbm, down_hbm)

    mask_copy.start()
    high, wide = 16, 256
    index = iota((high, wide), 1) * PROJ_ROWS + iota((high, wide), 0)
    start = index * INDEX_MUL
    first = lax.axis_index("tensor") * int32_wrap(width * PROJ_ROWS * INDEX_MUL)

    def fill(left, salt, step):
        offset = first + salt * SALT_MUL
        for col in range(step * TILE, (step + 1) * TILE, wide):
            for row in range(0, PROJ_ROWS, high):
                shift = offset + int32_wrap((col * PROJ_ROWS + row) * INDEX_MUL)
                signs = hash_sign(start + shift).astype(BF16)
                left[row : row + high, col : col + wide] = signs

    work = []
    for left, held, held_sems, salt in (
        (far_left, far, far_sems, 2 - 2 * kind),
        (near_left, near, near_sems, 2 * kind),
    ):
        waits = copies(hid_hbm, down_hbm, left, held, held_sems)
        for step in range(steps):
            work.append((left, held, salt, step, waits[:2] if step == 0 else [waits[step + 1]]))
    salts_copy.wait()
    fill(far_left, salts[2 - 2 * kind], 0)
    totals = []
    for turn, (left, held, _, step, waits) in enumerate(work):
        for copy in waits:
            copy.wait()
        if turn + 1 < len(work):
            after, _, salt, after_step, _ = work[turn + 1]
            fill(after, salts[salt], after_step)
        part = slice(step * TILE, (step + 1) * TILE)
        term = lax.dot_general(left[:, part], held[:, part], NT, preferred_element_type=F32)
        if step == 0:
            totals.append(term)
        else:
            totals[-1] = totals[-1] + term
        if turn + 1 == steps:
            mask_copy.wait()
            counted = token_row(mask[...]) != 0
            got = jnp.where(counted | (kind == 0), totals[0], 0.0)
            send_ref[:PROJ_ROWS] = got[:PROJ_ROWS].astype(BF16)
            keep_ref[PROJ_ROWS:] = split_pieces(got[PROJ_ROWS:])
    got = jnp.where(counted | (kind == 1), totals[1], 0.0)
    keep_ref[:PROJ_ROWS] = got[:PROJ_ROWS].astype(BF16)
    send_ref[PROJ_ROWS:] = split_pieces(got[PROJ_ROWS:])
    shape = mixer_ref.shape
    mixed, rank = iota(shape, 0) // ex_rows, iota(shape, 1) % ADAPTER_RANK
    index = (rank * ADAPTER_RANK + mixed) * INDEX_MUL
    mixer_ref[...] = hash_sign(index + salts[1 + 2 * kind] * SALT_MUL).astype(BF16)


def sketch_rows(salts, mask, down, up, hidden, cotangent, cross):
    ex_rows = mask.shape[0]
    tokens, width = hidden.shape
    rows = PROJ_ROWS + PIECES * ADAPTER_RANK
    arrays = (salts, mask, down, up, hidden, cotangent)
    return pl.pallas_call(
        functools.partial(rows_kernel, cross, ex_rows),
        out_shape=[jax.ShapeDtypeStruct((rows, tokens), BF16)] * 2
        + [jax.ShapeDtypeStruct((ADAPTER_RANK * ex_rows, 2 * PIECES * ADAPTER_RANK), BF16)],
        in_specs=[HBM] * 6,
        out_specs=[VMEM] * 3,
        scratch_shapes=[
            pltpu.SMEM(salts.shape, I32),
            pltpu.VMEM(mask.shape, I32),
            pltpu.VMEM((PROJ_ROWS + ADAPTER_RANK, width), BF16),
            pltpu.VMEM((PROJ_ROWS + ADAPTER_RANK, width), BF16),
            pltpu.VMEM((tokens, width), BF16),
            pltpu.VMEM((tokens, width), BF16),
            pltpu.SemaphoreType.DMA((2,)),
            pltpu.SemaphoreType.DMA((width // TILE + 1,)),
            pltpu.SemaphoreType.DMA((width // TILE + 1,)),
        ],
        compiler_params=pltpu.CompilerParams(vmem_limit_bytes=32 * 1024 * 1024),
    )(*[pltpu.with_memory_space_constraint(x, pltpu.HBM) for x in arrays])


def feature_kernel(ex_rows, mixer_ref, own_ref, other_ref, out_ref):
    tokens = own_ref.shape[1]
    rows = ADAPTER_RANK * ex_rows
    pieces = jnp.concatenate([own_ref[PROJ_ROWS:], other_ref[PROJ_ROWS:]], axis=0)
    coeffs = jnp.dot(mixer_ref[...], pieces, preferred_element_type=F32)
    owned = iota((rows, tokens), 1) // SEQ == iota((rows, tokens), 0) % ex_rows
    coeffs = jnp.where(owned, coeffs, 0.0).astype(BF16)
    projected = lax.dot_general(coeffs, own_ref[:PROJ_ROWS], NT, preferred_element_type=F32)
    projected += lax.dot_general(coeffs, other_ref[:PROJ_ROWS], NT, preferred_element_type=F32)
    features = (projected * SCALE).astype(BF16)
    parts = rows // out_ref.shape[1]
    for copy in range(out_ref.shape[0]):
        first = copy % parts * out_ref.shape[1]
        out_ref[copy] = features[first : first + out_ref.shape[1]]


def feature_rows(mixer, own, other, ex_rows, copies, parts):
    rows = ADAPTER_RANK * ex_rows
    return pl.pallas_call(
        functools.partial(feature_kernel, ex_rows),
        out_shape=jax.ShapeDtypeStruct((copies, rows // parts, PROJ_ROWS), BF16),
        in_specs=[VMEM, VMEM, VMEM],
        out_specs=VMEM,
        compiler_params=SMALL,
    )(mixer, own, other)


def fold_ranks(terms):
    half = terms.shape[0] // 2
    return terms[:half] + pltpu.roll(terms[half:], LANES - half, 1)


def pack_lanes(rows, ex_rows):
    parts = [rows[:, i : i + ex_rows] for i in range(0, LANES, 2 * ex_rows)]
    return jnp.concatenate(parts, axis=1)


def pair_kernel(ex_rows, got_ref, keep_ref, send_ref):
    blocks, rows, _ = got_ref.shape
    x = lax.axis_index("x")
    first = 2 * lax.axis_index("z")
    total = None
    for row in range(0, rows, 2 * ex_rows):
        part = pl.ds(row, 2 * ex_rows)
        left = [got_ref[first + x, part, :], got_ref[first + 1 - x, part, :]]
        left = jnp.concatenate(left, axis=0)
        right = jnp.concatenate([got_ref[b, part, :] for b in range(blocks)], axis=0)
        term = lax.dot_general(left, right, NT, preferred_element_type=F32)
        total = term if total is None else total + term
    keep_ref[...] = fold_ranks(total[: 2 * ex_rows])
    send_ref[...] = fold_ranks(total[2 * ex_rows :])


def pair_rows(got, ex_rows):
    return pl.pallas_call(
        functools.partial(pair_kernel, ex_rows),
        out_shape=[jax.ShapeDtypeStruct((ex_rows, LANES), F32)] * 2,
        in_specs=[VMEM],
        out_specs=[VMEM] * 2,
        compiler_params=SMALL,
    )(got)


def halves_kernel(own_ref, got_ref, keep_ref, send_ref):
    total = own_ref[...] + got_ref[...]
    half = keep_ref.shape[0]
    low = lax.axis_index("tensor") == 0
    keep_ref[...] = jnp.where(low, total[:half], total[half:])
    send_ref[...] = jnp.where(low, total[half:], total[:half])


def sum_halves(own, got):
    rows, lanes = own.shape
    return pl.pallas_call(
        halves_kernel,
        out_shape=[jax.ShapeDtypeStruct((rows // 2, lanes), F32)] * 2,
        in_specs=[VMEM] * 2,
        out_specs=[VMEM] * 2,
        compiler_params=SMALL,
    )(own, got)


def sum_kernel(ex_rows, keep_ref, got_ref, out_ref):
    out_ref[...] = pack_lanes(keep_ref[...] + got_ref[...], ex_rows)


def sum_rows(keep, got, ex_rows):
    return pl.pallas_call(
        functools.partial(sum_kernel, ex_rows),
        out_shape=jax.ShapeDtypeStruct((keep.shape[0], LANES // 2), F32),
        in_specs=[VMEM] * 2,
        out_specs=VMEM,
        compiler_params=SMALL,
    )(keep, got)


def swap_cores(value):
    return lax.ppermute(value, "tensor", [(0, 1), (1, 0)])


def swap_across(value):
    return lax.ppermute(value, ("x", "tensor"), [(i, i ^ 3) for i in range(4)])


def trade_kinds(parts):
    blocks, half = parts.shape[0], lax.axis_size("z") // 2
    groups = [[2 * b + (kind ^ (b // 2 // half)) for b in range(blocks)] for kind in range(2)]
    return lax.all_to_all(parts, BLK + ("tensor",), 0, 0, axis_index_groups=groups, tiled=True)


def body(
    hidden, cotangent, token_loss_mask, adapter_down_factor, adapter_up_factor, sign_table_salts
):
    ex_rows, seq, width_half = hidden.shape
    blocks = lax.axis_size("z") * lax.axis_size("x")
    fast = 2 * blocks * ex_rows == LANES and ex_rows == 8
    keep, send, mixer = sketch_rows(
        sign_table_salts,
        token_loss_mask,
        adapter_down_factor,
        adapter_up_factor.T,
        hidden.reshape(ex_rows * seq, width_half),
        cotangent.reshape(ex_rows * seq, width_half),
        fast,
    )
    other = swap_cores(send)
    if fast:
        got = trade_kinds(feature_rows(mixer, keep, other, ex_rows, blocks, 2))
        keep, send = pair_rows(got, ex_rows)
        keep, send = sum_halves(keep, swap_across(send))
        return sum_rows(keep, swap_cores(send), ex_rows)
    whole = feature_rows(mixer, keep, other, ex_rows, 1, 1)
    share = ADAPTER_RANK * PROJ_ROWS // blocks
    parts = whole.reshape(ADAPTER_RANK, ex_rows, PROJ_ROWS // share, share)
    parts = parts.swapaxes(1, 2).reshape(blocks, ex_rows, share)
    features = lax.all_to_all(parts, BLK, 0, 0, tiled=True).reshape(blocks * ex_rows, share)
    pairs = jnp.einsum("ep,fp->ef", features, features, preferred_element_type=F32)
    pairs = pairs.reshape(blocks, ex_rows, blocks * ex_rows)
    total = jnp.sum(lax.all_to_all(pairs, BLK, 0, 0, tiled=True), axis=0)
    halves = total.reshape(2, ex_rows // 2, blocks * ex_rows)
    core = lax.axis_index("tensor")
    send = lax.dynamic_index_in_dim(halves, 1 - core, 0, keepdims=False)
    return lax.dynamic_index_in_dim(halves, core, 0, keepdims=False) + swap_cores(send)


def solution(mesh):
    groups, blocks, cores = (mesh.shape[name] for name in ("groups", "blk", "tensor"))
    devices = mesh.devices.reshape(groups, blocks // 2, 2, cores)
    placed = (
        P(("groups", "z", "x"), None, "tensor"),
        P(("groups", "z", "x"), None, "tensor"),
        P(("groups", "z", "x"), None),
        P(None, "tensor"),
        P("tensor", None),
        P(),
    )
    return jax.shard_map(
        body,
        mesh=Mesh(devices, ("groups", "z", "x", "tensor")),
        in_specs=placed,
        out_specs=P(("groups", "z", "x", "tensor"), None),
        check_vma=False,
    )
```

```python
import functools
import math

import jax
import jax.numpy as jnp
from jax import lax
from jax.experimental import pallas as pl
from jax.experimental.pallas import tpu as pltpu
from jax.sharding import Mesh, PartitionSpec as P

MODEL_WIDTH = 4096
ADAPTER_RANK = 16
PROJ_ROWS = 256
SEQ = 64
SCALE = 1.0 / math.sqrt(PROJ_ROWS * ADAPTER_RANK * ADAPTER_RANK * SEQ * MODEL_WIDTH)
PIECES = 3
LANES = 128
TILE = 1024
BLK = ("z", "x")

F32 = jnp.float32
BF16 = jnp.bfloat16
I32 = jnp.int32
NT = (((1,), (1,)), ((), ()))
VMEM = pl.BlockSpec(memory_space=pltpu.VMEM)
SMEM = pl.BlockSpec(memory_space=pltpu.SMEM)
HBM = pl.BlockSpec(memory_space=pltpu.HBM)
SMALL = pltpu.CompilerParams(vmem_limit_bytes=16 * 1024 * 1024)

INDEX_MUL = -1640531535
SALT_MUL = 668265263


def int32_wrap(value):
    return (value + 2**31) % 2**32 - 2**31


def hash_sign(hashed):
    hashed = hashed ^ lax.shift_right_logical(hashed, 15)
    hashed = hashed * -2048144789
    hashed = hashed ^ lax.shift_right_logical(hashed, 13)
    hashed = hashed * int32_wrap(-1028477387 << 6)
    hashed = hashed ^ lax.shift_left(hashed, 16)
    return jnp.where(hashed < 0, 1.0, -1.0).astype(F32)


def iota(shape, dim):
    return lax.broadcasted_iota(I32, shape, dim)


def token_row(mask):
    ex_rows, seq = mask.shape
    tokens = ex_rows * seq
    tiled = jnp.concatenate([mask.astype(F32)] * ex_rows, axis=1)
    owner = iota((ex_rows, tokens), 1) // seq == iota((ex_rows, tokens), 0)
    return jnp.sum(jnp.where(owner, tiled, 0.0), axis=0, keepdims=True)


def split_pieces(value):
    pieces = []
    for _ in range(PIECES):
        pieces.append(value.astype(BF16))
        value = value - pieces[-1].astype(F32)
    return jnp.concatenate(pieces, axis=0)


def kind_of(cross):
    core = lax.axis_index("tensor")
    return core ^ (lax.axis_index("z") // (lax.axis_size("z") // 2)) if cross else core


def rows_kernel(
    cross, ex_rows,
    salts_hbm, mask_hbm, down_hbm, up_hbm, hid_hbm, cot_hbm,
    keep_ref, send_ref, mixer_ref,
    salts, mask, far_factor, near_factor, far, near, sems,
):
    tokens, width = near.shape
    kind = kind_of(cross)
    parts = 4
    share = width // parts

    def copies(inputs, factor, factor_held, held, first):
        out = [
            pltpu.make_async_copy(
                inputs.at[:, pl.ds(i * share, share)],
                held.at[:, pl.ds(i * share, share)],
                sems.at[first + i],
            )
            for i in range(parts)
        ]
        return [pltpu.make_async_copy(factor, factor_held, sems.at[first + parts])] + out

    salts_copy = pltpu.make_async_copy(salts_hbm, salts, sems.at[2 * parts + 3])
    salts_copy.start()
    mask_copy = pltpu.make_async_copy(mask_hbm, mask, sems.at[2 * parts + 2])

    @pl.when(kind == 0)
    def _():
        for copy in copies(hid_hbm, down_hbm, far_factor, far, 0):
            copy.start()
        for copy in copies(cot_hbm, up_hbm, near_factor, near, parts + 1):
            copy.start()

    @pl.when(kind == 1)
    def _():
        for copy in copies(cot_hbm, up_hbm, far_factor, far, 0):
            copy.start()
        for copy in copies(hid_hbm, down_hbm, near_factor, near, parts + 1):
            copy.start()

    mask_copy.start()
    high, wide = 16, 256
    index = iota((high, wide), 1) * PROJ_ROWS + iota((high, wide), 0)
    start = index * INDEX_MUL
    first = lax.axis_index("tensor") * int32_wrap(width * PROJ_ROWS * INDEX_MUL)

    def signs(salt, col):
        offset = first + salt * SALT_MUL
        rows = [
            hash_sign(start + (offset + int32_wrap((col * PROJ_ROWS + row) * INDEX_MUL)))
            for row in range(0, PROJ_ROWS, high)
        ]
        return [row.astype(BF16) for row in rows]

    def products(salt, factor, held, waits):
        waits[0].wait()
        total = None
        for col in range(0, width, TILE):
            part = slice(col, col + TILE)
            tiles = [
                jnp.concatenate(signs(salt, at), axis=0) for at in range(col, col + TILE, wide)
            ]
            left = jnp.concatenate([jnp.concatenate(tiles, axis=1), factor[:, part]], axis=0)
            for wait in waits[1 + col // share : 1 + (col + TILE) // share]:
                wait.wait()
            term = lax.dot_general(left, held[:, part], NT, preferred_element_type=F32)
            total = term if total is None else total + term
        return total

    salts_copy.wait()
    waits = copies(hid_hbm, down_hbm, far_factor, far, 0)
    got = products(salts[2 - 2 * kind], far_factor, far, waits)
    mask_copy.wait()
    counted = token_row(mask[...]) != 0
    got = jnp.where(counted | (kind == 0), got, 0.0)
    send_ref[:PROJ_ROWS] = got[:PROJ_ROWS].astype(BF16)
    keep_ref[PROJ_ROWS:] = split_pieces(got[PROJ_ROWS:])
    waits = copies(hid_hbm, down_hbm, near_factor, near, parts + 1)
    got = products(salts[2 * kind], near_factor, near, waits)
    got = jnp.where(counted | (kind == 1), got, 0.0)
    keep_ref[:PROJ_ROWS] = got[:PROJ_ROWS].astype(BF16)
    send_ref[PROJ_ROWS:] = split_pieces(got[PROJ_ROWS:])
    shape = mixer_ref.shape
    mixed, rank = iota(shape, 0) // ex_rows, iota(shape, 1) % ADAPTER_RANK
    index = (rank * ADAPTER_RANK + mixed) * INDEX_MUL
    mixer_ref[...] = hash_sign(index + salts[1 + 2 * kind] * SALT_MUL).astype(BF16)


def sketch_rows(salts, mask, down, up, hidden, cotangent, cross):
    ex_rows = mask.shape[0]
    tokens, width = hidden.shape
    rows = PROJ_ROWS + PIECES * ADAPTER_RANK
    arrays = (salts, mask, down, up, hidden, cotangent)
    return pl.pallas_call(
        functools.partial(rows_kernel, cross, ex_rows),
        out_shape=[jax.ShapeDtypeStruct((rows, tokens), BF16)] * 2
        + [jax.ShapeDtypeStruct((ADAPTER_RANK * ex_rows, 2 * PIECES * ADAPTER_RANK), BF16)],
        in_specs=[HBM] * 6,
        out_specs=[VMEM] * 3,
        scratch_shapes=[
            pltpu.SMEM(salts.shape, I32),
            pltpu.VMEM(mask.shape, I32),
            pltpu.VMEM((ADAPTER_RANK, width), BF16),
            pltpu.VMEM((ADAPTER_RANK, width), BF16),
            pltpu.VMEM((tokens, width), BF16),
            pltpu.VMEM((tokens, width), BF16),
            pltpu.SemaphoreType.DMA((12,)),
        ],
        compiler_params=pltpu.CompilerParams(vmem_limit_bytes=32 * 1024 * 1024),
    )(*[pltpu.with_memory_space_constraint(x, pltpu.HBM) for x in arrays])


def feature_kernel(ex_rows, mixer_ref, own_ref, other_ref, out_ref):
    tokens = own_ref.shape[1]
    rows = ADAPTER_RANK * ex_rows
    pieces = jnp.concatenate([own_ref[PROJ_ROWS:], other_ref[PROJ_ROWS:]], axis=0)
    coeffs = jnp.dot(mixer_ref[...], pieces, preferred_element_type=F32)
    owned = iota((rows, tokens), 1) // SEQ == iota((rows, tokens), 0) % ex_rows
    coeffs = jnp.where(owned, coeffs, 0.0).astype(BF16)
    projected = lax.dot_general(coeffs, own_ref[:PROJ_ROWS], NT, preferred_element_type=F32)
    projected += lax.dot_general(coeffs, other_ref[:PROJ_ROWS], NT, preferred_element_type=F32)
    features = (projected * SCALE).astype(BF16)
    parts = rows // out_ref.shape[1]
    for copy in range(out_ref.shape[0]):
        first = copy % parts * out_ref.shape[1]
        out_ref[copy] = features[first : first + out_ref.shape[1]]


def feature_rows(mixer, own, other, ex_rows, copies, parts):
    rows = ADAPTER_RANK * ex_rows
    return pl.pallas_call(
        functools.partial(feature_kernel, ex_rows),
        out_shape=jax.ShapeDtypeStruct((copies, rows // parts, PROJ_ROWS), BF16),
        in_specs=[VMEM, VMEM, VMEM],
        out_specs=VMEM,
        compiler_params=SMALL,
    )(mixer, own, other)


def fold_ranks(terms):
    half = terms.shape[0] // 2
    return terms[:half] + pltpu.roll(terms[half:], LANES - half, 1)


def pack_lanes(rows, ex_rows):
    parts = [rows[:, i : i + ex_rows] for i in range(0, LANES, 2 * ex_rows)]
    return jnp.concatenate(parts, axis=1)


def pair_kernel(ex_rows, got_ref, keep_ref, send_ref):
    blocks, rows, _ = got_ref.shape
    x = lax.axis_index("x")
    first = 2 * lax.axis_index("z")
    total = None
    for row in range(0, rows, 2 * ex_rows):
        part = pl.ds(row, 2 * ex_rows)
        left = [got_ref[first + x, part, :], got_ref[first + 1 - x, part, :]]
        left = jnp.concatenate(left, axis=0)
        right = jnp.concatenate([got_ref[b, part, :] for b in range(blocks)], axis=0)
        term = lax.dot_general(left, right, NT, preferred_element_type=F32)
        total = term if total is None else total + term
    keep_ref[...] = fold_ranks(total[: 2 * ex_rows])
    send_ref[...] = fold_ranks(total[2 * ex_rows :])


def pair_rows(got, ex_rows):
    return pl.pallas_call(
        functools.partial(pair_kernel, ex_rows),
        out_shape=[jax.ShapeDtypeStruct((ex_rows, LANES), F32)] * 2,
        in_specs=[VMEM],
        out_specs=[VMEM] * 2,
        compiler_params=SMALL,
    )(got)


def halves_kernel(own_ref, got_ref, keep_ref, send_ref):
    total = own_ref[...] + got_ref[...]
    half = keep_ref.shape[0]
    low = lax.axis_index("tensor") == 0
    keep_ref[...] = jnp.where(low, total[:half], total[half:])
    send_ref[...] = jnp.where(low, total[half:], total[:half])


def sum_halves(own, got):
    rows, lanes = own.shape
    return pl.pallas_call(
        halves_kernel,
        out_shape=[jax.ShapeDtypeStruct((rows // 2, lanes), F32)] * 2,
        in_specs=[VMEM] * 2,
        out_specs=[VMEM] * 2,
        compiler_params=SMALL,
    )(own, got)


def sum_kernel(ex_rows, keep_ref, got_ref, out_ref):
    out_ref[...] = pack_lanes(keep_ref[...] + got_ref[...], ex_rows)


def sum_rows(keep, got, ex_rows):
    return pl.pallas_call(
        functools.partial(sum_kernel, ex_rows),
        out_shape=jax.ShapeDtypeStruct((keep.shape[0], LANES // 2), F32),
        in_specs=[VMEM] * 2,
        out_specs=VMEM,
        compiler_params=SMALL,
    )(keep, got)


def swap_cores(value):
    return lax.ppermute(value, "tensor", [(0, 1), (1, 0)])


def swap_across(value):
    return lax.ppermute(value, ("x", "tensor"), [(i, i ^ 3) for i in range(4)])


def trade_kinds(parts):
    blocks, half = parts.shape[0], lax.axis_size("z") // 2
    groups = [[2 * b + (kind ^ (b // 2 // half)) for b in range(blocks)] for kind in range(2)]
    return lax.all_to_all(parts, BLK + ("tensor",), 0, 0, axis_index_groups=groups, tiled=True)


def body(
    hidden, cotangent, token_loss_mask, adapter_down_factor, adapter_up_factor, sign_table_salts
):
    ex_rows, seq, width_half = hidden.shape
    blocks = lax.axis_size("z") * lax.axis_size("x")
    fast = 2 * blocks * ex_rows == LANES and ex_rows == 8
    keep, send, mixer = sketch_rows(
        sign_table_salts,
        token_loss_mask,
        adapter_down_factor,
        adapter_up_factor.T,
        hidden.reshape(ex_rows * seq, width_half),
        cotangent.reshape(ex_rows * seq, width_half),
        fast,
    )
    other = swap_cores(send)
    if fast:
        got = trade_kinds(feature_rows(mixer, keep, other, ex_rows, blocks, 2))
        keep, send = pair_rows(got, ex_rows)
        keep, send = sum_halves(keep, swap_across(send))
        return sum_rows(keep, swap_cores(send), ex_rows)
    whole = feature_rows(mixer, keep, other, ex_rows, 1, 1)
    share = ADAPTER_RANK * PROJ_ROWS // blocks
    parts = whole.reshape(ADAPTER_RANK, ex_rows, PROJ_ROWS // share, share)
    parts = parts.swapaxes(1, 2).reshape(blocks, ex_rows, share)
    features = lax.all_to_all(parts, BLK, 0, 0, tiled=True).reshape(blocks * ex_rows, share)
    pairs = jnp.einsum("ep,fp->ef", features, features, preferred_element_type=F32)
    pairs = pairs.reshape(blocks, ex_rows, blocks * ex_rows)
    total = jnp.sum(lax.all_to_all(pairs, BLK, 0, 0, tiled=True), axis=0)
    halves = total.reshape(2, ex_rows // 2, blocks * ex_rows)
    core = lax.axis_index("tensor")
    send = lax.dynamic_index_in_dim(halves, 1 - core, 0, keepdims=False)
    return lax.dynamic_index_in_dim(halves, core, 0, keepdims=False) + swap_cores(send)


def solution(mesh):
    groups, blocks, cores = (mesh.shape[name] for name in ("groups", "blk", "tensor"))
    devices = mesh.devices.reshape(groups, blocks // 2, 2, cores)
    placed = (
        P(("groups", "z", "x"), None, "tensor"),
        P(("groups", "z", "x"), None, "tensor"),
        P(("groups", "z", "x"), None),
        P(None, "tensor"),
        P("tensor", None),
        P(),
    )
    return jax.shard_map(
        body,
        mesh=Mesh(devices, ("groups", "z", "x", "tensor")),
        in_specs=placed,
        out_specs=P(("groups", "z", "x", "tensor"), None),
        check_vma=False,
    )
```

```python
import functools
import math

import jax
import jax.numpy as jnp
from jax import lax
from jax.experimental import pallas as pl
from jax.experimental.pallas import tpu as pltpu
from jax.sharding import Mesh, PartitionSpec as P

MODEL_WIDTH = 4096
ADAPTER_RANK = 16
PROJ_ROWS = 256
SEQ = 64
SCALE = 1.0 / math.sqrt(PROJ_ROWS * ADAPTER_RANK * ADAPTER_RANK * SEQ * MODEL_WIDTH)
PIECES = 3
LANES = 128
BLOCK = (16, 256)
BLK = ("z", "x")

F32 = jnp.float32
BF16 = jnp.bfloat16
I32 = jnp.int32
NT = (((1,), (1,)), ((), ()))
VMEM = pl.BlockSpec(memory_space=pltpu.VMEM)
SMEM = pl.BlockSpec(memory_space=pltpu.SMEM)
HBM = pl.BlockSpec(memory_space=pltpu.HBM)
SMALL = pltpu.CompilerParams(vmem_limit_bytes=16 * 1024 * 1024)

INDEX_MUL = -1640531535
SALT_MUL = 668265263


def int32_wrap(value):
    return (value + 2**31) % 2**32 - 2**31


def hash_sign(hashed):
    hashed = hashed ^ lax.shift_right_logical(hashed, 15)
    hashed = hashed * -2048144789
    hashed = hashed ^ lax.shift_right_logical(hashed, 13)
    hashed = hashed * int32_wrap(-1028477387 << 6)
    hashed = hashed ^ lax.shift_left(hashed, 16)
    return jnp.where(hashed < 0, 1.0, -1.0).astype(F32)


def iota(shape, dim):
    return lax.broadcasted_iota(I32, shape, dim)


def token_row(mask):
    ex_rows, seq = mask.shape
    tokens = ex_rows * seq
    tiled = jnp.concatenate([mask.astype(F32)] * ex_rows, axis=1)
    owner = iota((ex_rows, tokens), 1) // seq == iota((ex_rows, tokens), 0)
    return jnp.sum(jnp.where(owner, tiled, 0.0), axis=0, keepdims=True)


def split_pieces(value):
    pieces = []
    for _ in range(PIECES):
        pieces.append(value.astype(BF16))
        value = value - pieces[-1].astype(F32)
    return jnp.concatenate(pieces, axis=0)


def kind_of(cross):
    core = lax.axis_index("tensor")
    return core ^ (lax.axis_index("z") // (lax.axis_size("z") // 2)) if cross else core


def table_start():
    index = iota(BLOCK, 1) * PROJ_ROWS + iota(BLOCK, 0)
    return index * INDEX_MUL


def sign_rows(start, col):
    high, wide = BLOCK
    rows = [
        hash_sign(start + int32_wrap((col * PROJ_ROWS + row) * INDEX_MUL)).astype(BF16)
        for row in range(0, PROJ_ROWS, high)
    ]
    return rows


def far_kernel(
    cross, ex_rows,
    salts_hbm, mask_hbm, down_hbm, up_hbm, hid_hbm, cot_hbm,
    send_ref, ranks_ref, near_ref, start_ref, kept_ref, mixer_ref,
    salts, mask, far_factor, near_factor, far, sems,
):
    tokens, width = far.shape
    kind = kind_of(cross)
    parts = 4
    share = width // parts
    wide = BLOCK[1]

    def copies(inputs, factor, factor_held, held, first):
        out = [pltpu.make_async_copy(factor, factor_held, sems.at[first])]
        for i in range(parts):
            cols = pl.ds(i * share, share)
            out.append(
                pltpu.make_async_copy(inputs.at[:, cols], held.at[:, cols], sems.at[first + 1 + i])
            )
        return out

    def start_copies(far_inputs, far_part, near_inputs, near_part):
        for copy in copies(far_inputs, far_part, far_factor, far, 2):
            copy.start()
        for copy in copies(near_inputs, near_part, near_factor, near_ref, parts + 3):
            copy.start()

    salts_copy = pltpu.make_async_copy(salts_hbm, salts, sems.at[0])
    mask_copy = pltpu.make_async_copy(mask_hbm, mask, sems.at[1])
    salts_copy.start()

    @pl.when(kind == 0)
    def _():
        start_copies(hid_hbm, down_hbm, cot_hbm, up_hbm)

    @pl.when(kind == 1)
    def _():
        start_copies(cot_hbm, up_hbm, hid_hbm, down_hbm)

    mask_copy.start()
    far_waits = copies(hid_hbm, down_hbm, far_factor, far, 2)
    near_waits = copies(hid_hbm, down_hbm, near_factor, near_ref, parts + 3)
    first = lax.axis_index("tensor") * int32_wrap(width * PROJ_ROWS * INDEX_MUL)
    start = table_start() + first
    salts_copy.wait()
    far_start = start + salts[2 - 2 * kind] * SALT_MUL
    far_waits[0].wait()
    total = None
    for col in range(0, width, wide):
        part = slice(col, col + wide)
        left = jnp.concatenate(sign_rows(far_start, col) + [far_factor[:, part]], axis=0)
        if col % share == 0:
            far_waits[1 + col // share].wait()
        term = lax.dot_general(left, far[:, part], NT, preferred_element_type=F32)
        total = term if total is None else total + term
    start_ref[...] = start + salts[2 * kind] * SALT_MUL
    shape = mixer_ref.shape
    mixed, rank = iota(shape, 0) // ex_rows, iota(shape, 1) % ADAPTER_RANK
    index = (rank * ADAPTER_RANK + mixed) * INDEX_MUL
    mixer_ref[...] = hash_sign(index + salts[1 + 2 * kind] * SALT_MUL).astype(BF16)
    mask_copy.wait()
    counted = token_row(mask[...]) != 0
    far_kept = counted | (kind == 0)
    near_kept = counted | (kind == 1)
    kept_ref[...] = jnp.broadcast_to(jnp.where(near_kept, 1.0, 0.0), kept_ref.shape)
    total = jnp.where(far_kept, total, 0.0)
    send_ref[:PROJ_ROWS] = total[:PROJ_ROWS].astype(BF16)
    ranks_ref[...] = split_pieces(total[PROJ_ROWS:])
    near_waits[0].wait()
    total = None
    for step in range(parts):
        part = slice(step * share, (step + 1) * share)
        near_waits[1 + step].wait()
        term = lax.dot_general(
            near_factor[:, part], near_ref[:, part], NT, preferred_element_type=F32
        )
        total = term if total is None else total + term
    send_ref[PROJ_ROWS:] = split_pieces(jnp.where(near_kept, total, 0.0))


def far_rows(salts, mask, down, up, hidden, cotangent, cross):
    ex_rows = mask.shape[0]
    tokens, width = hidden.shape
    pieces = PIECES * ADAPTER_RANK
    arrays = (salts, mask, down, up, hidden, cotangent)
    return pl.pallas_call(
        functools.partial(far_kernel, cross, ex_rows),
        out_shape=[
            jax.ShapeDtypeStruct((PROJ_ROWS + pieces, tokens), BF16),
            jax.ShapeDtypeStruct((pieces, tokens), BF16),
            jax.ShapeDtypeStruct((tokens, width), BF16),
            jax.ShapeDtypeStruct(BLOCK, I32),
            jax.ShapeDtypeStruct((8, tokens), F32),
            jax.ShapeDtypeStruct((ADAPTER_RANK * ex_rows, 2 * pieces), BF16),
        ],
        in_specs=[HBM] * 6,
        out_specs=[VMEM] * 6,
        scratch_shapes=[
            pltpu.SMEM(salts.shape, I32),
            pltpu.VMEM(mask.shape, I32),
            pltpu.VMEM((ADAPTER_RANK, width), BF16),
            pltpu.VMEM((ADAPTER_RANK, width), BF16),
            pltpu.VMEM((tokens, width), BF16),
            pltpu.SemaphoreType.DMA((12,)),
        ],
        compiler_params=SMALL,
    )(*[pltpu.with_memory_space_constraint(x, pltpu.HBM) for x in arrays])


def near_kernel(start_ref, kept_ref, near_ref, out_ref):
    start = start_ref[...]
    wide = BLOCK[1]
    total = None
    for col in range(0, near_ref.shape[1], wide):
        left = jnp.concatenate(sign_rows(start, col), axis=0)
        term = lax.dot_general(
            left, near_ref[:, col : col + wide], NT, preferred_element_type=F32
        )
        total = term if total is None else total + term
    out_ref[...] = jnp.where(kept_ref[:1] != 0, total, 0.0).astype(BF16)


def near_rows(start, kept, near):
    tokens, width = near.shape
    return pl.pallas_call(
        near_kernel,
        out_shape=jax.ShapeDtypeStruct((PROJ_ROWS, tokens), BF16),
        in_specs=[VMEM] * 3,
        out_specs=VMEM,
        compiler_params=SMALL,
        cost_estimate=pl.CostEstimate(
            flops=2 * tokens * width * PROJ_ROWS, bytes_accessed=2 * tokens * width, transcendentals=0
        ),
    )(start, kept, near)


def feature_kernel(ex_rows, mixer_ref, ranks_ref, own_ref, other_ref, out_ref):
    tokens = own_ref.shape[1]
    rows = ADAPTER_RANK * ex_rows
    pieces = jnp.concatenate([ranks_ref[...], other_ref[PROJ_ROWS:]], axis=0)
    coeffs = jnp.dot(mixer_ref[...], pieces, preferred_element_type=F32)
    owned = iota((rows, tokens), 1) // SEQ == iota((rows, tokens), 0) % ex_rows
    coeffs = jnp.where(owned, coeffs, 0.0).astype(BF16)
    projected = lax.dot_general(coeffs, own_ref[...], NT, preferred_element_type=F32)
    projected += lax.dot_general(coeffs, other_ref[:PROJ_ROWS], NT, preferred_element_type=F32)
    features = (projected * SCALE).astype(BF16)
    parts = rows // out_ref.shape[1]
    for copy in range(out_ref.shape[0]):
        first = copy % parts * out_ref.shape[1]
        out_ref[copy] = features[first : first + out_ref.shape[1]]


def feature_rows(mixer, ranks, own, other, ex_rows, copies, parts):
    rows = ADAPTER_RANK * ex_rows
    return pl.pallas_call(
        functools.partial(feature_kernel, ex_rows),
        out_shape=jax.ShapeDtypeStruct((copies, rows // parts, PROJ_ROWS), BF16),
        in_specs=[VMEM] * 4,
        out_specs=VMEM,
        compiler_params=SMALL,
    )(mixer, ranks, own, other)


def fold_ranks(terms):
    half = terms.shape[0] // 2
    return terms[:half] + pltpu.roll(terms[half:], LANES - half, 1)


def pack_lanes(rows, ex_rows):
    parts = [rows[:, i : i + ex_rows] for i in range(0, LANES, 2 * ex_rows)]
    return jnp.concatenate(parts, axis=1)


def pair_kernel(ex_rows, got_ref, keep_ref, send_ref):
    blocks, rows, _ = got_ref.shape
    x = lax.axis_index("x")
    first = 2 * lax.axis_index("z")
    total = None
    for row in range(0, rows, 2 * ex_rows):
        part = pl.ds(row, 2 * ex_rows)
        left = [got_ref[first + x, part, :], got_ref[first + 1 - x, part, :]]
        left = jnp.concatenate(left, axis=0)
        right = jnp.concatenate([got_ref[b, part, :] for b in range(blocks)], axis=0)
        term = lax.dot_general(left, right, NT, preferred_element_type=F32)
        total = term if total is None else total + term
    keep_ref[...] = fold_ranks(total[: 2 * ex_rows])
    send_ref[...] = fold_ranks(total[2 * ex_rows :])


def pair_rows(got, ex_rows):
    return pl.pallas_call(
        functools.partial(pair_kernel, ex_rows),
        out_shape=[jax.ShapeDtypeStruct((ex_rows, LANES), F32)] * 2,
        in_specs=[VMEM],
        out_specs=[VMEM] * 2,
        compiler_params=SMALL,
    )(got)


def halves_kernel(own_ref, got_ref, keep_ref, send_ref):
    total = own_ref[...] + got_ref[...]
    half = keep_ref.shape[0]
    low = lax.axis_index("tensor") == 0
    keep_ref[...] = jnp.where(low, total[:half], total[half:])
    send_ref[...] = jnp.where(low, total[half:], total[:half])


def sum_halves(own, got):
    rows, lanes = own.shape
    return pl.pallas_call(
        halves_kernel,
        out_shape=[jax.ShapeDtypeStruct((rows // 2, lanes), F32)] * 2,
        in_specs=[VMEM] * 2,
        out_specs=[VMEM] * 2,
        compiler_params=SMALL,
    )(own, got)


def sum_kernel(ex_rows, keep_ref, got_ref, out_ref):
    out_ref[...] = pack_lanes(keep_ref[...] + got_ref[...], ex_rows)


def sum_rows(keep, got, ex_rows):
    return pl.pallas_call(
        functools.partial(sum_kernel, ex_rows),
        out_shape=jax.ShapeDtypeStruct((keep.shape[0], LANES // 2), F32),
        in_specs=[VMEM] * 2,
        out_specs=VMEM,
        compiler_params=SMALL,
    )(keep, got)


def swap_cores(value):
    return lax.ppermute(value, "tensor", [(0, 1), (1, 0)])


def swap_across(value):
    return lax.ppermute(value, ("x", "tensor"), [(i, i ^ 3) for i in range(4)])


def trade_kinds(parts):
    blocks, half = parts.shape[0], lax.axis_size("z") // 2
    groups = [[2 * b + (kind ^ (b // 2 // half)) for b in range(blocks)] for kind in range(2)]
    return lax.all_to_all(parts, BLK + ("tensor",), 0, 0, axis_index_groups=groups, tiled=True)


def body(
    hidden, cotangent, token_loss_mask, adapter_down_factor, adapter_up_factor, sign_table_salts
):
    ex_rows, seq, width_half = hidden.shape
    blocks = lax.axis_size("z") * lax.axis_size("x")
    fast = 2 * blocks * ex_rows == LANES and ex_rows == 8
    send, ranks, near, start, kept, mixer = far_rows(
        sign_table_salts,
        token_loss_mask,
        adapter_down_factor,
        adapter_up_factor.T,
        hidden.reshape(ex_rows * seq, width_half),
        cotangent.reshape(ex_rows * seq, width_half),
        fast,
    )
    other = swap_cores(send)
    terms = (mixer, ranks, near_rows(start, kept, near), other)
    if fast:
        got = trade_kinds(feature_rows(*terms, ex_rows, blocks, 2))
        keep, send = pair_rows(got, ex_rows)
        keep, send = sum_halves(keep, swap_across(send))
        return sum_rows(keep, swap_cores(send), ex_rows)
    whole = feature_rows(*terms, ex_rows, 1, 1)
    share = ADAPTER_RANK * PROJ_ROWS // blocks
    parts = whole.reshape(ADAPTER_RANK, ex_rows, PROJ_ROWS // share, share)
    parts = parts.swapaxes(1, 2).reshape(blocks, ex_rows, share)
    features = lax.all_to_all(parts, BLK, 0, 0, tiled=True).reshape(blocks * ex_rows, share)
    pairs = jnp.einsum("ep,fp->ef", features, features, preferred_element_type=F32)
    pairs = pairs.reshape(blocks, ex_rows, blocks * ex_rows)
    total = jnp.sum(lax.all_to_all(pairs, BLK, 0, 0, tiled=True), axis=0)
    halves = total.reshape(2, ex_rows // 2, blocks * ex_rows)
    core = lax.axis_index("tensor")
    send = lax.dynamic_index_in_dim(halves, 1 - core, 0, keepdims=False)
    return lax.dynamic_index_in_dim(halves, core, 0, keepdims=False) + swap_cores(send)


def solution(mesh):
    groups, blocks, cores = (mesh.shape[name] for name in ("groups", "blk", "tensor"))
    devices = mesh.devices.reshape(groups, blocks // 2, 2, cores)
    placed = (
        P(("groups", "z", "x"), None, "tensor"),
        P(("groups", "z", "x"), None, "tensor"),
        P(("groups", "z", "x"), None),
        P(None, "tensor"),
        P("tensor", None),
        P(),
    )
    return jax.shard_map(
        body,
        mesh=Mesh(devices, ("groups", "z", "x", "tensor")),
        in_specs=placed,
        out_specs=P(("groups", "z", "x", "tensor"), None),
        check_vma=False,
    )
```

```python
import functools
import math

import jax
import jax.numpy as jnp
from jax import lax
from jax.experimental import pallas as pl
from jax.experimental.pallas import tpu as pltpu
from jax.sharding import Mesh, PartitionSpec as P

MODEL_WIDTH = 4096
ADAPTER_RANK = 16
PROJ_ROWS = 256
SEQ = 64
SCALE = 1.0 / math.sqrt(PROJ_ROWS * ADAPTER_RANK * ADAPTER_RANK * SEQ * MODEL_WIDTH)
PIECES = 3
LANES = 128
BLOCK = (16, 256)
LEAD = 2
BLK = ("z", "x")

F32 = jnp.float32
BF16 = jnp.bfloat16
I32 = jnp.int32
NT = (((1,), (1,)), ((), ()))
VMEM = pl.BlockSpec(memory_space=pltpu.VMEM)
SMEM = pl.BlockSpec(memory_space=pltpu.SMEM)
HBM = pl.BlockSpec(memory_space=pltpu.HBM)
SMALL = pltpu.CompilerParams(vmem_limit_bytes=16 * 1024 * 1024)

INDEX_MUL = -1640531535
SALT_MUL = 668265263


def int32_wrap(value):
    return (value + 2**31) % 2**32 - 2**31


def hash_sign(hashed):
    hashed = hashed ^ lax.shift_right_logical(hashed, 15)
    hashed = hashed * -2048144789
    hashed = hashed ^ lax.shift_right_logical(hashed, 13)
    hashed = hashed * int32_wrap(-1028477387 << 6)
    hashed = hashed ^ lax.shift_left(hashed, 16)
    return jnp.where(hashed < 0, 1.0, -1.0).astype(F32)


def iota(shape, dim):
    return lax.broadcasted_iota(I32, shape, dim)


def token_row(mask):
    ex_rows, seq = mask.shape
    tokens = ex_rows * seq
    tiled = jnp.concatenate([mask.astype(F32)] * ex_rows, axis=1)
    owner = iota((ex_rows, tokens), 1) // seq == iota((ex_rows, tokens), 0)
    return jnp.sum(jnp.where(owner, tiled, 0.0), axis=0, keepdims=True)


def split_pieces(value):
    pieces = []
    for _ in range(PIECES):
        pieces.append(value.astype(BF16))
        value = value - pieces[-1].astype(F32)
    return jnp.concatenate(pieces, axis=0)


def kind_of(cross):
    core = lax.axis_index("tensor")
    return core ^ (lax.axis_index("z") // (lax.axis_size("z") // 2)) if cross else core


def table_start():
    index = iota(BLOCK, 1) * PROJ_ROWS + iota(BLOCK, 0)
    return index * INDEX_MUL


def sign_rows(start, col):
    high, wide = BLOCK
    rows = [
        hash_sign(start + int32_wrap((col * PROJ_ROWS + row) * INDEX_MUL)).astype(BF16)
        for row in range(0, PROJ_ROWS, high)
    ]
    return rows


def far_kernel(
    cross, ex_rows,
    salts_hbm, mask_hbm, down_hbm, up_hbm, hid_hbm, cot_hbm,
    send_ref, ranks_ref, near_ref, start_ref, kept_ref, mixer_ref,
    salts, mask, far_factor, near_factor, far, sems,
):
    tokens, width = far.shape
    kind = kind_of(cross)
    parts = 4
    share = tokens // parts
    wide = BLOCK[1]

    def copies(inputs, factor, factor_held, held, first):
        out = [pltpu.make_async_copy(factor, factor_held, sems.at[first])]
        for i in range(parts):
            rows = pl.ds(i * share, share)
            out.append(
                pltpu.make_async_copy(inputs.at[rows], held.at[rows], sems.at[first + 1 + i])
            )
        return out

    def start_copies(far_inputs, far_part, near_inputs, near_part):
        for copy in copies(far_inputs, far_part, far_factor, far, 2):
            copy.start()
        for copy in copies(near_inputs, near_part, near_factor, near_ref, parts + 3):
            copy.start()

    salts_copy = pltpu.make_async_copy(salts_hbm, salts, sems.at[0])
    mask_copy = pltpu.make_async_copy(mask_hbm, mask, sems.at[1])
    salts_copy.start()

    @pl.when(kind == 0)
    def _():
        start_copies(hid_hbm, down_hbm, cot_hbm, up_hbm)

    @pl.when(kind == 1)
    def _():
        start_copies(cot_hbm, up_hbm, hid_hbm, down_hbm)

    mask_copy.start()
    far_waits = copies(hid_hbm, down_hbm, far_factor, far, 2)
    near_waits = copies(hid_hbm, down_hbm, near_factor, near_ref, parts + 3)
    first = lax.axis_index("tensor") * int32_wrap(width * PROJ_ROWS * INDEX_MUL)
    start = table_start() + first
    salts_copy.wait()
    far_start = start + salts[2 - 2 * kind] * SALT_MUL
    ahead = [sign_rows(far_start, col) for col in range(0, LEAD * wide, wide)]
    for wait in far_waits:
        wait.wait()
    total = None
    for col in range(0, width, wide):
        part = slice(col, col + wide)
        tile = ahead.pop(0) if ahead else sign_rows(far_start, col)
        left = jnp.concatenate(tile + [far_factor[:, part]], axis=0)
        term = lax.dot_general(left, far[:, part], NT, preferred_element_type=F32)
        total = term if total is None else total + term
    start_ref[...] = start + salts[2 * kind] * SALT_MUL
    shape = mixer_ref.shape
    mixed, rank = iota(shape, 0) // ex_rows, iota(shape, 1) % ADAPTER_RANK
    index = (rank * ADAPTER_RANK + mixed) * INDEX_MUL
    mixer_ref[...] = hash_sign(index + salts[1 + 2 * kind] * SALT_MUL).astype(BF16)
    mask_copy.wait()
    counted = token_row(mask[...]) != 0
    far_kept = counted | (kind == 0)
    near_kept = counted | (kind == 1)
    kept_ref[...] = jnp.broadcast_to(jnp.where(near_kept, 1.0, 0.0), kept_ref.shape)
    total = jnp.where(far_kept, total, 0.0)
    send_ref[:PROJ_ROWS] = total[:PROJ_ROWS].astype(BF16)
    ranks_ref[...] = split_pieces(total[PROJ_ROWS:])
    for wait in near_waits:
        wait.wait()
    total = lax.dot_general(near_factor[...], near_ref[...], NT, preferred_element_type=F32)
    send_ref[PROJ_ROWS:] = split_pieces(jnp.where(near_kept, total, 0.0))


def far_rows(salts, mask, down, up, hidden, cotangent, cross):
    ex_rows = mask.shape[0]
    tokens, width = hidden.shape
    pieces = PIECES * ADAPTER_RANK
    arrays = (salts, mask, down, up, hidden, cotangent)
    return pl.pallas_call(
        functools.partial(far_kernel, cross, ex_rows),
        out_shape=[
            jax.ShapeDtypeStruct((PROJ_ROWS + pieces, tokens), BF16),
            jax.ShapeDtypeStruct((pieces, tokens), BF16),
            jax.ShapeDtypeStruct((tokens, width), BF16),
            jax.ShapeDtypeStruct(BLOCK, I32),
            jax.ShapeDtypeStruct((8, tokens), F32),
            jax.ShapeDtypeStruct((ADAPTER_RANK * ex_rows, 2 * pieces), BF16),
        ],
        in_specs=[HBM] * 6,
        out_specs=[VMEM] * 6,
        scratch_shapes=[
            pltpu.SMEM(salts.shape, I32),
            pltpu.VMEM(mask.shape, I32),
            pltpu.VMEM((ADAPTER_RANK, width), BF16),
            pltpu.VMEM((ADAPTER_RANK, width), BF16),
            pltpu.VMEM((tokens, width), BF16),
            pltpu.SemaphoreType.DMA((12,)),
        ],
        compiler_params=SMALL,
    )(*[pltpu.with_memory_space_constraint(x, pltpu.HBM) for x in arrays])


def near_kernel(start_ref, kept_ref, near_ref, out_ref):
    start = start_ref[...]
    wide = BLOCK[1]
    total = None
    for col in range(0, near_ref.shape[1], wide):
        left = jnp.concatenate(sign_rows(start, col), axis=0)
        term = lax.dot_general(
            left, near_ref[:, col : col + wide], NT, preferred_element_type=F32
        )
        total = term if total is None else total + term
    out_ref[...] = jnp.where(kept_ref[:1] != 0, total, 0.0).astype(BF16)


def near_rows(start, kept, near):
    tokens, width = near.shape
    return pl.pallas_call(
        near_kernel,
        out_shape=jax.ShapeDtypeStruct((PROJ_ROWS, tokens), BF16),
        in_specs=[VMEM] * 3,
        out_specs=VMEM,
        compiler_params=SMALL,
        cost_estimate=pl.CostEstimate(
            flops=2 * tokens * width * PROJ_ROWS, bytes_accessed=2 * tokens * width, transcendentals=0
        ),
    )(start, kept, near)


def feature_kernel(ex_rows, mixer_ref, ranks_ref, own_ref, other_ref, out_ref):
    tokens = own_ref.shape[1]
    rows = ADAPTER_RANK * ex_rows
    pieces = jnp.concatenate([ranks_ref[...], other_ref[PROJ_ROWS:]], axis=0)
    coeffs = jnp.dot(mixer_ref[...], pieces, preferred_element_type=F32)
    owned = iota((rows, tokens), 1) // SEQ == iota((rows, tokens), 0) % ex_rows
    coeffs = jnp.where(owned, coeffs, 0.0).astype(BF16)
    projected = lax.dot_general(coeffs, own_ref[...], NT, preferred_element_type=F32)
    projected += lax.dot_general(coeffs, other_ref[:PROJ_ROWS], NT, preferred_element_type=F32)
    features = (projected * SCALE).astype(BF16)
    parts = rows // out_ref.shape[1]
    for copy in range(out_ref.shape[0]):
        first = copy % parts * out_ref.shape[1]
        out_ref[copy] = features[first : first + out_ref.shape[1]]


def feature_rows(mixer, ranks, own, other, ex_rows, copies, parts):
    rows = ADAPTER_RANK * ex_rows
    return pl.pallas_call(
        functools.partial(feature_kernel, ex_rows),
        out_shape=jax.ShapeDtypeStruct((copies, rows // parts, PROJ_ROWS), BF16),
        in_specs=[VMEM] * 4,
        out_specs=VMEM,
        compiler_params=SMALL,
    )(mixer, ranks, own, other)


def fold_ranks(terms):
    half = terms.shape[0] // 2
    return terms[:half] + pltpu.roll(terms[half:], LANES - half, 1)


def pack_lanes(rows, ex_rows):
    parts = [rows[:, i : i + ex_rows] for i in range(0, LANES, 2 * ex_rows)]
    return jnp.concatenate(parts, axis=1)


def pair_kernel(ex_rows, got_ref, keep_ref, send_ref):
    blocks, rows, _ = got_ref.shape
    x = lax.axis_index("x")
    first = 2 * lax.axis_index("z")
    total = None
    for row in range(0, rows, 2 * ex_rows):
        part = pl.ds(row, 2 * ex_rows)
        left = [got_ref[first + x, part, :], got_ref[first + 1 - x, part, :]]
        left = jnp.concatenate(left, axis=0)
        right = jnp.concatenate([got_ref[b, part, :] for b in range(blocks)], axis=0)
        term = lax.dot_general(left, right, NT, preferred_element_type=F32)
        total = term if total is None else total + term
    keep_ref[...] = fold_ranks(total[: 2 * ex_rows])
    send_ref[...] = fold_ranks(total[2 * ex_rows :])


def pair_rows(got, ex_rows):
    return pl.pallas_call(
        functools.partial(pair_kernel, ex_rows),
        out_shape=[jax.ShapeDtypeStruct((ex_rows, LANES), F32)] * 2,
        in_specs=[VMEM],
        out_specs=[VMEM] * 2,
        compiler_params=SMALL,
    )(got)


def halves_kernel(own_ref, got_ref, keep_ref, send_ref):
    total = own_ref[...] + got_ref[...]
    half = keep_ref.shape[0]
    low = lax.axis_index("tensor") == 0
    keep_ref[...] = jnp.where(low, total[:half], total[half:])
    send_ref[...] = jnp.where(low, total[half:], total[:half])


def sum_halves(own, got):
    rows, lanes = own.shape
    return pl.pallas_call(
        halves_kernel,
        out_shape=[jax.ShapeDtypeStruct((rows // 2, lanes), F32)] * 2,
        in_specs=[VMEM] * 2,
        out_specs=[VMEM] * 2,
        compiler_params=SMALL,
    )(own, got)


def sum_kernel(ex_rows, keep_ref, got_ref, out_ref):
    out_ref[...] = pack_lanes(keep_ref[...] + got_ref[...], ex_rows)


def sum_rows(keep, got, ex_rows):
    return pl.pallas_call(
        functools.partial(sum_kernel, ex_rows),
        out_shape=jax.ShapeDtypeStruct((keep.shape[0], LANES // 2), F32),
        in_specs=[VMEM] * 2,
        out_specs=VMEM,
        compiler_params=SMALL,
    )(keep, got)


def swap_cores(value):
    return lax.ppermute(value, "tensor", [(0, 1), (1, 0)])


def swap_across(value):
    return lax.ppermute(value, ("x", "tensor"), [(i, i ^ 3) for i in range(4)])


def trade_kinds(parts):
    blocks, half = parts.shape[0], lax.axis_size("z") // 2
    groups = [[2 * b + (kind ^ (b // 2 // half)) for b in range(blocks)] for kind in range(2)]
    return lax.all_to_all(parts, BLK + ("tensor",), 0, 0, axis_index_groups=groups, tiled=True)


def body(
    hidden, cotangent, token_loss_mask, adapter_down_factor, adapter_up_factor, sign_table_salts
):
    ex_rows, seq, width_half = hidden.shape
    blocks = lax.axis_size("z") * lax.axis_size("x")
    fast = 2 * blocks * ex_rows == LANES and ex_rows == 8
    send, ranks, near, start, kept, mixer = far_rows(
        sign_table_salts,
        token_loss_mask,
        adapter_down_factor,
        adapter_up_factor.T,
        hidden.reshape(ex_rows * seq, width_half),
        cotangent.reshape(ex_rows * seq, width_half),
        fast,
    )
    other = swap_cores(send)
    terms = (mixer, ranks, near_rows(start, kept, near), other)
    if fast:
        got = trade_kinds(feature_rows(*terms, ex_rows, blocks, 2))
        keep, send = pair_rows(got, ex_rows)
        keep, send = sum_halves(keep, swap_across(send))
        return sum_rows(keep, swap_cores(send), ex_rows)
    whole = feature_rows(*terms, ex_rows, 1, 1)
    share = ADAPTER_RANK * PROJ_ROWS // blocks
    parts = whole.reshape(ADAPTER_RANK, ex_rows, PROJ_ROWS // share, share)
    parts = parts.swapaxes(1, 2).reshape(blocks, ex_rows, share)
    features = lax.all_to_all(parts, BLK, 0, 0, tiled=True).reshape(blocks * ex_rows, share)
    pairs = jnp.einsum("ep,fp->ef", features, features, preferred_element_type=F32)
    pairs = pairs.reshape(blocks, ex_rows, blocks * ex_rows)
    total = jnp.sum(lax.all_to_all(pairs, BLK, 0, 0, tiled=True), axis=0)
    halves = total.reshape(2, ex_rows // 2, blocks * ex_rows)
    core = lax.axis_index("tensor")
    send = lax.dynamic_index_in_dim(halves, 1 - core, 0, keepdims=False)
    return lax.dynamic_index_in_dim(halves, core, 0, keepdims=False) + swap_cores(send)


def solution(mesh):
    groups, blocks, cores = (mesh.shape[name] for name in ("groups", "blk", "tensor"))
    devices = mesh.devices.reshape(groups, blocks // 2, 2, cores)
    placed = (
        P(("groups", "z", "x"), None, "tensor"),
        P(("groups", "z", "x"), None, "tensor"),
        P(("groups", "z", "x"), None),
        P(None, "tensor"),
        P("tensor", None),
        P(),
    )
    return jax.shard_map(
        body,
        mesh=Mesh(devices, ("groups", "z", "x", "tensor")),
        in_specs=placed,
        out_specs=P(("groups", "z", "x", "tensor"), None),
        check_vma=False,
    )
```

```python
import functools
import math

import jax
import jax.numpy as jnp
from jax import lax
from jax.experimental import pallas as pl
from jax.experimental.pallas import tpu as pltpu
from jax.sharding import Mesh, PartitionSpec as P

MODEL_WIDTH = 4096
ADAPTER_RANK = 16
PROJ_ROWS = 256
SEQ = 64
SCALE = 1.0 / math.sqrt(PROJ_ROWS * ADAPTER_RANK * ADAPTER_RANK * SEQ * MODEL_WIDTH)
PIECES = 3
LANES = 128
BLOCK = (16, 256)
BLK = ("z", "x")

F32 = jnp.float32
BF16 = jnp.bfloat16
I32 = jnp.int32
NT = (((1,), (1,)), ((), ()))
VMEM = pl.BlockSpec(memory_space=pltpu.VMEM)
SMEM = pl.BlockSpec(memory_space=pltpu.SMEM)
HBM = pl.BlockSpec(memory_space=pltpu.HBM)
SMALL = pltpu.CompilerParams(vmem_limit_bytes=16 * 1024 * 1024)

INDEX_MUL = -1640531535
SALT_MUL = 668265263


def int32_wrap(value):
    return (value + 2**31) % 2**32 - 2**31


def hash_sign(hashed):
    hashed = hashed ^ lax.shift_right_logical(hashed, 15)
    hashed = hashed * -2048144789
    hashed = hashed ^ lax.shift_right_logical(hashed, 13)
    hashed = hashed * int32_wrap(-1028477387 << 6)
    hashed = hashed ^ lax.shift_left(hashed, 16)
    return jnp.where(hashed < 0, 1.0, -1.0).astype(F32)


def iota(shape, dim):
    return lax.broadcasted_iota(I32, shape, dim)


def token_row(mask):
    ex_rows, seq = mask.shape
    tokens = ex_rows * seq
    tiled = jnp.concatenate([mask.astype(F32)] * ex_rows, axis=1)
    owner = iota((ex_rows, tokens), 1) // seq == iota((ex_rows, tokens), 0)
    return jnp.sum(jnp.where(owner, tiled, 0.0), axis=0, keepdims=True)


def split_pieces(value):
    pieces = []
    for _ in range(PIECES):
        pieces.append(value.astype(BF16))
        value = value - pieces[-1].astype(F32)
    return jnp.concatenate(pieces, axis=0)


def kind_of(cross):
    core = lax.axis_index("tensor")
    return core ^ (lax.axis_index("z") // (lax.axis_size("z") // 2)) if cross else core


def table_start():
    index = iota(BLOCK, 1) * PROJ_ROWS + iota(BLOCK, 0)
    return index * INDEX_MUL


def sign_rows(start, col):
    high, wide = BLOCK
    rows = [
        hash_sign(start + int32_wrap((col * PROJ_ROWS + row) * INDEX_MUL)).astype(BF16)
        for row in range(0, PROJ_ROWS, high)
    ]
    return rows


def far_kernel(
    cross, ex_rows,
    salts_hbm, mask_hbm, down_hbm, up_hbm, hid_hbm, cot_hbm,
    send_ref, ranks_ref, near_ref, near_factor, start_ref, kept_ref, mixer_ref,
    salts, mask, far_factor, far, sems,
):
    tokens, width = far.shape
    kind = kind_of(cross)
    parts = 4
    share = width // parts
    wide = BLOCK[1]

    def copies(inputs, factor, factor_held, held, first):
        out = [pltpu.make_async_copy(factor, factor_held, sems.at[first])]
        for i in range(parts):
            cols = pl.ds(i * share, share)
            out.append(
                pltpu.make_async_copy(inputs.at[:, cols], held.at[:, cols], sems.at[first + 1 + i])
            )
        return out

    def start_copies(far_inputs, far_part, near_inputs, near_part):
        for copy in copies(far_inputs, far_part, far_factor, far, 2):
            copy.start()
        for copy in copies(near_inputs, near_part, near_factor, near_ref, parts + 3):
            copy.start()

    salts_copy = pltpu.make_async_copy(salts_hbm, salts, sems.at[0])
    mask_copy = pltpu.make_async_copy(mask_hbm, mask, sems.at[1])
    salts_copy.start()

    @pl.when(kind == 0)
    def _():
        start_copies(hid_hbm, down_hbm, cot_hbm, up_hbm)

    @pl.when(kind == 1)
    def _():
        start_copies(cot_hbm, up_hbm, hid_hbm, down_hbm)

    mask_copy.start()
    far_waits = copies(hid_hbm, down_hbm, far_factor, far, 2)
    near_waits = copies(hid_hbm, down_hbm, near_factor, near_ref, parts + 3)
    first = lax.axis_index("tensor") * int32_wrap(width * PROJ_ROWS * INDEX_MUL)
    start = table_start() + first
    salts_copy.wait()
    far_start = start + salts[2 - 2 * kind] * SALT_MUL
    far_waits[0].wait()
    total = None
    for col in range(0, width, wide):
        part = slice(col, col + wide)
        left = jnp.concatenate(sign_rows(far_start, col) + [far_factor[:, part]], axis=0)
        if col % share == 0:
            far_waits[1 + col // share].wait()
        term = lax.dot_general(left, far[:, part], NT, preferred_element_type=F32)
        total = term if total is None else total + term
    start_ref[...] = start + salts[2 * kind] * SALT_MUL
    shape = mixer_ref.shape
    mixed, rank = iota(shape, 0) // ex_rows, iota(shape, 1) % ADAPTER_RANK
    index = (rank * ADAPTER_RANK + mixed) * INDEX_MUL
    mixer_ref[...] = hash_sign(index + salts[1 + 2 * kind] * SALT_MUL).astype(BF16)
    mask_copy.wait()
    counted = token_row(mask[...]) != 0
    far_kept = counted | (kind == 0)
    near_kept = counted | (kind == 1)
    kept_ref[...] = jnp.broadcast_to(jnp.where(near_kept, 1.0, 0.0), kept_ref.shape)
    total = jnp.where(far_kept, total, 0.0)
    send_ref[...] = total[:PROJ_ROWS].astype(BF16)
    ranks_ref[...] = split_pieces(total[PROJ_ROWS:])
    for wait in near_waits:
        wait.wait()


def far_rows(salts, mask, down, up, hidden, cotangent, cross):
    ex_rows = mask.shape[0]
    tokens, width = hidden.shape
    pieces = PIECES * ADAPTER_RANK
    arrays = (salts, mask, down, up, hidden, cotangent)
    return pl.pallas_call(
        functools.partial(far_kernel, cross, ex_rows),
        out_shape=[
            jax.ShapeDtypeStruct((PROJ_ROWS, tokens), BF16),
            jax.ShapeDtypeStruct((pieces, tokens), BF16),
            jax.ShapeDtypeStruct((tokens, width), BF16),
            jax.ShapeDtypeStruct((ADAPTER_RANK, width), BF16),
            jax.ShapeDtypeStruct(BLOCK, I32),
            jax.ShapeDtypeStruct((8, tokens), F32),
            jax.ShapeDtypeStruct((ADAPTER_RANK * ex_rows, 2 * pieces), BF16),
        ],
        in_specs=[HBM] * 6,
        out_specs=[VMEM] * 7,
        scratch_shapes=[
            pltpu.SMEM(salts.shape, I32),
            pltpu.VMEM(mask.shape, I32),
            pltpu.VMEM((ADAPTER_RANK, width), BF16),
            pltpu.VMEM((tokens, width), BF16),
            pltpu.SemaphoreType.DMA((12,)),
        ],
        compiler_params=SMALL,
    )(*[pltpu.with_memory_space_constraint(x, pltpu.HBM) for x in arrays])


def near_kernel(start_ref, kept_ref, factor_ref, near_ref, out_ref, ranks_ref):
    start = start_ref[...]
    wide = BLOCK[1]
    total = None
    for col in range(0, near_ref.shape[1], wide):
        part = slice(col, col + wide)
        left = jnp.concatenate(sign_rows(start, col) + [factor_ref[:, part]], axis=0)
        term = lax.dot_general(left, near_ref[:, part], NT, preferred_element_type=F32)
        total = term if total is None else total + term
    total = jnp.where(kept_ref[:1] != 0, total, 0.0)
    out_ref[...] = total[:PROJ_ROWS].astype(BF16)
    ranks_ref[...] = split_pieces(total[PROJ_ROWS:])


def near_rows(start, kept, factor, near):
    tokens, width = near.shape
    return pl.pallas_call(
        near_kernel,
        out_shape=[
            jax.ShapeDtypeStruct((PROJ_ROWS, tokens), BF16),
            jax.ShapeDtypeStruct((PIECES * ADAPTER_RANK, tokens), BF16),
        ],
        in_specs=[VMEM] * 4,
        out_specs=[VMEM] * 2,
        compiler_params=SMALL,
        cost_estimate=pl.CostEstimate(
            flops=2 * tokens * width * PROJ_ROWS, bytes_accessed=2 * tokens * width, transcendentals=0
        ),
    )(start, kept, factor, near)


def feature_kernel(ex_rows, mixer_ref, ranks_ref, own_ref, got_ranks_ref, got_ref, out_ref):
    tokens = own_ref.shape[1]
    rows = ADAPTER_RANK * ex_rows
    pieces = jnp.concatenate([ranks_ref[...], got_ranks_ref[...]], axis=0)
    coeffs = jnp.dot(mixer_ref[...], pieces, preferred_element_type=F32)
    owned = iota((rows, tokens), 1) // SEQ == iota((rows, tokens), 0) % ex_rows
    coeffs = jnp.where(owned, coeffs, 0.0).astype(BF16)
    projected = lax.dot_general(coeffs, own_ref[...], NT, preferred_element_type=F32)
    projected += lax.dot_general(coeffs, got_ref[...], NT, preferred_element_type=F32)
    features = (projected * SCALE).astype(BF16)
    parts = rows // out_ref.shape[1]
    for copy in range(out_ref.shape[0]):
        first = copy % parts * out_ref.shape[1]
        out_ref[copy] = features[first : first + out_ref.shape[1]]


def feature_rows(mixer, ranks, own, got_ranks, got, ex_rows, copies, parts):
    rows = ADAPTER_RANK * ex_rows
    return pl.pallas_call(
        functools.partial(feature_kernel, ex_rows),
        out_shape=jax.ShapeDtypeStruct((copies, rows // parts, PROJ_ROWS), BF16),
        in_specs=[VMEM] * 5,
        out_specs=VMEM,
        compiler_params=SMALL,
    )(mixer, ranks, own, got_ranks, got)


def fold_ranks(terms):
    half = terms.shape[0] // 2
    return terms[:half] + pltpu.roll(terms[half:], LANES - half, 1)


def pack_lanes(rows, ex_rows):
    parts = [rows[:, i : i + ex_rows] for i in range(0, LANES, 2 * ex_rows)]
    return jnp.concatenate(parts, axis=1)


def pair_kernel(ex_rows, got_ref, keep_ref, send_ref):
    blocks, rows, _ = got_ref.shape
    x = lax.axis_index("x")
    first = 2 * lax.axis_index("z")
    total = None
    for row in range(0, rows, 2 * ex_rows):
        part = pl.ds(row, 2 * ex_rows)
        left = [got_ref[first + x, part, :], got_ref[first + 1 - x, part, :]]
        left = jnp.concatenate(left, axis=0)
        right = jnp.concatenate([got_ref[b, part, :] for b in range(blocks)], axis=0)
        term = lax.dot_general(left, right, NT, preferred_element_type=F32)
        total = term if total is None else total + term
    keep_ref[...] = fold_ranks(total[: 2 * ex_rows])
    send_ref[...] = fold_ranks(total[2 * ex_rows :])


def pair_rows(got, ex_rows):
    return pl.pallas_call(
        functools.partial(pair_kernel, ex_rows),
        out_shape=[jax.ShapeDtypeStruct((ex_rows, LANES), F32)] * 2,
        in_specs=[VMEM],
        out_specs=[VMEM] * 2,
        compiler_params=SMALL,
    )(got)


def halves_kernel(own_ref, got_ref, keep_ref, send_ref):
    total = own_ref[...] + got_ref[...]
    half = keep_ref.shape[0]
    low = lax.axis_index("tensor") == 0
    keep_ref[...] = jnp.where(low, total[:half], total[half:])
    send_ref[...] = jnp.where(low, total[half:], total[:half])


def sum_halves(own, got):
    rows, lanes = own.shape
    return pl.pallas_call(
        halves_kernel,
        out_shape=[jax.ShapeDtypeStruct((rows // 2, lanes), F32)] * 2,
        in_specs=[VMEM] * 2,
        out_specs=[VMEM] * 2,
        compiler_params=SMALL,
    )(own, got)


def sum_kernel(ex_rows, keep_ref, got_ref, out_ref):
    out_ref[...] = pack_lanes(keep_ref[...] + got_ref[...], ex_rows)


def sum_rows(keep, got, ex_rows):
    return pl.pallas_call(
        functools.partial(sum_kernel, ex_rows),
        out_shape=jax.ShapeDtypeStruct((keep.shape[0], LANES // 2), F32),
        in_specs=[VMEM] * 2,
        out_specs=VMEM,
        compiler_params=SMALL,
    )(keep, got)


def swap_cores(value):
    return lax.ppermute(value, "tensor", [(0, 1), (1, 0)])


def swap_across(value):
    return lax.ppermute(value, ("x", "tensor"), [(i, i ^ 3) for i in range(4)])


def trade_kinds(parts):
    blocks, half = parts.shape[0], lax.axis_size("z") // 2
    groups = [[2 * b + (kind ^ (b // 2 // half)) for b in range(blocks)] for kind in range(2)]
    return lax.all_to_all(parts, BLK + ("tensor",), 0, 0, axis_index_groups=groups, tiled=True)


def body(
    hidden, cotangent, token_loss_mask, adapter_down_factor, adapter_up_factor, sign_table_salts
):
    ex_rows, seq, width_half = hidden.shape
    blocks = lax.axis_size("z") * lax.axis_size("x")
    fast = 2 * blocks * ex_rows == LANES and ex_rows == 8
    send, ranks, near, factor, start, kept, mixer = far_rows(
        sign_table_salts,
        token_loss_mask,
        adapter_down_factor,
        adapter_up_factor.T,
        hidden.reshape(ex_rows * seq, width_half),
        cotangent.reshape(ex_rows * seq, width_half),
        fast,
    )
    got = swap_cores(send)
    own, send = near_rows(start, kept, factor, near)
    terms = (mixer, ranks, own, swap_cores(send), got)
    if fast:
        got = trade_kinds(feature_rows(*terms, ex_rows, blocks, 2))
        keep, send = pair_rows(got, ex_rows)
        keep, send = sum_halves(keep, swap_across(send))
        return sum_rows(keep, swap_cores(send), ex_rows)
    whole = feature_rows(*terms, ex_rows, 1, 1)
    share = ADAPTER_RANK * PROJ_ROWS // blocks
    parts = whole.reshape(ADAPTER_RANK, ex_rows, PROJ_ROWS // share, share)
    parts = parts.swapaxes(1, 2).reshape(blocks, ex_rows, share)
    features = lax.all_to_all(parts, BLK, 0, 0, tiled=True).reshape(blocks * ex_rows, share)
    pairs = jnp.einsum("ep,fp->ef", features, features, preferred_element_type=F32)
    pairs = pairs.reshape(blocks, ex_rows, blocks * ex_rows)
    total = jnp.sum(lax.all_to_all(pairs, BLK, 0, 0, tiled=True), axis=0)
    halves = total.reshape(2, ex_rows // 2, blocks * ex_rows)
    core = lax.axis_index("tensor")
    send = lax.dynamic_index_in_dim(halves, 1 - core, 0, keepdims=False)
    return lax.dynamic_index_in_dim(halves, core, 0, keepdims=False) + swap_cores(send)


def solution(mesh):
    groups, blocks, cores = (mesh.shape[name] for name in ("groups", "blk", "tensor"))
    devices = mesh.devices.reshape(groups, blocks // 2, 2, cores)
    placed = (
        P(("groups", "z", "x"), None, "tensor"),
        P(("groups", "z", "x"), None, "tensor"),
        P(("groups", "z", "x"), None),
        P(None, "tensor"),
        P("tensor", None),
        P(),
    )
    return jax.shard_map(
        body,
        mesh=Mesh(devices, ("groups", "z", "x", "tensor")),
        in_specs=placed,
        out_specs=P(("groups", "z", "x", "tensor"), None),
        check_vma=False,
    )
```

```python
import functools
import math

import jax
import jax.numpy as jnp
from jax import lax
from jax.experimental import pallas as pl
from jax.experimental.pallas import tpu as pltpu
from jax.sharding import Mesh, PartitionSpec as P

MODEL_WIDTH = 4096
ADAPTER_RANK = 16
PROJ_ROWS = 256
SEQ = 64
SCALE = 1.0 / math.sqrt(PROJ_ROWS * ADAPTER_RANK * ADAPTER_RANK * SEQ * MODEL_WIDTH)
PIECES = 3
LANES = 128
BLOCK = (16, 256)
BLK = ("z", "x")

F32 = jnp.float32
BF16 = jnp.bfloat16
I32 = jnp.int32
NT = (((1,), (1,)), ((), ()))
VMEM = pl.BlockSpec(memory_space=pltpu.VMEM)
SMEM = pl.BlockSpec(memory_space=pltpu.SMEM)
HBM = pl.BlockSpec(memory_space=pltpu.HBM)
SMALL = pltpu.CompilerParams(vmem_limit_bytes=16 * 1024 * 1024)

INDEX_MUL = -1640531535
SALT_MUL = 668265263


def int32_wrap(value):
    return (value + 2**31) % 2**32 - 2**31


def hash_sign(hashed):
    hashed = hashed ^ lax.shift_right_logical(hashed, 15)
    hashed = hashed * -2048144789
    hashed = hashed ^ lax.shift_right_logical(hashed, 13)
    hashed = hashed * int32_wrap(-1028477387 << 6)
    hashed = hashed ^ lax.shift_left(hashed, 16)
    return jnp.where(hashed < 0, 1.0, -1.0).astype(F32)


def iota(shape, dim):
    return lax.broadcasted_iota(I32, shape, dim)


def token_row(mask):
    ex_rows, seq = mask.shape
    tokens = ex_rows * seq
    tiled = jnp.concatenate([mask.astype(F32)] * ex_rows, axis=1)
    owner = iota((ex_rows, tokens), 1) // seq == iota((ex_rows, tokens), 0)
    return jnp.sum(jnp.where(owner, tiled, 0.0), axis=0, keepdims=True)


def split_pieces(value):
    pieces = []
    for _ in range(PIECES):
        pieces.append(value.astype(BF16))
        value = value - pieces[-1].astype(F32)
    return jnp.concatenate(pieces, axis=0)


def kind_of(cross):
    core = lax.axis_index("tensor")
    return core ^ (lax.axis_index("z") // (lax.axis_size("z") // 2)) if cross else core


def table_start():
    index = iota(BLOCK, 1) * PROJ_ROWS + iota(BLOCK, 0)
    return index * INDEX_MUL


def sign_rows(start, col):
    high, wide = BLOCK
    rows = [
        hash_sign(start + int32_wrap((col * PROJ_ROWS + row) * INDEX_MUL)).astype(BF16)
        for row in range(0, PROJ_ROWS, high)
    ]
    return rows


def far_kernel(
    cross, ex_rows,
    salts_hbm, mask_hbm, down_hbm, up_hbm, hid_hbm, cot_hbm,
    send_ref, ranks_ref, near_ref, start_ref, kept_ref, mixer_ref,
    salts, mask, far_factor, near_factor, far, sems,
):
    tokens, width = far.shape
    kind = kind_of(cross)
    parts = 4
    share = width // parts
    wide = BLOCK[1]

    def copies(inputs, factor, factor_held, held, first):
        out = [pltpu.make_async_copy(factor, factor_held, sems.at[first])]
        for i in range(parts):
            cols = pl.ds(i * share, share)
            out.append(
                pltpu.make_async_copy(inputs.at[:, cols], held.at[:, cols], sems.at[first + 1 + i])
            )
        return out

    def start_copies(far_inputs, far_part, near_inputs, near_part):
        far_copies = copies(far_inputs, far_part, far_factor, far, 2)
        near_copies = copies(near_inputs, near_part, near_factor, near_ref, parts + 3)
        for pair in zip(far_copies, near_copies):
            for copy in pair:
                copy.start()

    salts_copy = pltpu.make_async_copy(salts_hbm, salts, sems.at[0])
    mask_copy = pltpu.make_async_copy(mask_hbm, mask, sems.at[1])
    salts_copy.start()

    @pl.when(kind == 0)
    def _():
        start_copies(hid_hbm, down_hbm, cot_hbm, up_hbm)

    @pl.when(kind == 1)
    def _():
        start_copies(cot_hbm, up_hbm, hid_hbm, down_hbm)

    mask_copy.start()
    far_waits = copies(hid_hbm, down_hbm, far_factor, far, 2)
    near_waits = copies(hid_hbm, down_hbm, near_factor, near_ref, parts + 3)
    first = lax.axis_index("tensor") * int32_wrap(width * PROJ_ROWS * INDEX_MUL)
    start = table_start() + first
    salts_copy.wait()
    far_start = start + salts[2 - 2 * kind] * SALT_MUL
    far_waits[0].wait()
    near_waits[0].wait()
    total = ranks = None
    for col in range(0, width, wide):
        part = slice(col, col + wide)
        left = jnp.concatenate(sign_rows(far_start, col) + [far_factor[:, part]], axis=0)
        if col % share == 0:
            far_waits[1 + col // share].wait()
            near_waits[1 + col // share].wait()
        term = lax.dot_general(left, far[:, part], NT, preferred_element_type=F32)
        total = term if total is None else total + term
        term = lax.dot_general(
            near_factor[:, part], near_ref[:, part], NT, preferred_element_type=F32
        )
        ranks = term if ranks is None else ranks + term
    start_ref[...] = start + salts[2 * kind] * SALT_MUL
    shape = mixer_ref.shape
    mixed, rank = iota(shape, 0) // ex_rows, iota(shape, 1) % ADAPTER_RANK
    index = (rank * ADAPTER_RANK + mixed) * INDEX_MUL
    mixer_ref[...] = hash_sign(index + salts[1 + 2 * kind] * SALT_MUL).astype(BF16)
    mask_copy.wait()
    counted = token_row(mask[...]) != 0
    far_kept = counted | (kind == 0)
    near_kept = counted | (kind == 1)
    kept_ref[...] = jnp.broadcast_to(jnp.where(near_kept, 1.0, 0.0), kept_ref.shape)
    total = jnp.where(far_kept, total, 0.0)
    send_ref[:PROJ_ROWS] = total[:PROJ_ROWS].astype(BF16)
    ranks_ref[...] = split_pieces(total[PROJ_ROWS:])
    send_ref[PROJ_ROWS:] = split_pieces(jnp.where(near_kept, ranks, 0.0))


def far_rows(salts, mask, down, up, hidden, cotangent, cross):
    ex_rows = mask.shape[0]
    tokens, width = hidden.shape
    pieces = PIECES * ADAPTER_RANK
    arrays = (salts, mask, down, up, hidden, cotangent)
    return pl.pallas_call(
        functools.partial(far_kernel, cross, ex_rows),
        out_shape=[
            jax.ShapeDtypeStruct((PROJ_ROWS + pieces, tokens), BF16),
            jax.ShapeDtypeStruct((pieces, tokens), BF16),
            jax.ShapeDtypeStruct((tokens, width), BF16),
            jax.ShapeDtypeStruct(BLOCK, I32),
            jax.ShapeDtypeStruct((8, tokens), F32),
            jax.ShapeDtypeStruct((ADAPTER_RANK * ex_rows, 2 * pieces), BF16),
        ],
        in_specs=[HBM] * 6,
        out_specs=[VMEM] * 6,
        scratch_shapes=[
            pltpu.SMEM(salts.shape, I32),
            pltpu.VMEM(mask.shape, I32),
            pltpu.VMEM((ADAPTER_RANK, width), BF16),
            pltpu.VMEM((ADAPTER_RANK, width), BF16),
            pltpu.VMEM((tokens, width), BF16),
            pltpu.SemaphoreType.DMA((12,)),
        ],
        compiler_params=SMALL,
    )(*[pltpu.with_memory_space_constraint(x, pltpu.HBM) for x in arrays])


def near_kernel(start_ref, kept_ref, near_ref, out_ref):
    start = start_ref[...]
    wide = BLOCK[1]
    total = None
    for col in range(0, near_ref.shape[1], wide):
        left = jnp.concatenate(sign_rows(start, col), axis=0)
        term = lax.dot_general(
            left, near_ref[:, col : col + wide], NT, preferred_element_type=F32
        )
        total = term if total is None else total + term
    out_ref[...] = jnp.where(kept_ref[:1] != 0, total, 0.0).astype(BF16)


def near_rows(start, kept, near):
    tokens, width = near.shape
    return pl.pallas_call(
        near_kernel,
        out_shape=jax.ShapeDtypeStruct((PROJ_ROWS, tokens), BF16),
        in_specs=[VMEM] * 3,
        out_specs=VMEM,
        compiler_params=SMALL,
        cost_estimate=pl.CostEstimate(
            flops=2 * tokens * width * PROJ_ROWS, bytes_accessed=2 * tokens * width, transcendentals=0
        ),
    )(start, kept, near)


def feature_kernel(ex_rows, mixer_ref, ranks_ref, own_ref, other_ref, out_ref, copies_ref):
    tokens = own_ref.shape[1]
    rows = ADAPTER_RANK * ex_rows
    pieces = jnp.concatenate([ranks_ref[...], other_ref[PROJ_ROWS:]], axis=0)
    coeffs = jnp.dot(mixer_ref[...], pieces, preferred_element_type=F32)
    owned = iota((rows, tokens), 1) // SEQ == iota((rows, tokens), 0) % ex_rows
    coeffs = jnp.where(owned, coeffs, 0.0).astype(BF16)
    projected = lax.dot_general(coeffs, own_ref[...], NT, preferred_element_type=F32)
    projected += lax.dot_general(coeffs, other_ref[:PROJ_ROWS], NT, preferred_element_type=F32)
    features = (projected * SCALE).astype(BF16)
    out_ref[...] = features
    for copy in range(copies_ref.shape[0]):
        copies_ref[copy] = features


def feature_rows(mixer, ranks, own, other, ex_rows, copies):
    rows = ADAPTER_RANK * ex_rows
    return pl.pallas_call(
        functools.partial(feature_kernel, ex_rows),
        out_shape=[
            jax.ShapeDtypeStruct((rows, PROJ_ROWS), BF16),
            jax.ShapeDtypeStruct((copies, rows, PROJ_ROWS), BF16),
        ],
        in_specs=[VMEM] * 4,
        out_specs=[VMEM] * 2,
        compiler_params=SMALL,
    )(mixer, ranks, own, other)


def fold_ranks(terms):
    half = terms.shape[0] // 2
    folded = terms[:half] + pltpu.roll(terms[half:], LANES - half, 1)
    return jnp.where(iota(folded.shape, 1) % (2 * half) < half, folded, 0.0)


def pair_kernel(ex_rows, own_ref, near_ref, got_ref, keep_ref, send_ref):
    blocks, rows, _ = got_ref.shape
    total = None
    for row in range(0, rows, 2 * ex_rows):
        part = slice(row, row + 2 * ex_rows)
        left = jnp.concatenate([own_ref[part, :], near_ref[part, :]], axis=0)
        right = jnp.concatenate([got_ref[b, part, :] for b in range(blocks)] * 2, axis=0)
        term = lax.dot_general(left, right, NT, preferred_element_type=F32)
        total = term if total is None else total + term
    keep_ref[...] = fold_ranks(total[: 2 * ex_rows])
    send_ref[...] = fold_ranks(total[2 * ex_rows :])


def pair_rows(own, near, got, ex_rows):
    return pl.pallas_call(
        functools.partial(pair_kernel, ex_rows),
        out_shape=[jax.ShapeDtypeStruct((ex_rows, LANES), F32)] * 2,
        in_specs=[VMEM] * 3,
        out_specs=[VMEM] * 2,
        compiler_params=SMALL,
    )(own, near, got)


def halves_kernel(own_ref, got_ref, keep_ref, send_ref):
    ex_rows, _ = own_ref.shape
    low_x = lax.axis_index("x") == 0
    first = jnp.where(low_x, own_ref[...], got_ref[...])
    second = jnp.where(low_x, got_ref[...], own_ref[...])
    total = first + pltpu.roll(second, ex_rows, 1)
    half = keep_ref.shape[0]
    low = lax.axis_index("tensor") == 0
    keep_ref[...] = jnp.where(low, total[:half], total[half:])
    send_ref[...] = jnp.where(low, total[half:], total[:half])


def join_halves(own, got):
    rows, lanes = own.shape
    return pl.pallas_call(
        halves_kernel,
        out_shape=[jax.ShapeDtypeStruct((rows // 2, lanes), F32)] * 2,
        in_specs=[VMEM] * 2,
        out_specs=[VMEM] * 2,
        compiler_params=SMALL,
    )(own, got)


def sum_kernel(keep_ref, got_ref, out_ref):
    out_ref[...] = (keep_ref[...] + got_ref[...])[:, : out_ref.shape[1]]


def sum_rows(keep, got):
    return pl.pallas_call(
        sum_kernel,
        out_shape=jax.ShapeDtypeStruct((keep.shape[0], LANES // 2), F32),
        in_specs=[VMEM] * 2,
        out_specs=VMEM,
        compiler_params=SMALL,
    )(keep, got)


def swap_cores(value):
    return lax.ppermute(value, "tensor", [(0, 1), (1, 0)])


def swap_across(value):
    return lax.ppermute(value, ("x", "tensor"), [(i, i ^ 3) for i in range(4)])


def swap_x(value):
    return lax.ppermute(value, "x", [(0, 1), (1, 0)])


def trade_z(parts):
    count = parts.shape[0]
    groups = [
        [4 * z + 2 * x + (kind ^ (z // (count // 2))) for z in range(count)]
        for x in range(2)
        for kind in range(2)
    ]
    return lax.all_to_all(parts, BLK + ("tensor",), 0, 0, axis_index_groups=groups, tiled=True)


def body(
    hidden, cotangent, token_loss_mask, adapter_down_factor, adapter_up_factor, sign_table_salts
):
    ex_rows, seq, width_half = hidden.shape
    blocks = lax.axis_size("z") * lax.axis_size("x")
    fast = 2 * blocks * ex_rows == LANES and ex_rows == 8
    send, ranks, near, start, kept, mixer = far_rows(
        sign_table_salts,
        token_loss_mask,
        adapter_down_factor,
        adapter_up_factor.T,
        hidden.reshape(ex_rows * seq, width_half),
        cotangent.reshape(ex_rows * seq, width_half),
        fast,
    )
    other = swap_cores(send)
    terms = (mixer, ranks, near_rows(start, kept, near), other)
    if fast:
        features, copies = feature_rows(*terms, ex_rows, blocks // 2)
        keep, send = pair_rows(features, swap_x(features), trade_z(copies), ex_rows)
        keep, send = join_halves(keep, swap_across(send))
        return sum_rows(keep, swap_cores(send))
    whole, _ = feature_rows(*terms, ex_rows, 1)
    share = ADAPTER_RANK * PROJ_ROWS // blocks
    parts = whole.reshape(ADAPTER_RANK, ex_rows, PROJ_ROWS // share, share)
    parts = parts.swapaxes(1, 2).reshape(blocks, ex_rows, share)
    features = lax.all_to_all(parts, BLK, 0, 0, tiled=True).reshape(blocks * ex_rows, share)
    pairs = jnp.einsum("ep,fp->ef", features, features, preferred_element_type=F32)
    pairs = pairs.reshape(blocks, ex_rows, blocks * ex_rows)
    total = jnp.sum(lax.all_to_all(pairs, BLK, 0, 0, tiled=True), axis=0)
    halves = total.reshape(2, ex_rows // 2, blocks * ex_rows)
    core = lax.axis_index("tensor")
    send = lax.dynamic_index_in_dim(halves, 1 - core, 0, keepdims=False)
    return lax.dynamic_index_in_dim(halves, core, 0, keepdims=False) + swap_cores(send)


def solution(mesh):
    groups, blocks, cores = (mesh.shape[name] for name in ("groups", "blk", "tensor"))
    devices = mesh.devices.reshape(groups, blocks // 2, 2, cores)
    placed = (
        P(("groups", "z", "x"), None, "tensor"),
        P(("groups", "z", "x"), None, "tensor"),
        P(("groups", "z", "x"), None),
        P(None, "tensor"),
        P("tensor", None),
        P(),
    )
    return jax.shard_map(
        body,
        mesh=Mesh(devices, ("groups", "z", "x", "tensor")),
        in_specs=placed,
        out_specs=P(("groups", "z", "x", "tensor"), None),
        check_vma=False,
    )
```

```python
import functools
import math

import jax
import jax.numpy as jnp
from jax import lax
from jax.experimental import pallas as pl
from jax.experimental.pallas import tpu as pltpu
from jax.sharding import Mesh, PartitionSpec as P

MODEL_WIDTH = 4096
ADAPTER_RANK = 16
PROJ_ROWS = 256
SEQ = 64
SCALE = 1.0 / math.sqrt(PROJ_ROWS * ADAPTER_RANK * ADAPTER_RANK * SEQ * MODEL_WIDTH)
PIECES = 3
LANES = 128
BLOCK = (16, 256)
BLK = ("z", "x")

F32 = jnp.float32
BF16 = jnp.bfloat16
I32 = jnp.int32
NT = (((1,), (1,)), ((), ()))
VMEM = pl.BlockSpec(memory_space=pltpu.VMEM)
SMEM = pl.BlockSpec(memory_space=pltpu.SMEM)
HBM = pl.BlockSpec(memory_space=pltpu.HBM)
SMALL = pltpu.CompilerParams(vmem_limit_bytes=16 * 1024 * 1024)

INDEX_MUL = -1640531535
SALT_MUL = 668265263


def int32_wrap(value):
    return (value + 2**31) % 2**32 - 2**31


def hash_sign(hashed):
    hashed = hashed ^ lax.shift_right_logical(hashed, 15)
    hashed = hashed * -2048144789
    hashed = hashed ^ lax.shift_right_logical(hashed, 13)
    hashed = hashed * int32_wrap(-1028477387 << 6)
    hashed = hashed ^ lax.shift_left(hashed, 16)
    return jnp.where(hashed < 0, 1.0, -1.0).astype(F32)


def iota(shape, dim):
    return lax.broadcasted_iota(I32, shape, dim)


def token_row(mask):
    ex_rows, seq = mask.shape
    tokens = ex_rows * seq
    tiled = jnp.concatenate([mask.astype(F32)] * ex_rows, axis=1)
    owner = iota((ex_rows, tokens), 1) // seq == iota((ex_rows, tokens), 0)
    return jnp.sum(jnp.where(owner, tiled, 0.0), axis=0, keepdims=True)


def split_pieces(value):
    pieces = []
    for _ in range(PIECES):
        pieces.append(value.astype(BF16))
        value = value - pieces[-1].astype(F32)
    return jnp.concatenate(pieces, axis=0)


def kind_of(cross):
    core = lax.axis_index("tensor")
    return core ^ (lax.axis_index("z") // (lax.axis_size("z") // 2)) if cross else core


def table_start():
    index = iota(BLOCK, 1) * PROJ_ROWS + iota(BLOCK, 0)
    return index * INDEX_MUL


def sign_rows(start, col):
    high, wide = BLOCK
    rows = [
        hash_sign(start + int32_wrap((col * PROJ_ROWS + row) * INDEX_MUL)).astype(BF16)
        for row in range(0, PROJ_ROWS, high)
    ]
    return rows


def far_kernel(
    cross, ex_rows,
    salts_hbm, mask_hbm, down_hbm, up_hbm, hid_hbm, cot_hbm,
    send_ref, ranks_ref, near_ref, start_ref, kept_ref, mixer_ref,
    salts, mask, far_factor, near_factor, far, sems,
):
    tokens, width = far.shape
    kind = kind_of(cross)
    parts = 4
    share = width // parts
    wide = BLOCK[1]

    def copies(inputs, factor, factor_held, held, first):
        out = [pltpu.make_async_copy(factor, factor_held, sems.at[first])]
        for i in range(parts):
            cols = pl.ds(i * share, share)
            out.append(
                pltpu.make_async_copy(inputs.at[:, cols], held.at[:, cols], sems.at[first + 1 + i])
            )
        return out

    def start_copies(far_inputs, far_part, near_inputs, near_part):
        far_copies = copies(far_inputs, far_part, far_factor, far, 2)
        near_copies = copies(near_inputs, near_part, near_factor, near_ref, parts + 3)
        for pair in zip(far_copies, near_copies):
            for copy in pair:
                copy.start()

    salts_copy = pltpu.make_async_copy(salts_hbm, salts, sems.at[0])
    mask_copy = pltpu.make_async_copy(mask_hbm, mask, sems.at[1])
    salts_copy.start()

    @pl.when(kind == 0)
    def _():
        start_copies(hid_hbm, down_hbm, cot_hbm, up_hbm)

    @pl.when(kind == 1)
    def _():
        start_copies(cot_hbm, up_hbm, hid_hbm, down_hbm)

    mask_copy.start()
    far_waits = copies(hid_hbm, down_hbm, far_factor, far, 2)
    near_waits = copies(hid_hbm, down_hbm, near_factor, near_ref, parts + 3)
    first = lax.axis_index("tensor") * int32_wrap(width * PROJ_ROWS * INDEX_MUL)
    start = table_start() + first
    salts_copy.wait()
    far_start = start + salts[2 - 2 * kind] * SALT_MUL
    far_waits[0].wait()
    near_waits[0].wait()
    total = ranks = None
    for col in range(0, width, wide):
        part = slice(col, col + wide)
        left = jnp.concatenate(sign_rows(far_start, col) + [far_factor[:, part]], axis=0)
        if col % share == 0:
            far_waits[1 + col // share].wait()
            near_waits[1 + col // share].wait()
        term = lax.dot_general(left, far[:, part], NT, preferred_element_type=F32)
        total = term if total is None else total + term
        term = lax.dot_general(
            near_factor[:, part], near_ref[:, part], NT, preferred_element_type=F32
        )
        ranks = term if ranks is None else ranks + term
    start_ref[...] = start + salts[2 * kind] * SALT_MUL
    shape = mixer_ref.shape
    mixed, rank = iota(shape, 0) // ex_rows, iota(shape, 1) % ADAPTER_RANK
    index = (rank * ADAPTER_RANK + mixed) * INDEX_MUL
    mixer_ref[...] = hash_sign(index + salts[1 + 2 * kind] * SALT_MUL).astype(BF16)
    mask_copy.wait()
    counted = token_row(mask[...]) != 0
    far_kept = counted | (kind == 0)
    near_kept = counted | (kind == 1)
    kept_ref[...] = jnp.broadcast_to(jnp.where(near_kept, 1.0, 0.0), kept_ref.shape)
    total = jnp.where(far_kept, total, 0.0)
    send_ref[:PROJ_ROWS] = total[:PROJ_ROWS].astype(BF16)
    ranks_ref[...] = split_pieces(total[PROJ_ROWS:])
    send_ref[PROJ_ROWS:] = split_pieces(jnp.where(near_kept, ranks, 0.0))


def far_rows(salts, mask, down, up, hidden, cotangent, cross):
    ex_rows = mask.shape[0]
    tokens, width = hidden.shape
    pieces = PIECES * ADAPTER_RANK
    arrays = (salts, mask, down, up, hidden, cotangent)
    return pl.pallas_call(
        functools.partial(far_kernel, cross, ex_rows),
        out_shape=[
            jax.ShapeDtypeStruct((PROJ_ROWS + pieces, tokens), BF16),
            jax.ShapeDtypeStruct((pieces, tokens), BF16),
            jax.ShapeDtypeStruct((tokens, width), BF16),
            jax.ShapeDtypeStruct(BLOCK, I32),
            jax.ShapeDtypeStruct((8, tokens), F32),
            jax.ShapeDtypeStruct((ADAPTER_RANK * ex_rows, 2 * pieces), BF16),
        ],
        in_specs=[HBM] * 6,
        out_specs=[VMEM] * 6,
        scratch_shapes=[
            pltpu.SMEM(salts.shape, I32),
            pltpu.VMEM(mask.shape, I32),
            pltpu.VMEM((ADAPTER_RANK, width), BF16),
            pltpu.VMEM((ADAPTER_RANK, width), BF16),
            pltpu.VMEM((tokens, width), BF16),
            pltpu.SemaphoreType.DMA((12,)),
        ],
        compiler_params=SMALL,
    )(*[pltpu.with_memory_space_constraint(x, pltpu.HBM) for x in arrays])


def near_kernel(start_ref, kept_ref, near_ref, out_ref):
    start = start_ref[...]
    wide = BLOCK[1]
    total = None
    for col in range(0, near_ref.shape[1], wide):
        left = jnp.concatenate(sign_rows(start, col), axis=0)
        term = lax.dot_general(
            left, near_ref[:, col : col + wide], NT, preferred_element_type=F32
        )
        total = term if total is None else total + term
    out_ref[...] = jnp.where(kept_ref[:1] != 0, total, 0.0).astype(BF16)


def near_rows(start, kept, near):
    tokens, width = near.shape
    return pl.pallas_call(
        near_kernel,
        out_shape=jax.ShapeDtypeStruct((PROJ_ROWS, tokens), BF16),
        in_specs=[VMEM] * 3,
        out_specs=VMEM,
        compiler_params=SMALL,
        cost_estimate=pl.CostEstimate(
            flops=2 * tokens * width * PROJ_ROWS, bytes_accessed=2 * tokens * width, transcendentals=0
        ),
    )(start, kept, near)


def feature_kernel(ex_rows, mixer_ref, ranks_ref, own_ref, other_ref, out_ref):
    tokens = own_ref.shape[1]
    rows = ADAPTER_RANK * ex_rows
    pieces = jnp.concatenate([ranks_ref[...], other_ref[PROJ_ROWS:]], axis=0)
    coeffs = jnp.dot(mixer_ref[...], pieces, preferred_element_type=F32)
    owned = iota((rows, tokens), 1) // SEQ == iota((rows, tokens), 0) % ex_rows
    coeffs = jnp.where(owned, coeffs, 0.0).astype(BF16)
    projected = lax.dot_general(coeffs, own_ref[...], NT, preferred_element_type=F32)
    projected += lax.dot_general(coeffs, other_ref[:PROJ_ROWS], NT, preferred_element_type=F32)
    out_ref[...] = (projected * SCALE).astype(BF16)


def feature_rows(mixer, ranks, own, other, ex_rows):
    return pl.pallas_call(
        functools.partial(feature_kernel, ex_rows),
        out_shape=jax.ShapeDtypeStruct((ADAPTER_RANK * ex_rows, PROJ_ROWS), BF16),
        in_specs=[VMEM] * 4,
        out_specs=VMEM,
        compiler_params=SMALL,
    )(mixer, ranks, own, other)


def fold_ranks(terms):
    half = terms.shape[0] // 2
    folded = terms[:half] + pltpu.roll(terms[half:], LANES - half, 1)
    return jnp.where(iota(folded.shape, 1) % (2 * half) < half, folded, 0.0)


def order_blocks(rows, wide):
    z = lax.axis_index("z")
    rows = jnp.where((z & 2) != 0, pltpu.roll(rows, 2 * wide, 1), rows)
    even = (iota(rows.shape, 1) // wide) % 2 == 0
    swapped = jnp.where(even, pltpu.roll(rows, LANES - wide, 1), pltpu.roll(rows, wide, 1))
    return jnp.where((z & 1) != 0, swapped, rows)


def pair_kernel(ex_rows, near_ref, *refs):
    *z_refs, keep_ref, send_ref = refs
    wide = 2 * ex_rows
    total = None
    for row in range(0, near_ref.shape[0], wide):
        part = slice(row, row + wide)
        left = jnp.concatenate([z_refs[0][part, :], near_ref[part, :]], axis=0)
        right = jnp.concatenate([ref[part, :] for ref in z_refs] * 2, axis=0)
        term = lax.dot_general(left, right, NT, preferred_element_type=F32)
        total = term if total is None else total + term
    keep_ref[...] = order_blocks(fold_ranks(total[:wide]), wide)
    send_ref[...] = order_blocks(fold_ranks(total[wide:]), wide)


def pair_rows(near, by_z, ex_rows):
    return pl.pallas_call(
        functools.partial(pair_kernel, ex_rows),
        out_shape=[jax.ShapeDtypeStruct((ex_rows, LANES), F32)] * 2,
        in_specs=[VMEM] * (1 + len(by_z)),
        out_specs=[VMEM] * 2,
        compiler_params=SMALL,
    )(near, *by_z)


def halves_kernel(own_ref, got_ref, keep_ref, send_ref):
    ex_rows, _ = own_ref.shape
    low_x = lax.axis_index("x") == 0
    first = jnp.where(low_x, own_ref[...], got_ref[...])
    second = jnp.where(low_x, got_ref[...], own_ref[...])
    total = first + pltpu.roll(second, ex_rows, 1)
    half = keep_ref.shape[0]
    low = lax.axis_index("tensor") == 0
    keep_ref[...] = jnp.where(low, total[:half], total[half:])
    send_ref[...] = jnp.where(low, total[half:], total[:half])


def join_halves(own, got):
    rows, lanes = own.shape
    return pl.pallas_call(
        halves_kernel,
        out_shape=[jax.ShapeDtypeStruct((rows // 2, lanes), F32)] * 2,
        in_specs=[VMEM] * 2,
        out_specs=[VMEM] * 2,
        compiler_params=SMALL,
    )(own, got)


def sum_kernel(keep_ref, got_ref, out_ref):
    out_ref[...] = (keep_ref[...] + got_ref[...])[:, : out_ref.shape[1]]


def sum_rows(keep, got):
    return pl.pallas_call(
        sum_kernel,
        out_shape=jax.ShapeDtypeStruct((keep.shape[0], LANES // 2), F32),
        in_specs=[VMEM] * 2,
        out_specs=VMEM,
        compiler_params=SMALL,
    )(keep, got)


def swap_cores(value):
    return lax.ppermute(value, "tensor", [(0, 1), (1, 0)])


def swap_across(value):
    return lax.ppermute(value, ("x", "tensor"), [(i, i ^ 3) for i in range(4)])


def swap_x(value):
    return lax.ppermute(value, "x", [(0, 1), (1, 0)])


def swap_z(value, step):
    other = 4 * step + (step > 1)
    return lax.ppermute(value, BLK + ("tensor",), [(i, i ^ other) for i in range(16)])


def body(
    hidden, cotangent, token_loss_mask, adapter_down_factor, adapter_up_factor, sign_table_salts
):
    ex_rows, seq, width_half = hidden.shape
    blocks = lax.axis_size("z") * lax.axis_size("x")
    fast = blocks == 8 and ex_rows == 8
    send, ranks, near, start, kept, mixer = far_rows(
        sign_table_salts,
        token_loss_mask,
        adapter_down_factor,
        adapter_up_factor.T,
        hidden.reshape(ex_rows * seq, width_half),
        cotangent.reshape(ex_rows * seq, width_half),
        fast,
    )
    other = swap_cores(send)
    terms = (mixer, ranks, near_rows(start, kept, near), other)
    features = feature_rows(*terms, ex_rows)
    if fast:
        third = swap_z(features, 3)
        second = swap_z(features, 2)
        first = swap_z(features, 1)
        near = swap_x(features)
        keep, send = pair_rows(near, (features, first, second, third), ex_rows)
        keep, send = join_halves(keep, swap_across(send))
        return sum_rows(keep, swap_cores(send))
    share = ADAPTER_RANK * PROJ_ROWS // blocks
    parts = features.reshape(ADAPTER_RANK, ex_rows, PROJ_ROWS // share, share)
    parts = parts.swapaxes(1, 2).reshape(blocks, ex_rows, share)
    features = lax.all_to_all(parts, BLK, 0, 0, tiled=True).reshape(blocks * ex_rows, share)
    pairs = jnp.einsum("ep,fp->ef", features, features, preferred_element_type=F32)
    pairs = pairs.reshape(blocks, ex_rows, blocks * ex_rows)
    total = jnp.sum(lax.all_to_all(pairs, BLK, 0, 0, tiled=True), axis=0)
    halves = total.reshape(2, ex_rows // 2, blocks * ex_rows)
    core = lax.axis_index("tensor")
    send = lax.dynamic_index_in_dim(halves, 1 - core, 0, keepdims=False)
    return lax.dynamic_index_in_dim(halves, core, 0, keepdims=False) + swap_cores(send)


def solution(mesh):
    groups, blocks, cores = (mesh.shape[name] for name in ("groups", "blk", "tensor"))
    devices = mesh.devices.reshape(groups, blocks // 2, 2, cores)
    placed = (
        P(("groups", "z", "x"), None, "tensor"),
        P(("groups", "z", "x"), None, "tensor"),
        P(("groups", "z", "x"), None),
        P(None, "tensor"),
        P("tensor", None),
        P(),
    )
    return jax.shard_map(
        body,
        mesh=Mesh(devices, ("groups", "z", "x", "tensor")),
        in_specs=placed,
        out_specs=P(("groups", "z", "x", "tensor"), None),
        check_vma=False,
    )
```

```python
import functools
import math

import jax
import jax.numpy as jnp
from jax import lax
from jax.experimental import pallas as pl
from jax.experimental.pallas import tpu as pltpu
from jax.sharding import Mesh, PartitionSpec as P

MODEL_WIDTH = 4096
ADAPTER_RANK = 16
PROJ_ROWS = 256
SEQ = 64
SCALE = 1.0 / math.sqrt(PROJ_ROWS * ADAPTER_RANK * ADAPTER_RANK * SEQ * MODEL_WIDTH)
PIECES = 3
LANES = 128
BLOCK = (16, 256)
BLK = ("z", "x")

F32 = jnp.float32
BF16 = jnp.bfloat16
I32 = jnp.int32
NT = (((1,), (1,)), ((), ()))
VMEM = pl.BlockSpec(memory_space=pltpu.VMEM)
SMEM = pl.BlockSpec(memory_space=pltpu.SMEM)
HBM = pl.BlockSpec(memory_space=pltpu.HBM)
SMALL = pltpu.CompilerParams(vmem_limit_bytes=16 * 1024 * 1024)

INDEX_MUL = -1640531535
SALT_MUL = 668265263


def int32_wrap(value):
    return (value + 2**31) % 2**32 - 2**31


def hash_sign(hashed):
    hashed = hashed ^ lax.shift_right_logical(hashed, 15)
    hashed = hashed * -2048144789
    hashed = hashed ^ lax.shift_right_logical(hashed, 13)
    hashed = hashed * int32_wrap(-1028477387 << 6)
    hashed = hashed ^ lax.shift_left(hashed, 16)
    return jnp.where(hashed < 0, 1.0, -1.0).astype(F32)


def iota(shape, dim):
    return lax.broadcasted_iota(I32, shape, dim)


def token_row(mask):
    ex_rows, seq = mask.shape
    tokens = ex_rows * seq
    tiled = jnp.concatenate([mask.astype(F32)] * ex_rows, axis=1)
    owner = iota((ex_rows, tokens), 1) // seq == iota((ex_rows, tokens), 0)
    return jnp.sum(jnp.where(owner, tiled, 0.0), axis=0, keepdims=True)


def split_pieces(value):
    pieces = []
    for _ in range(PIECES):
        pieces.append(value.astype(BF16))
        value = value - pieces[-1].astype(F32)
    return jnp.concatenate(pieces, axis=0)


def kind_of(cross):
    core = lax.axis_index("tensor")
    return core ^ (lax.axis_index("z") // (lax.axis_size("z") // 2)) if cross else core


def table_start():
    index = iota(BLOCK, 1) * PROJ_ROWS + iota(BLOCK, 0)
    return index * INDEX_MUL


def sign_rows(start, col):
    high, wide = BLOCK
    rows = [
        hash_sign(start + int32_wrap((col * PROJ_ROWS + row) * INDEX_MUL)).astype(BF16)
        for row in range(0, PROJ_ROWS, high)
    ]
    return rows


def far_kernel(
    cross, ex_rows,
    salts_hbm, mask_hbm, down_hbm, up_hbm, hid_hbm, cot_hbm,
    send_ref, ranks_ref, near_ref, start_ref, kept_ref, mixer_ref,
    salts, mask, far_factor, near_factor, far, sems,
):
    tokens, width = far.shape
    kind = kind_of(cross)
    parts = 4
    share = width // parts
    wide = BLOCK[1]

    def copies(inputs, factor, factor_held, held, first):
        out = [pltpu.make_async_copy(factor, factor_held, sems.at[first])]
        for i in range(parts):
            cols = pl.ds(i * share, share)
            out.append(
                pltpu.make_async_copy(inputs.at[:, cols], held.at[:, cols], sems.at[first + 1 + i])
            )
        return out

    def start_copies(far_inputs, far_part, near_inputs, near_part):
        far_copies = copies(far_inputs, far_part, far_factor, far, 2)
        near_copies = copies(near_inputs, near_part, near_factor, near_ref, parts + 3)
        for pair in zip(far_copies, near_copies):
            for copy in pair:
                copy.start()

    salts_copy = pltpu.make_async_copy(salts_hbm, salts, sems.at[0])
    mask_copy = pltpu.make_async_copy(mask_hbm, mask, sems.at[1])
    salts_copy.start()

    @pl.when(kind == 0)
    def _():
        start_copies(hid_hbm, down_hbm, cot_hbm, up_hbm)

    @pl.when(kind == 1)
    def _():
        start_copies(cot_hbm, up_hbm, hid_hbm, down_hbm)

    mask_copy.start()
    far_waits = copies(hid_hbm, down_hbm, far_factor, far, 2)
    near_waits = copies(hid_hbm, down_hbm, near_factor, near_ref, parts + 3)
    first = lax.axis_index("tensor") * int32_wrap(width * PROJ_ROWS * INDEX_MUL)
    start = table_start() + first
    salts_copy.wait()
    far_start = start + salts[2 - 2 * kind] * SALT_MUL
    far_waits[0].wait()
    near_waits[0].wait()
    total = ranks = None
    for col in range(0, width, wide):
        part = slice(col, col + wide)
        left = jnp.concatenate(sign_rows(far_start, col) + [far_factor[:, part]], axis=0)
        if col % share == 0:
            far_waits[1 + col // share].wait()
            near_waits[1 + col // share].wait()
        term = lax.dot_general(left, far[:, part], NT, preferred_element_type=F32)
        total = term if total is None else total + term
        term = lax.dot_general(
            near_factor[:, part], near_ref[:, part], NT, preferred_element_type=F32
        )
        ranks = term if ranks is None else ranks + term
    start_ref[...] = start + salts[2 * kind] * SALT_MUL
    shape = mixer_ref.shape
    mixed, rank = iota(shape, 0) // ex_rows, iota(shape, 1) % ADAPTER_RANK
    index = (rank * ADAPTER_RANK + mixed) * INDEX_MUL
    mixer_ref[...] = hash_sign(index + salts[1 + 2 * kind] * SALT_MUL).astype(BF16)
    mask_copy.wait()
    counted = token_row(mask[...]) != 0
    far_kept = counted | (kind == 0)
    near_kept = counted | (kind == 1)
    kept_ref[...] = jnp.broadcast_to(jnp.where(near_kept, 1.0, 0.0), kept_ref.shape)
    total = jnp.where(far_kept, total, 0.0)
    send_ref[:PROJ_ROWS] = total[:PROJ_ROWS].astype(BF16)
    ranks_ref[...] = split_pieces(total[PROJ_ROWS:])
    send_ref[PROJ_ROWS:] = split_pieces(jnp.where(near_kept, ranks, 0.0))


def far_rows(salts, mask, down, up, hidden, cotangent, cross):
    ex_rows = mask.shape[0]
    tokens, width = hidden.shape
    pieces = PIECES * ADAPTER_RANK
    arrays = (salts, mask, down, up, hidden, cotangent)
    return pl.pallas_call(
        functools.partial(far_kernel, cross, ex_rows),
        out_shape=[
            jax.ShapeDtypeStruct((PROJ_ROWS + pieces, tokens), BF16),
            jax.ShapeDtypeStruct((pieces, tokens), BF16),
            jax.ShapeDtypeStruct((tokens, width), BF16),
            jax.ShapeDtypeStruct(BLOCK, I32),
            jax.ShapeDtypeStruct((8, tokens), F32),
            jax.ShapeDtypeStruct((ADAPTER_RANK * ex_rows, 2 * pieces), BF16),
        ],
        in_specs=[HBM] * 6,
        out_specs=[VMEM] * 6,
        scratch_shapes=[
            pltpu.SMEM(salts.shape, I32),
            pltpu.VMEM(mask.shape, I32),
            pltpu.VMEM((ADAPTER_RANK, width), BF16),
            pltpu.VMEM((ADAPTER_RANK, width), BF16),
            pltpu.VMEM((tokens, width), BF16),
            pltpu.SemaphoreType.DMA((12,)),
        ],
        compiler_params=SMALL,
    )(*[pltpu.with_memory_space_constraint(x, pltpu.HBM) for x in arrays])


def near_kernel(start_ref, kept_ref, near_ref, out_ref):
    start = start_ref[...]
    wide = BLOCK[1]
    total = None
    for col in range(0, near_ref.shape[1], wide):
        left = jnp.concatenate(sign_rows(start, col), axis=0)
        term = lax.dot_general(
            left, near_ref[:, col : col + wide], NT, preferred_element_type=F32
        )
        total = term if total is None else total + term
    out_ref[...] = jnp.where(kept_ref[:1] != 0, total, 0.0).astype(BF16)


def near_rows(start, kept, near):
    tokens, width = near.shape
    return pl.pallas_call(
        near_kernel,
        out_shape=jax.ShapeDtypeStruct((PROJ_ROWS, tokens), BF16),
        in_specs=[VMEM] * 3,
        out_specs=VMEM,
        compiler_params=SMALL,
        cost_estimate=pl.CostEstimate(
            flops=2 * tokens * width * PROJ_ROWS, bytes_accessed=2 * tokens * width, transcendentals=0
        ),
    )(start, kept, near)


def feature_kernel(ex_rows, mixer_ref, ranks_ref, own_ref, other_ref, out_ref):
    tokens = own_ref.shape[1]
    rows = ADAPTER_RANK * ex_rows
    pieces = jnp.concatenate([ranks_ref[...], other_ref[PROJ_ROWS:]], axis=0)
    coeffs = jnp.dot(mixer_ref[...], pieces, preferred_element_type=F32)
    owned = iota((rows, tokens), 1) // SEQ == iota((rows, tokens), 0) % ex_rows
    coeffs = jnp.where(owned, coeffs, 0.0).astype(BF16)
    projected = lax.dot_general(coeffs, own_ref[...], NT, preferred_element_type=F32)
    projected += lax.dot_general(coeffs, other_ref[:PROJ_ROWS], NT, preferred_element_type=F32)
    out_ref[...] = (projected * SCALE).astype(BF16)


def feature_rows(mixer, ranks, own, other, ex_rows):
    return pl.pallas_call(
        functools.partial(feature_kernel, ex_rows),
        out_shape=jax.ShapeDtypeStruct((ADAPTER_RANK * ex_rows, PROJ_ROWS), BF16),
        in_specs=[VMEM] * 4,
        out_specs=VMEM,
        compiler_params=SMALL,
    )(mixer, ranks, own, other)


def fold_ranks(terms):
    half = terms.shape[0] // 2
    folded = terms[:half] + pltpu.roll(terms[half:], LANES - half, 1)
    return jnp.where(iota(folded.shape, 1) % (2 * half) < half, folded, 0.0)


def order_blocks(rows, wide):
    z = lax.axis_index("z")
    rows = jnp.where((z & 2) != 0, pltpu.roll(rows, 2 * wide, 1), rows)
    even = (iota(rows.shape, 1) // wide) % 2 == 0
    swapped = jnp.where(even, pltpu.roll(rows, LANES - wide, 1), pltpu.roll(rows, wide, 1))
    return jnp.where((z & 1) != 0, swapped, rows)


def pair_kernel(ex_rows, own_ref, *refs):
    *got_refs, keep_ref, send_ref = refs
    z = lax.axis_index("z")
    high, pair_23, pair_13, pair_12, pair_02, pair_03, low, pair_01 = got_refs
    upper, odd = z >= 2, (z & 1) != 0
    choices = (
        (upper, high, low),
        (upper, pair_23, pair_01),
        (odd, pair_13, pair_02),
        ((z == 1) | (z == 2), pair_12, pair_03),
    )
    wide = 2 * ex_rows
    total = None
    for row in range(0, own_ref.shape[0], wide):
        part = slice(row, row + wide)
        own = own_ref[part, :]
        near, *others = [
            jnp.where(here, one[part, :], two[part, :]) for here, one, two in choices
        ]
        left = jnp.concatenate([own, near], axis=0)
        right = jnp.concatenate([own, *others] * 2, axis=0)
        term = lax.dot_general(left, right, NT, preferred_element_type=F32)
        total = term if total is None else total + term
    keep_ref[...] = order_blocks(fold_ranks(total[:wide]), wide)
    send_ref[...] = order_blocks(fold_ranks(total[wide:]), wide)


def pair_rows(own, got, ex_rows):
    return pl.pallas_call(
        functools.partial(pair_kernel, ex_rows),
        out_shape=[jax.ShapeDtypeStruct((ex_rows, LANES), F32)] * 2,
        in_specs=[VMEM] * (1 + len(got)),
        out_specs=[VMEM] * 2,
        compiler_params=SMALL,
    )(own, *got)


def halves_kernel(own_ref, got_ref, keep_ref, send_ref):
    ex_rows, _ = own_ref.shape
    low_x = lax.axis_index("x") == 0
    first = jnp.where(low_x, own_ref[...], got_ref[...])
    second = jnp.where(low_x, got_ref[...], own_ref[...])
    total = first + pltpu.roll(second, ex_rows, 1)
    half = keep_ref.shape[0]
    low = lax.axis_index("tensor") == 0
    keep_ref[...] = jnp.where(low, total[:half], total[half:])
    send_ref[...] = jnp.where(low, total[half:], total[:half])


def join_halves(own, got):
    rows, lanes = own.shape
    return pl.pallas_call(
        halves_kernel,
        out_shape=[jax.ShapeDtypeStruct((rows // 2, lanes), F32)] * 2,
        in_specs=[VMEM] * 2,
        out_specs=[VMEM] * 2,
        compiler_params=SMALL,
    )(own, got)


def sum_kernel(keep_ref, got_ref, out_ref):
    out_ref[...] = (keep_ref[...] + got_ref[...])[:, : out_ref.shape[1]]


def sum_rows(keep, got):
    return pl.pallas_call(
        sum_kernel,
        out_shape=jax.ShapeDtypeStruct((keep.shape[0], LANES // 2), F32),
        in_specs=[VMEM] * 2,
        out_specs=VMEM,
        compiler_params=SMALL,
    )(keep, got)


def swap_cores(value):
    return lax.ppermute(value, "tensor", [(0, 1), (1, 0)])


def swap_across(value):
    return lax.ppermute(value, ("x", "tensor"), [(i, i ^ 3) for i in range(4)])


def device(z, x, kind):
    return 4 * z + 2 * x + (kind ^ (z // 2))


def swap_pair(value, one, two):
    pairs = []
    for x in range(2):
        for kind in range(2):
            ends = device(one, x, kind), device(two, x, kind)
            pairs += [ends, ends[::-1]]
    return lax.ppermute(value, BLK + ("tensor",), pairs)


def swap_x(value, zs):
    pairs = [
        (device(z, x, kind), device(z, 1 - x, kind)) for z in zs for x in range(2) for kind in range(2)
    ]
    return lax.ppermute(value, BLK + ("tensor",), pairs)


def swap_features(value):
    low = swap_x(value, (0, 1))
    high = swap_x(value, (2, 3))
    one = [swap_pair(value, *ends) for ends in ((2, 3), (0, 1))]
    two = [swap_pair(value, *ends) for ends in ((1, 3), (0, 2))]
    three = [swap_pair(value, *ends) for ends in ((1, 2), (0, 3))]
    return [high, one[0], two[0], three[0], two[1], three[1], low, one[1]]


def body(
    hidden, cotangent, token_loss_mask, adapter_down_factor, adapter_up_factor, sign_table_salts
):
    ex_rows, seq, width_half = hidden.shape
    blocks = lax.axis_size("z") * lax.axis_size("x")
    fast = blocks == 8 and ex_rows == 8
    send, ranks, near, start, kept, mixer = far_rows(
        sign_table_salts,
        token_loss_mask,
        adapter_down_factor,
        adapter_up_factor.T,
        hidden.reshape(ex_rows * seq, width_half),
        cotangent.reshape(ex_rows * seq, width_half),
        fast,
    )
    other = swap_cores(send)
    terms = (mixer, ranks, near_rows(start, kept, near), other)
    features = feature_rows(*terms, ex_rows)
    if fast:
        keep, send = pair_rows(features, swap_features(features), ex_rows)
        keep, send = join_halves(keep, swap_across(send))
        return sum_rows(keep, swap_cores(send))
    share = ADAPTER_RANK * PROJ_ROWS // blocks
    parts = features.reshape(ADAPTER_RANK, ex_rows, PROJ_ROWS // share, share)
    parts = parts.swapaxes(1, 2).reshape(blocks, ex_rows, share)
    features = lax.all_to_all(parts, BLK, 0, 0, tiled=True).reshape(blocks * ex_rows, share)
    pairs = jnp.einsum("ep,fp->ef", features, features, preferred_element_type=F32)
    pairs = pairs.reshape(blocks, ex_rows, blocks * ex_rows)
    total = jnp.sum(lax.all_to_all(pairs, BLK, 0, 0, tiled=True), axis=0)
    halves = total.reshape(2, ex_rows // 2, blocks * ex_rows)
    core = lax.axis_index("tensor")
    send = lax.dynamic_index_in_dim(halves, 1 - core, 0, keepdims=False)
    return lax.dynamic_index_in_dim(halves, core, 0, keepdims=False) + swap_cores(send)


def solution(mesh):
    groups, blocks, cores = (mesh.shape[name] for name in ("groups", "blk", "tensor"))
    devices = mesh.devices.reshape(groups, blocks // 2, 2, cores)
    placed = (
        P(("groups", "z", "x"), None, "tensor"),
        P(("groups", "z", "x"), None, "tensor"),
        P(("groups", "z", "x"), None),
        P(None, "tensor"),
        P("tensor", None),
        P(),
    )
    return jax.shard_map(
        body,
        mesh=Mesh(devices, ("groups", "z", "x", "tensor")),
        in_specs=placed,
        out_specs=P(("groups", "z", "x", "tensor"), None),
        check_vma=False,
    )
```

```python
import functools
import math

import jax
import jax.numpy as jnp
from jax import lax
from jax.experimental import pallas as pl
from jax.experimental.pallas import tpu as pltpu
from jax.sharding import Mesh, PartitionSpec as P

MODEL_WIDTH = 4096
ADAPTER_RANK = 16
PROJ_ROWS = 256
SEQ = 64
SCALE = 1.0 / math.sqrt(PROJ_ROWS * ADAPTER_RANK * ADAPTER_RANK * SEQ * MODEL_WIDTH)
PIECES = 3
LANES = 128
BLOCK = (16, 256)
BLK = ("z", "x")

F32 = jnp.float32
BF16 = jnp.bfloat16
I32 = jnp.int32
NT = (((1,), (1,)), ((), ()))
VMEM = pl.BlockSpec(memory_space=pltpu.VMEM)
SMEM = pl.BlockSpec(memory_space=pltpu.SMEM)
HBM = pl.BlockSpec(memory_space=pltpu.HBM)
SMALL = pltpu.CompilerParams(vmem_limit_bytes=16 * 1024 * 1024)

INDEX_MUL = -1640531535
SALT_MUL = 668265263


def int32_wrap(value):
    return (value + 2**31) % 2**32 - 2**31


def hash_sign(hashed):
    hashed = hashed ^ lax.shift_right_logical(hashed, 15)
    hashed = hashed * -2048144789
    hashed = hashed ^ lax.shift_right_logical(hashed, 13)
    hashed = hashed * int32_wrap(-1028477387 << 6)
    hashed = hashed ^ lax.shift_left(hashed, 16)
    return jnp.where(hashed < 0, 1.0, -1.0).astype(F32)


def iota(shape, dim):
    return lax.broadcasted_iota(I32, shape, dim)


def token_row(mask):
    ex_rows, seq = mask.shape
    tokens = ex_rows * seq
    tiled = jnp.concatenate([mask.astype(F32)] * ex_rows, axis=1)
    owner = iota((ex_rows, tokens), 1) // seq == iota((ex_rows, tokens), 0)
    return jnp.sum(jnp.where(owner, tiled, 0.0), axis=0, keepdims=True)


def split_pieces(value):
    pieces = []
    for _ in range(PIECES):
        pieces.append(value.astype(BF16))
        value = value - pieces[-1].astype(F32)
    return jnp.concatenate(pieces, axis=0)


def kind_of(cross):
    core = lax.axis_index("tensor")
    return core ^ (lax.axis_index("z") // (lax.axis_size("z") // 2)) if cross else core


def table_start():
    index = iota(BLOCK, 1) * PROJ_ROWS + iota(BLOCK, 0)
    return index * INDEX_MUL


def sign_rows(start, col):
    high, wide = BLOCK
    rows = [
        hash_sign(start + int32_wrap((col * PROJ_ROWS + row) * INDEX_MUL)).astype(BF16)
        for row in range(0, PROJ_ROWS, high)
    ]
    return rows


def far_kernel(
    cross, ex_rows,
    salts_hbm, mask_hbm, down_hbm, up_hbm, hid_hbm, cot_hbm,
    send_ref, ranks_ref, near_ref, start_ref, kept_ref, mixer_ref,
    salts, mask, far_factor, near_factor, far, sems,
):
    tokens, width = far.shape
    kind = kind_of(cross)
    parts = 4
    share = width // parts
    wide = BLOCK[1]

    def copies(inputs, factor, factor_held, held, first):
        out = [pltpu.make_async_copy(factor, factor_held, sems.at[first])]
        for i in range(parts):
            cols = pl.ds(i * share, share)
            out.append(
                pltpu.make_async_copy(inputs.at[:, cols], held.at[:, cols], sems.at[first + 1 + i])
            )
        return out

    def start_copies(far_inputs, far_part, near_inputs, near_part):
        far_copies = copies(far_inputs, far_part, far_factor, far, 2)
        near_copies = copies(near_inputs, near_part, near_factor, near_ref, parts + 3)
        for pair in zip(far_copies, near_copies):
            for copy in pair:
                copy.start()

    salts_copy = pltpu.make_async_copy(salts_hbm, salts, sems.at[0])
    mask_copy = pltpu.make_async_copy(mask_hbm, mask, sems.at[1])
    salts_copy.start()

    @pl.when(kind == 0)
    def _():
        start_copies(hid_hbm, down_hbm, cot_hbm, up_hbm)

    @pl.when(kind == 1)
    def _():
        start_copies(cot_hbm, up_hbm, hid_hbm, down_hbm)

    mask_copy.start()
    far_waits = copies(hid_hbm, down_hbm, far_factor, far, 2)
    near_waits = copies(hid_hbm, down_hbm, near_factor, near_ref, parts + 3)
    first = lax.axis_index("tensor") * int32_wrap(width * PROJ_ROWS * INDEX_MUL)
    start = table_start() + first
    salts_copy.wait()
    far_start = start + salts[2 - 2 * kind] * SALT_MUL
    far_waits[0].wait()
    near_waits[0].wait()
    total = ranks = None
    for col in range(0, width, wide):
        part = slice(col, col + wide)
        left = jnp.concatenate(sign_rows(far_start, col) + [far_factor[:, part]], axis=0)
        if col % share == 0:
            far_waits[1 + col // share].wait()
            near_waits[1 + col // share].wait()
        term = lax.dot_general(left, far[:, part], NT, preferred_element_type=F32)
        total = term if total is None else total + term
        term = lax.dot_general(
            near_factor[:, part], near_ref[:, part], NT, preferred_element_type=F32
        )
        ranks = term if ranks is None else ranks + term
    start_ref[...] = start + salts[2 * kind] * SALT_MUL
    shape = mixer_ref.shape
    mixed, rank = iota(shape, 0) // ex_rows, iota(shape, 1) % ADAPTER_RANK
    index = (rank * ADAPTER_RANK + mixed) * INDEX_MUL
    mixer_ref[...] = hash_sign(index + salts[1 + 2 * kind] * SALT_MUL).astype(BF16)
    mask_copy.wait()
    counted = token_row(mask[...]) != 0
    far_kept = counted | (kind == 0)
    near_kept = counted | (kind == 1)
    kept_ref[...] = jnp.broadcast_to(jnp.where(near_kept, 1.0, 0.0), kept_ref.shape)
    total = jnp.where(far_kept, total, 0.0)
    send_ref[:PROJ_ROWS] = total[:PROJ_ROWS].astype(BF16)
    ranks_ref[...] = split_pieces(total[PROJ_ROWS:])
    send_ref[PROJ_ROWS:] = split_pieces(jnp.where(near_kept, ranks, 0.0))


def far_rows(salts, mask, down, up, hidden, cotangent, cross):
    ex_rows = mask.shape[0]
    tokens, width = hidden.shape
    pieces = PIECES * ADAPTER_RANK
    arrays = (salts, mask, down, up, hidden, cotangent)
    return pl.pallas_call(
        functools.partial(far_kernel, cross, ex_rows),
        out_shape=[
            jax.ShapeDtypeStruct((PROJ_ROWS + pieces, tokens), BF16),
            jax.ShapeDtypeStruct((pieces, tokens), BF16),
            jax.ShapeDtypeStruct((tokens, width), BF16),
            jax.ShapeDtypeStruct(BLOCK, I32),
            jax.ShapeDtypeStruct((8, tokens), F32),
            jax.ShapeDtypeStruct((ADAPTER_RANK * ex_rows, 2 * pieces), BF16),
        ],
        in_specs=[HBM] * 6,
        out_specs=[VMEM] * 6,
        scratch_shapes=[
            pltpu.SMEM(salts.shape, I32),
            pltpu.VMEM(mask.shape, I32),
            pltpu.VMEM((ADAPTER_RANK, width), BF16),
            pltpu.VMEM((ADAPTER_RANK, width), BF16),
            pltpu.VMEM((tokens, width), BF16),
            pltpu.SemaphoreType.DMA((12,)),
        ],
        compiler_params=SMALL,
    )(*[pltpu.with_memory_space_constraint(x, pltpu.HBM) for x in arrays])


def near_kernel(start_ref, kept_ref, near_ref, out_ref):
    start = start_ref[...]
    wide = BLOCK[1]
    total = None
    for col in range(0, near_ref.shape[1], wide):
        left = jnp.concatenate(sign_rows(start, col), axis=0)
        term = lax.dot_general(
            left, near_ref[:, col : col + wide], NT, preferred_element_type=F32
        )
        total = term if total is None else total + term
    out_ref[...] = jnp.where(kept_ref[:1] != 0, total, 0.0).astype(BF16)


def near_rows(start, kept, near):
    tokens, width = near.shape
    return pl.pallas_call(
        near_kernel,
        out_shape=jax.ShapeDtypeStruct((PROJ_ROWS, tokens), BF16),
        in_specs=[VMEM] * 3,
        out_specs=VMEM,
        compiler_params=SMALL,
        cost_estimate=pl.CostEstimate(
            flops=2 * tokens * width * PROJ_ROWS, bytes_accessed=2 * tokens * width, transcendentals=0
        ),
    )(start, kept, near)


def feature_kernel(ex_rows, mixer_ref, ranks_ref, own_ref, other_ref, out_ref):
    tokens = own_ref.shape[1]
    rows = ADAPTER_RANK * ex_rows
    pieces = jnp.concatenate([ranks_ref[...], other_ref[PROJ_ROWS:]], axis=0)
    coeffs = jnp.dot(mixer_ref[...], pieces, preferred_element_type=F32)
    owned = iota((rows, tokens), 1) // SEQ == iota((rows, tokens), 0) % ex_rows
    coeffs = jnp.where(owned, coeffs, 0.0).astype(BF16)
    projected = lax.dot_general(coeffs, own_ref[...], NT, preferred_element_type=F32)
    projected += lax.dot_general(coeffs, other_ref[:PROJ_ROWS], NT, preferred_element_type=F32)
    out_ref[...] = (projected * SCALE).astype(BF16)


def feature_rows(mixer, ranks, own, other, ex_rows):
    return pl.pallas_call(
        functools.partial(feature_kernel, ex_rows),
        out_shape=jax.ShapeDtypeStruct((ADAPTER_RANK * ex_rows, PROJ_ROWS), BF16),
        in_specs=[VMEM] * 4,
        out_specs=VMEM,
        compiler_params=SMALL,
    )(mixer, ranks, own, other)


def fold_ranks(terms):
    half = terms.shape[0] // 2
    folded = terms[:half] + pltpu.roll(terms[half:], LANES - half, 1)
    return jnp.where(iota(folded.shape, 1) % (2 * half) < half, folded, 0.0)


def order_blocks(rows, wide):
    z = lax.axis_index("z")
    rows = jnp.where((z & 1) != 0, pltpu.roll(rows, wide, 1), rows)
    return jnp.where((z & 2) != 0, pltpu.roll(rows, 2 * wide, 1), rows)


def pair_kernel(ex_rows, own_ref, next_ref, near_ref, second_ref, last_ref, keep_ref, send_ref):
    wide = 2 * ex_rows
    z_refs = (own_ref, next_ref, second_ref, last_ref)
    total = None
    for row in range(0, own_ref.shape[0], wide):
        part = slice(row, row + wide)
        left = jnp.concatenate([own_ref[part, :], near_ref[part, :]], axis=0)
        right = jnp.concatenate([ref[part, :] for ref in z_refs] * 2, axis=0)
        term = lax.dot_general(left, right, NT, preferred_element_type=F32)
        total = term if total is None else total + term
    keep_ref[...] = order_blocks(fold_ranks(total[:wide]), wide)
    send_ref[...] = order_blocks(fold_ranks(total[wide:]), wide)


def pair_rows(own, after, near, second, last, ex_rows):
    return pl.pallas_call(
        functools.partial(pair_kernel, ex_rows),
        out_shape=[jax.ShapeDtypeStruct((ex_rows, LANES), F32)] * 2,
        in_specs=[VMEM] * 5,
        out_specs=[VMEM] * 2,
        compiler_params=SMALL,
    )(own, after, near, second, last)


def halves_kernel(own_ref, got_ref, keep_ref, send_ref):
    ex_rows, _ = own_ref.shape
    low_x = lax.axis_index("x") == 0
    first = jnp.where(low_x, own_ref[...], got_ref[...])
    second = jnp.where(low_x, got_ref[...], own_ref[...])
    total = first + pltpu.roll(second, ex_rows, 1)
    half = keep_ref.shape[0]
    low = lax.axis_index("tensor") == 0
    keep_ref[...] = jnp.where(low, total[:half], total[half:])
    send_ref[...] = jnp.where(low, total[half:], total[:half])


def join_halves(own, got):
    rows, lanes = own.shape
    return pl.pallas_call(
        halves_kernel,
        out_shape=[jax.ShapeDtypeStruct((rows // 2, lanes), F32)] * 2,
        in_specs=[VMEM] * 2,
        out_specs=[VMEM] * 2,
        compiler_params=SMALL,
    )(own, got)


def sum_kernel(keep_ref, got_ref, out_ref):
    out_ref[...] = (keep_ref[...] + got_ref[...])[:, : out_ref.shape[1]]


def sum_rows(keep, got):
    return pl.pallas_call(
        sum_kernel,
        out_shape=jax.ShapeDtypeStruct((keep.shape[0], LANES // 2), F32),
        in_specs=[VMEM] * 2,
        out_specs=VMEM,
        compiler_params=SMALL,
    )(keep, got)


def swap_cores(value):
    return lax.ppermute(value, "tensor", [(0, 1), (1, 0)])


def swap_across(value):
    return lax.ppermute(value, ("x", "tensor"), [(i, i ^ 3) for i in range(4)])


def swap_x(value):
    return lax.ppermute(value, "x", [(0, 1), (1, 0)])


def turn_z(value, step):
    pairs = []
    for z in range(4):
        to = (z + step) % 4
        for x in range(2):
            for kind in range(2):
                ends = [4 * at + 2 * x + (kind ^ (at // 2)) for at in (z, to)]
                pairs.append(tuple(ends))
    return lax.ppermute(value, BLK + ("tensor",), pairs)


def body(
    hidden, cotangent, token_loss_mask, adapter_down_factor, adapter_up_factor, sign_table_salts
):
    ex_rows, seq, width_half = hidden.shape
    blocks = lax.axis_size("z") * lax.axis_size("x")
    fast = blocks == 8 and ex_rows == 8
    send, ranks, near, start, kept, mixer = far_rows(
        sign_table_salts,
        token_loss_mask,
        adapter_down_factor,
        adapter_up_factor.T,
        hidden.reshape(ex_rows * seq, width_half),
        cotangent.reshape(ex_rows * seq, width_half),
        fast,
    )
    other = swap_cores(send)
    terms = (mixer, ranks, near_rows(start, kept, near), other)
    features = feature_rows(*terms, ex_rows)
    if fast:
        last = turn_z(features, 1)
        second = turn_z(features, 2)
        near = swap_x(features)
        after = turn_z(features, 3)
        keep, send = pair_rows(features, after, near, second, last, ex_rows)
        keep, send = join_halves(keep, swap_across(send))
        return sum_rows(keep, swap_cores(send))
    share = ADAPTER_RANK * PROJ_ROWS // blocks
    parts = features.reshape(ADAPTER_RANK, ex_rows, PROJ_ROWS // share, share)
    parts = parts.swapaxes(1, 2).reshape(blocks, ex_rows, share)
    features = lax.all_to_all(parts, BLK, 0, 0, tiled=True).reshape(blocks * ex_rows, share)
    pairs = jnp.einsum("ep,fp->ef", features, features, preferred_element_type=F32)
    pairs = pairs.reshape(blocks, ex_rows, blocks * ex_rows)
    total = jnp.sum(lax.all_to_all(pairs, BLK, 0, 0, tiled=True), axis=0)
    halves = total.reshape(2, ex_rows // 2, blocks * ex_rows)
    core = lax.axis_index("tensor")
    send = lax.dynamic_index_in_dim(halves, 1 - core, 0, keepdims=False)
    return lax.dynamic_index_in_dim(halves, core, 0, keepdims=False) + swap_cores(send)


def solution(mesh):
    groups, blocks, cores = (mesh.shape[name] for name in ("groups", "blk", "tensor"))
    devices = mesh.devices.reshape(groups, blocks // 2, 2, cores)
    placed = (
        P(("groups", "z", "x"), None, "tensor"),
        P(("groups", "z", "x"), None, "tensor"),
        P(("groups", "z", "x"), None),
        P(None, "tensor"),
        P("tensor", None),
        P(),
    )
    return jax.shard_map(
        body,
        mesh=Mesh(devices, ("groups", "z", "x", "tensor")),
        in_specs=placed,
        out_specs=P(("groups", "z", "x", "tensor"), None),
        check_vma=False,
    )
```

```python
import functools
import math

import jax
import jax.numpy as jnp
from jax import lax
from jax.experimental import pallas as pl
from jax.experimental.pallas import tpu as pltpu
from jax.sharding import Mesh, PartitionSpec as P

MODEL_WIDTH = 4096
ADAPTER_RANK = 16
PROJ_ROWS = 256
SEQ = 64
SCALE = 1.0 / math.sqrt(PROJ_ROWS * ADAPTER_RANK * ADAPTER_RANK * SEQ * MODEL_WIDTH)
PIECES = 3
LANES = 128
BLOCK = (16, 256)
BLK = ("z", "x")

F32 = jnp.float32
BF16 = jnp.bfloat16
I32 = jnp.int32
NT = (((1,), (1,)), ((), ()))
VMEM = pl.BlockSpec(memory_space=pltpu.VMEM)
SMEM = pl.BlockSpec(memory_space=pltpu.SMEM)
HBM = pl.BlockSpec(memory_space=pltpu.HBM)
SMALL = pltpu.CompilerParams(vmem_limit_bytes=16 * 1024 * 1024)

INDEX_MUL = -1640531535
SALT_MUL = 668265263


def int32_wrap(value):
    return (value + 2**31) % 2**32 - 2**31


def hash_sign(hashed):
    hashed = hashed ^ lax.shift_right_logical(hashed, 15)
    hashed = hashed * -2048144789
    hashed = hashed ^ lax.shift_right_logical(hashed, 13)
    hashed = hashed * int32_wrap(-1028477387 << 6)
    hashed = hashed ^ lax.shift_left(hashed, 16)
    return jnp.where(hashed < 0, 1.0, -1.0).astype(F32)


def iota(shape, dim):
    return lax.broadcasted_iota(I32, shape, dim)


def token_row(mask):
    ex_rows, seq = mask.shape
    tokens = ex_rows * seq
    tiled = jnp.concatenate([mask.astype(F32)] * ex_rows, axis=1)
    owner = iota((ex_rows, tokens), 1) // seq == iota((ex_rows, tokens), 0)
    return jnp.sum(jnp.where(owner, tiled, 0.0), axis=0, keepdims=True)


def split_pieces(value):
    pieces = []
    for _ in range(PIECES):
        pieces.append(value.astype(BF16))
        value = value - pieces[-1].astype(F32)
    return jnp.concatenate(pieces, axis=0)


def kind_of(cross):
    core = lax.axis_index("tensor")
    return core ^ (lax.axis_index("z") // (lax.axis_size("z") // 2)) if cross else core


def table_start():
    index = iota(BLOCK, 1) * PROJ_ROWS + iota(BLOCK, 0)
    return index * INDEX_MUL


def sign_rows(start, col):
    high, wide = BLOCK
    rows = [
        hash_sign(start + int32_wrap((col * PROJ_ROWS + row) * INDEX_MUL)).astype(BF16)
        for row in range(0, PROJ_ROWS, high)
    ]
    return rows


def far_kernel(
    cross, ex_rows,
    salts_hbm, mask_hbm, down_hbm, up_hbm, hid_hbm, cot_hbm,
    send_ref, ranks_ref, near_ref, start_ref, kept_ref, mixer_ref,
    salts, mask, far_factor, near_factor, far, sems,
):
    tokens, width = far.shape
    kind = kind_of(cross)
    parts = 4
    share = width // parts
    wide = BLOCK[1]

    def copies(inputs, factor, factor_held, held, first):
        out = [pltpu.make_async_copy(factor, factor_held, sems.at[first])]
        for i in range(parts):
            cols = pl.ds(i * share, share)
            out.append(
                pltpu.make_async_copy(inputs.at[:, cols], held.at[:, cols], sems.at[first + 1 + i])
            )
        return out

    def start_copies(far_inputs, far_part, near_inputs, near_part):
        far_copies = copies(far_inputs, far_part, far_factor, far, 2)
        near_copies = copies(near_inputs, near_part, near_factor, near_ref, parts + 3)
        for pair in zip(far_copies, near_copies):
            for copy in pair:
                copy.start()

    salts_copy = pltpu.make_async_copy(salts_hbm, salts, sems.at[0])
    mask_copy = pltpu.make_async_copy(mask_hbm, mask, sems.at[1])
    salts_copy.start()

    @pl.when(kind == 0)
    def _():
        start_copies(hid_hbm, down_hbm, cot_hbm, up_hbm)

    @pl.when(kind == 1)
    def _():
        start_copies(cot_hbm, up_hbm, hid_hbm, down_hbm)

    mask_copy.start()
    far_waits = copies(hid_hbm, down_hbm, far_factor, far, 2)
    near_waits = copies(hid_hbm, down_hbm, near_factor, near_ref, parts + 3)
    first = lax.axis_index("tensor") * int32_wrap(width * PROJ_ROWS * INDEX_MUL)
    start = table_start() + first
    salts_copy.wait()
    far_start = start + salts[2 - 2 * kind] * SALT_MUL
    far_waits[0].wait()
    near_waits[0].wait()
    total = ranks = None
    for col in range(0, width, wide):
        part = slice(col, col + wide)
        left = jnp.concatenate(sign_rows(far_start, col) + [far_factor[:, part]], axis=0)
        if col % share == 0:
            far_waits[1 + col // share].wait()
            near_waits[1 + col // share].wait()
        term = lax.dot_general(left, far[:, part], NT, preferred_element_type=F32)
        total = term if total is None else total + term
        term = lax.dot_general(
            near_factor[:, part], near_ref[:, part], NT, preferred_element_type=F32
        )
        ranks = term if ranks is None else ranks + term
    start_ref[...] = start + salts[2 * kind] * SALT_MUL
    shape = mixer_ref.shape
    mixed, rank = iota(shape, 0) // ex_rows, iota(shape, 1) % ADAPTER_RANK
    index = (rank * ADAPTER_RANK + mixed) * INDEX_MUL
    mixer_ref[...] = hash_sign(index + salts[1 + 2 * kind] * SALT_MUL).astype(BF16)
    mask_copy.wait()
    counted = token_row(mask[...]) != 0
    far_kept = counted | (kind == 0)
    near_kept = counted | (kind == 1)
    kept_ref[...] = jnp.broadcast_to(jnp.where(near_kept, 1.0, 0.0), kept_ref.shape)
    total = jnp.where(far_kept, total, 0.0)
    send_ref[:PROJ_ROWS] = total[:PROJ_ROWS].astype(BF16)
    ranks_ref[...] = split_pieces(total[PROJ_ROWS:])
    send_ref[PROJ_ROWS:] = split_pieces(jnp.where(near_kept, ranks, 0.0))


def far_rows(salts, mask, down, up, hidden, cotangent, cross):
    ex_rows = mask.shape[0]
    tokens, width = hidden.shape
    pieces = PIECES * ADAPTER_RANK
    arrays = (salts, mask, down, up, hidden, cotangent)
    return pl.pallas_call(
        functools.partial(far_kernel, cross, ex_rows),
        out_shape=[
            jax.ShapeDtypeStruct((PROJ_ROWS + pieces, tokens), BF16),
            jax.ShapeDtypeStruct((pieces, tokens), BF16),
            jax.ShapeDtypeStruct((tokens, width), BF16),
            jax.ShapeDtypeStruct(BLOCK, I32),
            jax.ShapeDtypeStruct((8, tokens), F32),
            jax.ShapeDtypeStruct((ADAPTER_RANK * ex_rows, 2 * pieces), BF16),
        ],
        in_specs=[HBM] * 6,
        out_specs=[VMEM] * 6,
        scratch_shapes=[
            pltpu.SMEM(salts.shape, I32),
            pltpu.VMEM(mask.shape, I32),
            pltpu.VMEM((ADAPTER_RANK, width), BF16),
            pltpu.VMEM((ADAPTER_RANK, width), BF16),
            pltpu.VMEM((tokens, width), BF16),
            pltpu.SemaphoreType.DMA((12,)),
        ],
        compiler_params=SMALL,
    )(*[pltpu.with_memory_space_constraint(x, pltpu.HBM) for x in arrays])


def near_kernel(start_ref, kept_ref, near_ref, out_ref):
    start = start_ref[...]
    wide = BLOCK[1]
    total = None
    for col in range(0, near_ref.shape[1], wide):
        left = jnp.concatenate(sign_rows(start, col), axis=0)
        term = lax.dot_general(
            left, near_ref[:, col : col + wide], NT, preferred_element_type=F32
        )
        total = term if total is None else total + term
    out_ref[...] = jnp.where(kept_ref[:1] != 0, total, 0.0).astype(BF16)


def near_rows(start, kept, near):
    tokens, width = near.shape
    return pl.pallas_call(
        near_kernel,
        out_shape=jax.ShapeDtypeStruct((PROJ_ROWS, tokens), BF16),
        in_specs=[VMEM] * 3,
        out_specs=VMEM,
        compiler_params=SMALL,
        cost_estimate=pl.CostEstimate(
            flops=2 * tokens * width * PROJ_ROWS, bytes_accessed=2 * tokens * width, transcendentals=0
        ),
    )(start, kept, near)


def feature_kernel(ex_rows, mixer_ref, ranks_ref, own_ref, other_ref, out_ref):
    tokens = own_ref.shape[1]
    rows = ADAPTER_RANK * ex_rows
    pieces = jnp.concatenate([ranks_ref[...], other_ref[PROJ_ROWS:]], axis=0)
    coeffs = jnp.dot(mixer_ref[...], pieces, preferred_element_type=F32)
    owned = iota((rows, tokens), 1) // SEQ == iota((rows, tokens), 0) % ex_rows
    coeffs = jnp.where(owned, coeffs, 0.0).astype(BF16)
    projected = lax.dot_general(coeffs, own_ref[...], NT, preferred_element_type=F32)
    projected += lax.dot_general(coeffs, other_ref[:PROJ_ROWS], NT, preferred_element_type=F32)
    out_ref[...] = (projected * SCALE).astype(BF16)


def feature_rows(mixer, ranks, own, other, ex_rows):
    return pl.pallas_call(
        functools.partial(feature_kernel, ex_rows),
        out_shape=jax.ShapeDtypeStruct((ADAPTER_RANK * ex_rows, PROJ_ROWS), BF16),
        in_specs=[VMEM] * 4,
        out_specs=VMEM,
        compiler_params=SMALL,
    )(mixer, ranks, own, other)


def fold_ranks(terms):
    half = terms.shape[0] // 2
    folded = terms[:half] + pltpu.roll(terms[half:], LANES - half, 1)
    return jnp.where(iota(folded.shape, 1) % (2 * half) < half, folded, 0.0)


def order_blocks(rows, wide):
    z = lax.axis_index("z")
    rows = jnp.where((z & 2) != 0, pltpu.roll(rows, 2 * wide, 1), rows)
    even = (iota(rows.shape, 1) // wide) % 2 == 0
    swapped = jnp.where(even, pltpu.roll(rows, LANES - wide, 1), pltpu.roll(rows, wide, 1))
    return jnp.where((z & 1) != 0, swapped, rows)


def back_lanes(rows, ex_rows):
    z = lax.axis_index("z")
    lane = iota(rows.shape, 1)
    both = rows + pltpu.roll(rows, LANES - ex_rows, 1)
    both = jnp.where(lane % (4 * ex_rows) < 2 * ex_rows, both, 0.0)
    both = jnp.where((z & 1) != 0, pltpu.roll(both, 2 * ex_rows, 1), both)
    return jnp.where(lane // (2 * ex_rows) == z, both, 0.0)


def pair_kernel(ex_rows, own_ref, near_ref, far_ref, first_ref, keep_ref, send_ref, back_ref):
    wide = 2 * ex_rows
    low_x = lax.axis_index("x") == 0
    total = back = None
    for row in range(0, own_ref.shape[0], wide):
        part = slice(row, row + wide)
        own, near, far, first = (
            ref[part, :] for ref in (own_ref, near_ref, far_ref, first_ref)
        )
        left = jnp.concatenate([own, near], axis=0)
        right = jnp.concatenate([own, first, far, far] * 2, axis=0)
        term = lax.dot_general(left, right, NT, preferred_element_type=F32)
        total = term if total is None else total + term
        by_x = [jnp.where(low_x, own, near), jnp.where(low_x, near, own)]
        right = jnp.concatenate(by_x * 4, axis=0)
        term = lax.dot_general(far, right, NT, preferred_element_type=F32)
        back = term if back is None else back + term
    far_block = jnp.where(lax.axis_index("z") < 2, 2, 3)
    block = iota((ex_rows, LANES), 1) // wide % 4
    here = (block < 2) | (block == far_block)
    for out_ref, rows in ((keep_ref, total[:wide]), (send_ref, total[wide:])):
        out_ref[...] = order_blocks(jnp.where(here, fold_ranks(rows), 0.0), wide)
    back_ref[...] = back_lanes(fold_ranks(back), ex_rows)


def pair_rows(own, near, far, first, ex_rows):
    return pl.pallas_call(
        functools.partial(pair_kernel, ex_rows),
        out_shape=[jax.ShapeDtypeStruct((ex_rows, LANES), F32)] * 3,
        in_specs=[VMEM] * 4,
        out_specs=[VMEM] * 3,
        compiler_params=SMALL,
    )(own, near, far, first)


def halves_kernel(own_ref, got_ref, back_ref, keep_ref, send_ref):
    ex_rows, _ = own_ref.shape
    low_x = lax.axis_index("x") == 0
    first = jnp.where(low_x, own_ref[...], got_ref[...])
    second = jnp.where(low_x, got_ref[...], own_ref[...])
    total = first + pltpu.roll(second, ex_rows, 1) + back_ref[...]
    half = keep_ref.shape[0]
    low = lax.axis_index("tensor") == 0
    keep_ref[...] = jnp.where(low, total[:half], total[half:])
    send_ref[...] = jnp.where(low, total[half:], total[:half])


def join_halves(own, got, back):
    rows, lanes = own.shape
    return pl.pallas_call(
        halves_kernel,
        out_shape=[jax.ShapeDtypeStruct((rows // 2, lanes), F32)] * 2,
        in_specs=[VMEM] * 3,
        out_specs=[VMEM] * 2,
        compiler_params=SMALL,
    )(own, got, back)


def sum_kernel(keep_ref, got_ref, out_ref):
    out_ref[...] = (keep_ref[...] + got_ref[...])[:, : out_ref.shape[1]]


def sum_rows(keep, got):
    return pl.pallas_call(
        sum_kernel,
        out_shape=jax.ShapeDtypeStruct((keep.shape[0], LANES // 2), F32),
        in_specs=[VMEM] * 2,
        out_specs=VMEM,
        compiler_params=SMALL,
    )(keep, got)


def swap_cores(value):
    return lax.ppermute(value, "tensor", [(0, 1), (1, 0)])


def swap_across(value):
    return lax.ppermute(value, ("x", "tensor"), [(i, i ^ 3) for i in range(4)])


def swap_x(value):
    return lax.ppermute(value, "x", [(0, 1), (1, 0)])


def send_z(value, targets):
    pairs = []
    for z, target in enumerate(targets):
        for x in range(2):
            for kind in range(2):
                pairs.append(tuple(4 * at + 2 * x + (kind ^ (at // 2)) for at in (z, target)))
    return lax.ppermute(value, BLK + ("tensor",), pairs)


def body(
    hidden, cotangent, token_loss_mask, adapter_down_factor, adapter_up_factor, sign_table_salts
):
    ex_rows, seq, width_half = hidden.shape
    blocks = lax.axis_size("z") * lax.axis_size("x")
    fast = blocks == 8 and ex_rows == 8
    send, ranks, near, start, kept, mixer = far_rows(
        sign_table_salts,
        token_loss_mask,
        adapter_down_factor,
        adapter_up_factor.T,
        hidden.reshape(ex_rows * seq, width_half),
        cotangent.reshape(ex_rows * seq, width_half),
        fast,
    )
    other = swap_cores(send)
    terms = (mixer, ranks, near_rows(start, kept, near), other)
    features = feature_rows(*terms, ex_rows)
    if fast:
        first = send_z(features, (1, 0, 3, 2))
        far = send_z(features, (3, 2, 0, 1))
        near = swap_x(features)
        keep, send, back = pair_rows(features, near, far, first, ex_rows)
        back = send_z(back, (2, 3, 1, 0))
        keep, send = join_halves(keep, swap_across(send), back)
        return sum_rows(keep, swap_cores(send))
    share = ADAPTER_RANK * PROJ_ROWS // blocks
    parts = features.reshape(ADAPTER_RANK, ex_rows, PROJ_ROWS // share, share)
    parts = parts.swapaxes(1, 2).reshape(blocks, ex_rows, share)
    features = lax.all_to_all(parts, BLK, 0, 0, tiled=True).reshape(blocks * ex_rows, share)
    pairs = jnp.einsum("ep,fp->ef", features, features, preferred_element_type=F32)
    pairs = pairs.reshape(blocks, ex_rows, blocks * ex_rows)
    total = jnp.sum(lax.all_to_all(pairs, BLK, 0, 0, tiled=True), axis=0)
    halves = total.reshape(2, ex_rows // 2, blocks * ex_rows)
    core = lax.axis_index("tensor")
    send = lax.dynamic_index_in_dim(halves, 1 - core, 0, keepdims=False)
    return lax.dynamic_index_in_dim(halves, core, 0, keepdims=False) + swap_cores(send)


def solution(mesh):
    groups, blocks, cores = (mesh.shape[name] for name in ("groups", "blk", "tensor"))
    devices = mesh.devices.reshape(groups, blocks // 2, 2, cores)
    placed = (
        P(("groups", "z", "x"), None, "tensor"),
        P(("groups", "z", "x"), None, "tensor"),
        P(("groups", "z", "x"), None),
        P(None, "tensor"),
        P("tensor", None),
        P(),
    )
    return jax.shard_map(
        body,
        mesh=Mesh(devices, ("groups", "z", "x", "tensor")),
        in_specs=placed,
        out_specs=P(("groups", "z", "x", "tensor"), None),
        check_vma=False,
    )
```

```python
import functools
import math

import jax
import jax.numpy as jnp
from jax import lax
from jax.experimental import pallas as pl
from jax.experimental.pallas import tpu as pltpu
from jax.sharding import Mesh, PartitionSpec as P

MODEL_WIDTH = 4096
ADAPTER_RANK = 16
PROJ_ROWS = 256
SEQ = 64
SCALE = 1.0 / math.sqrt(PROJ_ROWS * ADAPTER_RANK * ADAPTER_RANK * SEQ * MODEL_WIDTH)
PIECES = 3
LANES = 128
BLOCK = (16, 256)
BLK = ("z", "x")

F32 = jnp.float32
BF16 = jnp.bfloat16
I32 = jnp.int32
NT = (((1,), (1,)), ((), ()))
VMEM = pl.BlockSpec(memory_space=pltpu.VMEM)
SMEM = pl.BlockSpec(memory_space=pltpu.SMEM)
HBM = pl.BlockSpec(memory_space=pltpu.HBM)
SMALL = pltpu.CompilerParams(vmem_limit_bytes=16 * 1024 * 1024)

INDEX_MUL = -1640531535
SALT_MUL = 668265263


def int32_wrap(value):
    return (value + 2**31) % 2**32 - 2**31


def hash_sign(hashed):
    hashed = hashed ^ lax.shift_right_logical(hashed, 15)
    hashed = hashed * -2048144789
    hashed = hashed ^ lax.shift_right_logical(hashed, 13)
    hashed = hashed * int32_wrap(-1028477387 << 6)
    hashed = hashed ^ lax.shift_left(hashed, 16)
    return jnp.where(hashed < 0, 1.0, -1.0).astype(F32)


def iota(shape, dim):
    return lax.broadcasted_iota(I32, shape, dim)


def token_row(mask):
    ex_rows, seq = mask.shape
    tokens = ex_rows * seq
    tiled = jnp.concatenate([mask.astype(F32)] * ex_rows, axis=1)
    owner = iota((ex_rows, tokens), 1) // seq == iota((ex_rows, tokens), 0)
    return jnp.sum(jnp.where(owner, tiled, 0.0), axis=0, keepdims=True)


def split_pieces(value):
    pieces = []
    for _ in range(PIECES):
        pieces.append(value.astype(BF16))
        value = value - pieces[-1].astype(F32)
    return jnp.concatenate(pieces, axis=0)


def kind_of(cross):
    core = lax.axis_index("tensor")
    return core ^ (lax.axis_index("z") // (lax.axis_size("z") // 2)) if cross else core


def table_start():
    index = iota(BLOCK, 1) * PROJ_ROWS + iota(BLOCK, 0)
    return index * INDEX_MUL


def sign_rows(start, col):
    high, wide = BLOCK
    rows = [
        hash_sign(start + int32_wrap((col * PROJ_ROWS + row) * INDEX_MUL)).astype(BF16)
        for row in range(0, PROJ_ROWS, high)
    ]
    return rows


def far_kernel(
    cross, ex_rows,
    salts_hbm, mask_hbm, down_hbm, up_hbm, hid_hbm, cot_hbm,
    send_ref, ranks_ref, near_ref, start_ref, kept_ref, mixer_ref,
    salts, mask, far_factor, near_factor, far, sems,
):
    tokens, width = far.shape
    kind = kind_of(cross)
    parts = 8
    share = width // parts
    wide = BLOCK[1]

    def copies(inputs, factor, factor_held, held, first):
        out = [pltpu.make_async_copy(factor, factor_held, sems.at[first])]
        for i in range(parts):
            cols = pl.ds(i * share, share)
            out.append(
                pltpu.make_async_copy(inputs.at[:, cols], held.at[:, cols], sems.at[first + 1 + i])
            )
        return out

    def start_copies(far_inputs, far_part, near_inputs, near_part):
        far_copies = copies(far_inputs, far_part, far_factor, far, 2)
        near_copies = copies(near_inputs, near_part, near_factor, near_ref, parts + 3)
        for pair in zip(far_copies, near_copies):
            for copy in pair:
                copy.start()

    salts_copy = pltpu.make_async_copy(salts_hbm, salts, sems.at[0])
    mask_copy = pltpu.make_async_copy(mask_hbm, mask, sems.at[1])
    salts_copy.start()

    @pl.when(kind == 0)
    def _():
        start_copies(hid_hbm, down_hbm, cot_hbm, up_hbm)

    @pl.when(kind == 1)
    def _():
        start_copies(cot_hbm, up_hbm, hid_hbm, down_hbm)

    mask_copy.start()
    far_waits = copies(hid_hbm, down_hbm, far_factor, far, 2)
    near_waits = copies(hid_hbm, down_hbm, near_factor, near_ref, parts + 3)
    first = lax.axis_index("tensor") * int32_wrap(width * PROJ_ROWS * INDEX_MUL)
    start = table_start() + first
    salts_copy.wait()
    far_start = start + salts[2 - 2 * kind] * SALT_MUL
    far_waits[0].wait()
    near_waits[0].wait()
    total = ranks = None
    for col in range(0, width, wide):
        part = slice(col, col + wide)
        left = jnp.concatenate(sign_rows(far_start, col) + [far_factor[:, part]], axis=0)
        if col % share == 0:
            far_waits[1 + col // share].wait()
            near_waits[1 + col // share].wait()
        term = lax.dot_general(left, far[:, part], NT, preferred_element_type=F32)
        total = term if total is None else total + term
        term = lax.dot_general(
            near_factor[:, part], near_ref[:, part], NT, preferred_element_type=F32
        )
        ranks = term if ranks is None else ranks + term
    start_ref[...] = start + salts[2 * kind] * SALT_MUL
    shape = mixer_ref.shape
    mixed, rank = iota(shape, 0) // ex_rows, iota(shape, 1) % ADAPTER_RANK
    index = (rank * ADAPTER_RANK + mixed) * INDEX_MUL
    mixer_ref[...] = hash_sign(index + salts[1 + 2 * kind] * SALT_MUL).astype(BF16)
    mask_copy.wait()
    counted = token_row(mask[...]) != 0
    far_kept = counted | (kind == 0)
    near_kept = counted | (kind == 1)
    kept_ref[...] = jnp.broadcast_to(jnp.where(near_kept, 1.0, 0.0), kept_ref.shape)
    total = jnp.where(far_kept, total, 0.0)
    send_ref[:PROJ_ROWS] = total[:PROJ_ROWS].astype(BF16)
    ranks_ref[...] = split_pieces(total[PROJ_ROWS:])
    send_ref[PROJ_ROWS:] = split_pieces(jnp.where(near_kept, ranks, 0.0))


def far_rows(salts, mask, down, up, hidden, cotangent, cross):
    ex_rows = mask.shape[0]
    tokens, width = hidden.shape
    pieces = PIECES * ADAPTER_RANK
    arrays = (salts, mask, down, up, hidden, cotangent)
    return pl.pallas_call(
        functools.partial(far_kernel, cross, ex_rows),
        out_shape=[
            jax.ShapeDtypeStruct((PROJ_ROWS + pieces, tokens), BF16),
            jax.ShapeDtypeStruct((pieces, tokens), BF16),
            jax.ShapeDtypeStruct((tokens, width), BF16),
            jax.ShapeDtypeStruct(BLOCK, I32),
            jax.ShapeDtypeStruct((8, tokens), F32),
            jax.ShapeDtypeStruct((ADAPTER_RANK * ex_rows, 2 * pieces), BF16),
        ],
        in_specs=[HBM] * 6,
        out_specs=[VMEM] * 6,
        scratch_shapes=[
            pltpu.SMEM(salts.shape, I32),
            pltpu.VMEM(mask.shape, I32),
            pltpu.VMEM((ADAPTER_RANK, width), BF16),
            pltpu.VMEM((ADAPTER_RANK, width), BF16),
            pltpu.VMEM((tokens, width), BF16),
            pltpu.SemaphoreType.DMA((20,)),
        ],
        compiler_params=SMALL,
    )(*[pltpu.with_memory_space_constraint(x, pltpu.HBM) for x in arrays])


def near_kernel(start_ref, kept_ref, near_ref, out_ref):
    start = start_ref[...]
    wide = BLOCK[1]
    total = None
    for col in range(0, near_ref.shape[1], wide):
        left = jnp.concatenate(sign_rows(start, col), axis=0)
        term = lax.dot_general(
            left, near_ref[:, col : col + wide], NT, preferred_element_type=F32
        )
        total = term if total is None else total + term
    out_ref[...] = jnp.where(kept_ref[:1] != 0, total, 0.0).astype(BF16)


def near_rows(start, kept, near):
    tokens, width = near.shape
    return pl.pallas_call(
        near_kernel,
        out_shape=jax.ShapeDtypeStruct((PROJ_ROWS, tokens), BF16),
        in_specs=[VMEM] * 3,
        out_specs=VMEM,
        compiler_params=SMALL,
        cost_estimate=pl.CostEstimate(
            flops=2 * tokens * width * PROJ_ROWS, bytes_accessed=2 * tokens * width, transcendentals=0
        ),
    )(start, kept, near)


def feature_kernel(ex_rows, mixer_ref, ranks_ref, own_ref, other_ref, out_ref):
    tokens = own_ref.shape[1]
    rows = ADAPTER_RANK * ex_rows
    pieces = jnp.concatenate([ranks_ref[...], other_ref[PROJ_ROWS:]], axis=0)
    coeffs = jnp.dot(mixer_ref[...], pieces, preferred_element_type=F32)
    owned = iota((rows, tokens), 1) // SEQ == iota((rows, tokens), 0) % ex_rows
    coeffs = jnp.where(owned, coeffs, 0.0).astype(BF16)
    projected = lax.dot_general(coeffs, own_ref[...], NT, preferred_element_type=F32)
    projected += lax.dot_general(coeffs, other_ref[:PROJ_ROWS], NT, preferred_element_type=F32)
    out_ref[...] = (projected * SCALE).astype(BF16)


def feature_rows(mixer, ranks, own, other, ex_rows):
    return pl.pallas_call(
        functools.partial(feature_kernel, ex_rows),
        out_shape=jax.ShapeDtypeStruct((ADAPTER_RANK * ex_rows, PROJ_ROWS), BF16),
        in_specs=[VMEM] * 4,
        out_specs=VMEM,
        compiler_params=SMALL,
    )(mixer, ranks, own, other)


def fold_ranks(terms):
    half = terms.shape[0] // 2
    folded = terms[:half] + pltpu.roll(terms[half:], LANES - half, 1)
    return jnp.where(iota(folded.shape, 1) % (2 * half) < half, folded, 0.0)


def order_blocks(rows, wide):
    z = lax.axis_index("z")
    rows = jnp.where((z & 2) != 0, pltpu.roll(rows, 2 * wide, 1), rows)
    even = (iota(rows.shape, 1) // wide) % 2 == 0
    swapped = jnp.where(even, pltpu.roll(rows, LANES - wide, 1), pltpu.roll(rows, wide, 1))
    return jnp.where((z & 1) != 0, swapped, rows)


def pair_kernel(ex_rows, near_ref, *refs):
    z_refs, out_refs = refs[:4], refs[4:]
    wide = 2 * ex_rows
    total = None
    for row in range(0, near_ref.shape[0], wide):
        part = slice(row, row + wide)
        left = jnp.concatenate([z_refs[0][part, :], near_ref[part, :]], axis=0)
        right = jnp.concatenate([ref[part, :] for ref in z_refs] * 2, axis=0)
        term = lax.dot_general(left, right, NT, preferred_element_type=F32)
        total = term if total is None else total + term
    half = ex_rows // 2
    low = lax.axis_index("tensor") == 0
    for rows, (same_ref, other_ref) in (
        (total[:wide], out_refs[:2]),
        (total[wide:], out_refs[2:]),
    ):
        rows = order_blocks(fold_ranks(rows), wide)
        same_ref[...] = jnp.where(low, rows[:half], rows[half:])
        other_ref[...] = jnp.where(low, rows[half:], rows[:half])


def pair_rows(near, by_z, ex_rows):
    return pl.pallas_call(
        functools.partial(pair_kernel, ex_rows),
        out_shape=[jax.ShapeDtypeStruct((ex_rows // 2, LANES), F32)] * 4,
        in_specs=[VMEM] * (1 + len(by_z)),
        out_specs=[VMEM] * 4,
        compiler_params=SMALL,
    )(near, *by_z)


def sum_kernel(ex_rows, core_ref, x_ref, both_ref, keep_ref, out_ref):
    here = keep_ref[...] + core_ref[...]
    there = x_ref[...] + both_ref[...]
    low_x = lax.axis_index("x") == 0
    first = jnp.where(low_x, here, there)
    second = jnp.where(low_x, there, here)
    out_ref[...] = (first + pltpu.roll(second, ex_rows, 1))[:, : out_ref.shape[1]]


def sum_rows(core, x, both, keep, ex_rows):
    return pl.pallas_call(
        functools.partial(sum_kernel, ex_rows),
        out_shape=jax.ShapeDtypeStruct((keep.shape[0], LANES // 2), F32),
        in_specs=[VMEM] * 4,
        out_specs=VMEM,
        compiler_params=SMALL,
    )(core, x, both, keep)


def swap_cores(value):
    return lax.ppermute(value, "tensor", [(0, 1), (1, 0)])


def swap_across(value):
    return lax.ppermute(value, ("x", "tensor"), [(i, i ^ 3) for i in range(4)])


def swap_x(value):
    return lax.ppermute(value, "x", [(0, 1), (1, 0)])


def swap_z(value, step):
    other = 4 * step + (step > 1)
    return lax.ppermute(value, BLK + ("tensor",), [(i, i ^ other) for i in range(16)])


def body(
    hidden, cotangent, token_loss_mask, adapter_down_factor, adapter_up_factor, sign_table_salts
):
    ex_rows, seq, width_half = hidden.shape
    blocks = lax.axis_size("z") * lax.axis_size("x")
    fast = blocks == 8 and ex_rows == 8
    send, ranks, near, start, kept, mixer = far_rows(
        sign_table_salts,
        token_loss_mask,
        adapter_down_factor,
        adapter_up_factor.T,
        hidden.reshape(ex_rows * seq, width_half),
        cotangent.reshape(ex_rows * seq, width_half),
        fast,
    )
    other = swap_cores(send)
    terms = (mixer, ranks, near_rows(start, kept, near), other)
    features = feature_rows(*terms, ex_rows)
    if fast:
        third = swap_z(features, 3)
        second = swap_z(features, 2)
        first = swap_z(features, 1)
        near = swap_x(features)
        terms = pair_rows(near, (features, first, second, third), ex_rows)
        keep, core, x, both = terms
        return sum_rows(swap_cores(core), swap_x(x), swap_across(both), keep, ex_rows)
    share = ADAPTER_RANK * PROJ_ROWS // blocks
    parts = features.reshape(ADAPTER_RANK, ex_rows, PROJ_ROWS // share, share)
    parts = parts.swapaxes(1, 2).reshape(blocks, ex_rows, share)
    features = lax.all_to_all(parts, BLK, 0, 0, tiled=True).reshape(blocks * ex_rows, share)
    pairs = jnp.einsum("ep,fp->ef", features, features, preferred_element_type=F32)
    pairs = pairs.reshape(blocks, ex_rows, blocks * ex_rows)
    total = jnp.sum(lax.all_to_all(pairs, BLK, 0, 0, tiled=True), axis=0)
    halves = total.reshape(2, ex_rows // 2, blocks * ex_rows)
    core = lax.axis_index("tensor")
    send = lax.dynamic_index_in_dim(halves, 1 - core, 0, keepdims=False)
    return lax.dynamic_index_in_dim(halves, core, 0, keepdims=False) + swap_cores(send)


def solution(mesh):
    groups, blocks, cores = (mesh.shape[name] for name in ("groups", "blk", "tensor"))
    devices = mesh.devices.reshape(groups, blocks // 2, 2, cores)
    placed = (
        P(("groups", "z", "x"), None, "tensor"),
        P(("groups", "z", "x"), None, "tensor"),
        P(("groups", "z", "x"), None),
        P(None, "tensor"),
        P("tensor", None),
        P(),
    )
    return jax.shard_map(
        body,
        mesh=Mesh(devices, ("groups", "z", "x", "tensor")),
        in_specs=placed,
        out_specs=P(("groups", "z", "x", "tensor"), None),
        check_vma=False,
    )
```

```python
import functools
import math

import jax
import jax.numpy as jnp
from jax import lax
from jax.experimental import pallas as pl
from jax.experimental.pallas import tpu as pltpu
from jax.sharding import Mesh, PartitionSpec as P

MODEL_WIDTH = 4096
ADAPTER_RANK = 16
PROJ_ROWS = 256
SEQ = 64
SCALE = 1.0 / math.sqrt(PROJ_ROWS * ADAPTER_RANK * ADAPTER_RANK * SEQ * MODEL_WIDTH)
PIECES = 3
LANES = 128
BLOCK = (16, 256)
BLK = ("z", "x")

F32 = jnp.float32
BF16 = jnp.bfloat16
I32 = jnp.int32
NT = (((1,), (1,)), ((), ()))
VMEM = pl.BlockSpec(memory_space=pltpu.VMEM)
SMEM = pl.BlockSpec(memory_space=pltpu.SMEM)
HBM = pl.BlockSpec(memory_space=pltpu.HBM)
SMALL = pltpu.CompilerParams(vmem_limit_bytes=16 * 1024 * 1024)

INDEX_MUL = -1640531535
SALT_MUL = 668265263


def int32_wrap(value):
    return (value + 2**31) % 2**32 - 2**31


def hash_sign(hashed):
    hashed = hashed ^ lax.shift_right_logical(hashed, 15)
    hashed = hashed * -2048144789
    hashed = hashed ^ lax.shift_right_logical(hashed, 13)
    hashed = hashed * int32_wrap(-1028477387 << 6)
    hashed = hashed ^ lax.shift_left(hashed, 16)
    return jnp.where(hashed < 0, 1.0, -1.0).astype(F32)


def iota(shape, dim):
    return lax.broadcasted_iota(I32, shape, dim)


def token_row(mask):
    ex_rows, seq = mask.shape
    tokens = ex_rows * seq
    tiled = jnp.concatenate([mask.astype(F32)] * ex_rows, axis=1)
    owner = iota((ex_rows, tokens), 1) // seq == iota((ex_rows, tokens), 0)
    return jnp.sum(jnp.where(owner, tiled, 0.0), axis=0, keepdims=True)


def split_pieces(value):
    pieces = []
    for _ in range(PIECES):
        pieces.append(value.astype(BF16))
        value = value - pieces[-1].astype(F32)
    return jnp.concatenate(pieces, axis=0)


def kind_of(cross):
    core = lax.axis_index("tensor")
    return core ^ (lax.axis_index("z") // (lax.axis_size("z") // 2)) if cross else core


def table_start():
    index = iota(BLOCK, 1) * PROJ_ROWS + iota(BLOCK, 0)
    return index * INDEX_MUL


def sign_rows(start, col):
    high, wide = BLOCK
    rows = [
        hash_sign(start + int32_wrap((col * PROJ_ROWS + row) * INDEX_MUL)).astype(BF16)
        for row in range(0, PROJ_ROWS, high)
    ]
    return rows


def far_kernel(
    cross, ex_rows,
    salts_hbm, mask_hbm, down_hbm, up_hbm, hid_hbm, cot_hbm,
    send_ref, ranks_ref, near_ref, start_ref, kept_ref, mixer_ref,
    salts, mask, far_factor, near_factor, far, sems,
):
    tokens, width = far.shape
    kind = kind_of(cross)
    parts = 4
    share = width // parts
    wide = BLOCK[1]

    def copies(inputs, factor, factor_held, held, first):
        out = [pltpu.make_async_copy(factor, factor_held, sems.at[first])]
        for i in range(parts):
            cols = pl.ds(i * share, share)
            out.append(
                pltpu.make_async_copy(inputs.at[:, cols], held.at[:, cols], sems.at[first + 1 + i])
            )
        return out

    def start_copies(far_inputs, far_part, near_inputs, near_part):
        far_copies = copies(far_inputs, far_part, far_factor, far, 2)
        near_copies = copies(near_inputs, near_part, near_factor, near_ref, parts + 3)
        for pair in zip(far_copies, near_copies):
            for copy in pair:
                copy.start()

    salts_copy = pltpu.make_async_copy(salts_hbm, salts, sems.at[0])
    mask_copy = pltpu.make_async_copy(mask_hbm, mask, sems.at[1])
    salts_copy.start()

    @pl.when(kind == 0)
    def _():
        start_copies(hid_hbm, down_hbm, cot_hbm, up_hbm)

    @pl.when(kind == 1)
    def _():
        start_copies(cot_hbm, up_hbm, hid_hbm, down_hbm)

    mask_copy.start()
    far_waits = copies(hid_hbm, down_hbm, far_factor, far, 2)
    near_waits = copies(hid_hbm, down_hbm, near_factor, near_ref, parts + 3)
    first = lax.axis_index("tensor") * int32_wrap(width * PROJ_ROWS * INDEX_MUL)
    start = table_start() + first
    salts_copy.wait()
    far_start = start + salts[2 - 2 * kind] * SALT_MUL
    far_waits[0].wait()
    near_waits[0].wait()
    total = ranks = None
    for col in range(0, width, wide):
        part = slice(col, col + wide)
        left = jnp.concatenate(sign_rows(far_start, col) + [far_factor[:, part]], axis=0)
        if col % share == 0:
            far_waits[1 + col // share].wait()
            near_waits[1 + col // share].wait()
        term = lax.dot_general(left, far[:, part], NT, preferred_element_type=F32)
        total = term if total is None else total + term
        term = lax.dot_general(
            near_factor[:, part], near_ref[:, part], NT, preferred_element_type=F32
        )
        ranks = term if ranks is None else ranks + term
    start_ref[...] = start + salts[2 * kind] * SALT_MUL
    shape = mixer_ref.shape
    mixed, rank = iota(shape, 0) // ex_rows, iota(shape, 1) % ADAPTER_RANK
    index = (rank * ADAPTER_RANK + mixed) * INDEX_MUL
    mixer_ref[...] = hash_sign(index + salts[1 + 2 * kind] * SALT_MUL).astype(BF16)
    mask_copy.wait()
    counted = token_row(mask[...]) != 0
    far_kept = counted | (kind == 0)
    near_kept = counted | (kind == 1)
    kept_ref[...] = jnp.broadcast_to(jnp.where(near_kept, 1.0, 0.0), kept_ref.shape)
    total = jnp.where(far_kept, total, 0.0)
    send_ref[:PROJ_ROWS] = total[:PROJ_ROWS].astype(BF16)
    ranks_ref[...] = split_pieces(total[PROJ_ROWS:])
    send_ref[PROJ_ROWS:] = split_pieces(jnp.where(near_kept, ranks, 0.0))


def far_rows(salts, mask, down, up, hidden, cotangent, cross):
    ex_rows = mask.shape[0]
    tokens, width = hidden.shape
    pieces = PIECES * ADAPTER_RANK
    arrays = (salts, mask, down, up, hidden, cotangent)
    return pl.pallas_call(
        functools.partial(far_kernel, cross, ex_rows),
        out_shape=[
            jax.ShapeDtypeStruct((PROJ_ROWS + pieces, tokens), BF16),
            jax.ShapeDtypeStruct((pieces, tokens), BF16),
            jax.ShapeDtypeStruct((tokens, width), BF16),
            jax.ShapeDtypeStruct(BLOCK, I32),
            jax.ShapeDtypeStruct((8, tokens), F32),
            jax.ShapeDtypeStruct((ADAPTER_RANK * ex_rows, 2 * pieces), BF16),
        ],
        in_specs=[HBM] * 6,
        out_specs=[VMEM] * 6,
        scratch_shapes=[
            pltpu.SMEM(salts.shape, I32),
            pltpu.VMEM(mask.shape, I32),
            pltpu.VMEM((ADAPTER_RANK, width), BF16),
            pltpu.VMEM((ADAPTER_RANK, width), BF16),
            pltpu.VMEM((tokens, width), BF16),
            pltpu.SemaphoreType.DMA((12,)),
        ],
        compiler_params=SMALL,
    )(*[pltpu.with_memory_space_constraint(x, pltpu.HBM) for x in arrays])


def near_kernel(start_ref, kept_ref, near_ref, out_ref):
    start = start_ref[...]
    wide = BLOCK[1]
    total = None
    for col in range(0, near_ref.shape[1], wide):
        left = jnp.concatenate(sign_rows(start, col), axis=0)
        term = lax.dot_general(
            left, near_ref[:, col : col + wide], NT, preferred_element_type=F32
        )
        total = term if total is None else total + term
    out_ref[...] = jnp.where(kept_ref[:1] != 0, total, 0.0).astype(BF16)


def near_rows(start, kept, near):
    tokens, width = near.shape
    return pl.pallas_call(
        near_kernel,
        out_shape=jax.ShapeDtypeStruct((PROJ_ROWS, tokens), BF16),
        in_specs=[VMEM] * 3,
        out_specs=VMEM,
        compiler_params=SMALL,
        cost_estimate=pl.CostEstimate(
            flops=2 * tokens * width * PROJ_ROWS, bytes_accessed=2 * tokens * width, transcendentals=0
        ),
    )(start, kept, near)


def feature_kernel(ex_rows, mixer_ref, ranks_ref, own_ref, other_ref, out_ref):
    tokens = own_ref.shape[1]
    rows = ADAPTER_RANK * ex_rows
    pieces = jnp.concatenate([ranks_ref[...], other_ref[PROJ_ROWS:]], axis=0)
    coeffs = jnp.dot(mixer_ref[...], pieces, preferred_element_type=F32)
    owned = iota((rows, tokens), 1) // SEQ == iota((rows, tokens), 0) % ex_rows
    coeffs = jnp.where(owned, coeffs, 0.0).astype(BF16)
    projected = lax.dot_general(coeffs, own_ref[...], NT, preferred_element_type=F32)
    projected += lax.dot_general(coeffs, other_ref[:PROJ_ROWS], NT, preferred_element_type=F32)
    out_ref[...] = (projected * SCALE).astype(BF16)


def feature_rows(mixer, ranks, own, other, ex_rows):
    return pl.pallas_call(
        functools.partial(feature_kernel, ex_rows),
        out_shape=jax.ShapeDtypeStruct((ADAPTER_RANK * ex_rows, PROJ_ROWS), BF16),
        in_specs=[VMEM] * 4,
        out_specs=VMEM,
        compiler_params=SMALL,
    )(mixer, ranks, own, other)


def fold_ranks(terms):
    half = terms.shape[0] // 2
    folded = terms[:half] + pltpu.roll(terms[half:], LANES - half, 1)
    return jnp.where(iota(folded.shape, 1) % (2 * half) < half, folded, 0.0)


def order_blocks(rows, wide):
    z = lax.axis_index("z")
    rows = jnp.where((z & 2) != 0, pltpu.roll(rows, 2 * wide, 1), rows)
    even = (iota(rows.shape, 1) // wide) % 2 == 0
    swapped = jnp.where(even, pltpu.roll(rows, LANES - wide, 1), pltpu.roll(rows, wide, 1))
    return jnp.where((z & 1) != 0, swapped, rows)


def pair_kernel(ex_rows, own_ref, third_got_ref, near_ref, second_got_ref, first_got_ref, *out_refs):
    keep_ref, send_ref = out_refs
    z = lax.axis_index("z")
    inner = (z == 1) | (z == 2)
    wide = 2 * ex_rows
    total = None
    for row in range(0, own_ref.shape[0], wide):
        part = slice(row, row + wide)
        own, one, two = own_ref[part, :], first_got_ref[part, :], third_got_ref[part, :]
        left = jnp.concatenate([own, near_ref[part, :]], axis=0)
        by_z = [own, jnp.where(inner, one, two), jnp.where(inner, two, one)]
        right = jnp.concatenate((by_z + [second_got_ref[part, :]]) * 2, axis=0)
        term = lax.dot_general(left, right, NT, preferred_element_type=F32)
        total = term if total is None else total + term
    keep_ref[...] = order_blocks(fold_ranks(total[:wide]), wide)
    send_ref[...] = order_blocks(fold_ranks(total[wide:]), wide)


def pair_rows(own, third, near, second, first, ex_rows):
    return pl.pallas_call(
        functools.partial(pair_kernel, ex_rows),
        out_shape=[jax.ShapeDtypeStruct((ex_rows, LANES), F32)] * 2,
        in_specs=[VMEM] * 5,
        out_specs=[VMEM] * 2,
        compiler_params=SMALL,
    )(own, third, near, second, first)


def halves_kernel(own_ref, got_ref, keep_ref, send_ref):
    ex_rows, _ = own_ref.shape
    low_x = lax.axis_index("x") == 0
    first = jnp.where(low_x, own_ref[...], got_ref[...])
    second = jnp.where(low_x, got_ref[...], own_ref[...])
    total = first + pltpu.roll(second, ex_rows, 1)
    half = keep_ref.shape[0]
    low = lax.axis_index("tensor") == 0
    keep_ref[...] = jnp.where(low, total[:half], total[half:])
    send_ref[...] = jnp.where(low, total[half:], total[:half])


def join_halves(own, got):
    rows, lanes = own.shape
    return pl.pallas_call(
        halves_kernel,
        out_shape=[jax.ShapeDtypeStruct((rows // 2, lanes), F32)] * 2,
        in_specs=[VMEM] * 2,
        out_specs=[VMEM] * 2,
        compiler_params=SMALL,
    )(own, got)


def sum_kernel(keep_ref, got_ref, out_ref):
    out_ref[...] = (keep_ref[...] + got_ref[...])[:, : out_ref.shape[1]]


def sum_rows(keep, got):
    return pl.pallas_call(
        sum_kernel,
        out_shape=jax.ShapeDtypeStruct((keep.shape[0], LANES // 2), F32),
        in_specs=[VMEM] * 2,
        out_specs=VMEM,
        compiler_params=SMALL,
    )(keep, got)


def swap_cores(value):
    return lax.ppermute(value, "tensor", [(0, 1), (1, 0)])


def swap_across(value):
    return lax.ppermute(value, ("x", "tensor"), [(i, i ^ 3) for i in range(4)])


def swap_x(value):
    return lax.ppermute(value, "x", [(0, 1), (1, 0)])


def step_z(value, targets):
    pairs = []
    for z, target in enumerate(targets):
        for x in range(2):
            for kind in range(2):
                pairs.append(tuple(4 * at + 2 * x + (kind ^ (at // 2)) for at in (z, target)))
    return lax.ppermute(value, BLK + ("tensor",), pairs)


def body(
    hidden, cotangent, token_loss_mask, adapter_down_factor, adapter_up_factor, sign_table_salts
):
    ex_rows, seq, width_half = hidden.shape
    blocks = lax.axis_size("z") * lax.axis_size("x")
    fast = blocks == 8 and ex_rows == 8
    send, ranks, near, start, kept, mixer = far_rows(
        sign_table_salts,
        token_loss_mask,
        adapter_down_factor,
        adapter_up_factor.T,
        hidden.reshape(ex_rows * seq, width_half),
        cotangent.reshape(ex_rows * seq, width_half),
        fast,
    )
    other = swap_cores(send)
    terms = (mixer, ranks, near_rows(start, kept, near), other)
    features = feature_rows(*terms, ex_rows)
    if fast:
        first = step_z(features, (1, 3, 0, 2))
        second = step_z(features, (3, 2, 1, 0))
        near = swap_x(features)
        third = step_z(features, (2, 0, 3, 1))
        keep, send = pair_rows(features, third, near, second, first, ex_rows)
        keep, send = join_halves(keep, swap_across(send))
        return sum_rows(keep, swap_cores(send))
    share = ADAPTER_RANK * PROJ_ROWS // blocks
    parts = features.reshape(ADAPTER_RANK, ex_rows, PROJ_ROWS // share, share)
    parts = parts.swapaxes(1, 2).reshape(blocks, ex_rows, share)
    features = lax.all_to_all(parts, BLK, 0, 0, tiled=True).reshape(blocks * ex_rows, share)
    pairs = jnp.einsum("ep,fp->ef", features, features, preferred_element_type=F32)
    pairs = pairs.reshape(blocks, ex_rows, blocks * ex_rows)
    total = jnp.sum(lax.all_to_all(pairs, BLK, 0, 0, tiled=True), axis=0)
    halves = total.reshape(2, ex_rows // 2, blocks * ex_rows)
    core = lax.axis_index("tensor")
    send = lax.dynamic_index_in_dim(halves, 1 - core, 0, keepdims=False)
    return lax.dynamic_index_in_dim(halves, core, 0, keepdims=False) + swap_cores(send)


def solution(mesh):
    groups, blocks, cores = (mesh.shape[name] for name in ("groups", "blk", "tensor"))
    devices = mesh.devices.reshape(groups, blocks // 2, 2, cores)
    placed = (
        P(("groups", "z", "x"), None, "tensor"),
        P(("groups", "z", "x"), None, "tensor"),
        P(("groups", "z", "x"), None),
        P(None, "tensor"),
        P("tensor", None),
        P(),
    )
    return jax.shard_map(
        body,
        mesh=Mesh(devices, ("groups", "z", "x", "tensor")),
        in_specs=placed,
        out_specs=P(("groups", "z", "x", "tensor"), None),
        check_vma=False,
    )
```

```python
import functools
import math

import jax
import jax.numpy as jnp
from jax import lax
from jax.experimental import pallas as pl
from jax.experimental.pallas import tpu as pltpu
from jax.sharding import Mesh, PartitionSpec as P

MODEL_WIDTH = 4096
ADAPTER_RANK = 16
PROJ_ROWS = 256
SEQ = 64
SCALE = 1.0 / math.sqrt(PROJ_ROWS * ADAPTER_RANK * ADAPTER_RANK * SEQ * MODEL_WIDTH)
PIECES = 3
LANES = 128
BLOCK = (16, 256)
BLK = ("z", "x")

F32 = jnp.float32
BF16 = jnp.bfloat16
I32 = jnp.int32
NT = (((1,), (1,)), ((), ()))
VMEM = pl.BlockSpec(memory_space=pltpu.VMEM)
SMEM = pl.BlockSpec(memory_space=pltpu.SMEM)
HBM = pl.BlockSpec(memory_space=pltpu.HBM)
SMALL = pltpu.CompilerParams(vmem_limit_bytes=16 * 1024 * 1024)

INDEX_MUL = -1640531535
SALT_MUL = 668265263


def int32_wrap(value):
    return (value + 2**31) % 2**32 - 2**31


def hash_sign(hashed):
    hashed = hashed ^ lax.shift_right_logical(hashed, 15)
    hashed = hashed * -2048144789
    hashed = hashed ^ lax.shift_right_logical(hashed, 13)
    hashed = hashed * int32_wrap(-1028477387 << 6)
    hashed = hashed ^ lax.shift_left(hashed, 16)
    return jnp.where(hashed < 0, 1.0, -1.0).astype(F32)


def iota(shape, dim):
    return lax.broadcasted_iota(I32, shape, dim)


def token_row(mask):
    ex_rows, seq = mask.shape
    tokens = ex_rows * seq
    tiled = jnp.concatenate([mask.astype(F32)] * ex_rows, axis=1)
    owner = iota((ex_rows, tokens), 1) // seq == iota((ex_rows, tokens), 0)
    return jnp.sum(jnp.where(owner, tiled, 0.0), axis=0, keepdims=True)


def split_pieces(value):
    pieces = []
    for _ in range(PIECES):
        pieces.append(value.astype(BF16))
        value = value - pieces[-1].astype(F32)
    return jnp.concatenate(pieces, axis=0)


def kind_of(cross):
    core = lax.axis_index("tensor")
    return core ^ (lax.axis_index("z") // (lax.axis_size("z") // 2)) if cross else core


def table_start():
    index = iota(BLOCK, 1) * PROJ_ROWS + iota(BLOCK, 0)
    return index * INDEX_MUL


def sign_rows(start, col):
    high, wide = BLOCK
    rows = [
        hash_sign(start + int32_wrap((col * PROJ_ROWS + row) * INDEX_MUL)).astype(BF16)
        for row in range(0, PROJ_ROWS, high)
    ]
    return rows


def far_kernel(
    cross, ex_rows,
    salts_hbm, mask_hbm, down_hbm, up_hbm, hid_hbm, cot_hbm,
    send_ref, ranks_ref, near_ref, start_ref, kept_ref, mixer_ref,
    salts, mask, far_factor, near_factor, far, sems,
):
    tokens, width = far.shape
    kind = kind_of(cross)
    wide = BLOCK[1]
    share = width // 4
    ends = [0, share, 2 * share, 3 * share, width - wide, width]
    parts = len(ends) - 1

    def copies(inputs, factor, factor_held, held, first):
        out = [pltpu.make_async_copy(factor, factor_held, sems.at[first])]
        for i in range(parts):
            cols = pl.ds(ends[i], ends[i + 1] - ends[i])
            out.append(
                pltpu.make_async_copy(inputs.at[:, cols], held.at[:, cols], sems.at[first + 1 + i])
            )
        return out

    def start_copies(far_inputs, far_part, near_inputs, near_part):
        far_copies = copies(far_inputs, far_part, far_factor, far, 2)
        near_copies = copies(near_inputs, near_part, near_factor, near_ref, parts + 3)
        for pair in zip(far_copies, near_copies):
            for copy in pair:
                copy.start()

    salts_copy = pltpu.make_async_copy(salts_hbm, salts, sems.at[0])
    mask_copy = pltpu.make_async_copy(mask_hbm, mask, sems.at[1])
    salts_copy.start()
    mask_copy.start()

    @pl.when(kind == 0)
    def _():
        start_copies(hid_hbm, down_hbm, cot_hbm, up_hbm)

    @pl.when(kind == 1)
    def _():
        start_copies(cot_hbm, up_hbm, hid_hbm, down_hbm)

    far_waits = copies(hid_hbm, down_hbm, far_factor, far, 2)
    near_waits = copies(hid_hbm, down_hbm, near_factor, near_ref, parts + 3)
    first = lax.axis_index("tensor") * int32_wrap(width * PROJ_ROWS * INDEX_MUL)
    start = table_start() + first
    salts_copy.wait()
    far_start = start + salts[2 - 2 * kind] * SALT_MUL
    start_ref[...] = start + salts[2 * kind] * SALT_MUL
    shape = mixer_ref.shape
    mixed, rank = iota(shape, 0) // ex_rows, iota(shape, 1) % ADAPTER_RANK
    index = (rank * ADAPTER_RANK + mixed) * INDEX_MUL
    mixer_ref[...] = hash_sign(index + salts[1 + 2 * kind] * SALT_MUL).astype(BF16)
    mask_copy.wait()
    counted = token_row(mask[...]) != 0
    far_kept = counted | (kind == 0)
    near_kept = counted | (kind == 1)
    kept_ref[...] = jnp.broadcast_to(jnp.where(near_kept, 1.0, 0.0), kept_ref.shape)
    far_waits[0].wait()
    near_waits[0].wait()
    total = ranks = None
    for col in range(0, width, wide):
        part = slice(col, col + wide)
        left = jnp.concatenate(sign_rows(far_start, col) + [far_factor[:, part]], axis=0)
        if col in ends:
            far_waits[1 + ends.index(col)].wait()
            near_waits[1 + ends.index(col)].wait()
        term = lax.dot_general(left, far[:, part], NT, preferred_element_type=F32)
        total = term if total is None else total + term
        term = lax.dot_general(
            near_factor[:, part], near_ref[:, part], NT, preferred_element_type=F32
        )
        ranks = term if ranks is None else ranks + term
    total = jnp.where(far_kept, total, 0.0)
    send_ref[:PROJ_ROWS] = total[:PROJ_ROWS].astype(BF16)
    ranks_ref[...] = split_pieces(total[PROJ_ROWS:])
    send_ref[PROJ_ROWS:] = split_pieces(jnp.where(near_kept, ranks, 0.0))


def far_rows(salts, mask, down, up, hidden, cotangent, cross):
    ex_rows = mask.shape[0]
    tokens, width = hidden.shape
    pieces = PIECES * ADAPTER_RANK
    arrays = (salts, mask, down, up, hidden, cotangent)
    return pl.pallas_call(
        functools.partial(far_kernel, cross, ex_rows),
        out_shape=[
            jax.ShapeDtypeStruct((PROJ_ROWS + pieces, tokens), BF16),
            jax.ShapeDtypeStruct((pieces, tokens), BF16),
            jax.ShapeDtypeStruct((tokens, width), BF16),
            jax.ShapeDtypeStruct(BLOCK, I32),
            jax.ShapeDtypeStruct((8, tokens), F32),
            jax.ShapeDtypeStruct((ADAPTER_RANK * ex_rows, 2 * pieces), BF16),
        ],
        in_specs=[HBM] * 6,
        out_specs=[VMEM] * 6,
        scratch_shapes=[
            pltpu.SMEM(salts.shape, I32),
            pltpu.VMEM(mask.shape, I32),
            pltpu.VMEM((ADAPTER_RANK, width), BF16),
            pltpu.VMEM((ADAPTER_RANK, width), BF16),
            pltpu.VMEM((tokens, width), BF16),
            pltpu.SemaphoreType.DMA((14,)),
        ],
        compiler_params=SMALL,
    )(*[pltpu.with_memory_space_constraint(x, pltpu.HBM) for x in arrays])


def near_kernel(start_ref, kept_ref, near_ref, out_ref):
    start = start_ref[...]
    wide = BLOCK[1]
    total = None
    for col in range(0, near_ref.shape[1], wide):
        left = jnp.concatenate(sign_rows(start, col), axis=0)
        term = lax.dot_general(
            left, near_ref[:, col : col + wide], NT, preferred_element_type=F32
        )
        total = term if total is None else total + term
    out_ref[...] = jnp.where(kept_ref[:1] != 0, total, 0.0).astype(BF16)


def near_rows(start, kept, near):
    tokens, width = near.shape
    return pl.pallas_call(
        near_kernel,
        out_shape=jax.ShapeDtypeStruct((PROJ_ROWS, tokens), BF16),
        in_specs=[VMEM] * 3,
        out_specs=VMEM,
        compiler_params=SMALL,
        cost_estimate=pl.CostEstimate(
            flops=2 * tokens * width * PROJ_ROWS, bytes_accessed=2 * tokens * width, transcendentals=0
        ),
    )(start, kept, near)


def feature_kernel(ex_rows, mixer_ref, ranks_ref, own_ref, other_ref, out_ref):
    tokens = own_ref.shape[1]
    rows = ADAPTER_RANK * ex_rows
    pieces = jnp.concatenate([ranks_ref[...], other_ref[PROJ_ROWS:]], axis=0)
    coeffs = jnp.dot(mixer_ref[...], pieces, preferred_element_type=F32)
    owned = iota((rows, tokens), 1) // SEQ == iota((rows, tokens), 0) % ex_rows
    coeffs = jnp.where(owned, coeffs, 0.0).astype(BF16)
    projected = lax.dot_general(coeffs, own_ref[...], NT, preferred_element_type=F32)
    projected += lax.dot_general(coeffs, other_ref[:PROJ_ROWS], NT, preferred_element_type=F32)
    out_ref[...] = (projected * SCALE).astype(BF16)


def feature_rows(mixer, ranks, own, other, ex_rows):
    return pl.pallas_call(
        functools.partial(feature_kernel, ex_rows),
        out_shape=jax.ShapeDtypeStruct((ADAPTER_RANK * ex_rows, PROJ_ROWS), BF16),
        in_specs=[VMEM] * 4,
        out_specs=VMEM,
        compiler_params=SMALL,
    )(mixer, ranks, own, other)


def fold_ranks(terms):
    half = terms.shape[0] // 2
    folded = terms[:half] + pltpu.roll(terms[half:], LANES - half, 1)
    return jnp.where(iota(folded.shape, 1) % (2 * half) < half, folded, 0.0)


def order_blocks(rows, wide):
    z = lax.axis_index("z")
    rows = jnp.where((z & 2) != 0, pltpu.roll(rows, 2 * wide, 1), rows)
    even = (iota(rows.shape, 1) // wide) % 2 == 0
    swapped = jnp.where(even, pltpu.roll(rows, LANES - wide, 1), pltpu.roll(rows, wide, 1))
    return jnp.where((z & 1) != 0, swapped, rows)


def pair_kernel(ex_rows, near_ref, *refs):
    *z_refs, keep_ref, send_ref = refs
    wide = 2 * ex_rows
    total = None
    for row in range(0, near_ref.shape[0], wide):
        part = slice(row, row + wide)
        left = jnp.concatenate([z_refs[0][part, :], near_ref[part, :]], axis=0)
        right = jnp.concatenate([ref[part, :] for ref in z_refs], axis=0)
        term = lax.dot_general(left, right, NT, preferred_element_type=F32)
        total = term if total is None else total + term
    total = jnp.concatenate([total, total], axis=1)
    keep_ref[...] = order_blocks(fold_ranks(total[:wide]), wide)
    send_ref[...] = order_blocks(fold_ranks(total[wide:]), wide)


def pair_rows(near, by_z, ex_rows):
    return pl.pallas_call(
        functools.partial(pair_kernel, ex_rows),
        out_shape=[jax.ShapeDtypeStruct((ex_rows, LANES), F32)] * 2,
        in_specs=[VMEM] * (1 + len(by_z)),
        out_specs=[VMEM] * 2,
        compiler_params=SMALL,
    )(near, *by_z)


def halves_kernel(own_ref, got_ref, keep_ref, send_ref):
    ex_rows, _ = own_ref.shape
    low_x = lax.axis_index("x") == 0
    first = jnp.where(low_x, own_ref[...], got_ref[...])
    second = jnp.where(low_x, got_ref[...], own_ref[...])
    total = first + pltpu.roll(second, ex_rows, 1)
    half = keep_ref.shape[0]
    low = lax.axis_index("tensor") == 0
    keep_ref[...] = jnp.where(low, total[:half], total[half:])
    send_ref[...] = jnp.where(low, total[half:], total[:half])


def join_halves(own, got):
    rows, lanes = own.shape
    return pl.pallas_call(
        halves_kernel,
        out_shape=[jax.ShapeDtypeStruct((rows // 2, lanes), F32)] * 2,
        in_specs=[VMEM] * 2,
        out_specs=[VMEM] * 2,
        compiler_params=SMALL,
    )(own, got)


def sum_kernel(keep_ref, got_ref, out_ref):
    out_ref[...] = (keep_ref[...] + got_ref[...])[:, : out_ref.shape[1]]


def sum_rows(keep, got):
    return pl.pallas_call(
        sum_kernel,
        out_shape=jax.ShapeDtypeStruct((keep.shape[0], LANES // 2), F32),
        in_specs=[VMEM] * 2,
        out_specs=VMEM,
        compiler_params=SMALL,
    )(keep, got)


def swap_cores(value):
    return lax.ppermute(value, "tensor", [(0, 1), (1, 0)])


def swap_across(value):
    return lax.ppermute(value, ("x", "tensor"), [(i, i ^ 3) for i in range(4)])


def swap_x(value):
    return lax.ppermute(value, "x", [(0, 1), (1, 0)])


def swap_z(value, step):
    other = 4 * step + (step > 1)
    return lax.ppermute(value, BLK + ("tensor",), [(i, i ^ other) for i in range(16)])


def body(
    hidden, cotangent, token_loss_mask, adapter_down_factor, adapter_up_factor, sign_table_salts
):
    ex_rows, seq, width_half = hidden.shape
    blocks = lax.axis_size("z") * lax.axis_size("x")
    fast = blocks == 8 and ex_rows == 8
    send, ranks, near, start, kept, mixer = far_rows(
        sign_table_salts,
        token_loss_mask,
        adapter_down_factor,
        adapter_up_factor.T,
        hidden.reshape(ex_rows * seq, width_half),
        cotangent.reshape(ex_rows * seq, width_half),
        fast,
    )
    other = swap_cores(send)
    terms = (mixer, ranks, near_rows(start, kept, near), other)
    features = feature_rows(*terms, ex_rows)
    if fast:
        third = swap_z(features, 3)
        second = swap_z(features, 2)
        first = swap_z(features, 1)
        near = swap_x(features)
        keep, send = pair_rows(near, (features, first, second, third), ex_rows)
        keep, send = join_halves(keep, swap_across(send))
        return sum_rows(keep, swap_cores(send))
    share = ADAPTER_RANK * PROJ_ROWS // blocks
    parts = features.reshape(ADAPTER_RANK, ex_rows, PROJ_ROWS // share, share)
    parts = parts.swapaxes(1, 2).reshape(blocks, ex_rows, share)
    features = lax.all_to_all(parts, BLK, 0, 0, tiled=True).reshape(blocks * ex_rows, share)
    pairs = jnp.einsum("ep,fp->ef", features, features, preferred_element_type=F32)
    pairs = pairs.reshape(blocks, ex_rows, blocks * ex_rows)
    total = jnp.sum(lax.all_to_all(pairs, BLK, 0, 0, tiled=True), axis=0)
    halves = total.reshape(2, ex_rows // 2, blocks * ex_rows)
    core = lax.axis_index("tensor")
    send = lax.dynamic_index_in_dim(halves, 1 - core, 0, keepdims=False)
    return lax.dynamic_index_in_dim(halves, core, 0, keepdims=False) + swap_cores(send)


def solution(mesh):
    groups, blocks, cores = (mesh.shape[name] for name in ("groups", "blk", "tensor"))
    devices = mesh.devices.reshape(groups, blocks // 2, 2, cores)
    placed = (
        P(("groups", "z", "x"), None, "tensor"),
        P(("groups", "z", "x"), None, "tensor"),
        P(("groups", "z", "x"), None),
        P(None, "tensor"),
        P("tensor", None),
        P(),
    )
    return jax.shard_map(
        body,
        mesh=Mesh(devices, ("groups", "z", "x", "tensor")),
        in_specs=placed,
        out_specs=P(("groups", "z", "x", "tensor"), None),
        check_vma=False,
    )
```

```python
import functools
import math

import jax
import jax.numpy as jnp
from jax import lax
from jax.experimental import pallas as pl
from jax.experimental.pallas import tpu as pltpu
from jax.sharding import Mesh, PartitionSpec as P

MODEL_WIDTH = 4096
ADAPTER_RANK = 16
PROJ_ROWS = 256
SEQ = 64
SCALE = 1.0 / math.sqrt(PROJ_ROWS * ADAPTER_RANK * ADAPTER_RANK * SEQ * MODEL_WIDTH)
PIECES = 3
LANES = 128
BLOCK = (16, 256)
BLK = ("z", "x")

F32 = jnp.float32
BF16 = jnp.bfloat16
I32 = jnp.int32
NT = (((1,), (1,)), ((), ()))
VMEM = pl.BlockSpec(memory_space=pltpu.VMEM)
SMEM = pl.BlockSpec(memory_space=pltpu.SMEM)
HBM = pl.BlockSpec(memory_space=pltpu.HBM)
SMALL = pltpu.CompilerParams(vmem_limit_bytes=16 * 1024 * 1024)

INDEX_MUL = -1640531535
SALT_MUL = 668265263


def int32_wrap(value):
    return (value + 2**31) % 2**32 - 2**31


def hash_sign(hashed):
    hashed = hashed ^ lax.shift_right_logical(hashed, 15)
    hashed = hashed * -2048144789
    hashed = hashed ^ lax.shift_right_logical(hashed, 13)
    hashed = hashed * int32_wrap(-1028477387 << 6)
    hashed = hashed ^ lax.shift_left(hashed, 16)
    return jnp.where(hashed < 0, 1.0, -1.0).astype(F32)


def iota(shape, dim):
    return lax.broadcasted_iota(I32, shape, dim)


def token_row(mask):
    ex_rows, seq = mask.shape
    tokens = ex_rows * seq
    tiled = jnp.concatenate([mask.astype(F32)] * ex_rows, axis=1)
    owner = iota((ex_rows, tokens), 1) // seq == iota((ex_rows, tokens), 0)
    return jnp.sum(jnp.where(owner, tiled, 0.0), axis=0, keepdims=True)


def split_pieces(value):
    pieces = []
    for _ in range(PIECES):
        pieces.append(value.astype(BF16))
        value = value - pieces[-1].astype(F32)
    return jnp.concatenate(pieces, axis=0)


def kind_of(cross):
    core = lax.axis_index("tensor")
    return core ^ (lax.axis_index("z") // (lax.axis_size("z") // 2)) if cross else core


def table_start():
    index = iota(BLOCK, 1) * PROJ_ROWS + iota(BLOCK, 0)
    return index * INDEX_MUL


def sign_rows(start, col):
    high, wide = BLOCK
    rows = [
        hash_sign(start + int32_wrap((col * PROJ_ROWS + row) * INDEX_MUL)).astype(BF16)
        for row in range(0, PROJ_ROWS, high)
    ]
    return rows


def far_kernel(
    cross, ex_rows,
    salts_hbm, mask_hbm, down_hbm, up_hbm, hid_hbm, cot_hbm,
    send_ref, ranks_ref, near_ref, start_ref, kept_ref, mixer_ref,
    salts, mask, far_factor, near_factor, far, sems,
):
    tokens, width = far.shape
    kind = kind_of(cross)
    wide = BLOCK[1]
    share = width // 4
    ends = [0, share, 2 * share, 3 * share, width - wide, width]
    parts = len(ends) - 1

    def copies(inputs, factor, factor_held, held, first):
        out = [pltpu.make_async_copy(factor, factor_held, sems.at[first])]
        for i in range(parts):
            cols = pl.ds(ends[i], ends[i + 1] - ends[i])
            out.append(
                pltpu.make_async_copy(inputs.at[:, cols], held.at[:, cols], sems.at[first + 1 + i])
            )
        return out

    def start_copies(far_inputs, far_part, near_inputs, near_part):
        far_copies = copies(far_inputs, far_part, far_factor, far, 2)
        near_copies = copies(near_inputs, near_part, near_factor, near_ref, parts + 3)
        for pair in zip(far_copies, near_copies):
            for copy in pair:
                copy.start()

    salts_copy = pltpu.make_async_copy(salts_hbm, salts, sems.at[0])
    mask_copy = pltpu.make_async_copy(mask_hbm, mask, sems.at[1])
    salts_copy.start()
    mask_copy.start()

    @pl.when(kind == 0)
    def _():
        start_copies(hid_hbm, down_hbm, cot_hbm, up_hbm)

    @pl.when(kind == 1)
    def _():
        start_copies(cot_hbm, up_hbm, hid_hbm, down_hbm)

    far_waits = copies(hid_hbm, down_hbm, far_factor, far, 2)
    near_waits = copies(hid_hbm, down_hbm, near_factor, near_ref, parts + 3)
    first = lax.axis_index("tensor") * int32_wrap(width * PROJ_ROWS * INDEX_MUL)
    start = table_start() + first
    salts_copy.wait()
    far_start = start + salts[2 - 2 * kind] * SALT_MUL
    start_ref[...] = start + salts[2 * kind] * SALT_MUL
    shape = mixer_ref.shape
    mixed, rank = iota(shape, 0) // ex_rows, iota(shape, 1) % ADAPTER_RANK
    index = (rank * ADAPTER_RANK + mixed) * INDEX_MUL
    mixer_ref[...] = hash_sign(index + salts[1 + 2 * kind] * SALT_MUL).astype(BF16)
    mask_copy.wait()
    counted = token_row(mask[...]) != 0
    far_kept = counted | (kind == 0)
    near_kept = counted | (kind == 1)
    kept_ref[...] = jnp.broadcast_to(jnp.where(near_kept, 1.0, 0.0), kept_ref.shape)
    far_waits[0].wait()
    near_waits[0].wait()
    total = ranks = None
    for col in range(0, width, wide):
        part = slice(col, col + wide)
        left = jnp.concatenate(sign_rows(far_start, col) + [far_factor[:, part]], axis=0)
        if col in ends:
            far_waits[1 + ends.index(col)].wait()
            near_waits[1 + ends.index(col)].wait()
        term = lax.dot_general(left, far[:, part], NT, preferred_element_type=F32)
        total = term if total is None else total + term
        term = lax.dot_general(
            near_factor[:, part], near_ref[:, part], NT, preferred_element_type=F32
        )
        ranks = term if ranks is None else ranks + term
    total = jnp.where(far_kept, total, 0.0)
    send_ref[:PROJ_ROWS] = total[:PROJ_ROWS].astype(BF16)
    ranks_ref[...] = split_pieces(total[PROJ_ROWS:])
    send_ref[PROJ_ROWS:] = split_pieces(jnp.where(near_kept, ranks, 0.0))


def far_rows(salts, mask, down, up, hidden, cotangent, cross):
    ex_rows = mask.shape[0]
    tokens, width = hidden.shape
    pieces = PIECES * ADAPTER_RANK
    arrays = (salts, mask, down, up, hidden, cotangent)
    return pl.pallas_call(
        functools.partial(far_kernel, cross, ex_rows),
        out_shape=[
            jax.ShapeDtypeStruct((PROJ_ROWS + pieces, tokens), BF16),
            jax.ShapeDtypeStruct((pieces, tokens), BF16),
            jax.ShapeDtypeStruct((tokens, width), BF16),
            jax.ShapeDtypeStruct(BLOCK, I32),
            jax.ShapeDtypeStruct((8, tokens), F32),
            jax.ShapeDtypeStruct((ADAPTER_RANK * ex_rows, 2 * pieces), BF16),
        ],
        in_specs=[HBM] * 6,
        out_specs=[VMEM] * 6,
        scratch_shapes=[
            pltpu.SMEM(salts.shape, I32),
            pltpu.VMEM(mask.shape, I32),
            pltpu.VMEM((ADAPTER_RANK, width), BF16),
            pltpu.VMEM((ADAPTER_RANK, width), BF16),
            pltpu.VMEM((tokens, width), BF16),
            pltpu.SemaphoreType.DMA((14,)),
        ],
        compiler_params=SMALL,
    )(*[pltpu.with_memory_space_constraint(x, pltpu.HBM) for x in arrays])


def near_kernel(start_ref, kept_ref, near_ref, out_ref):
    start = start_ref[...]
    wide = BLOCK[1]
    total = None
    for col in range(0, near_ref.shape[1], wide):
        left = jnp.concatenate(sign_rows(start, col), axis=0)
        term = lax.dot_general(
            left, near_ref[:, col : col + wide], NT, preferred_element_type=F32
        )
        total = term if total is None else total + term
    out_ref[...] = jnp.where(kept_ref[:1] != 0, total, 0.0).astype(BF16)


def near_rows(start, kept, near):
    tokens, width = near.shape
    return pl.pallas_call(
        near_kernel,
        out_shape=jax.ShapeDtypeStruct((PROJ_ROWS, tokens), BF16),
        in_specs=[VMEM] * 3,
        out_specs=VMEM,
        compiler_params=SMALL,
        cost_estimate=pl.CostEstimate(
            flops=2 * tokens * width * PROJ_ROWS, bytes_accessed=2 * tokens * width, transcendentals=0
        ),
    )(start, kept, near)


def feature_kernel(ex_rows, mixer_ref, ranks_ref, own_ref, other_ref, out_ref):
    tokens = own_ref.shape[1]
    rows = ADAPTER_RANK * ex_rows
    pieces = jnp.concatenate([ranks_ref[...], other_ref[PROJ_ROWS:]], axis=0)
    coeffs = jnp.dot(mixer_ref[...], pieces, preferred_element_type=F32)
    owned = iota((rows, tokens), 1) // SEQ == iota((rows, tokens), 0) % ex_rows
    coeffs = jnp.where(owned, coeffs, 0.0).astype(BF16)
    projected = lax.dot_general(coeffs, own_ref[...], NT, preferred_element_type=F32)
    projected += lax.dot_general(coeffs, other_ref[:PROJ_ROWS], NT, preferred_element_type=F32)
    out_ref[...] = (projected * SCALE).astype(BF16)


def feature_rows(mixer, ranks, own, other, ex_rows):
    return pl.pallas_call(
        functools.partial(feature_kernel, ex_rows),
        out_shape=jax.ShapeDtypeStruct((ADAPTER_RANK * ex_rows, PROJ_ROWS), BF16),
        in_specs=[VMEM] * 4,
        out_specs=VMEM,
        compiler_params=SMALL,
    )(mixer, ranks, own, other)


def fold_ranks(terms):
    half = terms.shape[0] // 2
    folded = terms[:half] + pltpu.roll(terms[half:], LANES - half, 1)
    return jnp.where(iota(folded.shape, 1) % (2 * half) < half, folded, 0.0)


def order_blocks(rows, wide):
    z = lax.axis_index("z")
    rows = jnp.where((z & 2) != 0, pltpu.roll(rows, 2 * wide, 1), rows)
    even = (iota(rows.shape, 1) // wide) % 2 == 0
    swapped = jnp.where(even, pltpu.roll(rows, LANES - wide, 1), pltpu.roll(rows, wide, 1))
    return jnp.where((z & 1) != 0, swapped, rows)


def pair_kernel(ex_rows, near_ref, own_ref, first_ref, third_ref, second_ref, keep_ref, send_ref):
    z_refs = (own_ref, first_ref, second_ref, third_ref)
    wide = 2 * ex_rows
    total = None
    for row in range(0, near_ref.shape[0], wide):
        part = slice(row, row + wide)
        left = jnp.concatenate([z_refs[0][part, :], near_ref[part, :]], axis=0)
        right = jnp.concatenate([ref[part, :] for ref in z_refs], axis=0)
        term = lax.dot_general(left, right, NT, preferred_element_type=F32)
        total = term if total is None else total + term
    total = jnp.concatenate([total, total], axis=1)
    keep_ref[...] = order_blocks(fold_ranks(total[:wide]), wide)
    send_ref[...] = order_blocks(fold_ranks(total[wide:]), wide)


def pair_rows(near, own, first, third, second, ex_rows):
    return pl.pallas_call(
        functools.partial(pair_kernel, ex_rows),
        out_shape=[jax.ShapeDtypeStruct((ex_rows, LANES), F32)] * 2,
        in_specs=[VMEM] * 5,
        out_specs=[VMEM] * 2,
        compiler_params=SMALL,
    )(near, own, first, third, second)


def halves_kernel(own_ref, got_ref, keep_ref, send_ref):
    ex_rows, _ = own_ref.shape
    low_x = lax.axis_index("x") == 0
    first = jnp.where(low_x, own_ref[...], got_ref[...])
    second = jnp.where(low_x, got_ref[...], own_ref[...])
    total = first + pltpu.roll(second, ex_rows, 1)
    half = keep_ref.shape[0]
    low = lax.axis_index("tensor") == 0
    keep_ref[...] = jnp.where(low, total[:half], total[half:])
    send_ref[...] = jnp.where(low, total[half:], total[:half])


def join_halves(own, got):
    rows, lanes = own.shape
    return pl.pallas_call(
        halves_kernel,
        out_shape=[jax.ShapeDtypeStruct((rows // 2, lanes), F32)] * 2,
        in_specs=[VMEM] * 2,
        out_specs=[VMEM] * 2,
        compiler_params=SMALL,
    )(own, got)


def sum_kernel(keep_ref, got_ref, out_ref):
    out_ref[...] = (keep_ref[...] + got_ref[...])[:, : out_ref.shape[1]]


def sum_rows(keep, got):
    return pl.pallas_call(
        sum_kernel,
        out_shape=jax.ShapeDtypeStruct((keep.shape[0], LANES // 2), F32),
        in_specs=[VMEM] * 2,
        out_specs=VMEM,
        compiler_params=SMALL,
    )(keep, got)


def swap_cores(value):
    return lax.ppermute(value, "tensor", [(0, 1), (1, 0)])


def swap_across(value):
    return lax.ppermute(value, ("x", "tensor"), [(i, i ^ 3) for i in range(4)])


def swap_x(value):
    return lax.ppermute(value, "x", [(0, 1), (1, 0)])


def swap_z(value, step):
    other = 4 * step + (step > 1)
    return lax.ppermute(value, BLK + ("tensor",), [(i, i ^ other) for i in range(16)])


def body(
    hidden, cotangent, token_loss_mask, adapter_down_factor, adapter_up_factor, sign_table_salts
):
    ex_rows, seq, width_half = hidden.shape
    blocks = lax.axis_size("z") * lax.axis_size("x")
    fast = blocks == 8 and ex_rows == 8
    send, ranks, near, start, kept, mixer = far_rows(
        sign_table_salts,
        token_loss_mask,
        adapter_down_factor,
        adapter_up_factor.T,
        hidden.reshape(ex_rows * seq, width_half),
        cotangent.reshape(ex_rows * seq, width_half),
        fast,
    )
    other = swap_cores(send)
    terms = (mixer, ranks, near_rows(start, kept, near), other)
    features = feature_rows(*terms, ex_rows)
    if fast:
        second = swap_z(features, 2)
        third = swap_z(features, 3)
        first = swap_z(features, 1)
        near = swap_x(features)
        keep, send = pair_rows(near, features, first, third, second, ex_rows)
        keep, send = join_halves(keep, swap_across(send))
        return sum_rows(keep, swap_cores(send))
    share = ADAPTER_RANK * PROJ_ROWS // blocks
    parts = features.reshape(ADAPTER_RANK, ex_rows, PROJ_ROWS // share, share)
    parts = parts.swapaxes(1, 2).reshape(blocks, ex_rows, share)
    features = lax.all_to_all(parts, BLK, 0, 0, tiled=True).reshape(blocks * ex_rows, share)
    pairs = jnp.einsum("ep,fp->ef", features, features, preferred_element_type=F32)
    pairs = pairs.reshape(blocks, ex_rows, blocks * ex_rows)
    total = jnp.sum(lax.all_to_all(pairs, BLK, 0, 0, tiled=True), axis=0)
    halves = total.reshape(2, ex_rows // 2, blocks * ex_rows)
    core = lax.axis_index("tensor")
    send = lax.dynamic_index_in_dim(halves, 1 - core, 0, keepdims=False)
    return lax.dynamic_index_in_dim(halves, core, 0, keepdims=False) + swap_cores(send)


def solution(mesh):
    groups, blocks, cores = (mesh.shape[name] for name in ("groups", "blk", "tensor"))
    devices = mesh.devices.reshape(groups, blocks // 2, 2, cores)
    placed = (
        P(("groups", "z", "x"), None, "tensor"),
        P(("groups", "z", "x"), None, "tensor"),
        P(("groups", "z", "x"), None),
        P(None, "tensor"),
        P("tensor", None),
        P(),
    )
    return jax.shard_map(
        body,
        mesh=Mesh(devices, ("groups", "z", "x", "tensor")),
        in_specs=placed,
        out_specs=P(("groups", "z", "x", "tensor"), None),
        check_vma=False,
    )
```

```python
import functools
import math

import jax
import jax.numpy as jnp
from jax import lax
from jax.experimental import pallas as pl
from jax.experimental.pallas import tpu as pltpu
from jax.sharding import Mesh, PartitionSpec as P

MODEL_WIDTH = 4096
ADAPTER_RANK = 16
PROJ_ROWS = 256
SEQ = 64
SCALE = 1.0 / math.sqrt(PROJ_ROWS * ADAPTER_RANK * ADAPTER_RANK * SEQ * MODEL_WIDTH)
PIECES = 3
LANES = 128
BLOCK = (16, 256)
BLK = ("z", "x")

F32 = jnp.float32
BF16 = jnp.bfloat16
I32 = jnp.int32
NT = (((1,), (1,)), ((), ()))
VMEM = pl.BlockSpec(memory_space=pltpu.VMEM)
SMEM = pl.BlockSpec(memory_space=pltpu.SMEM)
HBM = pl.BlockSpec(memory_space=pltpu.HBM)
SMALL = pltpu.CompilerParams(vmem_limit_bytes=16 * 1024 * 1024)

INDEX_MUL = -1640531535
SALT_MUL = 668265263


def int32_wrap(value):
    return (value + 2**31) % 2**32 - 2**31


def hash_sign(hashed):
    hashed = hashed ^ lax.shift_right_logical(hashed, 15)
    hashed = hashed * -2048144789
    hashed = hashed ^ lax.shift_right_logical(hashed, 13)
    hashed = hashed * int32_wrap(-1028477387 << 6)
    hashed = hashed ^ lax.shift_left(hashed, 16)
    return jnp.where(hashed < 0, 1.0, -1.0).astype(F32)


def iota(shape, dim):
    return lax.broadcasted_iota(I32, shape, dim)


def token_row(mask):
    ex_rows, seq = mask.shape
    tokens = ex_rows * seq
    tiled = jnp.concatenate([mask.astype(F32)] * ex_rows, axis=1)
    owner = iota((ex_rows, tokens), 1) // seq == iota((ex_rows, tokens), 0)
    return jnp.sum(jnp.where(owner, tiled, 0.0), axis=0, keepdims=True)


def split_pieces(value):
    pieces = []
    for _ in range(PIECES):
        pieces.append(value.astype(BF16))
        value = value - pieces[-1].astype(F32)
    return jnp.concatenate(pieces, axis=0)


def kind_of(cross):
    core = lax.axis_index("tensor")
    return core ^ (lax.axis_index("z") // (lax.axis_size("z") // 2)) if cross else core


def table_start():
    index = iota(BLOCK, 1) * PROJ_ROWS + iota(BLOCK, 0)
    return index * INDEX_MUL


def sign_rows(start, col):
    high, wide = BLOCK
    rows = [
        hash_sign(start + int32_wrap((col * PROJ_ROWS + row) * INDEX_MUL)).astype(BF16)
        for row in range(0, PROJ_ROWS, high)
    ]
    return rows


def far_kernel(
    cross, ex_rows,
    salts_hbm, mask_hbm, down_hbm, up_hbm, hid_hbm, cot_hbm,
    send_ref, ranks_ref, near_ref, start_ref, kept_ref, mixer_ref,
    salts, mask, far_factor, near_factor, far, sems,
):
    tokens, width = far.shape
    kind = kind_of(cross)
    wide = BLOCK[1]
    share = width // 4
    ends = [0, share, 2 * share, 3 * share, width - wide, width]
    parts = len(ends) - 1

    def copies(inputs, factor, factor_held, held, first):
        out = [pltpu.make_async_copy(factor, factor_held, sems.at[first])]
        for i in range(parts):
            cols = pl.ds(ends[i], ends[i + 1] - ends[i])
            out.append(
                pltpu.make_async_copy(inputs.at[:, cols], held.at[:, cols], sems.at[first + 1 + i])
            )
        return out

    def start_copies(far_inputs, far_part, near_inputs, near_part):
        far_copies = copies(far_inputs, far_part, far_factor, far, 2)
        near_copies = copies(near_inputs, near_part, near_factor, near_ref, parts + 3)
        for pair in zip(far_copies, near_copies):
            for copy in pair:
                copy.start()

    salts_copy = pltpu.make_async_copy(salts_hbm, salts, sems.at[0])
    mask_copy = pltpu.make_async_copy(mask_hbm, mask, sems.at[1])
    salts_copy.start()
    mask_copy.start()

    @pl.when(kind == 0)
    def _():
        start_copies(hid_hbm, down_hbm, cot_hbm, up_hbm)

    @pl.when(kind == 1)
    def _():
        start_copies(cot_hbm, up_hbm, hid_hbm, down_hbm)

    far_waits = copies(hid_hbm, down_hbm, far_factor, far, 2)
    near_waits = copies(hid_hbm, down_hbm, near_factor, near_ref, parts + 3)
    first = lax.axis_index("tensor") * int32_wrap(width * PROJ_ROWS * INDEX_MUL)
    start = table_start() + first
    salts_copy.wait()
    far_start = start + salts[2 - 2 * kind] * SALT_MUL
    start_ref[...] = start + salts[2 * kind] * SALT_MUL
    shape = mixer_ref.shape
    mixed, rank = iota(shape, 0) // ex_rows, iota(shape, 1) % ADAPTER_RANK
    index = (rank * ADAPTER_RANK + mixed) * INDEX_MUL
    mixer_ref[...] = hash_sign(index + salts[1 + 2 * kind] * SALT_MUL).astype(BF16)
    mask_copy.wait()
    counted = token_row(mask[...]) != 0
    far_kept = counted | (kind == 0)
    near_kept = counted | (kind == 1)
    kept_ref[...] = jnp.broadcast_to(jnp.where(near_kept, 1.0, 0.0), kept_ref.shape)
    far_waits[0].wait()
    near_waits[0].wait()
    total = ranks = None
    for col in range(0, width, wide):
        part = slice(col, col + wide)
        left = jnp.concatenate(sign_rows(far_start, col) + [far_factor[:, part]], axis=0)
        if col in ends:
            far_waits[1 + ends.index(col)].wait()
            near_waits[1 + ends.index(col)].wait()
        term = lax.dot_general(left, far[:, part], NT, preferred_element_type=F32)
        total = term if total is None else total + term
        term = lax.dot_general(
            near_factor[:, part], near_ref[:, part], NT, preferred_element_type=F32
        )
        ranks = term if ranks is None else ranks + term
    total = jnp.where(far_kept, total, 0.0)
    send_ref[:PROJ_ROWS] = total[:PROJ_ROWS].astype(BF16)
    ranks_ref[...] = split_pieces(total[PROJ_ROWS:])
    send_ref[PROJ_ROWS:] = split_pieces(jnp.where(near_kept, ranks, 0.0))


def far_rows(salts, mask, down, up, hidden, cotangent, cross):
    ex_rows = mask.shape[0]
    tokens, width = hidden.shape
    pieces = PIECES * ADAPTER_RANK
    arrays = (salts, mask, down, up, hidden, cotangent)
    return pl.pallas_call(
        functools.partial(far_kernel, cross, ex_rows),
        out_shape=[
            jax.ShapeDtypeStruct((PROJ_ROWS + pieces, tokens), BF16),
            jax.ShapeDtypeStruct((pieces, tokens), BF16),
            jax.ShapeDtypeStruct((tokens, width), BF16),
            jax.ShapeDtypeStruct(BLOCK, I32),
            jax.ShapeDtypeStruct((8, tokens), F32),
            jax.ShapeDtypeStruct((ADAPTER_RANK * ex_rows, 2 * pieces), BF16),
        ],
        in_specs=[HBM] * 6,
        out_specs=[VMEM] * 6,
        scratch_shapes=[
            pltpu.SMEM(salts.shape, I32),
            pltpu.VMEM(mask.shape, I32),
            pltpu.VMEM((ADAPTER_RANK, width), BF16),
            pltpu.VMEM((ADAPTER_RANK, width), BF16),
            pltpu.VMEM((tokens, width), BF16),
            pltpu.SemaphoreType.DMA((14,)),
        ],
        compiler_params=SMALL,
    )(*[pltpu.with_memory_space_constraint(x, pltpu.HBM) for x in arrays])


def near_kernel(start_ref, kept_ref, near_ref, out_ref):
    start = start_ref[...]
    wide = BLOCK[1]
    total = None
    for col in range(0, near_ref.shape[1], wide):
        left = jnp.concatenate(sign_rows(start, col), axis=0)
        term = lax.dot_general(
            left, near_ref[:, col : col + wide], NT, preferred_element_type=F32
        )
        total = term if total is None else total + term
    out_ref[...] = jnp.where(kept_ref[:1] != 0, total, 0.0).astype(BF16)


def near_rows(start, kept, near):
    tokens, width = near.shape
    return pl.pallas_call(
        near_kernel,
        out_shape=jax.ShapeDtypeStruct((PROJ_ROWS, tokens), BF16),
        in_specs=[VMEM] * 3,
        out_specs=VMEM,
        compiler_params=SMALL,
        cost_estimate=pl.CostEstimate(
            flops=2 * tokens * width * PROJ_ROWS, bytes_accessed=2 * tokens * width, transcendentals=0
        ),
    )(start, kept, near)


def feature_kernel(ex_rows, mixer_ref, ranks_ref, own_ref, other_ref, out_ref):
    tokens = own_ref.shape[1]
    rows = ADAPTER_RANK * ex_rows
    pieces = jnp.concatenate([ranks_ref[...], other_ref[PROJ_ROWS:]], axis=0)
    coeffs = jnp.dot(mixer_ref[...], pieces, preferred_element_type=F32)
    owned = iota((rows, tokens), 1) // SEQ == iota((rows, tokens), 0) % ex_rows
    coeffs = jnp.where(owned, coeffs, 0.0).astype(BF16)
    projected = lax.dot_general(coeffs, own_ref[...], NT, preferred_element_type=F32)
    projected += lax.dot_general(coeffs, other_ref[:PROJ_ROWS], NT, preferred_element_type=F32)
    out_ref[...] = (projected * SCALE).astype(BF16)


def feature_rows(mixer, ranks, own, other, ex_rows):
    return pl.pallas_call(
        functools.partial(feature_kernel, ex_rows),
        out_shape=jax.ShapeDtypeStruct((ADAPTER_RANK * ex_rows, PROJ_ROWS), BF16),
        in_specs=[VMEM] * 4,
        out_specs=VMEM,
        compiler_params=SMALL,
    )(mixer, ranks, own, other)


def fold_ranks(terms):
    half = terms.shape[0] // 2
    folded = terms[:half] + pltpu.roll(terms[half:], LANES - half, 1)
    return jnp.where(iota(folded.shape, 1) % (2 * half) < half, folded, 0.0)


def order_blocks(rows, wide):
    z = lax.axis_index("z")
    rows = jnp.where((z & 2) != 0, pltpu.roll(rows, 2 * wide, 1), rows)
    even = (iota(rows.shape, 1) // wide) % 2 == 0
    swapped = jnp.where(even, pltpu.roll(rows, LANES - wide, 1), pltpu.roll(rows, wide, 1))
    return jnp.where((z & 1) != 0, swapped, rows)


def pair_kernel(ex_rows, near_ref, own_ref, third_ref, first_ref, second_ref, keep_ref, send_ref):
    z_refs = (own_ref, first_ref, second_ref, third_ref)
    wide = 2 * ex_rows
    total = None
    for row in range(0, near_ref.shape[0], wide):
        part = slice(row, row + wide)
        left = jnp.concatenate([z_refs[0][part, :], near_ref[part, :]], axis=0)
        right = jnp.concatenate([ref[part, :] for ref in z_refs], axis=0)
        term = lax.dot_general(left, right, NT, preferred_element_type=F32)
        total = term if total is None else total + term
    total = jnp.concatenate([total, total], axis=1)
    keep_ref[...] = order_blocks(fold_ranks(total[:wide]), wide)
    send_ref[...] = order_blocks(fold_ranks(total[wide:]), wide)


def pair_rows(near, own, third, first, second, ex_rows):
    return pl.pallas_call(
        functools.partial(pair_kernel, ex_rows),
        out_shape=[jax.ShapeDtypeStruct((ex_rows, LANES), F32)] * 2,
        in_specs=[VMEM] * 5,
        out_specs=[VMEM] * 2,
        compiler_params=SMALL,
    )(near, own, third, first, second)


def halves_kernel(own_ref, got_ref, keep_ref, send_ref):
    ex_rows, _ = own_ref.shape
    low_x = lax.axis_index("x") == 0
    first = jnp.where(low_x, own_ref[...], got_ref[...])
    second = jnp.where(low_x, got_ref[...], own_ref[...])
    total = first + pltpu.roll(second, ex_rows, 1)
    half = keep_ref.shape[0]
    low = lax.axis_index("tensor") == 0
    keep_ref[...] = jnp.where(low, total[:half], total[half:])
    send_ref[...] = jnp.where(low, total[half:], total[:half])


def join_halves(own, got):
    rows, lanes = own.shape
    return pl.pallas_call(
        halves_kernel,
        out_shape=[jax.ShapeDtypeStruct((rows // 2, lanes), F32)] * 2,
        in_specs=[VMEM] * 2,
        out_specs=[VMEM] * 2,
        compiler_params=SMALL,
    )(own, got)


def sum_kernel(keep_ref, got_ref, out_ref):
    out_ref[...] = (keep_ref[...] + got_ref[...])[:, : out_ref.shape[1]]


def sum_rows(keep, got):
    return pl.pallas_call(
        sum_kernel,
        out_shape=jax.ShapeDtypeStruct((keep.shape[0], LANES // 2), F32),
        in_specs=[VMEM] * 2,
        out_specs=VMEM,
        compiler_params=SMALL,
    )(keep, got)


def swap_cores(value):
    return lax.ppermute(value, "tensor", [(0, 1), (1, 0)])


def swap_across(value):
    return lax.ppermute(value, ("x", "tensor"), [(i, i ^ 3) for i in range(4)])


def swap_x(value):
    return lax.ppermute(value, "x", [(0, 1), (1, 0)])


def swap_z(value, step):
    other = 4 * step + (step > 1)
    return lax.ppermute(value, BLK + ("tensor",), [(i, i ^ other) for i in range(16)])


def body(
    hidden, cotangent, token_loss_mask, adapter_down_factor, adapter_up_factor, sign_table_salts
):
    ex_rows, seq, width_half = hidden.shape
    blocks = lax.axis_size("z") * lax.axis_size("x")
    fast = blocks == 8 and ex_rows == 8
    send, ranks, near, start, kept, mixer = far_rows(
        sign_table_salts,
        token_loss_mask,
        adapter_down_factor,
        adapter_up_factor.T,
        hidden.reshape(ex_rows * seq, width_half),
        cotangent.reshape(ex_rows * seq, width_half),
        fast,
    )
    other = swap_cores(send)
    terms = (mixer, ranks, near_rows(start, kept, near), other)
    features = feature_rows(*terms, ex_rows)
    if fast:
        second = swap_z(features, 2)
        third = swap_z(features, 3)
        first = swap_z(features, 1)
        near = swap_x(features)
        keep, send = pair_rows(near, features, third, first, second, ex_rows)
        keep, send = join_halves(keep, swap_across(send))
        return sum_rows(keep, swap_cores(send))
    share = ADAPTER_RANK * PROJ_ROWS // blocks
    parts = features.reshape(ADAPTER_RANK, ex_rows, PROJ_ROWS // share, share)
    parts = parts.swapaxes(1, 2).reshape(blocks, ex_rows, share)
    features = lax.all_to_all(parts, BLK, 0, 0, tiled=True).reshape(blocks * ex_rows, share)
    pairs = jnp.einsum("ep,fp->ef", features, features, preferred_element_type=F32)
    pairs = pairs.reshape(blocks, ex_rows, blocks * ex_rows)
    total = jnp.sum(lax.all_to_all(pairs, BLK, 0, 0, tiled=True), axis=0)
    halves = total.reshape(2, ex_rows // 2, blocks * ex_rows)
    core = lax.axis_index("tensor")
    send = lax.dynamic_index_in_dim(halves, 1 - core, 0, keepdims=False)
    return lax.dynamic_index_in_dim(halves, core, 0, keepdims=False) + swap_cores(send)


def solution(mesh):
    groups, blocks, cores = (mesh.shape[name] for name in ("groups", "blk", "tensor"))
    devices = mesh.devices.reshape(groups, blocks // 2, 2, cores)
    placed = (
        P(("groups", "z", "x"), None, "tensor"),
        P(("groups", "z", "x"), None, "tensor"),
        P(("groups", "z", "x"), None),
        P(None, "tensor"),
        P("tensor", None),
        P(),
    )
    return jax.shard_map(
        body,
        mesh=Mesh(devices, ("groups", "z", "x", "tensor")),
        in_specs=placed,
        out_specs=P(("groups", "z", "x", "tensor"), None),
        check_vma=False,
    )
```

```python
import functools
import math

import jax
import jax.numpy as jnp
from jax import lax
from jax.experimental import pallas as pl
from jax.experimental.pallas import tpu as pltpu
from jax.sharding import Mesh, PartitionSpec as P

MODEL_WIDTH = 4096
ADAPTER_RANK = 16
PROJ_ROWS = 256
SEQ = 64
SCALE = 1.0 / math.sqrt(PROJ_ROWS * ADAPTER_RANK * ADAPTER_RANK * SEQ * MODEL_WIDTH)
PIECES = 3
LANES = 128
BLOCK = (16, 256)
BLK = ("z", "x")

F32 = jnp.float32
BF16 = jnp.bfloat16
I32 = jnp.int32
NT = (((1,), (1,)), ((), ()))
VMEM = pl.BlockSpec(memory_space=pltpu.VMEM)
SMEM = pl.BlockSpec(memory_space=pltpu.SMEM)
HBM = pl.BlockSpec(memory_space=pltpu.HBM)
SMALL = pltpu.CompilerParams(vmem_limit_bytes=16 * 1024 * 1024)

INDEX_MUL = -1640531535
SALT_MUL = 668265263


def int32_wrap(value):
    return (value + 2**31) % 2**32 - 2**31


def hash_sign(hashed):
    hashed = hashed ^ lax.shift_right_logical(hashed, 15)
    hashed = hashed * -2048144789
    hashed = hashed ^ lax.shift_right_logical(hashed, 13)
    hashed = hashed * int32_wrap(-1028477387 << 6)
    hashed = hashed ^ lax.shift_left(hashed, 16)
    return jnp.where(hashed < 0, 1.0, -1.0).astype(F32)


def iota(shape, dim):
    return lax.broadcasted_iota(I32, shape, dim)


def token_row(mask):
    ex_rows, seq = mask.shape
    tokens = ex_rows * seq
    tiled = jnp.concatenate([mask.astype(F32)] * ex_rows, axis=1)
    owner = iota((ex_rows, tokens), 1) // seq == iota((ex_rows, tokens), 0)
    return jnp.sum(jnp.where(owner, tiled, 0.0), axis=0, keepdims=True)


def split_pieces(value):
    pieces = []
    for _ in range(PIECES):
        pieces.append(value.astype(BF16))
        value = value - pieces[-1].astype(F32)
    return jnp.concatenate(pieces, axis=0)


def table_start():
    index = iota(BLOCK, 1) * PROJ_ROWS + iota(BLOCK, 0)
    return index * INDEX_MUL


def sign_rows(start, col):
    high, wide = BLOCK
    rows = [
        hash_sign(start + int32_wrap((col * PROJ_ROWS + row) * INDEX_MUL)).astype(BF16)
        for row in range(0, PROJ_ROWS, high)
    ]
    return rows


def far_kernel(
    ex_rows,
    salts_hbm, mask_hbm, down_hbm, up_hbm, hid_hbm, cot_hbm,
    send_ref, ranks_ref, near_ref, start_ref, kept_ref, mixer_ref,
    salts, mask, far_factor, near_factor, far, sems,
):
    tokens, width = far.shape
    kind = lax.axis_index("tensor")
    wide = BLOCK[1]
    share = width // 4
    ends = [0, share, 2 * share, 3 * share, width - wide, width]
    parts = len(ends) - 1

    def copies(inputs, factor, factor_held, held, first):
        out = [pltpu.make_async_copy(factor, factor_held, sems.at[first])]
        for i in range(parts):
            cols = pl.ds(ends[i], ends[i + 1] - ends[i])
            out.append(
                pltpu.make_async_copy(inputs.at[:, cols], held.at[:, cols], sems.at[first + 1 + i])
            )
        return out

    def start_copies(far_inputs, far_part, near_inputs, near_part):
        far_copies = copies(far_inputs, far_part, far_factor, far, 2)
        near_copies = copies(near_inputs, near_part, near_factor, near_ref, parts + 3)
        for pair in zip(far_copies, near_copies):
            for copy in pair:
                copy.start()

    salts_copy = pltpu.make_async_copy(salts_hbm, salts, sems.at[0])
    mask_copy = pltpu.make_async_copy(mask_hbm, mask, sems.at[1])
    salts_copy.start()
    mask_copy.start()

    @pl.when(kind == 0)
    def _():
        start_copies(hid_hbm, down_hbm, cot_hbm, up_hbm)

    @pl.when(kind == 1)
    def _():
        start_copies(cot_hbm, up_hbm, hid_hbm, down_hbm)

    far_waits = copies(hid_hbm, down_hbm, far_factor, far, 2)
    near_waits = copies(hid_hbm, down_hbm, near_factor, near_ref, parts + 3)
    first = lax.axis_index("tensor") * int32_wrap(width * PROJ_ROWS * INDEX_MUL)
    start = table_start() + first
    salts_copy.wait()
    far_start = start + salts[2 - 2 * kind] * SALT_MUL
    start_ref[...] = start + salts[2 * kind] * SALT_MUL
    shape = mixer_ref.shape
    mixed, rank = iota(shape, 0) // ex_rows, iota(shape, 1) % ADAPTER_RANK
    index = (rank * ADAPTER_RANK + mixed) * INDEX_MUL
    mixer_ref[...] = hash_sign(index + salts[1 + 2 * kind] * SALT_MUL).astype(BF16)
    mask_copy.wait()
    counted = token_row(mask[...]) != 0
    far_kept = counted | (kind == 0)
    near_kept = counted | (kind == 1)
    kept_ref[...] = jnp.broadcast_to(jnp.where(near_kept, 1.0, 0.0), kept_ref.shape)
    far_waits[0].wait()
    near_waits[0].wait()
    total = ranks = None
    for col in range(0, width, wide):
        part = slice(col, col + wide)
        left = jnp.concatenate(sign_rows(far_start, col) + [far_factor[:, part]], axis=0)
        if col in ends:
            far_waits[1 + ends.index(col)].wait()
            near_waits[1 + ends.index(col)].wait()
        term = lax.dot_general(left, far[:, part], NT, preferred_element_type=F32)
        total = term if total is None else total + term
        term = lax.dot_general(
            near_factor[:, part], near_ref[:, part], NT, preferred_element_type=F32
        )
        ranks = term if ranks is None else ranks + term
    total = jnp.where(far_kept, total, 0.0)
    send_ref[:PROJ_ROWS] = total[:PROJ_ROWS].astype(BF16)
    ranks_ref[...] = split_pieces(total[PROJ_ROWS:])
    send_ref[PROJ_ROWS:] = split_pieces(jnp.where(near_kept, ranks, 0.0))


def far_rows(salts, mask, down, up, hidden, cotangent):
    ex_rows = mask.shape[0]
    tokens, width = hidden.shape
    pieces = PIECES * ADAPTER_RANK
    arrays = (salts, mask, down, up, hidden, cotangent)
    return pl.pallas_call(
        functools.partial(far_kernel, ex_rows),
        out_shape=[
            jax.ShapeDtypeStruct((PROJ_ROWS + pieces, tokens), BF16),
            jax.ShapeDtypeStruct((pieces, tokens), BF16),
            jax.ShapeDtypeStruct((tokens, width), BF16),
            jax.ShapeDtypeStruct(BLOCK, I32),
            jax.ShapeDtypeStruct((8, tokens), F32),
            jax.ShapeDtypeStruct((ADAPTER_RANK * ex_rows, 2 * pieces), BF16),
        ],
        in_specs=[HBM] * 6,
        out_specs=[VMEM] * 6,
        scratch_shapes=[
            pltpu.SMEM(salts.shape, I32),
            pltpu.VMEM(mask.shape, I32),
            pltpu.VMEM((ADAPTER_RANK, width), BF16),
            pltpu.VMEM((ADAPTER_RANK, width), BF16),
            pltpu.VMEM((tokens, width), BF16),
            pltpu.SemaphoreType.DMA((14,)),
        ],
        compiler_params=SMALL,
    )(*[pltpu.with_memory_space_constraint(x, pltpu.HBM) for x in arrays])


def near_kernel(start_ref, kept_ref, near_ref, out_ref):
    start = start_ref[...]
    wide = BLOCK[1]
    total = None
    for col in range(0, near_ref.shape[1], wide):
        left = jnp.concatenate(sign_rows(start, col), axis=0)
        term = lax.dot_general(
            left, near_ref[:, col : col + wide], NT, preferred_element_type=F32
        )
        total = term if total is None else total + term
    out_ref[...] = jnp.where(kept_ref[:1] != 0, total, 0.0).astype(BF16)


def near_rows(start, kept, near):
    tokens, width = near.shape
    return pl.pallas_call(
        near_kernel,
        out_shape=jax.ShapeDtypeStruct((PROJ_ROWS, tokens), BF16),
        in_specs=[VMEM] * 3,
        out_specs=VMEM,
        compiler_params=SMALL,
        cost_estimate=pl.CostEstimate(
            flops=2 * tokens * width * PROJ_ROWS, bytes_accessed=2 * tokens * width, transcendentals=0
        ),
    )(start, kept, near)


def feature_kernel(ex_rows, mixer_ref, ranks_ref, own_ref, other_ref, out_ref):
    tokens = own_ref.shape[1]
    rows = ADAPTER_RANK * ex_rows
    pieces = jnp.concatenate([ranks_ref[...], other_ref[PROJ_ROWS:]], axis=0)
    coeffs = jnp.dot(mixer_ref[...], pieces, preferred_element_type=F32)
    owned = iota((rows, tokens), 1) // SEQ == iota((rows, tokens), 0) % ex_rows
    coeffs = jnp.where(owned, coeffs, 0.0).astype(BF16)
    projected = lax.dot_general(coeffs, own_ref[...], NT, preferred_element_type=F32)
    projected += lax.dot_general(coeffs, other_ref[:PROJ_ROWS], NT, preferred_element_type=F32)
    out_ref[...] = (projected * SCALE).astype(BF16)


def feature_rows(mixer, ranks, own, other, ex_rows):
    return pl.pallas_call(
        functools.partial(feature_kernel, ex_rows),
        out_shape=jax.ShapeDtypeStruct((ADAPTER_RANK * ex_rows, PROJ_ROWS), BF16),
        in_specs=[VMEM] * 4,
        out_specs=VMEM,
        compiler_params=SMALL,
    )(mixer, ranks, own, other)


def fold_ranks(terms):
    half = terms.shape[0] // 2
    folded = terms[:half] + pltpu.roll(terms[half:], LANES - half, 1)
    return jnp.where(iota(folded.shape, 1) % (2 * half) < half, folded, 0.0)


def order_blocks(rows, wide):
    z = lax.axis_index("z")
    rows = jnp.where((z & 2) != 0, pltpu.roll(rows, 2 * wide, 1), rows)
    even = (iota(rows.shape, 1) // wide) % 2 == 0
    swapped = jnp.where(even, pltpu.roll(rows, LANES - wide, 1), pltpu.roll(rows, wide, 1))
    return jnp.where((z & 1) != 0, swapped, rows)


def pair_kernel(ex_rows, near_ref, *refs):
    *z_refs, keep_ref, send_ref = refs
    wide = 2 * ex_rows
    total = None
    for row in range(0, near_ref.shape[0], wide):
        part = slice(row, row + wide)
        left = jnp.concatenate([z_refs[0][part, :], near_ref[part, :]], axis=0)
        right = jnp.concatenate([ref[part, :] for ref in z_refs], axis=0)
        term = lax.dot_general(left, right, NT, preferred_element_type=F32)
        total = term if total is None else total + term
    total = jnp.concatenate([total, total], axis=1)
    keep_ref[...] = order_blocks(fold_ranks(total[:wide]), wide)
    send_ref[...] = order_blocks(fold_ranks(total[wide:]), wide)


def pair_rows(near, by_z, ex_rows):
    return pl.pallas_call(
        functools.partial(pair_kernel, ex_rows),
        out_shape=[jax.ShapeDtypeStruct((ex_rows, LANES), F32)] * 2,
        in_specs=[VMEM] * (1 + len(by_z)),
        out_specs=[VMEM] * 2,
        compiler_params=SMALL,
    )(near, *by_z)


def halves_kernel(own_ref, got_ref, keep_ref, send_ref):
    ex_rows, _ = own_ref.shape
    low_x = lax.axis_index("x") == 0
    first = jnp.where(low_x, own_ref[...], got_ref[...])
    second = jnp.where(low_x, got_ref[...], own_ref[...])
    total = first + pltpu.roll(second, ex_rows, 1)
    half = keep_ref.shape[0]
    low = lax.axis_index("tensor") == 0
    keep_ref[...] = jnp.where(low, total[:half], total[half:])
    send_ref[...] = jnp.where(low, total[half:], total[:half])


def join_halves(own, got):
    rows, lanes = own.shape
    return pl.pallas_call(
        halves_kernel,
        out_shape=[jax.ShapeDtypeStruct((rows // 2, lanes), F32)] * 2,
        in_specs=[VMEM] * 2,
        out_specs=[VMEM] * 2,
        compiler_params=SMALL,
    )(own, got)


def sum_kernel(keep_ref, got_ref, out_ref):
    out_ref[...] = (keep_ref[...] + got_ref[...])[:, : out_ref.shape[1]]


def sum_rows(keep, got):
    return pl.pallas_call(
        sum_kernel,
        out_shape=jax.ShapeDtypeStruct((keep.shape[0], LANES // 2), F32),
        in_specs=[VMEM] * 2,
        out_specs=VMEM,
        compiler_params=SMALL,
    )(keep, got)


def swap_cores(value):
    return lax.ppermute(value, "tensor", [(0, 1), (1, 0)])


def swap_across(value):
    return lax.ppermute(value, ("x", "tensor"), [(i, i ^ 3) for i in range(4)])


def swap_x(value):
    return lax.ppermute(value, "x", [(0, 1), (1, 0)])


def swap_z(value, step):
    other = 4 * step
    return lax.ppermute(value, BLK + ("tensor",), [(i, i ^ other) for i in range(16)])


def body(
    hidden, cotangent, token_loss_mask, adapter_down_factor, adapter_up_factor, sign_table_salts
):
    ex_rows, seq, width_half = hidden.shape
    blocks = lax.axis_size("z") * lax.axis_size("x")
    fast = blocks == 8 and ex_rows == 8
    send, ranks, near, start, kept, mixer = far_rows(
        sign_table_salts,
        token_loss_mask,
        adapter_down_factor,
        adapter_up_factor.T,
        hidden.reshape(ex_rows * seq, width_half),
        cotangent.reshape(ex_rows * seq, width_half),
    )
    other = swap_cores(send)
    terms = (mixer, ranks, near_rows(start, kept, near), other)
    features = feature_rows(*terms, ex_rows)
    if fast:
        third = swap_z(features, 3)
        second = swap_z(features, 2)
        first = swap_z(features, 1)
        near = swap_x(features)
        keep, send = pair_rows(near, (features, first, second, third), ex_rows)
        keep, send = join_halves(keep, swap_across(send))
        return sum_rows(keep, swap_cores(send))
    share = ADAPTER_RANK * PROJ_ROWS // blocks
    parts = features.reshape(ADAPTER_RANK, ex_rows, PROJ_ROWS // share, share)
    parts = parts.swapaxes(1, 2).reshape(blocks, ex_rows, share)
    features = lax.all_to_all(parts, BLK, 0, 0, tiled=True).reshape(blocks * ex_rows, share)
    pairs = jnp.einsum("ep,fp->ef", features, features, preferred_element_type=F32)
    pairs = pairs.reshape(blocks, ex_rows, blocks * ex_rows)
    total = jnp.sum(lax.all_to_all(pairs, BLK, 0, 0, tiled=True), axis=0)
    halves = total.reshape(2, ex_rows // 2, blocks * ex_rows)
    core = lax.axis_index("tensor")
    send = lax.dynamic_index_in_dim(halves, 1 - core, 0, keepdims=False)
    return lax.dynamic_index_in_dim(halves, core, 0, keepdims=False) + swap_cores(send)


def solution(mesh):
    groups, blocks, cores = (mesh.shape[name] for name in ("groups", "blk", "tensor"))
    devices = mesh.devices.reshape(groups, blocks // 2, 2, cores)
    placed = (
        P(("groups", "z", "x"), None, "tensor"),
        P(("groups", "z", "x"), None, "tensor"),
        P(("groups", "z", "x"), None),
        P(None, "tensor"),
        P("tensor", None),
        P(),
    )
    return jax.shard_map(
        body,
        mesh=Mesh(devices, ("groups", "z", "x", "tensor")),
        in_specs=placed,
        out_specs=P(("groups", "z", "x", "tensor"), None),
        check_vma=False,
    )
```

```python
import functools
import math

import jax
import jax.numpy as jnp
from jax import lax
from jax.experimental import pallas as pl
from jax.experimental.pallas import tpu as pltpu
from jax.sharding import Mesh, PartitionSpec as P

MODEL_WIDTH = 4096
ADAPTER_RANK = 16
PROJ_ROWS = 256
SEQ = 64
SCALE = 1.0 / math.sqrt(PROJ_ROWS * ADAPTER_RANK * ADAPTER_RANK * SEQ * MODEL_WIDTH)
PIECES = 3
LANES = 128
BLOCK = (16, 256)
BLK = ("z", "x")

F32 = jnp.float32
BF16 = jnp.bfloat16
I32 = jnp.int32
NT = (((1,), (1,)), ((), ()))
VMEM = pl.BlockSpec(memory_space=pltpu.VMEM)
SMEM = pl.BlockSpec(memory_space=pltpu.SMEM)
HBM = pl.BlockSpec(memory_space=pltpu.HBM)
SMALL = pltpu.CompilerParams(vmem_limit_bytes=16 * 1024 * 1024)

INDEX_MUL = -1640531535
SALT_MUL = 668265263


def int32_wrap(value):
    return (value + 2**31) % 2**32 - 2**31


def hash_sign(hashed):
    hashed = hashed ^ lax.shift_right_logical(hashed, 15)
    hashed = hashed * -2048144789
    hashed = hashed ^ lax.shift_right_logical(hashed, 13)
    hashed = hashed * int32_wrap(-1028477387 << 6)
    hashed = hashed ^ lax.shift_left(hashed, 16)
    return jnp.where(hashed < 0, 1.0, -1.0).astype(F32)


def iota(shape, dim):
    return lax.broadcasted_iota(I32, shape, dim)


def token_row(mask):
    ex_rows, seq = mask.shape
    tokens = ex_rows * seq
    tiled = jnp.concatenate([mask.astype(F32)] * ex_rows, axis=1)
    owner = iota((ex_rows, tokens), 1) // seq == iota((ex_rows, tokens), 0)
    return jnp.sum(jnp.where(owner, tiled, 0.0), axis=0, keepdims=True)


def split_pieces(value):
    pieces = []
    for _ in range(PIECES):
        pieces.append(value.astype(BF16))
        value = value - pieces[-1].astype(F32)
    return jnp.concatenate(pieces, axis=0)


def kind_of(cross):
    core = lax.axis_index("tensor")
    return core ^ (lax.axis_index("z") // (lax.axis_size("z") // 2)) if cross else core


def table_start():
    index = iota(BLOCK, 1) * PROJ_ROWS + iota(BLOCK, 0)
    return index * INDEX_MUL


def sign_rows(start, col):
    high, wide = BLOCK
    rows = [
        hash_sign(start + int32_wrap((col * PROJ_ROWS + row) * INDEX_MUL)).astype(BF16)
        for row in range(0, PROJ_ROWS, high)
    ]
    return rows


def far_kernel(
    cross, ex_rows,
    salts_hbm, mask_hbm, down_hbm, up_hbm, hid_hbm, cot_hbm,
    send_ref, ranks_ref, near_ref, start_ref, kept_ref, mixer_ref,
    salts, mask, far_factor, near_factor, far, sems,
):
    tokens, width = far.shape
    kind = kind_of(cross)
    wide = BLOCK[1]
    share = width // 4
    ends = [0, share, 2 * share, 3 * share, width - wide, width]
    parts = len(ends) - 1

    def copies(inputs, factor, factor_held, held, first):
        out = [pltpu.make_async_copy(factor, factor_held, sems.at[first])]
        for i in range(parts):
            cols = pl.ds(ends[i], ends[i + 1] - ends[i])
            out.append(
                pltpu.make_async_copy(inputs.at[:, cols], held.at[:, cols], sems.at[first + 1 + i])
            )
        return out

    def start_copies(far_inputs, far_part, near_inputs, near_part):
        far_copies = copies(far_inputs, far_part, far_factor, far, 2)
        near_copies = copies(near_inputs, near_part, near_factor, near_ref, parts + 3)
        for pair in zip(far_copies, near_copies):
            for copy in pair:
                copy.start()

    salts_copy = pltpu.make_async_copy(salts_hbm, salts, sems.at[0])
    mask_copy = pltpu.make_async_copy(mask_hbm, mask, sems.at[1])
    salts_copy.start()
    mask_copy.start()

    @pl.when(kind == 0)
    def _():
        start_copies(hid_hbm, down_hbm, cot_hbm, up_hbm)

    @pl.when(kind == 1)
    def _():
        start_copies(cot_hbm, up_hbm, hid_hbm, down_hbm)

    far_waits = copies(hid_hbm, down_hbm, far_factor, far, 2)
    near_waits = copies(hid_hbm, down_hbm, near_factor, near_ref, parts + 3)
    first = lax.axis_index("tensor") * int32_wrap(width * PROJ_ROWS * INDEX_MUL)
    start = table_start() + first
    salts_copy.wait()
    far_start = start + salts[2 - 2 * kind] * SALT_MUL
    start_ref[...] = start + salts[2 * kind] * SALT_MUL
    shape = mixer_ref.shape
    mixed, rank = iota(shape, 0) // ex_rows, iota(shape, 1) % ADAPTER_RANK
    index = (rank * ADAPTER_RANK + mixed) * INDEX_MUL
    mixer_ref[...] = hash_sign(index + salts[1 + 2 * kind] * SALT_MUL).astype(BF16)
    mask_copy.wait()
    counted = token_row(mask[...]) != 0
    far_kept = counted | (kind == 0)
    near_kept = counted | (kind == 1)
    kept_ref[...] = jnp.broadcast_to(jnp.where(near_kept, 1.0, 0.0), kept_ref.shape)
    far_waits[0].wait()
    near_waits[0].wait()
    total = ranks = None
    for col in range(0, width, wide):
        part = slice(col, col + wide)
        left = jnp.concatenate(sign_rows(far_start, col) + [far_factor[:, part]], axis=0)
        if col in ends:
            far_waits[1 + ends.index(col)].wait()
            near_waits[1 + ends.index(col)].wait()
        term = lax.dot_general(left, far[:, part], NT, preferred_element_type=F32)
        total = term if total is None else total + term
        term = lax.dot_general(
            near_factor[:, part], near_ref[:, part], NT, preferred_element_type=F32
        )
        ranks = term if ranks is None else ranks + term
    total = jnp.where(far_kept, total, 0.0)
    send_ref[:PROJ_ROWS] = total[:PROJ_ROWS].astype(BF16)
    ranks_ref[...] = split_pieces(total[PROJ_ROWS:])
    send_ref[PROJ_ROWS:] = split_pieces(jnp.where(near_kept, ranks, 0.0))


def far_rows(salts, mask, down, up, hidden, cotangent, cross):
    ex_rows = mask.shape[0]
    tokens, width = hidden.shape
    pieces = PIECES * ADAPTER_RANK
    arrays = (salts, mask, down, up, hidden, cotangent)
    return pl.pallas_call(
        functools.partial(far_kernel, cross, ex_rows),
        out_shape=[
            jax.ShapeDtypeStruct((PROJ_ROWS + pieces, tokens), BF16),
            jax.ShapeDtypeStruct((pieces, tokens), BF16),
            jax.ShapeDtypeStruct((tokens, width), BF16),
            jax.ShapeDtypeStruct(BLOCK, I32),
            jax.ShapeDtypeStruct((8, tokens), F32),
            jax.ShapeDtypeStruct((ADAPTER_RANK * ex_rows, 2 * pieces), BF16),
        ],
        in_specs=[HBM] * 6,
        out_specs=[VMEM] * 6,
        scratch_shapes=[
            pltpu.SMEM(salts.shape, I32),
            pltpu.VMEM(mask.shape, I32),
            pltpu.VMEM((ADAPTER_RANK, width), BF16),
            pltpu.VMEM((ADAPTER_RANK, width), BF16),
            pltpu.VMEM((tokens, width), BF16),
            pltpu.SemaphoreType.DMA((14,)),
        ],
        compiler_params=SMALL,
    )(*[pltpu.with_memory_space_constraint(x, pltpu.HBM) for x in arrays])


def near_kernel(start_ref, kept_ref, near_ref, out_ref):
    start = start_ref[...]
    wide = BLOCK[1]
    total = None
    for col in range(0, near_ref.shape[1], wide):
        left = jnp.concatenate(sign_rows(start, col), axis=0)
        term = lax.dot_general(
            left, near_ref[:, col : col + wide], NT, preferred_element_type=F32
        )
        total = term if total is None else total + term
    out_ref[...] = jnp.where(kept_ref[:1] != 0, total, 0.0).astype(BF16)


def near_rows(start, kept, near):
    tokens, width = near.shape
    return pl.pallas_call(
        near_kernel,
        out_shape=jax.ShapeDtypeStruct((PROJ_ROWS, tokens), BF16),
        in_specs=[VMEM] * 3,
        out_specs=VMEM,
        compiler_params=SMALL,
        cost_estimate=pl.CostEstimate(
            flops=2 * tokens * width * PROJ_ROWS, bytes_accessed=2 * tokens * width, transcendentals=0
        ),
    )(start, kept, near)


def feature_kernel(ex_rows, mixer_ref, ranks_ref, own_ref, other_ref, out_ref):
    tokens = own_ref.shape[1]
    rows = ADAPTER_RANK * ex_rows
    pieces = jnp.concatenate([ranks_ref[...], other_ref[PROJ_ROWS:]], axis=0)
    coeffs = jnp.dot(mixer_ref[...], pieces, preferred_element_type=F32)
    owned = iota((rows, tokens), 1) // SEQ == iota((rows, tokens), 0) % ex_rows
    coeffs = jnp.where(owned, coeffs, 0.0).astype(BF16)
    projected = lax.dot_general(coeffs, own_ref[...], NT, preferred_element_type=F32)
    projected += lax.dot_general(coeffs, other_ref[:PROJ_ROWS], NT, preferred_element_type=F32)
    out_ref[...] = (projected * SCALE).astype(BF16)


def feature_rows(mixer, ranks, own, other, ex_rows):
    return pl.pallas_call(
        functools.partial(feature_kernel, ex_rows),
        out_shape=jax.ShapeDtypeStruct((ADAPTER_RANK * ex_rows, PROJ_ROWS), BF16),
        in_specs=[VMEM] * 4,
        out_specs=VMEM,
        compiler_params=SMALL,
    )(mixer, ranks, own, other)


def fold_ranks(terms):
    half = terms.shape[0] // 2
    folded = terms[:half] + pltpu.roll(terms[half:], LANES - half, 1)
    return jnp.where(iota(folded.shape, 1) % (2 * half) < half, folded, 0.0)


def order_blocks(rows, wide):
    z = lax.axis_index("z")
    rows = jnp.where((z & 2) != 0, pltpu.roll(rows, 2 * wide, 1), rows)
    even = (iota(rows.shape, 1) // wide) % 2 == 0
    swapped = jnp.where(even, pltpu.roll(rows, LANES - wide, 1), pltpu.roll(rows, wide, 1))
    return jnp.where((z & 1) != 0, swapped, rows)


def pair_kernel(ex_rows, near_ref, own_ref, third_got_ref, second_got_ref, first_got_ref, *out_refs):
    keep_ref, send_ref = out_refs
    z = lax.axis_index("z")
    inner = (z == 1) | (z == 2)
    wide = 2 * ex_rows
    total = None
    for row in range(0, own_ref.shape[0], wide):
        part = slice(row, row + wide)
        own, one, two = own_ref[part, :], first_got_ref[part, :], third_got_ref[part, :]
        left = jnp.concatenate([own, near_ref[part, :]], axis=0)
        by_z = [own, jnp.where(inner, one, two), jnp.where(inner, two, one)]
        right = jnp.concatenate(by_z + [second_got_ref[part, :]], axis=0)
        term = lax.dot_general(left, right, NT, preferred_element_type=F32)
        total = term if total is None else total + term
    total = jnp.concatenate([total, total], axis=1)
    keep_ref[...] = order_blocks(fold_ranks(total[:wide]), wide)
    send_ref[...] = order_blocks(fold_ranks(total[wide:]), wide)


def pair_rows(near, own, third, second, first, ex_rows):
    return pl.pallas_call(
        functools.partial(pair_kernel, ex_rows),
        out_shape=[jax.ShapeDtypeStruct((ex_rows, LANES), F32)] * 2,
        in_specs=[VMEM] * 5,
        out_specs=[VMEM] * 2,
        compiler_params=SMALL,
    )(near, own, third, second, first)


def halves_kernel(own_ref, got_ref, keep_ref, send_ref):
    ex_rows, _ = own_ref.shape
    low_x = lax.axis_index("x") == 0
    first = jnp.where(low_x, own_ref[...], got_ref[...])
    second = jnp.where(low_x, got_ref[...], own_ref[...])
    total = first + pltpu.roll(second, ex_rows, 1)
    half = keep_ref.shape[0]
    low = lax.axis_index("tensor") == 0
    keep_ref[...] = jnp.where(low, total[:half], total[half:])
    send_ref[...] = jnp.where(low, total[half:], total[:half])


def join_halves(own, got):
    rows, lanes = own.shape
    return pl.pallas_call(
        halves_kernel,
        out_shape=[jax.ShapeDtypeStruct((rows // 2, lanes), F32)] * 2,
        in_specs=[VMEM] * 2,
        out_specs=[VMEM] * 2,
        compiler_params=SMALL,
    )(own, got)


def sum_kernel(keep_ref, got_ref, out_ref):
    out_ref[...] = (keep_ref[...] + got_ref[...])[:, : out_ref.shape[1]]


def sum_rows(keep, got):
    return pl.pallas_call(
        sum_kernel,
        out_shape=jax.ShapeDtypeStruct((keep.shape[0], LANES // 2), F32),
        in_specs=[VMEM] * 2,
        out_specs=VMEM,
        compiler_params=SMALL,
    )(keep, got)


def swap_cores(value):
    return lax.ppermute(value, "tensor", [(0, 1), (1, 0)])


def swap_across(value):
    return lax.ppermute(value, ("x", "tensor"), [(i, i ^ 3) for i in range(4)])


def swap_x(value):
    return lax.ppermute(value, "x", [(0, 1), (1, 0)])


def step_z(value, targets):
    pairs = []
    for z, target in enumerate(targets):
        for x in range(2):
            for kind in range(2):
                pairs.append(tuple(4 * at + 2 * x + (kind ^ (at // 2)) for at in (z, target)))
    return lax.ppermute(value, BLK + ("tensor",), pairs)


def body(
    hidden, cotangent, token_loss_mask, adapter_down_factor, adapter_up_factor, sign_table_salts
):
    ex_rows, seq, width_half = hidden.shape
    blocks = lax.axis_size("z") * lax.axis_size("x")
    fast = blocks == 8 and ex_rows == 8
    send, ranks, near, start, kept, mixer = far_rows(
        sign_table_salts,
        token_loss_mask,
        adapter_down_factor,
        adapter_up_factor.T,
        hidden.reshape(ex_rows * seq, width_half),
        cotangent.reshape(ex_rows * seq, width_half),
        fast,
    )
    other = swap_cores(send)
    terms = (mixer, ranks, near_rows(start, kept, near), other)
    features = feature_rows(*terms, ex_rows)
    if fast:
        first = step_z(features, (1, 3, 0, 2))
        second = step_z(features, (3, 2, 1, 0))
        third = step_z(features, (2, 0, 3, 1))
        near = swap_x(features)
        keep, send = pair_rows(near, features, third, second, first, ex_rows)
        keep, send = join_halves(keep, swap_across(send))
        return sum_rows(keep, swap_cores(send))
    share = ADAPTER_RANK * PROJ_ROWS // blocks
    parts = features.reshape(ADAPTER_RANK, ex_rows, PROJ_ROWS // share, share)
    parts = parts.swapaxes(1, 2).reshape(blocks, ex_rows, share)
    features = lax.all_to_all(parts, BLK, 0, 0, tiled=True).reshape(blocks * ex_rows, share)
    pairs = jnp.einsum("ep,fp->ef", features, features, preferred_element_type=F32)
    pairs = pairs.reshape(blocks, ex_rows, blocks * ex_rows)
    total = jnp.sum(lax.all_to_all(pairs, BLK, 0, 0, tiled=True), axis=0)
    halves = total.reshape(2, ex_rows // 2, blocks * ex_rows)
    core = lax.axis_index("tensor")
    send = lax.dynamic_index_in_dim(halves, 1 - core, 0, keepdims=False)
    return lax.dynamic_index_in_dim(halves, core, 0, keepdims=False) + swap_cores(send)


def solution(mesh):
    groups, blocks, cores = (mesh.shape[name] for name in ("groups", "blk", "tensor"))
    devices = mesh.devices.reshape(groups, blocks // 2, 2, cores)
    placed = (
        P(("groups", "z", "x"), None, "tensor"),
        P(("groups", "z", "x"), None, "tensor"),
        P(("groups", "z", "x"), None),
        P(None, "tensor"),
        P("tensor", None),
        P(),
    )
    return jax.shard_map(
        body,
        mesh=Mesh(devices, ("groups", "z", "x", "tensor")),
        in_specs=placed,
        out_specs=P(("groups", "z", "x", "tensor"), None),
        check_vma=False,
    )
```

```python
import functools
import math

import jax
import jax.numpy as jnp
from jax import lax
from jax.experimental import pallas as pl
from jax.experimental.pallas import tpu as pltpu
from jax.sharding import Mesh, PartitionSpec as P

MODEL_WIDTH = 4096
ADAPTER_RANK = 16
PROJ_ROWS = 256
SEQ = 64
SCALE = 1.0 / math.sqrt(PROJ_ROWS * ADAPTER_RANK * ADAPTER_RANK * SEQ * MODEL_WIDTH)
PIECES = 3
LANES = 128
BLOCK = (16, 256)
BLK = ("z", "x")

F32 = jnp.float32
BF16 = jnp.bfloat16
I32 = jnp.int32
NT = (((1,), (1,)), ((), ()))
VMEM = pl.BlockSpec(memory_space=pltpu.VMEM)
SMEM = pl.BlockSpec(memory_space=pltpu.SMEM)
HBM = pl.BlockSpec(memory_space=pltpu.HBM)
SMALL = pltpu.CompilerParams(vmem_limit_bytes=16 * 1024 * 1024)

INDEX_MUL = -1640531535
SALT_MUL = 668265263


def int32_wrap(value):
    return (value + 2**31) % 2**32 - 2**31


def hash_sign(hashed):
    hashed = hashed ^ lax.shift_right_logical(hashed, 15)
    hashed = hashed * -2048144789
    hashed = hashed ^ lax.shift_right_logical(hashed, 13)
    hashed = hashed * int32_wrap(-1028477387 << 6)
    hashed = hashed ^ lax.shift_left(hashed, 16)
    return jnp.where(hashed < 0, 1.0, -1.0).astype(F32)


def iota(shape, dim):
    return lax.broadcasted_iota(I32, shape, dim)


def token_row(mask):
    ex_rows, seq = mask.shape
    tokens = ex_rows * seq
    tiled = jnp.concatenate([mask.astype(F32)] * ex_rows, axis=1)
    owner = iota((ex_rows, tokens), 1) // seq == iota((ex_rows, tokens), 0)
    return jnp.sum(jnp.where(owner, tiled, 0.0), axis=0, keepdims=True)


def split_pieces(value):
    pieces = []
    for _ in range(PIECES):
        pieces.append(value.astype(BF16))
        value = value - pieces[-1].astype(F32)
    return jnp.concatenate(pieces, axis=0)


def kind_of(cross):
    core = lax.axis_index("tensor")
    return core ^ (lax.axis_index("z") // (lax.axis_size("z") // 2)) if cross else core


def table_start():
    index = iota(BLOCK, 1) * PROJ_ROWS + iota(BLOCK, 0)
    return index * INDEX_MUL


def sign_rows(start, col):
    high, wide = BLOCK
    rows = [
        hash_sign(start + int32_wrap((col * PROJ_ROWS + row) * INDEX_MUL)).astype(BF16)
        for row in range(0, PROJ_ROWS, high)
    ]
    return rows


def far_kernel(
    cross, ex_rows,
    salts_hbm, mask_hbm, down_hbm, up_hbm, hid_hbm, cot_hbm,
    send_ref, ranks_ref, near_ref, near_factor, start_ref, kept_ref, mixer_ref,
    salts, mask, far_factor, far, sems,
):
    tokens, width = far.shape
    kind = kind_of(cross)
    wide = BLOCK[1]
    share = width // 4
    ends = [0, share, 2 * share, 3 * share, width - wide, width]
    parts = len(ends) - 1

    def copies(inputs, factor, factor_held, held, first):
        out = [pltpu.make_async_copy(factor, factor_held, sems.at[first])]
        for i in range(parts):
            cols = pl.ds(ends[i], ends[i + 1] - ends[i])
            out.append(
                pltpu.make_async_copy(inputs.at[:, cols], held.at[:, cols], sems.at[first + 1 + i])
            )
        return out

    def start_copies(far_inputs, far_part, near_inputs, near_part):
        far_copies = copies(far_inputs, far_part, far_factor, far, 2)
        near_copies = copies(near_inputs, near_part, near_factor, near_ref, parts + 3)
        for copy in far_copies + near_copies:
            copy.start()

    salts_copy = pltpu.make_async_copy(salts_hbm, salts, sems.at[0])
    mask_copy = pltpu.make_async_copy(mask_hbm, mask, sems.at[1])
    salts_copy.start()
    mask_copy.start()

    @pl.when(kind == 0)
    def _():
        start_copies(hid_hbm, down_hbm, cot_hbm, up_hbm)

    @pl.when(kind == 1)
    def _():
        start_copies(cot_hbm, up_hbm, hid_hbm, down_hbm)

    far_waits = copies(hid_hbm, down_hbm, far_factor, far, 2)
    near_waits = copies(hid_hbm, down_hbm, near_factor, near_ref, parts + 3)
    first = lax.axis_index("tensor") * int32_wrap(width * PROJ_ROWS * INDEX_MUL)
    start = table_start() + first
    salts_copy.wait()
    far_start = start + salts[2 - 2 * kind] * SALT_MUL
    start_ref[...] = start + salts[2 * kind] * SALT_MUL
    shape = mixer_ref.shape
    mixed, rank = iota(shape, 0) // ex_rows, iota(shape, 1) % ADAPTER_RANK
    index = (rank * ADAPTER_RANK + mixed) * INDEX_MUL
    mixer_ref[...] = hash_sign(index + salts[1 + 2 * kind] * SALT_MUL).astype(BF16)
    mask_copy.wait()
    counted = token_row(mask[...]) != 0
    far_kept = counted | (kind == 0)
    near_kept = counted | (kind == 1)
    kept_ref[...] = jnp.broadcast_to(jnp.where(near_kept, 1.0, 0.0), kept_ref.shape)
    far_waits[0].wait()
    total = None
    for col in range(0, width, wide):
        part = slice(col, col + wide)
        left = jnp.concatenate(sign_rows(far_start, col) + [far_factor[:, part]], axis=0)
        if col in ends:
            far_waits[1 + ends.index(col)].wait()
        term = lax.dot_general(left, far[:, part], NT, preferred_element_type=F32)
        total = term if total is None else total + term
    total = jnp.where(far_kept, total, 0.0)
    send_ref[...] = total[:PROJ_ROWS].astype(BF16)
    ranks_ref[...] = split_pieces(total[PROJ_ROWS:])
    for wait in near_waits:
        wait.wait()


def far_rows(salts, mask, down, up, hidden, cotangent, cross):
    ex_rows = mask.shape[0]
    tokens, width = hidden.shape
    pieces = PIECES * ADAPTER_RANK
    arrays = (salts, mask, down, up, hidden, cotangent)
    return pl.pallas_call(
        functools.partial(far_kernel, cross, ex_rows),
        out_shape=[
            jax.ShapeDtypeStruct((PROJ_ROWS, tokens), BF16),
            jax.ShapeDtypeStruct((pieces, tokens), BF16),
            jax.ShapeDtypeStruct((tokens, width), BF16),
            jax.ShapeDtypeStruct((ADAPTER_RANK, width), BF16),
            jax.ShapeDtypeStruct(BLOCK, I32),
            jax.ShapeDtypeStruct((8, tokens), F32),
            jax.ShapeDtypeStruct((ADAPTER_RANK * ex_rows, 2 * pieces), BF16),
        ],
        in_specs=[HBM] * 6,
        out_specs=[VMEM] * 7,
        scratch_shapes=[
            pltpu.SMEM(salts.shape, I32),
            pltpu.VMEM(mask.shape, I32),
            pltpu.VMEM((ADAPTER_RANK, width), BF16),
            pltpu.VMEM((tokens, width), BF16),
            pltpu.SemaphoreType.DMA((14,)),
        ],
        compiler_params=SMALL,
    )(*[pltpu.with_memory_space_constraint(x, pltpu.HBM) for x in arrays])


def ranks_kernel(kept_ref, factor_ref, near_ref, out_ref):
    ranks = lax.dot_general(factor_ref[...], near_ref[...], NT, preferred_element_type=F32)
    out_ref[...] = split_pieces(jnp.where(kept_ref[:1] != 0, ranks, 0.0))


def near_ranks(kept, factor, near):
    return pl.pallas_call(
        ranks_kernel,
        out_shape=jax.ShapeDtypeStruct((PIECES * ADAPTER_RANK, near.shape[0]), BF16),
        in_specs=[VMEM] * 3,
        out_specs=VMEM,
        compiler_params=SMALL,
    )(kept, factor, near)


def near_kernel(start_ref, kept_ref, near_ref, _, out_ref):
    start = start_ref[...]
    wide = BLOCK[1]
    total = None
    for col in range(0, near_ref.shape[1], wide):
        left = jnp.concatenate(sign_rows(start, col), axis=0)
        term = lax.dot_general(
            left, near_ref[:, col : col + wide], NT, preferred_element_type=F32
        )
        total = term if total is None else total + term
    out_ref[...] = jnp.where(kept_ref[:1] != 0, total, 0.0).astype(BF16)


def near_rows(start, kept, near, after):
    tokens, width = near.shape
    return pl.pallas_call(
        near_kernel,
        out_shape=jax.ShapeDtypeStruct((PROJ_ROWS, tokens), BF16),
        in_specs=[VMEM] * 4,
        out_specs=VMEM,
        compiler_params=SMALL,
        cost_estimate=pl.CostEstimate(
            flops=2 * tokens * width * PROJ_ROWS, bytes_accessed=2 * tokens * width, transcendentals=0
        ),
    )(start, kept, near, after)


def feature_kernel(ex_rows, mixer_ref, ranks_ref, own_ref, got_ref, got_ranks_ref, out_ref):
    tokens = own_ref.shape[1]
    rows = ADAPTER_RANK * ex_rows
    pieces = jnp.concatenate([ranks_ref[...], got_ranks_ref[...]], axis=0)
    coeffs = jnp.dot(mixer_ref[...], pieces, preferred_element_type=F32)
    owned = iota((rows, tokens), 1) // SEQ == iota((rows, tokens), 0) % ex_rows
    coeffs = jnp.where(owned, coeffs, 0.0).astype(BF16)
    projected = lax.dot_general(coeffs, own_ref[...], NT, preferred_element_type=F32)
    projected += lax.dot_general(coeffs, got_ref[...], NT, preferred_element_type=F32)
    out_ref[...] = (projected * SCALE).astype(BF16)


def feature_rows(mixer, ranks, own, got, got_ranks, ex_rows):
    return pl.pallas_call(
        functools.partial(feature_kernel, ex_rows),
        out_shape=jax.ShapeDtypeStruct((ADAPTER_RANK * ex_rows, PROJ_ROWS), BF16),
        in_specs=[VMEM] * 5,
        out_specs=VMEM,
        compiler_params=SMALL,
    )(mixer, ranks, own, got, got_ranks)


def fold_ranks(terms):
    half = terms.shape[0] // 2
    folded = terms[:half] + pltpu.roll(terms[half:], LANES - half, 1)
    return jnp.where(iota(folded.shape, 1) % (2 * half) < half, folded, 0.0)


def order_blocks(rows, wide):
    z = lax.axis_index("z")
    rows = jnp.where((z & 2) != 0, pltpu.roll(rows, 2 * wide, 1), rows)
    even = (iota(rows.shape, 1) // wide) % 2 == 0
    swapped = jnp.where(even, pltpu.roll(rows, LANES - wide, 1), pltpu.roll(rows, wide, 1))
    return jnp.where((z & 1) != 0, swapped, rows)


def pair_kernel(ex_rows, near_ref, *refs):
    *z_refs, keep_ref, send_ref = refs
    wide = 2 * ex_rows
    total = None
    for row in range(0, near_ref.shape[0], wide):
        part = slice(row, row + wide)
        left = jnp.concatenate([z_refs[0][part, :], near_ref[part, :]], axis=0)
        right = jnp.concatenate([ref[part, :] for ref in z_refs], axis=0)
        term = lax.dot_general(left, right, NT, preferred_element_type=F32)
        total = term if total is None else total + term
    total = jnp.concatenate([total, total], axis=1)
    keep_ref[...] = order_blocks(fold_ranks(total[:wide]), wide)
    send_ref[...] = order_blocks(fold_ranks(total[wide:]), wide)


def pair_rows(near, by_z, ex_rows):
    return pl.pallas_call(
        functools.partial(pair_kernel, ex_rows),
        out_shape=[jax.ShapeDtypeStruct((ex_rows, LANES), F32)] * 2,
        in_specs=[VMEM] * (1 + len(by_z)),
        out_specs=[VMEM] * 2,
        compiler_params=SMALL,
    )(near, *by_z)


def halves_kernel(own_ref, got_ref, keep_ref, send_ref):
    ex_rows, _ = own_ref.shape
    low_x = lax.axis_index("x") == 0
    first = jnp.where(low_x, own_ref[...], got_ref[...])
    second = jnp.where(low_x, got_ref[...], own_ref[...])
    total = first + pltpu.roll(second, ex_rows, 1)
    half = keep_ref.shape[0]
    low = lax.axis_index("tensor") == 0
    keep_ref[...] = jnp.where(low, total[:half], total[half:])
    send_ref[...] = jnp.where(low, total[half:], total[:half])


def join_halves(own, got):
    rows, lanes = own.shape
    return pl.pallas_call(
        halves_kernel,
        out_shape=[jax.ShapeDtypeStruct((rows // 2, lanes), F32)] * 2,
        in_specs=[VMEM] * 2,
        out_specs=[VMEM] * 2,
        compiler_params=SMALL,
    )(own, got)


def sum_kernel(keep_ref, got_ref, out_ref):
    out_ref[...] = (keep_ref[...] + got_ref[...])[:, : out_ref.shape[1]]


def sum_rows(keep, got):
    return pl.pallas_call(
        sum_kernel,
        out_shape=jax.ShapeDtypeStruct((keep.shape[0], LANES // 2), F32),
        in_specs=[VMEM] * 2,
        out_specs=VMEM,
        compiler_params=SMALL,
    )(keep, got)


def swap_cores(value):
    return lax.ppermute(value, "tensor", [(0, 1), (1, 0)])


def swap_across(value):
    return lax.ppermute(value, ("x", "tensor"), [(i, i ^ 3) for i in range(4)])


def swap_x(value):
    return lax.ppermute(value, "x", [(0, 1), (1, 0)])


def swap_z(value, step):
    other = 4 * step + (step > 1)
    return lax.ppermute(value, BLK + ("tensor",), [(i, i ^ other) for i in range(16)])


def body(
    hidden, cotangent, token_loss_mask, adapter_down_factor, adapter_up_factor, sign_table_salts
):
    ex_rows, seq, width_half = hidden.shape
    blocks = lax.axis_size("z") * lax.axis_size("x")
    fast = blocks == 8 and ex_rows == 8
    send, ranks, near, factor, start, kept, mixer = far_rows(
        sign_table_salts,
        token_loss_mask,
        adapter_down_factor,
        adapter_up_factor.T,
        hidden.reshape(ex_rows * seq, width_half),
        cotangent.reshape(ex_rows * seq, width_half),
        fast,
    )
    got = swap_cores(send)
    send = near_ranks(kept, factor, near)
    got_ranks = swap_cores(send)
    terms = (mixer, ranks, near_rows(start, kept, near, send), got, got_ranks)
    features = feature_rows(*terms, ex_rows)
    if fast:
        third = swap_z(features, 3)
        second = swap_z(features, 2)
        first = swap_z(features, 1)
        near = swap_x(features)
        keep, send = pair_rows(near, (features, first, second, third), ex_rows)
        keep, send = join_halves(keep, swap_across(send))
        return sum_rows(keep, swap_cores(send))
    share = ADAPTER_RANK * PROJ_ROWS // blocks
    parts = features.reshape(ADAPTER_RANK, ex_rows, PROJ_ROWS // share, share)
    parts = parts.swapaxes(1, 2).reshape(blocks, ex_rows, share)
    features = lax.all_to_all(parts, BLK, 0, 0, tiled=True).reshape(blocks * ex_rows, share)
    pairs = jnp.einsum("ep,fp->ef", features, features, preferred_element_type=F32)
    pairs = pairs.reshape(blocks, ex_rows, blocks * ex_rows)
    total = jnp.sum(lax.all_to_all(pairs, BLK, 0, 0, tiled=True), axis=0)
    halves = total.reshape(2, ex_rows // 2, blocks * ex_rows)
    core = lax.axis_index("tensor")
    send = lax.dynamic_index_in_dim(halves, 1 - core, 0, keepdims=False)
    return lax.dynamic_index_in_dim(halves, core, 0, keepdims=False) + swap_cores(send)


def solution(mesh):
    groups, blocks, cores = (mesh.shape[name] for name in ("groups", "blk", "tensor"))
    devices = mesh.devices.reshape(groups, blocks // 2, 2, cores)
    placed = (
        P(("groups", "z", "x"), None, "tensor"),
        P(("groups", "z", "x"), None, "tensor"),
        P(("groups", "z", "x"), None),
        P(None, "tensor"),
        P("tensor", None),
        P(),
    )
    return jax.shard_map(
        body,
        mesh=Mesh(devices, ("groups", "z", "x", "tensor")),
        in_specs=placed,
        out_specs=P(("groups", "z", "x", "tensor"), None),
        check_vma=False,
    )
```

```python
import functools
import math

import jax
import jax.numpy as jnp
from jax import lax
from jax.experimental import pallas as pl
from jax.experimental.pallas import tpu as pltpu
from jax.sharding import Mesh, PartitionSpec as P

MODEL_WIDTH = 4096
ADAPTER_RANK = 16
PROJ_ROWS = 256
SEQ = 64
SCALE = 1.0 / math.sqrt(PROJ_ROWS * ADAPTER_RANK * ADAPTER_RANK * SEQ * MODEL_WIDTH)
PIECES = 3
LANES = 128
BLOCK = (16, 256)
LEAD = 3
BLK = ("z", "x")

F32 = jnp.float32
BF16 = jnp.bfloat16
I32 = jnp.int32
NT = (((1,), (1,)), ((), ()))
VMEM = pl.BlockSpec(memory_space=pltpu.VMEM)
SMEM = pl.BlockSpec(memory_space=pltpu.SMEM)
HBM = pl.BlockSpec(memory_space=pltpu.HBM)
SMALL = pltpu.CompilerParams(vmem_limit_bytes=16 * 1024 * 1024)

INDEX_MUL = -1640531535
SALT_MUL = 668265263


def int32_wrap(value):
    return (value + 2**31) % 2**32 - 2**31


def hash_sign(hashed):
    hashed = hashed ^ lax.shift_right_logical(hashed, 15)
    hashed = hashed * -2048144789
    hashed = hashed ^ lax.shift_right_logical(hashed, 13)
    hashed = hashed * int32_wrap(-1028477387 << 6)
    hashed = hashed ^ lax.shift_left(hashed, 16)
    return jnp.where(hashed < 0, 1.0, -1.0).astype(F32)


def iota(shape, dim):
    return lax.broadcasted_iota(I32, shape, dim)


def token_row(mask):
    ex_rows, seq = mask.shape
    tokens = ex_rows * seq
    tiled = jnp.concatenate([mask.astype(F32)] * ex_rows, axis=1)
    owner = iota((ex_rows, tokens), 1) // seq == iota((ex_rows, tokens), 0)
    return jnp.sum(jnp.where(owner, tiled, 0.0), axis=0, keepdims=True)


def split_pieces(value):
    pieces = []
    for _ in range(PIECES):
        pieces.append(value.astype(BF16))
        value = value - pieces[-1].astype(F32)
    return jnp.concatenate(pieces, axis=0)


def kind_of(cross):
    core = lax.axis_index("tensor")
    return core ^ (lax.axis_index("z") // (lax.axis_size("z") // 2)) if cross else core


def table_start():
    index = iota(BLOCK, 1) * PROJ_ROWS + iota(BLOCK, 0)
    return index * INDEX_MUL


def sign_rows(start, col):
    high, wide = BLOCK
    rows = [
        hash_sign(start + int32_wrap((col * PROJ_ROWS + row) * INDEX_MUL)).astype(BF16)
        for row in range(0, PROJ_ROWS, high)
    ]
    return rows


def far_kernel(
    cross, ex_rows,
    salts_hbm, mask_hbm, down_hbm, up_hbm, hid_hbm, cot_hbm,
    send_ref, ranks_ref, near_ref, start_ref, kept_ref, mixer_ref,
    salts, mask, far_factor, near_factor, far, sems,
):
    tokens, width = far.shape
    kind = kind_of(cross)
    wide = BLOCK[1]
    share = width // 4
    ends = [0, share, 2 * share, 3 * share, width - wide, width]
    parts = len(ends) - 1

    def copies(inputs, factor, factor_held, held, first):
        out = [pltpu.make_async_copy(factor, factor_held, sems.at[first])]
        for i in range(parts):
            cols = pl.ds(ends[i], ends[i + 1] - ends[i])
            out.append(
                pltpu.make_async_copy(inputs.at[:, cols], held.at[:, cols], sems.at[first + 1 + i])
            )
        return out

    def start_copies(far_inputs, far_part, near_inputs, near_part):
        far_copies = copies(far_inputs, far_part, far_factor, far, 2)
        near_copies = copies(near_inputs, near_part, near_factor, near_ref, parts + 3)
        for pair in zip(far_copies, near_copies):
            for copy in pair:
                copy.start()

    salts_copy = pltpu.make_async_copy(salts_hbm, salts, sems.at[0])
    mask_copy = pltpu.make_async_copy(mask_hbm, mask, sems.at[1])
    salts_copy.start()
    mask_copy.start()

    @pl.when(kind == 0)
    def _():
        start_copies(hid_hbm, down_hbm, cot_hbm, up_hbm)

    @pl.when(kind == 1)
    def _():
        start_copies(cot_hbm, up_hbm, hid_hbm, down_hbm)

    far_waits = copies(hid_hbm, down_hbm, far_factor, far, 2)
    near_waits = copies(hid_hbm, down_hbm, near_factor, near_ref, parts + 3)
    first = lax.axis_index("tensor") * int32_wrap(width * PROJ_ROWS * INDEX_MUL)
    start = table_start() + first
    salts_copy.wait()
    far_start = start + salts[2 - 2 * kind] * SALT_MUL
    start_ref[...] = start + salts[2 * kind] * SALT_MUL
    shape = mixer_ref.shape
    mixed, rank = iota(shape, 0) // ex_rows, iota(shape, 1) % ADAPTER_RANK
    index = (rank * ADAPTER_RANK + mixed) * INDEX_MUL
    mixer_ref[...] = hash_sign(index + salts[1 + 2 * kind] * SALT_MUL).astype(BF16)
    mask_copy.wait()
    counted = token_row(mask[...]) != 0
    far_kept = counted | (kind == 0)
    near_kept = counted | (kind == 1)
    kept_ref[...] = jnp.broadcast_to(jnp.where(near_kept, 1.0, 0.0), kept_ref.shape)
    ahead = [sign_rows(far_start, col) for col in range(0, LEAD * wide, wide)]
    far_waits[0].wait()
    near_waits[0].wait()
    total = ranks = None
    for col in range(0, width, wide):
        part = slice(col, col + wide)
        if col + LEAD * wide < width:
            ahead.append(sign_rows(far_start, col + LEAD * wide))
        left = jnp.concatenate(ahead.pop(0) + [far_factor[:, part]], axis=0)
        if col in ends:
            far_waits[1 + ends.index(col)].wait()
            near_waits[1 + ends.index(col)].wait()
        term = lax.dot_general(left, far[:, part], NT, preferred_element_type=F32)
        total = term if total is None else total + term
        term = lax.dot_general(
            near_factor[:, part], near_ref[:, part], NT, preferred_element_type=F32
        )
        ranks = term if ranks is None else ranks + term
    total = jnp.where(far_kept, total, 0.0)
    send_ref[:PROJ_ROWS] = total[:PROJ_ROWS].astype(BF16)
    ranks_ref[...] = split_pieces(total[PROJ_ROWS:])
    send_ref[PROJ_ROWS:] = split_pieces(jnp.where(near_kept, ranks, 0.0))


def far_rows(salts, mask, down, up, hidden, cotangent, cross):
    ex_rows = mask.shape[0]
    tokens, width = hidden.shape
    pieces = PIECES * ADAPTER_RANK
    arrays = (salts, mask, down, up, hidden, cotangent)
    return pl.pallas_call(
        functools.partial(far_kernel, cross, ex_rows),
        out_shape=[
            jax.ShapeDtypeStruct((PROJ_ROWS + pieces, tokens), BF16),
            jax.ShapeDtypeStruct((pieces, tokens), BF16),
            jax.ShapeDtypeStruct((tokens, width), BF16),
            jax.ShapeDtypeStruct(BLOCK, I32),
            jax.ShapeDtypeStruct((8, tokens), F32),
            jax.ShapeDtypeStruct((ADAPTER_RANK * ex_rows, 2 * pieces), BF16),
        ],
        in_specs=[HBM] * 6,
        out_specs=[VMEM] * 6,
        scratch_shapes=[
            pltpu.SMEM(salts.shape, I32),
            pltpu.VMEM(mask.shape, I32),
            pltpu.VMEM((ADAPTER_RANK, width), BF16),
            pltpu.VMEM((ADAPTER_RANK, width), BF16),
            pltpu.VMEM((tokens, width), BF16),
            pltpu.SemaphoreType.DMA((14,)),
        ],
        compiler_params=SMALL,
    )(*[pltpu.with_memory_space_constraint(x, pltpu.HBM) for x in arrays])


def near_kernel(start_ref, kept_ref, near_ref, out_ref):
    start = start_ref[...]
    wide = BLOCK[1]
    total = None
    for col in range(0, near_ref.shape[1], wide):
        left = jnp.concatenate(sign_rows(start, col), axis=0)
        term = lax.dot_general(
            left, near_ref[:, col : col + wide], NT, preferred_element_type=F32
        )
        total = term if total is None else total + term
    out_ref[...] = jnp.where(kept_ref[:1] != 0, total, 0.0).astype(BF16)


def near_rows(start, kept, near):
    tokens, width = near.shape
    return pl.pallas_call(
        near_kernel,
        out_shape=jax.ShapeDtypeStruct((PROJ_ROWS, tokens), BF16),
        in_specs=[VMEM] * 3,
        out_specs=VMEM,
        compiler_params=SMALL,
        cost_estimate=pl.CostEstimate(
            flops=2 * tokens * width * PROJ_ROWS, bytes_accessed=2 * tokens * width, transcendentals=0
        ),
    )(start, kept, near)


def feature_kernel(ex_rows, mixer_ref, ranks_ref, own_ref, other_ref, out_ref):
    tokens = own_ref.shape[1]
    rows = ADAPTER_RANK * ex_rows
    pieces = jnp.concatenate([ranks_ref[...], other_ref[PROJ_ROWS:]], axis=0)
    coeffs = jnp.dot(mixer_ref[...], pieces, preferred_element_type=F32)
    owned = iota((rows, tokens), 1) // SEQ == iota((rows, tokens), 0) % ex_rows
    coeffs = jnp.where(owned, coeffs, 0.0).astype(BF16)
    projected = lax.dot_general(coeffs, own_ref[...], NT, preferred_element_type=F32)
    projected += lax.dot_general(coeffs, other_ref[:PROJ_ROWS], NT, preferred_element_type=F32)
    out_ref[...] = (projected * SCALE).astype(BF16)


def feature_rows(mixer, ranks, own, other, ex_rows):
    return pl.pallas_call(
        functools.partial(feature_kernel, ex_rows),
        out_shape=jax.ShapeDtypeStruct((ADAPTER_RANK * ex_rows, PROJ_ROWS), BF16),
        in_specs=[VMEM] * 4,
        out_specs=VMEM,
        compiler_params=SMALL,
    )(mixer, ranks, own, other)


def fold_ranks(terms):
    half = terms.shape[0] // 2
    folded = terms[:half] + pltpu.roll(terms[half:], LANES - half, 1)
    return jnp.where(iota(folded.shape, 1) % (2 * half) < half, folded, 0.0)


def order_blocks(rows, wide):
    z = lax.axis_index("z")
    rows = jnp.where((z & 2) != 0, pltpu.roll(rows, 2 * wide, 1), rows)
    even = (iota(rows.shape, 1) // wide) % 2 == 0
    swapped = jnp.where(even, pltpu.roll(rows, LANES - wide, 1), pltpu.roll(rows, wide, 1))
    return jnp.where((z & 1) != 0, swapped, rows)


def pair_kernel(ex_rows, near_ref, *refs):
    *z_refs, keep_ref, send_ref = refs
    wide = 2 * ex_rows
    total = None
    for row in range(0, near_ref.shape[0], wide):
        part = slice(row, row + wide)
        left = jnp.concatenate([z_refs[0][part, :], near_ref[part, :]], axis=0)
        right = jnp.concatenate([ref[part, :] for ref in z_refs], axis=0)
        term = lax.dot_general(left, right, NT, preferred_element_type=F32)
        total = term if total is None else total + term
    total = jnp.concatenate([total, total], axis=1)
    keep_ref[...] = order_blocks(fold_ranks(total[:wide]), wide)
    send_ref[...] = order_blocks(fold_ranks(total[wide:]), wide)


def pair_rows(near, by_z, ex_rows):
    return pl.pallas_call(
        functools.partial(pair_kernel, ex_rows),
        out_shape=[jax.ShapeDtypeStruct((ex_rows, LANES), F32)] * 2,
        in_specs=[VMEM] * (1 + len(by_z)),
        out_specs=[VMEM] * 2,
        compiler_params=SMALL,
    )(near, *by_z)


def halves_kernel(own_ref, got_ref, keep_ref, send_ref):
    ex_rows, _ = own_ref.shape
    low_x = lax.axis_index("x") == 0
    first = jnp.where(low_x, own_ref[...], got_ref[...])
    second = jnp.where(low_x, got_ref[...], own_ref[...])
    total = first + pltpu.roll(second, ex_rows, 1)
    half = keep_ref.shape[0]
    low = lax.axis_index("tensor") == 0
    keep_ref[...] = jnp.where(low, total[:half], total[half:])
    send_ref[...] = jnp.where(low, total[half:], total[:half])


def join_halves(own, got):
    rows, lanes = own.shape
    return pl.pallas_call(
        halves_kernel,
        out_shape=[jax.ShapeDtypeStruct((rows // 2, lanes), F32)] * 2,
        in_specs=[VMEM] * 2,
        out_specs=[VMEM] * 2,
        compiler_params=SMALL,
    )(own, got)


def sum_kernel(keep_ref, got_ref, out_ref):
    out_ref[...] = (keep_ref[...] + got_ref[...])[:, : out_ref.shape[1]]


def sum_rows(keep, got):
    return pl.pallas_call(
        sum_kernel,
        out_shape=jax.ShapeDtypeStruct((keep.shape[0], LANES // 2), F32),
        in_specs=[VMEM] * 2,
        out_specs=VMEM,
        compiler_params=SMALL,
    )(keep, got)


def swap_cores(value):
    return lax.ppermute(value, "tensor", [(0, 1), (1, 0)])


def swap_across(value):
    return lax.ppermute(value, ("x", "tensor"), [(i, i ^ 3) for i in range(4)])


def swap_x(value):
    return lax.ppermute(value, "x", [(0, 1), (1, 0)])


def swap_z(value, step):
    other = 4 * step + (step > 1)
    return lax.ppermute(value, BLK + ("tensor",), [(i, i ^ other) for i in range(16)])


def body(
    hidden, cotangent, token_loss_mask, adapter_down_factor, adapter_up_factor, sign_table_salts
):
    ex_rows, seq, width_half = hidden.shape
    blocks = lax.axis_size("z") * lax.axis_size("x")
    fast = blocks == 8 and ex_rows == 8
    send, ranks, near, start, kept, mixer = far_rows(
        sign_table_salts,
        token_loss_mask,
        adapter_down_factor,
        adapter_up_factor.T,
        hidden.reshape(ex_rows * seq, width_half),
        cotangent.reshape(ex_rows * seq, width_half),
        fast,
    )
    other = swap_cores(send)
    terms = (mixer, ranks, near_rows(start, kept, near), other)
    features = feature_rows(*terms, ex_rows)
    if fast:
        third = swap_z(features, 3)
        second = swap_z(features, 2)
        first = swap_z(features, 1)
        near = swap_x(features)
        keep, send = pair_rows(near, (features, first, second, third), ex_rows)
        keep, send = join_halves(keep, swap_across(send))
        return sum_rows(keep, swap_cores(send))
    share = ADAPTER_RANK * PROJ_ROWS // blocks
    parts = features.reshape(ADAPTER_RANK, ex_rows, PROJ_ROWS // share, share)
    parts = parts.swapaxes(1, 2).reshape(blocks, ex_rows, share)
    features = lax.all_to_all(parts, BLK, 0, 0, tiled=True).reshape(blocks * ex_rows, share)
    pairs = jnp.einsum("ep,fp->ef", features, features, preferred_element_type=F32)
    pairs = pairs.reshape(blocks, ex_rows, blocks * ex_rows)
    total = jnp.sum(lax.all_to_all(pairs, BLK, 0, 0, tiled=True), axis=0)
    halves = total.reshape(2, ex_rows // 2, blocks * ex_rows)
    core = lax.axis_index("tensor")
    send = lax.dynamic_index_in_dim(halves, 1 - core, 0, keepdims=False)
    return lax.dynamic_index_in_dim(halves, core, 0, keepdims=False) + swap_cores(send)


def solution(mesh):
    groups, blocks, cores = (mesh.shape[name] for name in ("groups", "blk", "tensor"))
    devices = mesh.devices.reshape(groups, blocks // 2, 2, cores)
    placed = (
        P(("groups", "z", "x"), None, "tensor"),
        P(("groups", "z", "x"), None, "tensor"),
        P(("groups", "z", "x"), None),
        P(None, "tensor"),
        P("tensor", None),
        P(),
    )
    return jax.shard_map(
        body,
        mesh=Mesh(devices, ("groups", "z", "x", "tensor")),
        in_specs=placed,
        out_specs=P(("groups", "z", "x", "tensor"), None),
        check_vma=False,
    )
```

```python
import functools
import math

import jax
import jax.numpy as jnp
from jax import lax
from jax.experimental import pallas as pl
from jax.experimental.pallas import tpu as pltpu
from jax.sharding import Mesh, PartitionSpec as P

MODEL_WIDTH = 4096
ADAPTER_RANK = 16
PROJ_ROWS = 256
SEQ = 64
SCALE = 1.0 / math.sqrt(PROJ_ROWS * ADAPTER_RANK * ADAPTER_RANK * SEQ * MODEL_WIDTH)
PIECES = 3
LANES = 128
BLOCK = (16, 256)
LEAD = 3
BLK = ("z", "x")

F32 = jnp.float32
BF16 = jnp.bfloat16
I32 = jnp.int32
NT = (((1,), (1,)), ((), ()))
VMEM = pl.BlockSpec(memory_space=pltpu.VMEM)
SMEM = pl.BlockSpec(memory_space=pltpu.SMEM)
HBM = pl.BlockSpec(memory_space=pltpu.HBM)
SMALL = pltpu.CompilerParams(vmem_limit_bytes=16 * 1024 * 1024)

INDEX_MUL = -1640531535
SALT_MUL = 668265263


def int32_wrap(value):
    return (value + 2**31) % 2**32 - 2**31


def hash_sign(hashed):
    hashed = hashed ^ lax.shift_right_logical(hashed, 15)
    hashed = hashed * -2048144789
    hashed = hashed ^ lax.shift_right_logical(hashed, 13)
    hashed = hashed * int32_wrap(-1028477387 << 6)
    hashed = hashed ^ lax.shift_left(hashed, 16)
    return jnp.where(hashed < 0, 1.0, -1.0).astype(F32)


def iota(shape, dim):
    return lax.broadcasted_iota(I32, shape, dim)


def token_row(mask):
    ex_rows, seq = mask.shape
    tokens = ex_rows * seq
    tiled = jnp.concatenate([mask.astype(F32)] * ex_rows, axis=1)
    owner = iota((ex_rows, tokens), 1) // seq == iota((ex_rows, tokens), 0)
    return jnp.sum(jnp.where(owner, tiled, 0.0), axis=0, keepdims=True)


def split_pieces(value):
    pieces = []
    for _ in range(PIECES):
        pieces.append(value.astype(BF16))
        value = value - pieces[-1].astype(F32)
    return jnp.concatenate(pieces, axis=0)


def kind_of(cross):
    core = lax.axis_index("tensor")
    return core ^ (lax.axis_index("z") // (lax.axis_size("z") // 2)) if cross else core


def table_start():
    index = iota(BLOCK, 1) * PROJ_ROWS + iota(BLOCK, 0)
    return index * INDEX_MUL


def sign_rows(start, col):
    high, wide = BLOCK
    rows = [
        hash_sign(start + int32_wrap((col * PROJ_ROWS + row) * INDEX_MUL)).astype(BF16)
        for row in range(0, PROJ_ROWS, high)
    ]
    return rows


def far_kernel(
    cross, ex_rows,
    salts_hbm, mask_hbm, down_hbm, up_hbm, hid_hbm, cot_hbm,
    send_ref, ranks_ref, near_ref, start_ref, kept_ref, mixer_ref,
    salts, mask, far_factor, near_factor, far, sems,
):
    tokens, width = far.shape
    kind = kind_of(cross)
    wide = BLOCK[1]
    share = width // 4
    ends = [0, share, 2 * share, 3 * share, width - wide, width]
    parts = len(ends) - 1

    def copies(inputs, factor, factor_held, held, first):
        out = [pltpu.make_async_copy(factor, factor_held, sems.at[first])]
        for i in range(parts):
            cols = pl.ds(ends[i], ends[i + 1] - ends[i])
            out.append(
                pltpu.make_async_copy(inputs.at[:, cols], held.at[:, cols], sems.at[first + 1 + i])
            )
        return out

    def start_copies(far_inputs, far_part, near_inputs, near_part):
        far_copies = copies(far_inputs, far_part, far_factor, far, 2)
        near_copies = copies(near_inputs, near_part, near_factor, near_ref, parts + 3)
        for pair in zip(far_copies, near_copies):
            for copy in pair:
                copy.start()

    salts_copy = pltpu.make_async_copy(salts_hbm, salts, sems.at[0])
    mask_copy = pltpu.make_async_copy(mask_hbm, mask, sems.at[1])
    salts_copy.start()
    mask_copy.start()

    @pl.when(kind == 0)
    def _():
        start_copies(hid_hbm, down_hbm, cot_hbm, up_hbm)

    @pl.when(kind == 1)
    def _():
        start_copies(cot_hbm, up_hbm, hid_hbm, down_hbm)

    far_waits = copies(hid_hbm, down_hbm, far_factor, far, 2)
    near_waits = copies(hid_hbm, down_hbm, near_factor, near_ref, parts + 3)
    first = lax.axis_index("tensor") * int32_wrap(width * PROJ_ROWS * INDEX_MUL)
    start = table_start() + first
    salts_copy.wait()
    far_start = start + salts[2 - 2 * kind] * SALT_MUL
    start_ref[...] = start + salts[2 * kind] * SALT_MUL
    shape = mixer_ref.shape
    mixed, rank = iota(shape, 0) // ex_rows, iota(shape, 1) % ADAPTER_RANK
    index = (rank * ADAPTER_RANK + mixed) * INDEX_MUL
    mixer_ref[...] = hash_sign(index + salts[1 + 2 * kind] * SALT_MUL).astype(BF16)
    mask_copy.wait()
    counted = token_row(mask[...]) != 0
    far_kept = counted | (kind == 0)
    near_kept = counted | (kind == 1)
    kept_ref[...] = jnp.broadcast_to(jnp.where(near_kept, 1.0, 0.0), kept_ref.shape)
    ahead = [sign_rows(far_start, col) for col in range(0, LEAD * wide, wide)]
    far_waits[0].wait()
    near_waits[0].wait()
    total = ranks = None
    for col in range(0, width, wide):
        part = slice(col, col + wide)
        if col + LEAD * wide < width:
            ahead.append(sign_rows(far_start, col + LEAD * wide))
        left = jnp.concatenate(ahead.pop(0) + [far_factor[:, part]], axis=0)
        if col in ends:
            far_waits[1 + ends.index(col)].wait()
            near_waits[1 + ends.index(col)].wait()
        term = lax.dot_general(left, far[:, part], NT, preferred_element_type=F32)
        total = term if total is None else total + term
        if col + wide in ends[-2:]:
            part = slice(0 if ranks is None else ends[-2], col + wide)
            term = lax.dot_general(
                near_factor[:, part], near_ref[:, part], NT, preferred_element_type=F32
            )
            ranks = term if ranks is None else ranks + term
    total = jnp.where(far_kept, total, 0.0)
    send_ref[:PROJ_ROWS] = total[:PROJ_ROWS].astype(BF16)
    ranks_ref[...] = split_pieces(total[PROJ_ROWS:])
    send_ref[PROJ_ROWS:] = split_pieces(jnp.where(near_kept, ranks, 0.0))


def far_rows(salts, mask, down, up, hidden, cotangent, cross):
    ex_rows = mask.shape[0]
    tokens, width = hidden.shape
    pieces = PIECES * ADAPTER_RANK
    arrays = (salts, mask, down, up, hidden, cotangent)
    return pl.pallas_call(
        functools.partial(far_kernel, cross, ex_rows),
        out_shape=[
            jax.ShapeDtypeStruct((PROJ_ROWS + pieces, tokens), BF16),
            jax.ShapeDtypeStruct((pieces, tokens), BF16),
            jax.ShapeDtypeStruct((tokens, width), BF16),
            jax.ShapeDtypeStruct(BLOCK, I32),
            jax.ShapeDtypeStruct((8, tokens), F32),
            jax.ShapeDtypeStruct((ADAPTER_RANK * ex_rows, 2 * pieces), BF16),
        ],
        in_specs=[HBM] * 6,
        out_specs=[VMEM] * 6,
        scratch_shapes=[
            pltpu.SMEM(salts.shape, I32),
            pltpu.VMEM(mask.shape, I32),
            pltpu.VMEM((ADAPTER_RANK, width), BF16),
            pltpu.VMEM((ADAPTER_RANK, width), BF16),
            pltpu.VMEM((tokens, width), BF16),
            pltpu.SemaphoreType.DMA((14,)),
        ],
        compiler_params=SMALL,
    )(*[pltpu.with_memory_space_constraint(x, pltpu.HBM) for x in arrays])


def near_kernel(start_ref, kept_ref, near_ref, out_ref):
    start = start_ref[...]
    wide = BLOCK[1]
    total = None
    for col in range(0, near_ref.shape[1], wide):
        left = jnp.concatenate(sign_rows(start, col), axis=0)
        term = lax.dot_general(
            left, near_ref[:, col : col + wide], NT, preferred_element_type=F32
        )
        total = term if total is None else total + term
    out_ref[...] = jnp.where(kept_ref[:1] != 0, total, 0.0).astype(BF16)


def near_rows(start, kept, near):
    tokens, width = near.shape
    return pl.pallas_call(
        near_kernel,
        out_shape=jax.ShapeDtypeStruct((PROJ_ROWS, tokens), BF16),
        in_specs=[VMEM] * 3,
        out_specs=VMEM,
        compiler_params=SMALL,
        cost_estimate=pl.CostEstimate(
            flops=2 * tokens * width * PROJ_ROWS, bytes_accessed=2 * tokens * width, transcendentals=0
        ),
    )(start, kept, near)


def feature_kernel(ex_rows, mixer_ref, ranks_ref, own_ref, other_ref, out_ref):
    tokens = own_ref.shape[1]
    rows = ADAPTER_RANK * ex_rows
    pieces = jnp.concatenate([ranks_ref[...], other_ref[PROJ_ROWS:]], axis=0)
    coeffs = jnp.dot(mixer_ref[...], pieces, preferred_element_type=F32)
    owned = iota((rows, tokens), 1) // SEQ == iota((rows, tokens), 0) % ex_rows
    coeffs = jnp.where(owned, coeffs, 0.0).astype(BF16)
    projected = lax.dot_general(coeffs, own_ref[...], NT, preferred_element_type=F32)
    projected += lax.dot_general(coeffs, other_ref[:PROJ_ROWS], NT, preferred_element_type=F32)
    out_ref[...] = (projected * SCALE).astype(BF16)


def feature_rows(mixer, ranks, own, other, ex_rows):
    return pl.pallas_call(
        functools.partial(feature_kernel, ex_rows),
        out_shape=jax.ShapeDtypeStruct((ADAPTER_RANK * ex_rows, PROJ_ROWS), BF16),
        in_specs=[VMEM] * 4,
        out_specs=VMEM,
        compiler_params=SMALL,
    )(mixer, ranks, own, other)


def fold_ranks(terms):
    half = terms.shape[0] // 2
    folded = terms[:half] + pltpu.roll(terms[half:], LANES - half, 1)
    return jnp.where(iota(folded.shape, 1) % (2 * half) < half, folded, 0.0)


def order_blocks(rows, wide):
    z = lax.axis_index("z")
    rows = jnp.where((z & 2) != 0, pltpu.roll(rows, 2 * wide, 1), rows)
    even = (iota(rows.shape, 1) // wide) % 2 == 0
    swapped = jnp.where(even, pltpu.roll(rows, LANES - wide, 1), pltpu.roll(rows, wide, 1))
    return jnp.where((z & 1) != 0, swapped, rows)


def pair_kernel(ex_rows, near_ref, *refs):
    *z_refs, keep_ref, send_ref = refs
    wide = 2 * ex_rows
    total = None
    for row in range(0, near_ref.shape[0], wide):
        part = slice(row, row + wide)
        left = jnp.concatenate([z_refs[0][part, :], near_ref[part, :]], axis=0)
        right = jnp.concatenate([ref[part, :] for ref in z_refs], axis=0)
        term = lax.dot_general(left, right, NT, preferred_element_type=F32)
        total = term if total is None else total + term
    total = jnp.concatenate([total, total], axis=1)
    keep_ref[...] = order_blocks(fold_ranks(total[:wide]), wide)
    send_ref[...] = order_blocks(fold_ranks(total[wide:]), wide)


def pair_rows(near, by_z, ex_rows):
    return pl.pallas_call(
        functools.partial(pair_kernel, ex_rows),
        out_shape=[jax.ShapeDtypeStruct((ex_rows, LANES), F32)] * 2,
        in_specs=[VMEM] * (1 + len(by_z)),
        out_specs=[VMEM] * 2,
        compiler_params=SMALL,
    )(near, *by_z)


def halves_kernel(own_ref, got_ref, keep_ref, send_ref):
    ex_rows, _ = own_ref.shape
    low_x = lax.axis_index("x") == 0
    first = jnp.where(low_x, own_ref[...], got_ref[...])
    second = jnp.where(low_x, got_ref[...], own_ref[...])
    total = first + pltpu.roll(second, ex_rows, 1)
    half = keep_ref.shape[0]
    low = lax.axis_index("tensor") == 0
    keep_ref[...] = jnp.where(low, total[:half], total[half:])
    send_ref[...] = jnp.where(low, total[half:], total[:half])


def join_halves(own, got):
    rows, lanes = own.shape
    return pl.pallas_call(
        halves_kernel,
        out_shape=[jax.ShapeDtypeStruct((rows // 2, lanes), F32)] * 2,
        in_specs=[VMEM] * 2,
        out_specs=[VMEM] * 2,
        compiler_params=SMALL,
    )(own, got)


def sum_kernel(keep_ref, got_ref, out_ref):
    out_ref[...] = (keep_ref[...] + got_ref[...])[:, : out_ref.shape[1]]


def sum_rows(keep, got):
    return pl.pallas_call(
        sum_kernel,
        out_shape=jax.ShapeDtypeStruct((keep.shape[0], LANES // 2), F32),
        in_specs=[VMEM] * 2,
        out_specs=VMEM,
        compiler_params=SMALL,
    )(keep, got)


def swap_cores(value):
    return lax.ppermute(value, "tensor", [(0, 1), (1, 0)])


def swap_across(value):
    return lax.ppermute(value, ("x", "tensor"), [(i, i ^ 3) for i in range(4)])


def swap_x(value):
    return lax.ppermute(value, "x", [(0, 1), (1, 0)])


def swap_z(value, step):
    other = 4 * step + (step > 1)
    return lax.ppermute(value, BLK + ("tensor",), [(i, i ^ other) for i in range(16)])


def body(
    hidden, cotangent, token_loss_mask, adapter_down_factor, adapter_up_factor, sign_table_salts
):
    ex_rows, seq, width_half = hidden.shape
    blocks = lax.axis_size("z") * lax.axis_size("x")
    fast = blocks == 8 and ex_rows == 8
    send, ranks, near, start, kept, mixer = far_rows(
        sign_table_salts,
        token_loss_mask,
        adapter_down_factor,
        adapter_up_factor.T,
        hidden.reshape(ex_rows * seq, width_half),
        cotangent.reshape(ex_rows * seq, width_half),
        fast,
    )
    other = swap_cores(send)
    terms = (mixer, ranks, near_rows(start, kept, near), other)
    features = feature_rows(*terms, ex_rows)
    if fast:
        third = swap_z(features, 3)
        second = swap_z(features, 2)
        first = swap_z(features, 1)
        near = swap_x(features)
        keep, send = pair_rows(near, (features, first, second, third), ex_rows)
        keep, send = join_halves(keep, swap_across(send))
        return sum_rows(keep, swap_cores(send))
    share = ADAPTER_RANK * PROJ_ROWS // blocks
    parts = features.reshape(ADAPTER_RANK, ex_rows, PROJ_ROWS // share, share)
    parts = parts.swapaxes(1, 2).reshape(blocks, ex_rows, share)
    features = lax.all_to_all(parts, BLK, 0, 0, tiled=True).reshape(blocks * ex_rows, share)
    pairs = jnp.einsum("ep,fp->ef", features, features, preferred_element_type=F32)
    pairs = pairs.reshape(blocks, ex_rows, blocks * ex_rows)
    total = jnp.sum(lax.all_to_all(pairs, BLK, 0, 0, tiled=True), axis=0)
    halves = total.reshape(2, ex_rows // 2, blocks * ex_rows)
    core = lax.axis_index("tensor")
    send = lax.dynamic_index_in_dim(halves, 1 - core, 0, keepdims=False)
    return lax.dynamic_index_in_dim(halves, core, 0, keepdims=False) + swap_cores(send)


def solution(mesh):
    groups, blocks, cores = (mesh.shape[name] for name in ("groups", "blk", "tensor"))
    devices = mesh.devices.reshape(groups, blocks // 2, 2, cores)
    placed = (
        P(("groups", "z", "x"), None, "tensor"),
        P(("groups", "z", "x"), None, "tensor"),
        P(("groups", "z", "x"), None),
        P(None, "tensor"),
        P("tensor", None),
        P(),
    )
    return jax.shard_map(
        body,
        mesh=Mesh(devices, ("groups", "z", "x", "tensor")),
        in_specs=placed,
        out_specs=P(("groups", "z", "x", "tensor"), None),
        check_vma=False,
    )
```
